32 devices in a mesh: section: 2 (over x), dp: 16 (over z, y, core).
Axes of the slice: x: 2, y: 2, z: 4, core: 2. Of those that a mesh axis runs over, the one named last changes fastest.
Arguments:
- tokens: bfloat16 [15360, 768], P('dp'), may hold values from -6 to 6
- cotangent: bfloat16 [15360, 768], P('dp'), may hold values from -6 to 6
- lengths: int32 [96], P('dp'), may hold values from 96 to 160, as said below
- spans: int32 [96, 2], P('dp'), may hold values from 1 to 79, as said below
- query_weight: bfloat16 [2, 768, 768], P('section'), may hold values from -0.21875 to 0.21875
- key_weight: bfloat16 [2, 768, 768], P('section'), may hold values from -0.21875 to 0.21875
- value_weight: bfloat16 [2, 768, 768], P('section'), may hold values from -0.21875 to 0.21875
- out_weight: bfloat16 [2, 768, 768], P('section'), may hold values from -0.875 to 0.875
- up_weight: bfloat16 [2, 768, 3072], P('section'), may hold values from -0.21875 to 0.21875
- down_weight: bfloat16 [2, 3072, 768], P('section'), may hold values from -0.109375 to 0.109375
- bias_rows: bfloat16 [2, 4, 768], P('section'), may hold values from -3 to 3
- up_bias: bfloat16 [2, 3072], P('section'), may hold values from -3 to 3
- norm_gains: bfloat16 [2, 2, 768], P('section'), may hold values from 0.5 to 1.5
- norm_shifts: bfloat16 [2, 2, 768], P('section'), may hold values from -2 to 2
Outputs:
- activations: bfloat16 [2, 15360, 768], P('section', 'dp')
- input_grads: float32 [2, 15360, 768], P('section', 'dp')
- query_grad: float32 [2, 768, 768], P('section')
- key_grad: float32 [2, 768, 768], P('section')
- value_grad: float32 [2, 768, 768], P('section')
- out_grad: float32 [2, 768, 768], P('section')
- up_grad: float32 [2, 768, 3072], P('section')
- down_grad: float32 [2, 3072, 768], P('section')
- bias_grad: float32 [2, 4, 768], P('section')
- up_bias_grad: float32 [2, 3072], P('section')
- gain_grad: float32 [2, 2, 768], P('section')
- shift_grad: float32 [2, 2, 768], P('section')
The draws below stay inside these ranges and needn't reach their ends.
Inputs may be any that keep to these rules, and one draw needn't show every extreme that they name: `lengths`: the first chain of each index of dp (chain numbers that are multiples of 6) has exactly 160 residues. For each chain, 1 <= spans[c, 0] <= 40 and 2 <= spans[c, 1] - spans[c, 0] < 40, so a span lies inside the chain's residues.
All inputs are finite; a program needn't handle non-finite values.
Results may differ from the reference program's by a relative error of at most 0.024.
Values may be sent and summed in bfloat16 or wider, within the bound.
A program may use at most 256 MiB of HBM per device.

```python
import jax
import jax.numpy as jnp
from jax import lax

D = 768
HEADS = 12
HEAD_DIM = 64
FF = 3072
LENGTH = 160
MICRO = 2
CHAINS_MB = 3
LAYERS = 2
CHAINS = 96
TOKENS = 15360


def draw_lengths(key, part):
    key = jax.random.fold_in(key, 11)
    draws = jax.random.randint(key, (CHAINS,), 0, 97, dtype=jnp.int32)
    shortfall = 2 * LENGTH // 5 * draws * draws * draws // (96 * 96 * 96)
    firsts = jnp.arange(CHAINS, dtype=jnp.int32) % (MICRO * CHAINS_MB) == 0
    return jnp.where(firsts, LENGTH, LENGTH - shortfall).astype(jnp.int32)


def draw_spans(key, part):
    key = jax.random.fold_in(key, 23)
    start_key, width_key = jax.random.split(key)
    starts = jax.random.randint(start_key, (CHAINS,), 1, LENGTH // 4 + 1, dtype=jnp.int32)
    widths = jax.random.randint(width_key, (CHAINS,), 2, LENGTH // 4, dtype=jnp.int32)
    return jnp.stack([starts, starts + widths], axis=1).astype(jnp.int32)


def steps_of(key, shape, cuts, least, high):
    level = 1.0
    for dim, shards_of in cuts:
        heights = jax.random.uniform(jax.random.fold_in(jax.random.fold_in(key, 6), dim), (shards_of,), jnp.float32, least / len(cuts), high / len(cuts))
        level = level * jnp.repeat(jnp.exp(heights), shape[dim] // shards_of).reshape((-1,) + (1,) * (len(shape) - 1 - dim))
    return level


def normal_values(own_key, dims, spread, bound, cuts=(), held_as=jnp.bfloat16):
    drawn = jax.random.normal(own_key, dims, jnp.float32) * spread
    if len(cuts) > 0:
        drawn = steps_of(own_key, dims, cuts, -0.22, 0.18) * drawn
    return jnp.clip(drawn, min=-bound, max=bound).astype(held_as)


def setup_inputs(seed: int = 0) -> dict:
    streams_of = jax.random.split(jax.random.key(seed), 15)
    return {
        "tokens": normal_values(streams_of[0], (TOKENS, D), 1.0, 6.0, ((0, 16),)),
        "cotangent": normal_values(streams_of[1], (TOKENS, D), 1.0, 6.0, ((0, 16),)),
        "lengths": draw_lengths(jax.random.fold_in(streams_of[14], 71), 0),
        "spans": draw_spans(jax.random.fold_in(streams_of[14], 71), 0),
        "query_weight": normal_values(streams_of[4], (LAYERS, D, D), D ** -0.5, 0.21875, ((0, 2),)),
        "key_weight": normal_values(streams_of[5], (LAYERS, D, D), D ** -0.5, 0.21875, ((0, 2),)),
        "value_weight": normal_values(streams_of[6], (LAYERS, D, D), D ** -0.5, 0.21875, ((0, 2),)),
        "out_weight": normal_values(streams_of[7], (LAYERS, D, D), (D // 16) ** -0.5, 0.875, ((0, 2),)),
        "up_weight": normal_values(streams_of[8], (LAYERS, D, FF), D ** -0.5, 0.21875, ((0, 2),)),
        "down_weight": normal_values(streams_of[9], (LAYERS, FF, D), FF ** -0.5, 0.109375, ((0, 2),)),
        "bias_rows": normal_values(streams_of[10], (LAYERS, 4, D), 0.5, 3.0, ((0, 2),)),
        "up_bias": normal_values(streams_of[11], (LAYERS, FF), 0.5, 3.0, ((0, 2),)),
        "norm_gains": jnp.clip(1.0 + 0.1 * jax.random.normal(streams_of[12], (LAYERS, 2, D), jnp.float32), 0.5, 1.5).astype(jnp.bfloat16),
        "norm_shifts": normal_values(streams_of[13], (LAYERS, 2, D), 0.3, 2.0, ((0, 2),)),
    }


@jax.custom_vjp
def low(v):
    return lax.optimization_barrier(v.astype(jnp.bfloat16)).astype(jnp.float32)

@jax.custom_vjp
def low_back(v):
    return v

def low_keep(v):
    return (low(v), None)

def low_pass(kept, grad):
    return (grad,)

def back_keep(v):
    return (v, None)

def back_low(kept, grad):
    return (low(grad),)
low.defvjp(low_keep, low_pass)
low_back.defvjp(back_keep, back_low)
HIGHEST_PRECISION = lax.Precision.HIGHEST

def round_both(values_in):
    return low(low_back(values_in))

def layer_norm(values_in, scale_row, offset):
    average = lax.optimization_barrier(jnp.mean(values_in, axis=-1, keepdims=True))
    centered = values_in - average
    variance = lax.optimization_barrier(jnp.mean(centered * centered, axis=-1, keepdims=True))
    return centered * lax.rsqrt(variance + 1e-05) * scale_row + offset

def heads_view(matrix, chains):
    return matrix.reshape(chains, LENGTH, HEADS, HEAD_DIM)

def encoder_layer(hidden, key_valid, params):
    query_weight, key_weight, value_weight, out_weight, up_weight, down_weight, bias_rows, up_bias, norm_gains, norm_shifts = params
    chains = hidden.shape[0]
    rows_flat = hidden.reshape(-1, D)
    queries = round_both(jnp.dot(rows_flat, query_weight, precision=HIGHEST_PRECISION) + bias_rows[0])
    key_rows = round_both(jnp.dot(rows_flat, key_weight, precision=HIGHEST_PRECISION))
    values = round_both(jnp.dot(rows_flat, value_weight, precision=HIGHEST_PRECISION) + bias_rows[1])
    scores = jnp.einsum('clhe,cmhe->chlm', heads_view(queries, chains), heads_view(key_rows, chains), precision=HIGHEST_PRECISION) * 0.125
    scores = low_back(jnp.where(key_valid[:, None, None, :], scores, -1000000000.0))
    attend = low(jax.nn.softmax(scores, axis=-1))
    mixture = jnp.einsum('chlm,cmhe->clhe', attend, heads_view(values, chains), precision=HIGHEST_PRECISION).reshape(-1, D)
    mixture = round_both(mixture)
    attended = low_back(jnp.dot(mixture, out_weight, precision=HIGHEST_PRECISION) + bias_rows[2])
    normed = layer_norm(rows_flat + attended, norm_gains[0], norm_shifts[0])
    inner_lin = low_back(jnp.dot(low(normed), up_weight, precision=HIGHEST_PRECISION) + up_bias)
    activated = low(jax.nn.gelu(inner_lin, approximate=False))
    outer_lin = low_back(jnp.dot(activated, down_weight, precision=HIGHEST_PRECISION) + bias_rows[3])
    result = layer_norm(normed + outer_lin, norm_gains[1], norm_shifts[1])
    return result.reshape(hidden.shape)

def group_pass(inputs, first_layer, second_layer):
    token_rows, delta_rows, length_rows, span_rows = inputs
    positions = jnp.arange(LENGTH, dtype=jnp.int32)
    key_valid = positions[None, :] < length_rows[:, None]
    masked = (positions[None, :] >= span_rows[:, 0:1]) & (positions[None, :] < span_rows[:, 1:2])
    kept_in = jnp.where(masked[:, :, None], jnp.zeros_like(token_rows), token_rows)
    middle = low(encoder_layer(kept_in, key_valid, first_layer))
    entry_rows = low_back(middle + delta_rows)
    final_rows = encoder_layer(entry_rows, key_valid, second_layer)
    return (middle, final_rows)

def reference(tokens, cotangent, lengths, spans, query_weight, key_weight, value_weight, out_weight, up_weight, down_weight, bias_rows, up_bias, norm_gains, norm_shifts):
    params = [weight.astype(jnp.float32) for weight in (query_weight, key_weight, value_weight, out_weight, up_weight, down_weight, bias_rows, up_bias, norm_gains, norm_shifts)]
    groups = TOKENS // (CHAINS_MB * LENGTH)
    token_groups = tokens.astype(jnp.float32).reshape(groups, CHAINS_MB, LENGTH, D)
    cot_groups = cotangent.astype(jnp.float32).reshape(groups, CHAINS_MB, LENGTH, D)
    delta_zero = jnp.zeros_like(token_groups)
    length_groups = lengths.astype(jnp.int32).reshape(groups, CHAINS_MB)
    span_groups = spans.astype(jnp.int32).reshape(groups, CHAINS_MB, 2)

    def whole_pass(token_in, delta_in, weights):
        first_layer = [weight[0] for weight in weights]
        second_layer = [weight[1] for weight in weights]
        stepper = jax.checkpoint(lambda inputs: group_pass(inputs, first_layer, second_layer))

        def scan_step(carried, inputs):
            return (carried, stepper(inputs))
        _, outputs = lax.scan(scan_step, None, (token_in, delta_in, length_groups, span_groups))
        return outputs
    (middle, final_rows), pullback = jax.vjp(whole_pass, token_groups, delta_zero, params)
    grad_tokens, grad_delta, grad_params = pullback((jnp.zeros_like(middle), cot_groups))
    activations = jnp.stack([middle, final_rows]).reshape(2, TOKENS, D).astype(jnp.bfloat16)
    input_grads = jnp.stack([grad_tokens, grad_delta]).reshape(2, TOKENS, D).astype(jnp.float32)
    return (activations, input_grads, grad_params[0], grad_params[1], grad_params[2], grad_params[3], grad_params[4], grad_params[5], grad_params[6], grad_params[7], grad_params[8], grad_params[9])
```

```python
import functools

import jax
import jax.numpy as jnp
from jax import lax
from jax.experimental import pallas as pl
from jax.experimental.pallas import tpu as pltpu
from jax.sharding import PartitionSpec as P

D = 768
HEADS = 12
HEAD_DIM = 64
PAIRS = HEADS // 2
FF = 3072
LENGTH = 160
CHAINS_MB = 2
ROWS = CHAINS_MB * LENGTH
SUB = 32
WIDE = 256

F32 = jnp.float32
BF16 = jnp.bfloat16
MESH = pl.DeviceIdType.MESH


def dot(left, right):
    return jnp.dot(left, right, preferred_element_type=F32)


def dot_t(left, right):
    return lax.dot_general(left, right, (((1,), (1,)), ((), ())), preferred_element_type=F32)


def t_dot(left, right):
    return lax.dot_general(left, right, (((0,), (0,)), ((), ())), preferred_element_type=F32)


def fold(block):
    return jnp.sum(block.reshape(-1, 8, block.shape[-1]), axis=0)


def gelu_parts(u):
    size = jnp.abs(u) * 0.7071067811865476
    t = pl.reciprocal(1.0 + 0.3275911 * size, approx=True)
    gauss = jnp.exp(-size * size)
    poly = t * (
        0.127414796 + t * (-0.142248368 + t * (0.7107068705 + t * (-0.7265760135 + t * 0.5307027145)))
    )
    tail = poly * gauss
    cdf = jnp.where(u >= 0, 1.0 - tail, tail)
    return u * cdf, cdf + u * (gauss * 0.3989422804014327)


def layers_kernel(
    micro_count,
    tokens, cotangent, lengths, spans,
    wq, wk, wv, wo, w1, w2, bias_in, up_bias_in, gains_in, shifts_in,
    act_out, dx_out, h_out, o_out, n_out, z_out, dq_out, dk_out, dv_out, da_out, df_out, du_out, small_out,
    wq_s, wk_s, wv_s, wo_s, w1_s, w2_s,
    h_s, q_s, k_s, v_s, p_s, o_s, n_s, xa_s, xb_s, z_s, g_s, inva_s, invb_s,
    y_s, dy_s, df_s, da_s, do_s, dx_s, wide_s, deep_s, acc_s, accu_s,
    w_sem, in_sem, out_sem, fwd_send, fwd_recv, bwd_send, bwd_recv,
):
    section = lax.axis_index("section")
    other = 1 - section
    first = section == 0
    last = section == 1

    barrier = pltpu.get_barrier_semaphore()
    pl.semaphore_signal(barrier, inc=1, device_id={"section": other}, device_id_type=MESH)

    weight_pairs = ((wq, wq_s), (wk, wk_s), (wv, wv_s), (wo, wo_s), (w1, w1_s), (w2, w2_s))

    def weight_copy(index):
        source, target = weight_pairs[index]
        return pltpu.make_async_copy(source.at[0], target, w_sem.at[index])

    def rows_of(index):
        return pl.ds(pl.multiple_of(index * ROWS, ROWS), ROWS)

    def entry_copy(index):
        return pltpu.make_async_copy(tokens.at[rows_of(index)], h_s.at[rows_of(index)], in_sem.at[index])

    def cot_copy(index):
        return pltpu.make_async_copy(cotangent.at[rows_of(index)], dy_s.at[rows_of(index)], in_sem.at[index])

    def forward_send(index):
        return pltpu.make_async_remote_copy(
            src_ref=y_s.at[rows_of(index)],
            dst_ref=h_s.at[rows_of(index)],
            send_sem=fwd_send.at[index],
            recv_sem=fwd_recv.at[index],
            device_id={"section": other},
            device_id_type=MESH,
        )

    def backward_send(index):
        return pltpu.make_async_remote_copy(
            src_ref=y_s.at[rows_of(index)],
            dst_ref=dy_s.at[rows_of(index)],
            send_sem=bwd_send.at[index],
            recv_sem=bwd_recv.at[index],
            device_id={"section": other},
            device_id_type=MESH,
        )

    forward_outs = ((h_s, h_out), (o_s, o_out), (n_s, n_out), (z_s, z_out), (y_s, act_out))
    backward_outs = (
        (q_s, dq_out), (k_s, dk_out), (v_s, dv_out), (da_s, da_out), (df_s, df_out), (g_s, du_out), (dx_s, dx_out),
    )

    def out_copy(slot, pair, index):
        source, target = pair
        return pltpu.make_async_copy(source.at[rows_of(index)], target.at[rows_of(index)], out_sem.at[slot, index])

    @pl.when(first)
    def _():
        for index in range(micro_count):
            entry_copy(index).start()

    @pl.when(last)
    def _():
        for index in range(micro_count):
            cot_copy(index).start()

    for index in range(6):
        weight_copy(index).start()

    acc_s[...] = jnp.zeros_like(acc_s)
    accu_s[...] = jnp.zeros_like(accu_s)

    bias = bias_in[0].astype(F32)
    gains = gains_in[0].astype(F32)
    shifts = shifts_in[0].astype(F32)
    lane = lax.broadcasted_iota(jnp.int32, (LENGTH, 2 * HEAD_DIM), 1)
    low_half = lane < HEAD_DIM

    def stacked(pair_block):
        zero = jnp.zeros_like(pair_block)
        return jnp.concatenate(
            [jnp.where(low_half, pair_block, zero), jnp.where(low_half, zero, pair_block)], axis=0
        )

    def merged(tall):
        return jnp.where(low_half, tall[:LENGTH], tall[LENGTH:])

    pl.semaphore_wait(barrier, 1)

    def forward(index, carry):
        base = index * ROWS
        rows = rows_of(index)

        @pl.when(first)
        def _():
            entry_copy(index).wait()
            for chain in range(CHAINS_MB):
                number = index * CHAINS_MB + chain
                start, stop = spans[number, 0], spans[number, 1]
                spot = lax.broadcasted_iota(jnp.int32, (LENGTH, D), 0)
                here = pl.ds(pl.multiple_of(base + chain * LENGTH, LENGTH), LENGTH)
                keep = (spot < start) | (spot >= stop)
                h_s[here, :] = jnp.where(keep, h_s[here, :].astype(F32), 0.0).astype(BF16)

        @pl.when(last)
        def _():
            forward_send(index).wait_recv()

        @pl.when(index == 0)
        def _():
            for number in range(3):
                weight_copy(number).wait()

        for weight, bias_row, target in ((wq_s, 0, q_s), (wk_s, None, k_s), (wv_s, 1, v_s)):
            for n0 in range(0, D, WIDE):
                block = dot(h_s[rows, :], weight[:, n0 : n0 + WIDE])
                if bias_row is not None:
                    block = block + bias[bias_row : bias_row + 1, n0 : n0 + WIDE]
                target[rows, n0 : n0 + WIDE] = block.astype(BF16)

        def chain_step(chain, carry):
            here = pl.ds(pl.multiple_of(base + chain * LENGTH, LENGTH), LENGTH)
            number = index * CHAINS_MB + chain
            valid = lax.broadcasted_iota(jnp.int32, (2, LENGTH, LENGTH), 1) < lengths[number]
            for pair in range(PAIRS):
                lanes = slice(pair * 128, pair * 128 + 128)
                tall = dot_t(stacked(k_s[here, lanes]), q_s[here, lanes])
                scores = jnp.where(valid, tall.reshape(2, LENGTH, LENGTH) * 0.125, -1000000000.0)
                top = jnp.max(scores, axis=1, keepdims=True)
                raised = jnp.exp(scores - top)
                total = jnp.sum(raised, axis=1, keepdims=True)
                attend = (raised * (1.0 / total)).astype(BF16).reshape(2 * LENGTH, LENGTH)
                p_s[number, pair] = attend
                o_s[here, lanes] = t_dot(attend, stacked(v_s[here, lanes])).astype(BF16)
            return carry

        lax.fori_loop(0, CHAINS_MB, chain_step, 0)

        @pl.when(index == 0)
        def _():
            weight_copy(3).wait()

        for n0 in range(0, D, WIDE):
            wide_s[:, n0 : n0 + WIDE] = dot(o_s[rows, :], wo_s[:, n0 : n0 + WIDE])

        def first_norm(step, carry):
            part = pl.ds(pl.multiple_of(step * SUB, SUB), SUB)
            here = pl.ds(pl.multiple_of(base + step * SUB, SUB), SUB)
            r = h_s[here, :].astype(F32) + wide_s[part, :] + bias[2:3]
            centered = r - jnp.mean(r, axis=-1, keepdims=True)
            inv = lax.rsqrt(jnp.mean(centered * centered, axis=-1, keepdims=True) + 1e-05)
            hat = centered * inv
            normed = hat * gains[0:1] + shifts[0:1]
            xa_s[here, :] = hat.astype(BF16)
            inva_s[here, :] = jnp.broadcast_to(inv, (SUB, 128))
            n_s[here, :] = normed.astype(BF16)
            wide_s[part, :] = normed
            return carry

        lax.fori_loop(0, ROWS // SUB, first_norm, 0, unroll=2)

        @pl.when(index == 0)
        def _():
            weight_copy(4).wait()
            weight_copy(5).wait()

        for n0 in range(0, FF, WIDE):
            block = dot(n_s[rows, :], w1_s[:, n0 : n0 + WIDE])
            up_bias = up_bias_in[0:1, n0 : n0 + WIDE].astype(F32)
            for r0 in range(0, ROWS, SUB):
                here = pl.ds(pl.multiple_of(base + r0, SUB), SUB)
                act, slope = gelu_parts(block[r0 : r0 + SUB] + up_bias)
                z_s[here, n0 : n0 + WIDE] = act.astype(BF16)
                g_s[here, n0 : n0 + WIDE] = slope.astype(BF16)

        for n0 in range(0, D, WIDE):
            wide_s[:, n0 : n0 + WIDE] += dot(z_s[rows, :], w2_s[:, n0 : n0 + WIDE])

        def second_norm(step, carry):
            part = pl.ds(pl.multiple_of(step * SUB, SUB), SUB)
            here = pl.ds(pl.multiple_of(base + step * SUB, SUB), SUB)
            r = wide_s[part, :] + bias[3:4]
            centered = r - jnp.mean(r, axis=-1, keepdims=True)
            inv = lax.rsqrt(jnp.mean(centered * centered, axis=-1, keepdims=True) + 1e-05)
            hat = centered * inv
            xb_s[here, :] = hat.astype(BF16)
            invb_s[here, :] = jnp.broadcast_to(inv, (SUB, 128))
            y_s[here, :] = (hat * gains[1:2] + shifts[1:2]).astype(BF16)
            return carry

        lax.fori_loop(0, ROWS // SUB, second_norm, 0, unroll=2)

        @pl.when(first)
        def _():
            forward_send(index).start()

        for slot, pair in enumerate(forward_outs):
            out_copy(slot, pair, index).start()
        return carry

    lax.fori_loop(0, micro_count, forward, 0)

    def forward_done(index, carry):
        @pl.when(first)
        def _():
            forward_send(index).wait_send()

        for slot, pair in enumerate(forward_outs):
            out_copy(slot, pair, index).wait()
        return carry

    lax.fori_loop(0, micro_count, forward_done, 0)

    def backward(index, carry):
        base = index * ROWS
        rows = rows_of(index)

        @pl.when(first)
        def _():
            backward_send(index).wait_recv()

        @pl.when(last)
        def _():
            cot_copy(index).wait()

        def second_back(step, carry):
            part = pl.ds(pl.multiple_of(step * SUB, SUB), SUB)
            here = pl.ds(pl.multiple_of(base + step * SUB, SUB), SUB)
            dy = dy_s[here, :].astype(F32)
            hat = xb_s[here, :].astype(F32)
            acc_s[9] += fold(dy * hat)
            acc_s[11] += fold(dy)
            scaled = dy * gains[1:2]
            mean_plain = jnp.mean(scaled, axis=-1, keepdims=True)
            mean_hat = jnp.mean(scaled * hat, axis=-1, keepdims=True)
            grad = (scaled - mean_plain - hat * mean_hat) * invb_s[here, 0:1]
            wide_s[part, :] = grad
            low = grad.astype(BF16)
            df_s[here, :] = low
            acc_s[3] += fold(low.astype(F32))
            return carry

        lax.fori_loop(0, ROWS // SUB, second_back, 0, unroll=2)

        for n0 in range(0, FF, WIDE):
            block = dot_t(df_s[rows, :], w2_s[n0 : n0 + WIDE, :])
            sums = jnp.zeros((8, WIDE), F32)
            for r0 in range(0, ROWS, SUB):
                here = pl.ds(pl.multiple_of(base + r0, SUB), SUB)
                low = (block[r0 : r0 + SUB] * g_s[here, n0 : n0 + WIDE].astype(F32)).astype(BF16)
                g_s[here, n0 : n0 + WIDE] = low
                sums = sums + fold(low.astype(F32))
            accu_s[:, n0 : n0 + WIDE] += sums

        for n0 in range(0, D, WIDE):
            wide_s[:, n0 : n0 + WIDE] += dot_t(g_s[rows, :], w1_s[n0 : n0 + WIDE, :])

        def first_back(step, carry):
            part = pl.ds(pl.multiple_of(step * SUB, SUB), SUB)
            here = pl.ds(pl.multiple_of(base + step * SUB, SUB), SUB)
            dn = wide_s[part, :]
            hat = xa_s[here, :].astype(F32)
            acc_s[8] += fold(dn * hat)
            acc_s[10] += fold(dn)
            scaled = dn * gains[0:1]
            mean_plain = jnp.mean(scaled, axis=-1, keepdims=True)
            mean_hat = jnp.mean(scaled * hat, axis=-1, keepdims=True)
            grad = (scaled - mean_plain - hat * mean_hat) * inva_s[here, 0:1]
            wide_s[part, :] = grad
            low = grad.astype(BF16)
            da_s[here, :] = low
            acc_s[2] += fold(low.astype(F32))
            return carry

        lax.fori_loop(0, ROWS // SUB, first_back, 0, unroll=2)

        for n0 in range(0, D, WIDE):
            do_s[:, n0 : n0 + WIDE] = dot_t(da_s[rows, :], wo_s[n0 : n0 + WIDE, :]).astype(BF16)

        def chain_step(chain, carry):
            here = pl.ds(pl.multiple_of(base + chain * LENGTH, LENGTH), LENGTH)
            near = pl.ds(pl.multiple_of(chain * LENGTH, LENGTH), LENGTH)
            number = index * CHAINS_MB + chain
            for pair in range(PAIRS):
                lanes = slice(pair * 128, pair * 128 + 128)
                query, key_rows, value = q_s[here, lanes], k_s[here, lanes], v_s[here, lanes]
                grad_mix = do_s[near, lanes]
                attend = p_s[number, pair]
                grad_attend = dot_t(stacked(value), grad_mix).reshape(2, LENGTH, LENGTH)
                attend_wide = attend.reshape(2, LENGTH, LENGTH).astype(F32)
                delta = jnp.sum(attend_wide * grad_attend, axis=1, keepdims=True)
                grad_scores = (attend_wide * (grad_attend - delta)).astype(BF16).reshape(2 * LENGTH, LENGTH)
                dv = merged(dot(attend, grad_mix)).astype(BF16)
                dk = (merged(dot(grad_scores, query)) * 0.125).astype(BF16)
                dq = (t_dot(grad_scores, stacked(key_rows)) * 0.125).astype(BF16)
                q_s[here, lanes] = dq
                k_s[here, lanes] = dk
                v_s[here, lanes] = dv
                acc_s[0, :, lanes] += fold(dq.astype(F32))
                acc_s[1, :, lanes] += fold(dv.astype(F32))
            return carry

        lax.fori_loop(0, CHAINS_MB, chain_step, 0)

        for n0 in range(0, D, WIDE):
            block = dot_t(q_s[rows, :], wq_s[n0 : n0 + WIDE, :])
            block = block + dot_t(k_s[rows, :], wk_s[n0 : n0 + WIDE, :])
            block = block + dot_t(v_s[rows, :], wv_s[n0 : n0 + WIDE, :])
            wide_s[:, n0 : n0 + WIDE] += block

        @pl.when(last)
        def _():
            low = wide_s[...].astype(BF16)
            y_s[rows, :] = low
            dx_s[rows, :] = low.astype(F32)
            backward_send(index).start()

        @pl.when(first)
        def _():
            for chain in range(CHAINS_MB):
                number = index * CHAINS_MB + chain
                start, stop = spans[number, 0], spans[number, 1]
                spot = lax.broadcasted_iota(jnp.int32, (LENGTH, D), 0)
                here = pl.ds(pl.multiple_of(base + chain * LENGTH, LENGTH), LENGTH)
                keep = (spot < start) | (spot >= stop)
                dx_s[here, :] = jnp.where(keep, wide_s[chain * LENGTH : (chain + 1) * LENGTH, :], 0.0)

        for slot, pair in enumerate(backward_outs):
            out_copy(slot + len(forward_outs), pair, index).start()
        return carry

    lax.fori_loop(0, micro_count, backward, 0)

    for number in range(12):
        if 4 <= number < 8:
            panel = accu_s[:, (number - 4) * D : (number - 3) * D]
        else:
            panel = acc_s[number]
        small_out[number : number + 1, :] = jnp.sum(panel, axis=0, keepdims=True)
    small_out[12:16, :] = jnp.zeros((4, D), F32)

    def backward_done(index, carry):
        @pl.when(last)
        def _():
            backward_send(index).wait_send()

        for slot, pair in enumerate(backward_outs):
            out_copy(slot + len(forward_outs), pair, index).wait()
        return carry

    lax.fori_loop(0, micro_count, backward_done, 0)


def run_layers(tokens, cotangent, lengths, spans, *weights):
    rows = tokens.shape[0]
    micro_count = rows // ROWS
    chains = rows // LENGTH
    anywhere = pl.BlockSpec(memory_space=pl.ANY)
    scalars = pl.BlockSpec(memory_space=pltpu.SMEM)
    vectors = pl.BlockSpec(memory_space=pltpu.VMEM)
    narrow = jax.ShapeDtypeStruct((rows, D), BF16)
    broad = jax.ShapeDtypeStruct((rows, FF), BF16)
    out_shape = (
        narrow, jax.ShapeDtypeStruct((rows, D), F32),
        narrow, narrow, narrow, broad, narrow, narrow, narrow, narrow, narrow, broad,
        jax.ShapeDtypeStruct((16, D), F32),
    )

    def vm(count, width=D, dtype=BF16):
        return pltpu.VMEM((count, width), dtype)

    scratch = [
        vm(D), vm(D), vm(D), vm(D), vm(D, FF), vm(FF),
        vm(rows), vm(rows), vm(rows), vm(rows),
        pltpu.VMEM((chains, PAIRS, 2 * LENGTH, LENGTH), BF16),
        vm(rows), vm(rows), vm(rows), vm(rows), vm(rows, FF), vm(rows, FF),
        vm(rows, 128, F32), vm(rows, 128, F32),
        vm(rows), vm(rows), vm(rows), vm(rows), vm(ROWS), vm(rows, D, F32),
        vm(ROWS, D, F32), vm(16, 128), pltpu.VMEM((12, 8, D), F32), vm(8, FF, F32),
        pltpu.SemaphoreType.DMA((6,)),
        pltpu.SemaphoreType.DMA((micro_count,)),
        pltpu.SemaphoreType.DMA((12, micro_count)),
        pltpu.SemaphoreType.DMA((micro_count,)),
        pltpu.SemaphoreType.DMA((micro_count,)),
        pltpu.SemaphoreType.DMA((micro_count,)),
        pltpu.SemaphoreType.DMA((micro_count,)),
    ]
    return pl.pallas_call(
        functools.partial(layers_kernel, micro_count),
        out_shape=out_shape,
        in_specs=[anywhere, anywhere, scalars, scalars] + [anywhere] * 6 + [vectors] * 4,
        out_specs=[anywhere] * 12 + [vectors],
        scratch_shapes=scratch,
        compiler_params=pltpu.CompilerParams(
            collective_id=0, has_side_effects=True, vmem_limit_bytes=60 * 1024 * 1024
        ),
        cost_estimate=pl.CostEstimate(
            flops=rows * 2 * 2 * 2 * 7077888, bytes_accessed=60000000, transcendentals=rows * FF * 2
        ),
    )(tokens, cotangent, lengths, spans, *weights)


def outer_sum(left, right):
    return t_dot(left, right).astype(BF16)


def per_device(tokens, cotangent, lengths, spans, *weights):
    act, dx, h, o, n, z, dq, dk, dv, da, df, du, small = run_layers(tokens, cotangent, lengths, spans, *weights)
    down = lax.psum(outer_sum(z, df), "dp").astype(F32)
    up = lax.psum(outer_sum(n, du), "dp").astype(F32)
    out = lax.psum(outer_sum(o, da), "dp").astype(F32)
    value = lax.psum(outer_sum(h, dv), "dp").astype(F32)
    query = lax.psum(outer_sum(h, dq), "dp").astype(F32)
    key_rows = lax.psum(outer_sum(h, dk), "dp").astype(F32)
    small = lax.psum(small, "dp")
    return (
        act[None], dx[None], query[None], key_rows[None], value[None], out[None], up[None], down[None],
        small[0:4][None], small[4:8].reshape(1, FF), small[8:10][None], small[10:12][None],
    )


def solution(mesh):
    in_specs = (
        P("dp", None), P("dp", None), P("dp"), P("dp", None),
        P("section", None, None), P("section", None, None), P("section", None, None),
        P("section", None, None), P("section", None, None), P("section", None, None),
        P("section", None, None), P("section", None), P("section", None, None), P("section", None, None),
    )
    out_specs = (
        P("section", "dp", None), P("section", "dp", None),
        P("section", None, None), P("section", None, None), P("section", None, None),
        P("section", None, None), P("section", None, None), P("section", None, None),
        P("section", None, None), P("section", None), P("section", None, None), P("section", None, None),
    )
    return jax.shard_map(per_device, mesh=mesh, in_specs=in_specs, out_specs=out_specs, check_vma=False)
```

```python
import functools

import jax
import jax.numpy as jnp
from jax import lax
from jax.experimental import pallas as pl
from jax.experimental.pallas import tpu as pltpu
from jax.sharding import PartitionSpec as P

D = 768
HEADS = 12
HEAD_DIM = 64
PAIRS = HEADS // 2
FF = 3072
LENGTH = 160
CHAINS_MB = 2
ROWS = CHAINS_MB * LENGTH
SUB = 32
WIDE = 256

F32 = jnp.float32
BF16 = jnp.bfloat16
MESH = pl.DeviceIdType.MESH


def dot(left, right):
    return jnp.dot(left, right, preferred_element_type=F32)


def dot_t(left, right):
    return lax.dot_general(left, right, (((1,), (1,)), ((), ())), preferred_element_type=F32)


def t_dot(left, right):
    return lax.dot_general(left, right, (((0,), (0,)), ((), ())), preferred_element_type=F32)


def fold(block):
    return jnp.sum(block.reshape(-1, 8, block.shape[-1]), axis=0)


def gelu_parts(u):
    size = jnp.abs(u) * 0.7071067811865476
    t = pl.reciprocal(1.0 + 0.3275911 * size, approx=True)
    gauss = jnp.exp(-size * size)
    poly = t * (
        0.127414796 + t * (-0.142248368 + t * (0.7107068705 + t * (-0.7265760135 + t * 0.5307027145)))
    )
    tail = poly * gauss
    cdf = jnp.where(u >= 0, 1.0 - tail, tail)
    return u * cdf, cdf + u * (gauss * 0.3989422804014327)


def layers_kernel(
    micro_count,
    tokens, cotangent, lengths, spans,
    wq, wk, wv, wo, w1, w2, bias_in, up_bias_in, gains_in, shifts_in,
    act_out, dx_out, left_out, right_out, small_out,
    wq_s, wk_s, wv_s, wo_s, w1_s, w2_s,
    h_s, q_s, k_s, v_s, p_s, o_s, n_s, xa_s, xb_s, z_s, g_s, inva_s, invb_s,
    y_s, dy_s, df_s, da_s, do_s, dx_s, wide_s, turn_s, acc_s, accu_s,
    w_sem, in_sem, out_sem, turn_sem, fwd_send, fwd_recv, bwd_send, bwd_recv,
):
    section = lax.axis_index("section")
    other = 1 - section
    first = section == 0
    last = section == 1

    barrier = pltpu.get_barrier_semaphore()
    pl.semaphore_signal(barrier, inc=1, device_id={"section": other}, device_id_type=MESH)

    weight_pairs = ((wq, wq_s), (wk, wk_s), (wv, wv_s), (wo, wo_s), (w1, w1_s), (w2, w2_s))

    def weight_copy(index):
        source, target = weight_pairs[index]
        return pltpu.make_async_copy(source.at[0], target, w_sem.at[index])

    def rows_of(index):
        return pl.ds(pl.multiple_of(index * ROWS, ROWS), ROWS)

    def entry_copy(index):
        return pltpu.make_async_copy(tokens.at[rows_of(index)], h_s.at[rows_of(index)], in_sem.at[index])

    def cot_copy(index):
        return pltpu.make_async_copy(cotangent.at[rows_of(index)], dy_s.at[rows_of(index)], in_sem.at[index])

    def forward_send(index):
        return pltpu.make_async_remote_copy(
            src_ref=y_s.at[rows_of(index)],
            dst_ref=h_s.at[rows_of(index)],
            send_sem=fwd_send.at[index],
            recv_sem=fwd_recv.at[index],
            device_id={"section": other},
            device_id_type=MESH,
        )

    def backward_send(index):
        return pltpu.make_async_remote_copy(
            src_ref=y_s.at[rows_of(index)],
            dst_ref=dy_s.at[rows_of(index)],
            send_sem=bwd_send.at[index],
            recv_sem=bwd_recv.at[index],
            device_id={"section": other},
            device_id_type=MESH,
        )

    backward_outs = ((q_s, 0), (k_s, 1), (v_s, 2), (da_s, 3), (df_s, 8))

    def act_copy(index):
        return pltpu.make_async_copy(y_s.at[rows_of(index)], act_out.at[rows_of(index)], out_sem.at[0, index])

    def dx_copy(index):
        return pltpu.make_async_copy(dx_s.at[rows_of(index)], dx_out.at[rows_of(index)], out_sem.at[1, index])

    def right_copies(index):
        for slot, (source, place) in enumerate(backward_outs):
            yield pltpu.make_async_copy(
                source.at[rows_of(index)], right_out.at[place, rows_of(index)], out_sem.at[2 + slot, index]
            )
        for panel in range(FF // D):
            yield pltpu.make_async_copy(
                g_s.at[rows_of(index), pl.ds(panel * D, D)],
                right_out.at[4 + panel, rows_of(index)],
                out_sem.at[7 + panel, index],
            )

    def turn_copy(slot, row):
        return pltpu.make_async_copy(
            turn_s.at[slot], left_out.at[pl.ds(pl.multiple_of(row, 128), 128)], turn_sem.at[slot]
        )

    def transpose_all():
        done = 0
        for source, tiles in ((h_s, D // 128), (o_s, D // 128), (n_s, D // 128), (z_s, FF // 128)):

            def tile_step(tile, carry, source=source, done=done):
                number = tile + done
                slot = lax.rem(number, 2)

                @pl.when(number >= 2)
                def _():
                    turn_copy(slot, (number - 2) * 128).wait()

                turn_s[slot] = source[:, pl.ds(pl.multiple_of(tile * 128, 128), 128)].T
                turn_copy(slot, number * 128).start()
                return carry

            lax.fori_loop(0, tiles, tile_step, 0)
            done += tiles
        for number in (done - 2, done - 1):
            turn_copy(number % 2, number * 128).wait()

    @pl.when(first)
    def _():
        for index in range(micro_count):
            entry_copy(index).start()

    @pl.when(last)
    def _():
        for index in range(micro_count):
            cot_copy(index).start()

    for index in range(6):
        weight_copy(index).start()

    acc_s[...] = jnp.zeros_like(acc_s)
    accu_s[...] = jnp.zeros_like(accu_s)

    bias = bias_in[0].astype(F32)
    gains = gains_in[0].astype(F32)
    shifts = shifts_in[0].astype(F32)
    lane = lax.broadcasted_iota(jnp.int32, (LENGTH, 2 * HEAD_DIM), 1)
    low_half = lane < HEAD_DIM

    def stacked(pair_block):
        zero = jnp.zeros_like(pair_block)
        return jnp.concatenate(
            [jnp.where(low_half, pair_block, zero), jnp.where(low_half, zero, pair_block)], axis=0
        )

    def merged(tall):
        return jnp.where(low_half, tall[:LENGTH], tall[LENGTH:])

    pl.semaphore_wait(barrier, 1)

    def forward(index, carry):
        base = index * ROWS
        rows = rows_of(index)

        @pl.when(first)
        def _():
            entry_copy(index).wait()
            for chain in range(CHAINS_MB):
                number = index * CHAINS_MB + chain
                start, stop = spans[number, 0], spans[number, 1]
                spot = lax.broadcasted_iota(jnp.int32, (LENGTH, D), 0)
                here = pl.ds(pl.multiple_of(base + chain * LENGTH, LENGTH), LENGTH)
                keep = (spot < start) | (spot >= stop)
                h_s[here, :] = jnp.where(keep, h_s[here, :].astype(F32), 0.0).astype(BF16)

        @pl.when(last)
        def _():
            forward_send(index).wait_recv()

        @pl.when(index == 0)
        def _():
            for number in range(3):
                weight_copy(number).wait()

        for weight, bias_row, target in ((wq_s, 0, q_s), (wk_s, None, k_s), (wv_s, 1, v_s)):
            for n0 in range(0, D, WIDE):
                block = dot(h_s[rows, :], weight[:, n0 : n0 + WIDE])
                if bias_row is not None:
                    block = block + bias[bias_row : bias_row + 1, n0 : n0 + WIDE]
                target[rows, n0 : n0 + WIDE] = block.astype(BF16)

        def chain_step(chain, carry):
            here = pl.ds(pl.multiple_of(base + chain * LENGTH, LENGTH), LENGTH)
            number = index * CHAINS_MB + chain
            valid = lax.broadcasted_iota(jnp.int32, (2, LENGTH, LENGTH), 1) < lengths[number]
            for pair in range(PAIRS):
                lanes = slice(pair * 128, pair * 128 + 128)
                tall = dot_t(stacked(k_s[here, lanes]), q_s[here, lanes])
                scores = jnp.where(valid, tall.reshape(2, LENGTH, LENGTH) * 0.125, -1000000000.0)
                top = jnp.max(scores, axis=1, keepdims=True)
                raised = jnp.exp(scores - top)
                total = jnp.sum(raised, axis=1, keepdims=True)
                attend = (raised * (1.0 / total)).astype(BF16).reshape(2 * LENGTH, LENGTH)
                p_s[number, pair] = attend
                o_s[here, lanes] = t_dot(attend, stacked(v_s[here, lanes])).astype(BF16)
            return carry

        lax.fori_loop(0, CHAINS_MB, chain_step, 0)

        @pl.when(index == 0)
        def _():
            weight_copy(3).wait()

        for n0 in range(0, D, WIDE):
            wide_s[:, n0 : n0 + WIDE] = dot(o_s[rows, :], wo_s[:, n0 : n0 + WIDE])

        def first_norm(step, carry):
            part = pl.ds(pl.multiple_of(step * SUB, SUB), SUB)
            here = pl.ds(pl.multiple_of(base + step * SUB, SUB), SUB)
            r = h_s[here, :].astype(F32) + wide_s[part, :] + bias[2:3]
            centered = r - jnp.mean(r, axis=-1, keepdims=True)
            inv = lax.rsqrt(jnp.mean(centered * centered, axis=-1, keepdims=True) + 1e-05)
            hat = centered * inv
            normed = hat * gains[0:1] + shifts[0:1]
            xa_s[here, :] = hat.astype(BF16)
            inva_s[here, :] = jnp.broadcast_to(inv, (SUB, 128))
            n_s[here, :] = normed.astype(BF16)
            wide_s[part, :] = normed
            return carry

        lax.fori_loop(0, ROWS // SUB, first_norm, 0, unroll=2)

        @pl.when(index == 0)
        def _():
            weight_copy(4).wait()
            weight_copy(5).wait()

        for n0 in range(0, FF, WIDE):
            block = dot(n_s[rows, :], w1_s[:, n0 : n0 + WIDE])
            up_bias = up_bias_in[0:1, n0 : n0 + WIDE].astype(F32)
            for r0 in range(0, ROWS, SUB):
                here = pl.ds(pl.multiple_of(base + r0, SUB), SUB)
                act, slope = gelu_parts(block[r0 : r0 + SUB] + up_bias)
                z_s[here, n0 : n0 + WIDE] = act.astype(BF16)
                g_s[here, n0 : n0 + WIDE] = slope.astype(BF16)

        for n0 in range(0, D, WIDE):
            wide_s[:, n0 : n0 + WIDE] += dot(z_s[rows, :], w2_s[:, n0 : n0 + WIDE])

        def second_norm(step, carry):
            part = pl.ds(pl.multiple_of(step * SUB, SUB), SUB)
            here = pl.ds(pl.multiple_of(base + step * SUB, SUB), SUB)
            r = wide_s[part, :] + bias[3:4]
            centered = r - jnp.mean(r, axis=-1, keepdims=True)
            inv = lax.rsqrt(jnp.mean(centered * centered, axis=-1, keepdims=True) + 1e-05)
            hat = centered * inv
            xb_s[here, :] = hat.astype(BF16)
            invb_s[here, :] = jnp.broadcast_to(inv, (SUB, 128))
            y_s[here, :] = (hat * gains[1:2] + shifts[1:2]).astype(BF16)
            return carry

        lax.fori_loop(0, ROWS // SUB, second_norm, 0, unroll=2)

        @pl.when(first)
        def _():
            forward_send(index).start()

        act_copy(index).start()
        return carry

    lax.fori_loop(0, micro_count, forward, 0)

    def forward_done(index, carry):
        @pl.when(first)
        def _():
            forward_send(index).wait_send()

        act_copy(index).wait()
        return carry

    lax.fori_loop(0, micro_count, forward_done, 0)

    @pl.when(first)
    def _():
        transpose_all()

    def backward(index, carry):
        base = index * ROWS
        rows = rows_of(index)

        @pl.when(first)
        def _():
            backward_send(index).wait_recv()

        @pl.when(last)
        def _():
            cot_copy(index).wait()

        def second_back(step, carry):
            part = pl.ds(pl.multiple_of(step * SUB, SUB), SUB)
            here = pl.ds(pl.multiple_of(base + step * SUB, SUB), SUB)
            dy = dy_s[here, :].astype(F32)
            hat = xb_s[here, :].astype(F32)
            acc_s[9] += fold(dy * hat)
            acc_s[11] += fold(dy)
            scaled = dy * gains[1:2]
            mean_plain = jnp.mean(scaled, axis=-1, keepdims=True)
            mean_hat = jnp.mean(scaled * hat, axis=-1, keepdims=True)
            grad = (scaled - mean_plain - hat * mean_hat) * invb_s[here, 0:1]
            wide_s[part, :] = grad
            low = grad.astype(BF16)
            df_s[here, :] = low
            acc_s[3] += fold(low.astype(F32))
            return carry

        lax.fori_loop(0, ROWS // SUB, second_back, 0, unroll=2)

        for n0 in range(0, FF, WIDE):
            block = dot_t(df_s[rows, :], w2_s[n0 : n0 + WIDE, :])
            sums = jnp.zeros((8, WIDE), F32)
            for r0 in range(0, ROWS, SUB):
                here = pl.ds(pl.multiple_of(base + r0, SUB), SUB)
                low = (block[r0 : r0 + SUB] * g_s[here, n0 : n0 + WIDE].astype(F32)).astype(BF16)
                g_s[here, n0 : n0 + WIDE] = low
                sums = sums + fold(low.astype(F32))
            accu_s[:, n0 : n0 + WIDE] += sums

        for n0 in range(0, D, WIDE):
            wide_s[:, n0 : n0 + WIDE] += dot_t(g_s[rows, :], w1_s[n0 : n0 + WIDE, :])

        def first_back(step, carry):
            part = pl.ds(pl.multiple_of(step * SUB, SUB), SUB)
            here = pl.ds(pl.multiple_of(base + step * SUB, SUB), SUB)
            dn = wide_s[part, :]
            hat = xa_s[here, :].astype(F32)
            acc_s[8] += fold(dn * hat)
            acc_s[10] += fold(dn)
            scaled = dn * gains[0:1]
            mean_plain = jnp.mean(scaled, axis=-1, keepdims=True)
            mean_hat = jnp.mean(scaled * hat, axis=-1, keepdims=True)
            grad = (scaled - mean_plain - hat * mean_hat) * inva_s[here, 0:1]
            wide_s[part, :] = grad
            low = grad.astype(BF16)
            da_s[here, :] = low
            acc_s[2] += fold(low.astype(F32))
            return carry

        lax.fori_loop(0, ROWS // SUB, first_back, 0, unroll=2)

        for n0 in range(0, D, WIDE):
            do_s[:, n0 : n0 + WIDE] = dot_t(da_s[rows, :], wo_s[n0 : n0 + WIDE, :]).astype(BF16)

        def chain_step(chain, carry):
            here = pl.ds(pl.multiple_of(base + chain * LENGTH, LENGTH), LENGTH)
            near = pl.ds(pl.multiple_of(chain * LENGTH, LENGTH), LENGTH)
            number = index * CHAINS_MB + chain
            for pair in range(PAIRS):
                lanes = slice(pair * 128, pair * 128 + 128)
                query, key_rows, value = q_s[here, lanes], k_s[here, lanes], v_s[here, lanes]
                grad_mix = do_s[near, lanes]
                attend = p_s[number, pair]
                grad_attend = dot_t(stacked(value), grad_mix).reshape(2, LENGTH, LENGTH)
                attend_wide = attend.reshape(2, LENGTH, LENGTH).astype(F32)
                delta = jnp.sum(attend_wide * grad_attend, axis=1, keepdims=True)
                grad_scores = (attend_wide * (grad_attend - delta)).astype(BF16).reshape(2 * LENGTH, LENGTH)
                dv = merged(dot(attend, grad_mix)).astype(BF16)
                dk = (merged(dot(grad_scores, query)) * 0.125).astype(BF16)
                dq = (t_dot(grad_scores, stacked(key_rows)) * 0.125).astype(BF16)
                q_s[here, lanes] = dq
                k_s[here, lanes] = dk
                v_s[here, lanes] = dv
                acc_s[0, :, lanes] += fold(dq.astype(F32))
                acc_s[1, :, lanes] += fold(dv.astype(F32))
            return carry

        lax.fori_loop(0, CHAINS_MB, chain_step, 0)

        for n0 in range(0, D, WIDE):
            block = dot_t(q_s[rows, :], wq_s[n0 : n0 + WIDE, :])
            block = block + dot_t(k_s[rows, :], wk_s[n0 : n0 + WIDE, :])
            block = block + dot_t(v_s[rows, :], wv_s[n0 : n0 + WIDE, :])
            wide_s[:, n0 : n0 + WIDE] += block

        @pl.when(last)
        def _():
            low = wide_s[...].astype(BF16)
            y_s[rows, :] = low
            dx_s[rows, :] = low.astype(F32)
            backward_send(index).start()

        @pl.when(first)
        def _():
            for chain in range(CHAINS_MB):
                number = index * CHAINS_MB + chain
                start, stop = spans[number, 0], spans[number, 1]
                spot = lax.broadcasted_iota(jnp.int32, (LENGTH, D), 0)
                here = pl.ds(pl.multiple_of(base + chain * LENGTH, LENGTH), LENGTH)
                keep = (spot < start) | (spot >= stop)
                dx_s[here, :] = jnp.where(keep, wide_s[chain * LENGTH : (chain + 1) * LENGTH, :], 0.0)

        dx_copy(index).start()
        for copy in right_copies(index):
            copy.start()
        return carry

    lax.fori_loop(0, micro_count, backward, 0)

    @pl.when(last)
    def _():
        transpose_all()

    for number in range(12):
        if 4 <= number < 8:
            panel = accu_s[:, (number - 4) * D : (number - 3) * D]
        else:
            panel = acc_s[number]
        small_out[number : number + 1, :] = jnp.sum(panel, axis=0, keepdims=True)
    small_out[12:16, :] = jnp.zeros((4, D), F32)

    def backward_done(index, carry):
        @pl.when(last)
        def _():
            backward_send(index).wait_send()

        dx_copy(index).wait()
        for copy in right_copies(index):
            copy.wait()
        return carry

    lax.fori_loop(0, micro_count, backward_done, 0)


def run_layers(tokens, cotangent, lengths, spans, *weights):
    rows = tokens.shape[0]
    micro_count = rows // ROWS
    chains = rows // LENGTH
    anywhere = pl.BlockSpec(memory_space=pl.ANY)
    scalars = pl.BlockSpec(memory_space=pltpu.SMEM)
    vectors = pl.BlockSpec(memory_space=pltpu.VMEM)
    out_shape = (
        jax.ShapeDtypeStruct((rows, D), BF16),
        jax.ShapeDtypeStruct((rows, D), F32),
        jax.ShapeDtypeStruct((3 * D + FF, rows), BF16),
        jax.ShapeDtypeStruct((9, rows, D), BF16),
        jax.ShapeDtypeStruct((16, D), F32),
    )

    def vm(count, width=D, dtype=BF16):
        return pltpu.VMEM((count, width), dtype)

    scratch = [
        vm(D), vm(D), vm(D), vm(D), vm(D, FF), vm(FF),
        vm(rows), vm(rows), vm(rows), vm(rows),
        pltpu.VMEM((chains, PAIRS, 2 * LENGTH, LENGTH), BF16),
        vm(rows), vm(rows), vm(rows), vm(rows), vm(rows, FF), vm(rows, FF),
        vm(rows, 128, F32), vm(rows, 128, F32),
        vm(rows), vm(rows), vm(rows), vm(rows), vm(ROWS), vm(rows, D, F32),
        vm(ROWS, D, F32), pltpu.VMEM((2, 128, rows), BF16), pltpu.VMEM((12, 8, D), F32), vm(8, FF, F32),
        pltpu.SemaphoreType.DMA((6,)),
        pltpu.SemaphoreType.DMA((micro_count,)),
        pltpu.SemaphoreType.DMA((11, micro_count)),
        pltpu.SemaphoreType.DMA((2,)),
        pltpu.SemaphoreType.DMA((micro_count,)),
        pltpu.SemaphoreType.DMA((micro_count,)),
        pltpu.SemaphoreType.DMA((micro_count,)),
        pltpu.SemaphoreType.DMA((micro_count,)),
    ]
    return pl.pallas_call(
        functools.partial(layers_kernel, micro_count),
        out_shape=out_shape,
        in_specs=[anywhere, anywhere, scalars, scalars] + [anywhere] * 6 + [vectors] * 4,
        out_specs=[anywhere] * 4 + [vectors],
        scratch_shapes=scratch,
        compiler_params=pltpu.CompilerParams(
            collective_id=0, has_side_effects=True, vmem_limit_bytes=60 * 1024 * 1024
        ),
        cost_estimate=pl.CostEstimate(
            flops=rows * 2 * 2 * 2 * 7077888, bytes_accessed=60000000, transcendentals=rows * FF * 2
        ),
    )(tokens, cotangent, lengths, spans, *weights)


RING = 8
PIECES = 3
PIECE = D // RING
PANELS = (
    (0, 0), (0, 1), (0, 2), (D, 3), (2 * D, 4), (2 * D, 5),
    (2 * D, 6), (2 * D, 7), (3 * D, 8), (4 * D, 8), (5 * D, 8), (6 * D, 8),
)


def sums_kernel(
    left, right, small_in, grads_out, small_out,
    left_s, right_s, total_s, give_s, take_s, ring_s, own_s,
    tiny_s, tiny_take_s, tiny_sum_s, tiny_go_s, tiny_ring_s, tiny_own_s,
    load_sem, give_sem, take_sem, ring_send, ring_recv, own_sem, round_send, round_recv, share_send, share_recv,
    tiny_sem, tiny_ring_send, tiny_ring_recv, tiny_round_send, tiny_round_recv,
):
    me = lax.axis_index("dp")
    core = lax.rem(me, 2)
    high = lax.rem(lax.div(me, 2), 2)
    depth = lax.div(me, 4)
    place = depth + high * (7 - 2 * depth)

    def device(spot, on_core):
        row = lax.div(spot, 4)
        return {"dp": 4 * (spot + row * (7 - 2 * spot)) + 2 * row + on_core}

    ahead = device(lax.rem(place + 1, RING), core)
    behind = device(lax.rem(place + RING - 1, RING), core)
    beside = device(place, 1 - core)
    targets = (ahead, behind)

    barrier = pltpu.get_barrier_semaphore()
    for peer in (ahead, behind, beside):
        pl.semaphore_signal(barrier, inc=1, device_id=peer, device_id_type=MESH)

    def block(way, step):
        return lax.rem(place - step + RING, RING) if way == 0 else lax.rem(place + step, RING)

    def late_block(way, step):
        return lax.rem(place + 1 - step + RING, RING) if way == 0 else lax.rem(place + RING - 1 + step, RING)

    def load_left(part):
        return pltpu.make_async_copy(left.at[pl.ds(part * D, D)], left_s.at[pl.ds(part * D, D)], load_sem.at[part])

    def load_right(part):
        return pltpu.make_async_copy(right.at[part], right_s.at[part], load_sem.at[7 + part])

    def remote(source, target, send, recv, peer):
        return pltpu.make_async_remote_copy(
            src_ref=source, dst_ref=target, send_sem=send, recv_sem=recv, device_id=peer, device_id_type=MESH
        )

    def give(way, step, piece):
        return remote(
            give_s.at[way, step, piece], take_s.at[way, step, piece],
            give_sem.at[way, step, piece], take_sem.at[way, step, piece], beside,
        )

    def ring_copy(way, step, piece):
        return remote(
            take_s.at[way, step, piece], ring_s.at[way, step, piece],
            ring_send.at[way, step, piece], ring_recv.at[way, step, piece], targets[way],
        )

    def region(way, spot, piece, on_core):
        rows = pl.ds(pl.multiple_of(spot * PIECE, PIECE), PIECE)
        return grads_out.at[6 * way + 3 * on_core + piece, rows]

    def own_copy(way, piece):
        return pltpu.make_async_copy(
            own_s.at[way, piece], region(way, late_block(way, 0), piece, core), own_sem.at[way, piece]
        )

    def round_copy(way, step, piece, source=None):
        target = region(way, late_block(way, step), piece, core)
        return remote(
            target if source is None else source, target,
            round_send.at[way, step, piece], round_recv.at[way, step, piece], targets[way],
        )

    def round_wait(way, step, piece):
        target = region(way, late_block(way, step + 1), piece, core)
        remote(
            target, target, round_send.at[way, step, piece], round_recv.at[way, step, piece], targets[way]
        ).wait_recv()

    def share_copy(way, step, piece, source=None):
        target = region(way, late_block(way, step), piece, core)
        return remote(
            target if source is None else source, target,
            share_send.at[way, step, piece], share_recv.at[way, step, piece], beside,
        )

    def share_wait(way, step, piece):
        target = region(way, late_block(way, step), piece, 1 - core)
        remote(
            target, target, share_send.at[way, step, piece], share_recv.at[way, step, piece], beside
        ).wait_recv()

    tiny_swap = remote(tiny_s, tiny_take_s, tiny_sem.at[0], tiny_sem.at[1], beside)

    def tiny_ring(step):
        return remote(
            tiny_go_s.at[step], tiny_ring_s.at[step], tiny_ring_send.at[step], tiny_ring_recv.at[step], ahead
        )

    def tiny_round(step):
        spot = late_block(0, step)
        return remote(
            tiny_own_s.at[spot], tiny_own_s.at[spot], tiny_round_send.at[step], tiny_round_recv.at[step], ahead
        )

    def tiny_round_wait(step):
        spot = late_block(0, step + 1)
        remote(
            tiny_own_s.at[spot], tiny_own_s.at[spot], tiny_round_send.at[step], tiny_round_recv.at[step], ahead
        ).wait_recv()

    loads = []
    for way in range(2):
        for piece in range(PIECES):
            for half in range(2):
                first_row, number = PANELS[6 * way + 3 * half + piece]
                for kind, part in ((load_right, number), (load_left, first_row // D)):
                    if (kind, part) not in [entry[:2] for entry in loads]:
                        loads.append((kind, part, way, piece))
    for kind, part, _, _ in loads:
        kind(part).start()

    for part in range(RING):
        if part * 128 < D:
            tiny_s[part] = small_in[:, part * 128 : part * 128 + 128]
        else:
            tiny_s[part] = jnp.zeros((16, 128), F32)

    pl.semaphore_wait(barrier, 3)
    tiny_swap.start()

    def products(group):
        for way in range(2):
            for piece in range(PIECES):

                @pl.when(group == 0)
                def _():
                    for kind, part, at_way, at_piece in loads:
                        if (at_way, at_piece) == (way, piece):
                            kind(part).wait()

                near, far = PANELS[6 * way + piece], PANELS[6 * way + 3 + piece]
                for mine in (False, True):
                    pick = core if mine else 1 - core
                    first_row = near[0] + pick * (far[0] - near[0])
                    number = near[1] + pick * (far[1] - near[1])
                    blocks = []
                    for step in (2 * group, 2 * group + 1):
                        start = pl.multiple_of(first_row + block(way, step) * PIECE, PIECE)
                        blocks.append(left_s[pl.ds(start, PIECE), :])
                    tall = jnp.concatenate(blocks, axis=0)
                    for n0 in range(0, D, WIDE):
                        product = dot(tall, right_s[number, :, n0 : n0 + WIDE])
                        for half in range(2):
                            step = 2 * group + half
                            part = product[half * PIECE : (half + 1) * PIECE]
                            if mine:
                                total_s[lax.rem(step, 4), way, piece, :, n0 : n0 + WIDE] = part
                            else:
                                give_s[way, step, piece, :, n0 : n0 + WIDE] = part.astype(BF16)
                    if not mine:
                        give(way, 2 * group, piece).start()
                        give(way, 2 * group + 1, piece).start()

    def reduce_step(step, carry):
        slot = lax.rem(step, 4)
        spot = block(0, step)

        @pl.when(step == 0)
        def _():
            tiny_swap.wait_recv()
            tiny_sum_s[...] = tiny_s[...] + tiny_take_s[...]
            tiny_go_s[0] = tiny_sum_s[spot]
            tiny_ring(0).start()

        @pl.when((step > 0) & (step < RING - 1))
        def _():
            tiny_ring(step - 1).wait_recv()
            tiny_go_s[step] = tiny_sum_s[spot] + tiny_ring_s[step - 1]
            tiny_ring(step).start()

        @pl.when(step == RING - 1)
        def _():
            tiny_ring(step - 1).wait_recv()
            tiny_own_s[spot] = tiny_sum_s[spot] + tiny_ring_s[step - 1]
            tiny_round(0).start()

        for piece in range(PIECES):
            for way in range(2):
                give(way, step, piece).wait_recv()

                @pl.when(step > 0)
                def _():
                    ring_copy(way, step - 1, piece).wait_recv()
                    for r0 in range(0, PIECE, SUB):
                        part = slice(r0, r0 + SUB)
                        total_s[slot, way, piece, part] += ring_s[way, step - 1, piece, part].astype(F32)

                @pl.when(step < RING - 1)
                def _():
                    for r0 in range(0, PIECE, SUB):
                        part = slice(r0, r0 + SUB)
                        whole = total_s[slot, way, piece, part] + take_s[way, step, piece, part].astype(F32)
                        take_s[way, step, piece, part] = whole.astype(BF16)
                    ring_copy(way, step, piece).start()

                @pl.when(step == RING - 1)
                def _():
                    for r0 in range(0, PIECE, SUB):
                        part = slice(r0, r0 + SUB)
                        whole = total_s[slot, way, piece, part] + take_s[way, step, piece, part].astype(F32)
                        own_s[way, piece, part] = whole.astype(BF16)
                    round_copy(way, 0, piece, own_s.at[way, piece]).start()
                    share_copy(way, 0, piece, own_s.at[way, piece]).start()
                    own_copy(way, piece).start()
        return carry

    def group_step(group, carry):
        @pl.when(group < RING // 2)
        def _():
            products(group)

        low = jnp.maximum(2 * group - 1, 0)
        top = jnp.minimum(2 * group + 1, RING)
        return lax.fori_loop(low, top, reduce_step, carry)

    lax.fori_loop(0, RING // 2 + 1, group_step, 0)

    def round_step(step, carry):
        tiny_round_wait(step - 1)

        @pl.when(step < RING - 1)
        def _():
            tiny_round(step).start()

        for piece in range(PIECES):
            for way in range(2):
                round_wait(way, step - 1, piece)

                @pl.when(step < RING - 1)
                def _():
                    round_copy(way, step, piece).start()

                share_copy(way, step, piece).start()
        return carry

    lax.fori_loop(1, RING, round_step, 0)

    for part in range(D // 128):
        small_out[:, part * 128 : part * 128 + 128] = tiny_own_s[part]
    tiny_swap.wait_send()

    def finish(step, carry):
        for way in range(2):
            for piece in range(PIECES):
                give(way, step, piece).wait_send()
                share_wait(way, step, piece)
                share_copy(way, step, piece).wait_send()

                @pl.when(step < RING - 1)
                def _():
                    ring_copy(way, step, piece).wait_send()
                    round_copy(way, step, piece).wait_send()

        @pl.when(step < RING - 1)
        def _():
            tiny_ring(step).wait_send()
            tiny_round(step).wait_send()

        return carry

    lax.fori_loop(0, RING, finish, 0)
    for way in range(2):
        for piece in range(PIECES):
            own_copy(way, piece).wait()


def run_sums(left, right, small):
    rows = right.shape[1]
    anywhere = pl.BlockSpec(memory_space=pl.ANY)
    vectors = pl.BlockSpec(memory_space=pltpu.VMEM)

    def pieces(*lead, dtype=BF16):
        return pltpu.VMEM((*lead, PIECE, D), dtype)

    dma = pltpu.SemaphoreType.DMA
    scratch = [
        pltpu.VMEM(left.shape, BF16), pltpu.VMEM(right.shape, BF16),
        pieces(4, 2, PIECES, dtype=F32), pieces(2, RING, PIECES), pieces(2, RING, PIECES),
        pieces(2, RING - 1, PIECES), pieces(2, PIECES),
        pltpu.VMEM((RING, 16, 128), F32), pltpu.VMEM((RING, 16, 128), F32), pltpu.VMEM((RING, 16, 128), F32),
        pltpu.VMEM((RING - 1, 16, 128), F32), pltpu.VMEM((RING - 1, 16, 128), F32), pltpu.VMEM((RING, 16, 128), F32),
        dma((16,)), dma((2, RING, PIECES)), dma((2, RING, PIECES)),
        dma((2, RING - 1, PIECES)), dma((2, RING - 1, PIECES)), dma((2, PIECES)),
        dma((2, RING - 1, PIECES)), dma((2, RING - 1, PIECES)), dma((2, RING, PIECES)), dma((2, RING, PIECES)),
        dma((2,)), dma((RING - 1,)), dma((RING - 1,)), dma((RING - 1,)), dma((RING - 1,)),
    ]
    return pl.pallas_call(
        sums_kernel,
        out_shape=(jax.ShapeDtypeStruct((12, D, D), BF16), jax.ShapeDtypeStruct((16, D), F32)),
        in_specs=[anywhere, anywhere, vectors],
        out_specs=[anywhere, vectors],
        scratch_shapes=scratch,
        compiler_params=pltpu.CompilerParams(
            collective_id=1, has_side_effects=True, vmem_limit_bytes=60 * 1024 * 1024
        ),
        cost_estimate=pl.CostEstimate(flops=rows * 2 * 7077888, bytes_accessed=70000000, transcendentals=0),
    )(left, right, small)


def plain_sums(left, right, small):
    panels = [dot(left[row : row + D], right[number]).astype(BF16) for row, number in PANELS]
    return lax.psum(jnp.stack(panels), "dp"), lax.psum(small, "dp")


def per_device(grid, tokens, cotangent, lengths, spans, *weights):
    act, dx, left, right, small = run_layers(tokens, cotangent, lengths, spans, *weights)
    grads, small = (run_sums if grid else plain_sums)(left, right, small)
    wide = grads.astype(F32)
    up = jnp.concatenate([wide[4], wide[5], wide[6], wide[7]], axis=1)
    down = wide[8:12].reshape(FF, D)
    return (
        act[None], dx[None], wide[0][None], wide[1][None], wide[2][None], wide[3][None], up[None], down[None],
        small[0:4][None], small[4:8].reshape(1, FF), small[8:10][None], small[10:12][None],
    )


def solution(mesh):
    in_specs = (
        P("dp", None), P("dp", None), P("dp"), P("dp", None),
        P("section", None, None), P("section", None, None), P("section", None, None),
        P("section", None, None), P("section", None, None), P("section", None, None),
        P("section", None, None), P("section", None), P("section", None, None), P("section", None, None),
    )
    out_specs = (
        P("section", "dp", None), P("section", "dp", None),
        P("section", None, None), P("section", None, None), P("section", None, None),
        P("section", None, None), P("section", None, None), P("section", None, None),
        P("section", None, None), P("section", None), P("section", None, None), P("section", None, None),
    )
    part = functools.partial(per_device, mesh.shape["dp"] == 2 * RING)
    return jax.shard_map(part, mesh=mesh, in_specs=in_specs, out_specs=out_specs, check_vma=False)
```

```python
import functools

import jax
import jax.numpy as jnp
from jax import lax
from jax.experimental import pallas as pl
from jax.experimental.pallas import tpu as pltpu
from jax.sharding import PartitionSpec as P

D = 768
HEADS = 12
HEAD_DIM = 64
PAIRS = HEADS // 2
FF = 3072
LENGTH = 160
LEAST = 96
CHAINS_MB = 2
ROWS = CHAINS_MB * LENGTH
SUB = 32
WIDE = 256

F32 = jnp.float32
BF16 = jnp.bfloat16
MESH = pl.DeviceIdType.MESH


def dot(left, right):
    return jnp.dot(left, right, preferred_element_type=F32)


def dot_t(left, right):
    return lax.dot_general(left, right, (((1,), (1,)), ((), ())), preferred_element_type=F32)


def t_dot(left, right):
    return lax.dot_general(left, right, (((0,), (0,)), ((), ())), preferred_element_type=F32)


def fold(block):
    return jnp.sum(block.reshape(-1, 8, block.shape[-1]), axis=0)


def gelu_parts(u):
    t = pl.reciprocal(1.0 + 0.23164189 * jnp.abs(u), approx=True)
    gauss = jnp.exp2(u * u * -0.7213475204444817)
    poly = t * (
        0.127414796 + t * (-0.142248368 + t * (0.7107068705 + t * (-0.7265760135 + t * 0.5307027145)))
    )
    tail = poly * gauss
    cdf = jnp.where(u >= 0, 1.0 - tail, tail)
    return u * cdf, cdf + (u * 0.3989422804014327) * gauss


def layers_kernel(
    micro_count,
    tokens, cotangent, lengths, spans,
    wq, wk, wv, wo, w1, w2, bias_in, up_bias_in, gains_in, shifts_in,
    act_out, dx_out, left_out, right_out, small_out,
    wq_s, wk_s, wv_s, wo_s, w1_s, w2_s,
    h_s, q_s, k_s, v_s, p_s, o_s, n_s, xa_s, xb_s, z_s, g_s, inva_s, invb_s,
    y_s, dy_s, df_s, da_s, do_s, dx_s, wide_s, turn_s, acc_s, accu_s,
    w_sem, in_sem, out_sem, turn_sem, fwd_send, fwd_recv, bwd_send, bwd_recv,
):
    section = lax.axis_index("section")
    other = 1 - section
    first = section == 0
    last = section == 1

    barrier = pltpu.get_barrier_semaphore()
    pl.semaphore_signal(barrier, inc=1, device_id={"section": other}, device_id_type=MESH)

    weight_pairs = ((wq, wq_s), (wk, wk_s), (wv, wv_s), (wo, wo_s), (w1, w1_s), (w2, w2_s))

    def weight_copy(index):
        source, target = weight_pairs[index]
        return pltpu.make_async_copy(source.at[0], target, w_sem.at[index])

    def rows_of(index):
        return pl.ds(pl.multiple_of(index * ROWS, ROWS), ROWS)

    def entry_copy(index):
        return pltpu.make_async_copy(tokens.at[rows_of(index)], h_s.at[rows_of(index)], in_sem.at[index])

    def cot_copy(index):
        return pltpu.make_async_copy(cotangent.at[rows_of(index)], dy_s.at[rows_of(index)], in_sem.at[index])

    def forward_send(index):
        return pltpu.make_async_remote_copy(
            src_ref=y_s.at[rows_of(index)],
            dst_ref=h_s.at[rows_of(index)],
            send_sem=fwd_send.at[index],
            recv_sem=fwd_recv.at[index],
            device_id={"section": other},
            device_id_type=MESH,
        )

    def backward_send(index):
        return pltpu.make_async_remote_copy(
            src_ref=y_s.at[rows_of(index)],
            dst_ref=dy_s.at[rows_of(index)],
            send_sem=bwd_send.at[index],
            recv_sem=bwd_recv.at[index],
            device_id={"section": other},
            device_id_type=MESH,
        )

    backward_outs = ((q_s, 0), (k_s, 1), (v_s, 2), (da_s, 3), (df_s, 8))

    def act_copy(index):
        return pltpu.make_async_copy(y_s.at[rows_of(index)], act_out.at[rows_of(index)], out_sem.at[0, index])

    def dx_copy(index):
        return pltpu.make_async_copy(dx_s.at[rows_of(index)], dx_out.at[rows_of(index)], out_sem.at[1, index])

    def right_copies(index):
        for slot, (source, place) in enumerate(backward_outs):
            yield pltpu.make_async_copy(
                source.at[rows_of(index)], right_out.at[place, rows_of(index)], out_sem.at[2 + slot, index]
            )
        for panel in range(FF // D):
            yield pltpu.make_async_copy(
                g_s.at[rows_of(index), pl.ds(panel * D, D)],
                right_out.at[4 + panel, rows_of(index)],
                out_sem.at[7 + panel, index],
            )

    def turn_copy(slot, row):
        return pltpu.make_async_copy(
            turn_s.at[slot], left_out.at[pl.ds(pl.multiple_of(row, 128), 128)], turn_sem.at[slot]
        )

    def transpose_all():
        done = 0
        for source, tiles in ((h_s, D // 128), (o_s, D // 128), (n_s, D // 128), (z_s, FF // 128)):

            def tile_step(tile, carry, source=source, done=done):
                number = tile + done
                slot = lax.rem(number, 2)

                @pl.when(number >= 2)
                def _():
                    turn_copy(slot, (number - 2) * 128).wait()

                turn_s[slot] = source[:, pl.ds(pl.multiple_of(tile * 128, 128), 128)].T
                turn_copy(slot, number * 128).start()
                return carry

            lax.fori_loop(0, tiles, tile_step, 0)
            done += tiles
        for number in (done - 2, done - 1):
            turn_copy(number % 2, number * 128).wait()

    @pl.when(first)
    def _():
        for index in range(micro_count):
            entry_copy(index).start()

    @pl.when(last)
    def _():
        for index in range(micro_count):
            cot_copy(index).start()

    for index in range(6):
        weight_copy(index).start()

    acc_s[...] = jnp.zeros_like(acc_s)
    accu_s[...] = jnp.zeros_like(accu_s)

    bias = bias_in[0].astype(F32)
    gains = gains_in[0].astype(F32)
    shifts = shifts_in[0].astype(F32)
    low_half = lax.broadcasted_iota(jnp.int32, (1, 8, 128), 2) < HEAD_DIM
    keep_low = jnp.where(lax.broadcasted_iota(jnp.int32, (1, 16, 128), 2) < HEAD_DIM, 1.0, 0.0)
    keep_high = (1.0 - keep_low).astype(BF16)
    keep_low = keep_low.astype(BF16)

    def stacked(pair_block):
        tiles = pair_block.reshape(-1, 16, 128)
        return jnp.concatenate([tiles * keep_low, tiles * keep_high], axis=0).reshape(2 * LENGTH, 128)

    def merged(tall):
        tiles = tall.reshape(2, LENGTH // 8, 8, 128)
        return jnp.where(low_half, tiles[0], tiles[1]).reshape(LENGTH, 128)

    pl.semaphore_wait(barrier, 1)

    def forward(index, carry):
        base = index * ROWS
        rows = rows_of(index)

        @pl.when(first)
        def _():
            entry_copy(index).wait()
            for chain in range(CHAINS_MB):
                number = index * CHAINS_MB + chain
                start, stop = spans[number, 0], spans[number, 1]
                spot = lax.broadcasted_iota(jnp.int32, (LENGTH, D), 0)
                here = pl.ds(pl.multiple_of(base + chain * LENGTH, LENGTH), LENGTH)
                keep = (spot < start) | (spot >= stop)
                h_s[here, :] = jnp.where(keep, h_s[here, :].astype(F32), 0.0).astype(BF16)

        @pl.when(last)
        def _():
            forward_send(index).wait_recv()

        @pl.when(index == 0)
        def _():
            for number in range(3):
                weight_copy(number).wait()

        for weight, bias_row, target in ((wq_s, 0, q_s), (wk_s, None, k_s), (wv_s, 1, v_s)):
            for n0 in range(0, D, WIDE):
                block = dot(h_s[rows, :], weight[:, n0 : n0 + WIDE])
                if bias_row is not None:
                    block = block + bias[bias_row : bias_row + 1, n0 : n0 + WIDE]
                if target is q_s:
                    block = block * 0.125
                target[rows, n0 : n0 + WIDE] = block.astype(BF16)

        def chain_step(chain, carry):
            here = pl.ds(pl.multiple_of(base + chain * LENGTH, LENGTH), LENGTH)
            number = index * CHAINS_MB + chain
            spot = lax.broadcasted_iota(jnp.int32, (LENGTH - LEAST, 2 * LENGTH), 0) + LEAST
            penalty = jnp.where(spot < lengths[number], 0.0, -1000000000.0)
            for pair in range(PAIRS):
                lanes = slice(pair * 128, pair * 128 + 128)
                scores = dot_t(k_s[here, lanes], stacked(q_s[here, lanes]))
                scores = jnp.concatenate([scores[:LEAST], scores[LEAST:] + penalty], axis=0)
                raised = jnp.exp(scores - jnp.max(scores, axis=0, keepdims=True))
                attend = (raised * (1.0 / jnp.sum(raised, axis=0, keepdims=True))).astype(BF16)
                p_s[number, pair] = attend
                o_s[here, lanes] = merged(t_dot(attend, v_s[here, lanes])).astype(BF16)
            return carry

        lax.fori_loop(0, CHAINS_MB, chain_step, 0)

        @pl.when(index == 0)
        def _():
            weight_copy(3).wait()

        for n0 in range(0, D, WIDE):
            wide_s[:, n0 : n0 + WIDE] = dot(o_s[rows, :], wo_s[:, n0 : n0 + WIDE])

        def first_norm(step, carry):
            part = pl.ds(pl.multiple_of(step * SUB, SUB), SUB)
            here = pl.ds(pl.multiple_of(base + step * SUB, SUB), SUB)
            r = h_s[here, :].astype(F32) + wide_s[part, :] + bias[2:3]
            centered = r - jnp.mean(r, axis=-1, keepdims=True)
            inv = lax.rsqrt(jnp.mean(centered * centered, axis=-1, keepdims=True) + 1e-05)
            hat = centered * inv
            normed = hat * gains[0:1] + shifts[0:1]
            xa_s[here, :] = hat.astype(BF16)
            inva_s[here, :] = jnp.broadcast_to(inv, (SUB, 128))
            n_s[here, :] = normed.astype(BF16)
            wide_s[part, :] = normed
            return carry

        lax.fori_loop(0, ROWS // SUB, first_norm, 0, unroll=5)

        @pl.when(index == 0)
        def _():
            weight_copy(4).wait()
            weight_copy(5).wait()

        def lift(n0):
            return dot(n_s[rows, :], w1_s[:, n0 : n0 + WIDE])

        following = lift(0)
        for n0 in range(0, FF, WIDE):
            block = following
            if n0 + WIDE < FF:
                following = lift(n0 + WIDE)
            up_bias = up_bias_in[0:1, n0 : n0 + WIDE].astype(F32)
            for r0 in range(0, ROWS, SUB):
                here = pl.ds(pl.multiple_of(base + r0, SUB), SUB)
                act, slope = gelu_parts(block[r0 : r0 + SUB] + up_bias)
                z_s[here, n0 : n0 + WIDE] = act.astype(BF16)
                g_s[here, n0 : n0 + WIDE] = slope.astype(BF16)

        for n0 in range(0, D, WIDE):
            wide_s[:, n0 : n0 + WIDE] += dot(z_s[rows, :], w2_s[:, n0 : n0 + WIDE])

        def second_norm(step, carry):
            part = pl.ds(pl.multiple_of(step * SUB, SUB), SUB)
            here = pl.ds(pl.multiple_of(base + step * SUB, SUB), SUB)
            r = wide_s[part, :] + bias[3:4]
            centered = r - jnp.mean(r, axis=-1, keepdims=True)
            inv = lax.rsqrt(jnp.mean(centered * centered, axis=-1, keepdims=True) + 1e-05)
            hat = centered * inv
            xb_s[here, :] = hat.astype(BF16)
            invb_s[here, :] = jnp.broadcast_to(inv, (SUB, 128))
            y_s[here, :] = (hat * gains[1:2] + shifts[1:2]).astype(BF16)
            return carry

        lax.fori_loop(0, ROWS // SUB, second_norm, 0, unroll=5)

        @pl.when(first)
        def _():
            forward_send(index).start()

        act_copy(index).start()
        return carry

    lax.fori_loop(0, micro_count, forward, 0)

    def forward_done(index, carry):
        @pl.when(first)
        def _():
            forward_send(index).wait_send()

        act_copy(index).wait()
        return carry

    lax.fori_loop(0, micro_count, forward_done, 0)

    @pl.when(first)
    def _():
        transpose_all()

    def backward(index, carry):
        base = index * ROWS
        rows = rows_of(index)

        @pl.when(first)
        def _():
            backward_send(index).wait_recv()

        @pl.when(last)
        def _():
            cot_copy(index).wait()

        def second_back(step, carry):
            part = pl.ds(pl.multiple_of(step * SUB, SUB), SUB)
            here = pl.ds(pl.multiple_of(base + step * SUB, SUB), SUB)
            dy = dy_s[here, :].astype(F32)
            hat = xb_s[here, :].astype(F32)
            acc_s[9] += fold(dy * hat)
            acc_s[11] += fold(dy)
            scaled = dy * gains[1:2]
            mean_plain = jnp.mean(scaled, axis=-1, keepdims=True)
            mean_hat = jnp.mean(scaled * hat, axis=-1, keepdims=True)
            grad = (scaled - mean_plain - hat * mean_hat) * invb_s[here, 0:1]
            wide_s[part, :] = grad
            df_s[here, :] = grad.astype(BF16)
            acc_s[3] += fold(grad)
            return carry

        lax.fori_loop(0, ROWS // SUB, second_back, 0, unroll=5)

        def drop(n0):
            return dot_t(df_s[rows, :], w2_s[n0 : n0 + WIDE, :])

        following = drop(0)
        for n0 in range(0, FF, WIDE):
            block = following
            if n0 + WIDE < FF:
                following = drop(n0 + WIDE)
            sums = jnp.zeros((8, WIDE), F32)
            for r0 in range(0, ROWS, SUB):
                here = pl.ds(pl.multiple_of(base + r0, SUB), SUB)
                part = block[r0 : r0 + SUB] * g_s[here, n0 : n0 + WIDE].astype(F32)
                g_s[here, n0 : n0 + WIDE] = part.astype(BF16)
                sums = sums + fold(part)
            accu_s[:, n0 : n0 + WIDE] += sums

        for n0 in range(0, D, WIDE):
            wide_s[:, n0 : n0 + WIDE] += dot_t(g_s[rows, :], w1_s[n0 : n0 + WIDE, :])

        def first_back(step, carry):
            part = pl.ds(pl.multiple_of(step * SUB, SUB), SUB)
            here = pl.ds(pl.multiple_of(base + step * SUB, SUB), SUB)
            dn = wide_s[part, :]
            hat = xa_s[here, :].astype(F32)
            acc_s[8] += fold(dn * hat)
            acc_s[10] += fold(dn)
            scaled = dn * gains[0:1]
            mean_plain = jnp.mean(scaled, axis=-1, keepdims=True)
            mean_hat = jnp.mean(scaled * hat, axis=-1, keepdims=True)
            grad = (scaled - mean_plain - hat * mean_hat) * inva_s[here, 0:1]
            wide_s[part, :] = grad
            da_s[here, :] = grad.astype(BF16)
            acc_s[2] += fold(grad)
            return carry

        lax.fori_loop(0, ROWS // SUB, first_back, 0, unroll=5)

        for n0 in range(0, D, WIDE):
            do_s[:, n0 : n0 + WIDE] = dot_t(da_s[rows, :], wo_s[n0 : n0 + WIDE, :]).astype(BF16)

        def chain_step(chain, carry):
            here = pl.ds(pl.multiple_of(base + chain * LENGTH, LENGTH), LENGTH)
            near = pl.ds(pl.multiple_of(chain * LENGTH, LENGTH), LENGTH)
            number = index * CHAINS_MB + chain
            for pair in range(PAIRS):
                lanes = slice(pair * 128, pair * 128 + 128)
                query, key_rows, value = q_s[here, lanes], k_s[here, lanes], v_s[here, lanes]
                grad_mix = do_s[near, lanes]
                attend = p_s[number, pair]
                grad_tall = stacked(grad_mix)
                grad_attend = dot_t(value, grad_tall)
                attend_wide = attend.astype(F32)
                weighted = attend_wide * grad_attend
                delta = jnp.sum(weighted, axis=0, keepdims=True) / jnp.sum(attend_wide, axis=0, keepdims=True)
                grad_scores = (weighted - attend_wide * delta).astype(BF16)
                dv = dot(attend, grad_tall)
                dk = dot(grad_scores, stacked(query))
                dq = merged(t_dot(grad_scores, key_rows)) * 0.125
                q_s[here, lanes] = dq.astype(BF16)
                k_s[here, lanes] = dk.astype(BF16)
                v_s[here, lanes] = dv.astype(BF16)
                acc_s[0, :, lanes] += fold(dq)
                acc_s[1, :, lanes] += fold(dv)
            return carry

        lax.fori_loop(0, CHAINS_MB, chain_step, 0)

        for n0 in range(0, D, WIDE):
            block = dot_t(q_s[rows, :], wq_s[n0 : n0 + WIDE, :])
            block = block + dot_t(k_s[rows, :], wk_s[n0 : n0 + WIDE, :])
            block = block + dot_t(v_s[rows, :], wv_s[n0 : n0 + WIDE, :])
            wide_s[:, n0 : n0 + WIDE] += block

        @pl.when(last)
        def _():
            low = wide_s[...].astype(BF16)
            y_s[rows, :] = low
            dx_s[rows, :] = low.astype(F32)
            backward_send(index).start()

        @pl.when(first)
        def _():
            for chain in range(CHAINS_MB):
                number = index * CHAINS_MB + chain
                start, stop = spans[number, 0], spans[number, 1]
                spot = lax.broadcasted_iota(jnp.int32, (LENGTH, D), 0)
                here = pl.ds(pl.multiple_of(base + chain * LENGTH, LENGTH), LENGTH)
                keep = (spot < start) | (spot >= stop)
                dx_s[here, :] = jnp.where(keep, wide_s[chain * LENGTH : (chain + 1) * LENGTH, :], 0.0)

        dx_copy(index).start()
        for copy in right_copies(index):
            copy.start()
        return carry

    lax.fori_loop(0, micro_count, backward, 0)

    @pl.when(last)
    def _():
        transpose_all()

    for number in range(12):
        if 4 <= number < 8:
            panel = accu_s[:, (number - 4) * D : (number - 3) * D]
        else:
            panel = acc_s[number]
        small_out[number : number + 1, :] = jnp.sum(panel, axis=0, keepdims=True)
    small_out[12:16, :] = jnp.zeros((4, D), F32)

    def backward_done(index, carry):
        @pl.when(last)
        def _():
            backward_send(index).wait_send()

        dx_copy(index).wait()
        for copy in right_copies(index):
            copy.wait()
        return carry

    lax.fori_loop(0, micro_count, backward_done, 0)


def run_layers(tokens, cotangent, lengths, spans, *weights):
    rows = tokens.shape[0]
    micro_count = rows // ROWS
    chains = rows // LENGTH
    anywhere = pl.BlockSpec(memory_space=pl.ANY)
    scalars = pl.BlockSpec(memory_space=pltpu.SMEM)
    vectors = pl.BlockSpec(memory_space=pltpu.VMEM)
    out_shape = (
        jax.ShapeDtypeStruct((rows, D), BF16),
        jax.ShapeDtypeStruct((rows, D), F32),
        jax.ShapeDtypeStruct((3 * D + FF, rows), BF16),
        jax.ShapeDtypeStruct((9, rows, D), BF16),
        jax.ShapeDtypeStruct((16, D), F32),
    )

    def vm(count, width=D, dtype=BF16):
        return pltpu.VMEM((count, width), dtype)

    scratch = [
        vm(D), vm(D), vm(D), vm(D), vm(D, FF), vm(FF),
        vm(rows), vm(rows), vm(rows), vm(rows),
        pltpu.VMEM((chains, PAIRS, LENGTH, 2 * LENGTH), BF16),
        vm(rows), vm(rows), vm(rows), vm(rows), vm(rows, FF), vm(rows, FF),
        vm(rows, 128, F32), vm(rows, 128, F32),
        vm(rows), vm(rows), vm(rows), vm(rows), vm(ROWS), vm(rows, D, F32),
        vm(ROWS, D, F32), pltpu.VMEM((2, 128, rows), BF16), pltpu.VMEM((12, 8, D), F32), vm(8, FF, F32),
        pltpu.SemaphoreType.DMA((6,)),
        pltpu.SemaphoreType.DMA((micro_count,)),
        pltpu.SemaphoreType.DMA((11, micro_count)),
        pltpu.SemaphoreType.DMA((2,)),
        pltpu.SemaphoreType.DMA((micro_count,)),
        pltpu.SemaphoreType.DMA((micro_count,)),
        pltpu.SemaphoreType.DMA((micro_count,)),
        pltpu.SemaphoreType.DMA((micro_count,)),
    ]
    return pl.pallas_call(
        functools.partial(layers_kernel, micro_count),
        out_shape=out_shape,
        in_specs=[anywhere, anywhere, scalars, scalars] + [anywhere] * 6 + [vectors] * 4,
        out_specs=[anywhere] * 4 + [vectors],
        scratch_shapes=scratch,
        compiler_params=pltpu.CompilerParams(
            collective_id=0, has_side_effects=True, vmem_limit_bytes=60 * 1024 * 1024
        ),
        cost_estimate=pl.CostEstimate(
            flops=rows * 2 * 2 * 2 * 7077888, bytes_accessed=60000000, transcendentals=rows * FF * 2
        ),
    )(tokens, cotangent, lengths, spans, *weights)


RING = 8
PIECES = 3
PIECE = D // RING
PANELS = (
    (0, 0), (0, 1), (0, 2), (D, 3), (2 * D, 4), (2 * D, 5),
    (2 * D, 6), (2 * D, 7), (3 * D, 8), (4 * D, 8), (5 * D, 8), (6 * D, 8),
)


def sums_kernel(
    left, right, small_in, grads_out, small_out,
    left_s, right_s, total_s, give_s, take_s, ring_s, own_s,
    tiny_s, tiny_take_s, tiny_sum_s, tiny_go_s, tiny_ring_s, tiny_own_s,
    load_sem, give_sem, take_sem, ring_send, ring_recv, own_sem, round_send, round_recv, share_send, share_recv,
    tiny_sem, tiny_ring_send, tiny_ring_recv, tiny_round_send, tiny_round_recv,
):
    me = lax.axis_index("dp")
    core = lax.rem(me, 2)
    high = lax.rem(lax.div(me, 2), 2)
    depth = lax.div(me, 4)
    place = depth + high * (7 - 2 * depth)

    def device(spot, on_core):
        row = lax.div(spot, 4)
        return {"dp": 4 * (spot + row * (7 - 2 * spot)) + 2 * row + on_core}

    ahead = device(lax.rem(place + 1, RING), core)
    behind = device(lax.rem(place + RING - 1, RING), core)
    beside = device(place, 1 - core)
    targets = (ahead, behind)

    barrier = pltpu.get_barrier_semaphore()
    for peer in (ahead, behind, beside):
        pl.semaphore_signal(barrier, inc=1, device_id=peer, device_id_type=MESH)

    def block(way, step):
        return lax.rem(place - step + RING, RING) if way == 0 else lax.rem(place + step, RING)

    def late_block(way, step):
        return lax.rem(place + 1 - step + RING, RING) if way == 0 else lax.rem(place + RING - 1 + step, RING)

    def load_left(part):
        return pltpu.make_async_copy(left.at[pl.ds(part * D, D)], left_s.at[pl.ds(part * D, D)], load_sem.at[part])

    def load_right(part):
        return pltpu.make_async_copy(right.at[part], right_s.at[part], load_sem.at[7 + part])

    def remote(source, target, send, recv, peer):
        return pltpu.make_async_remote_copy(
            src_ref=source, dst_ref=target, send_sem=send, recv_sem=recv, device_id=peer, device_id_type=MESH
        )

    def give(way, step, piece):
        return remote(
            give_s.at[way, step, piece], take_s.at[way, step, piece],
            give_sem.at[way, step, piece], take_sem.at[way, step, piece], beside,
        )

    def ring_copy(way, step, piece):
        return remote(
            take_s.at[way, step, piece], ring_s.at[way, step, piece],
            ring_send.at[way, step, piece], ring_recv.at[way, step, piece], targets[way],
        )

    def region(way, spot, piece, on_core):
        rows = pl.ds(pl.multiple_of(spot * PIECE, PIECE), PIECE)
        return grads_out.at[6 * way + 3 * on_core + piece, rows]

    def own_copy(way, piece):
        return pltpu.make_async_copy(
            own_s.at[way, piece], region(way, late_block(way, 0), piece, core), own_sem.at[way, piece]
        )

    def round_copy(way, step, piece, source=None):
        target = region(way, late_block(way, step), piece, core)
        return remote(
            target if source is None else source, target,
            round_send.at[way, step, piece], round_recv.at[way, step, piece], targets[way],
        )

    def round_wait(way, step, piece):
        target = region(way, late_block(way, step + 1), piece, core)
        remote(
            target, target, round_send.at[way, step, piece], round_recv.at[way, step, piece], targets[way]
        ).wait_recv()

    def share_copy(way, step, piece, source=None):
        target = region(way, late_block(way, step), piece, core)
        return remote(
            target if source is None else source, target,
            share_send.at[way, step, piece], share_recv.at[way, step, piece], beside,
        )

    def share_wait(way, step, piece):
        target = region(way, late_block(way, step), piece, 1 - core)
        remote(
            target, target, share_send.at[way, step, piece], share_recv.at[way, step, piece], beside
        ).wait_recv()

    tiny_swap = remote(tiny_s, tiny_take_s, tiny_sem.at[0], tiny_sem.at[1], beside)

    def tiny_ring(step):
        return remote(
            tiny_go_s.at[step], tiny_ring_s.at[step], tiny_ring_send.at[step], tiny_ring_recv.at[step], ahead
        )

    def tiny_round(step):
        spot = late_block(0, step)
        return remote(
            tiny_own_s.at[spot], tiny_own_s.at[spot], tiny_round_send.at[step], tiny_round_recv.at[step], ahead
        )

    def tiny_round_wait(step):
        spot = late_block(0, step + 1)
        remote(
            tiny_own_s.at[spot], tiny_own_s.at[spot], tiny_round_send.at[step], tiny_round_recv.at[step], ahead
        ).wait_recv()

    loads = []
    for piece in range(PIECES):
        for way in range(2):
            for half in range(2):
                first_row, number = PANELS[6 * way + 3 * half + piece]
                for kind, part in ((load_right, number), (load_left, first_row // D)):
                    if (kind, part) not in [entry[:2] for entry in loads]:
                        loads.append((kind, part, way, piece))
    for kind, part, _, _ in loads:
        kind(part).start()

    for part in range(RING):
        if part * 128 < D:
            tiny_s[part] = small_in[:, part * 128 : part * 128 + 128]
        else:
            tiny_s[part] = jnp.zeros((16, 128), F32)

    pl.semaphore_wait(barrier, 3)
    tiny_swap.start()

    def products(group, way, piece):
        near, far = PANELS[6 * way + piece], PANELS[6 * way + 3 + piece]
        for mine in (False, True):
            pick = core if mine else 1 - core
            first_row = near[0] + pick * (far[0] - near[0])
            number = near[1] + pick * (far[1] - near[1])
            blocks = []
            for step in (2 * group, 2 * group + 1):
                start = pl.multiple_of(first_row + block(way, step) * PIECE, PIECE)
                blocks.append(left_s[pl.ds(start, PIECE), :])
            tall = jnp.concatenate(blocks, axis=0)
            for n0 in range(0, D, WIDE):
                product = dot(tall, right_s[number, :, n0 : n0 + WIDE])
                for half in range(2):
                    step = 2 * group + half
                    part = product[half * PIECE : (half + 1) * PIECE]
                    if mine:
                        total_s[lax.rem(step, 4), way, piece, :, n0 : n0 + WIDE] = part
                    else:
                        give_s[way, step, piece, :, n0 : n0 + WIDE] = part.astype(BF16)
            if not mine:
                give(way, 2 * group, piece).start()
                give(way, 2 * group + 1, piece).start()

    def add_piece(step, way, piece, target):
        slot = lax.rem(step, 4)
        for r0 in range(0, PIECE, SUB):
            part = slice(r0, r0 + SUB)
            whole = total_s[slot, way, piece, part] + take_s[way, step, piece, part].astype(F32)
            target[part] = whole.astype(BF16)

    def reduce_step(step, carry):
        slot = lax.rem(step, 4)
        spot = block(0, step)

        @pl.when(step < RING - 1)
        def _():
            tiny_ring(step - 1).wait_recv()
            tiny_go_s[step] = tiny_sum_s[spot] + tiny_ring_s[step - 1]
            tiny_ring(step).start()

        @pl.when(step == RING - 1)
        def _():
            tiny_ring(step - 1).wait_recv()
            tiny_own_s[spot] = tiny_sum_s[spot] + tiny_ring_s[step - 1]
            tiny_round(0).start()

        for piece in range(PIECES):
            for way in range(2):
                give(way, step, piece).wait_recv()
                ring_copy(way, step - 1, piece).wait_recv()
                for r0 in range(0, PIECE, SUB):
                    part = slice(r0, r0 + SUB)
                    total_s[slot, way, piece, part] += ring_s[way, step - 1, piece, part].astype(F32)

                @pl.when(step < RING - 1)
                def _():
                    add_piece(step, way, piece, take_s.at[way, step, piece])
                    ring_copy(way, step, piece).start()

                @pl.when(step == RING - 1)
                def _():
                    add_piece(step, way, piece, own_s.at[way, piece])
                    round_copy(way, 0, piece, own_s.at[way, piece]).start()
                    share_copy(way, 0, piece, own_s.at[way, piece]).start()
                    own_copy(way, piece).start()
        return carry

    def first_piece(way, piece):
        give(way, 0, piece).wait_recv()
        add_piece(0, way, piece, take_s.at[way, 0, piece])
        ring_copy(way, 0, piece).start()

    order = [(way, piece) for piece in range(PIECES) for way in range(2)]
    for number, (way, piece) in enumerate(order):
        for kind, part, at_way, at_piece in loads:
            if (at_way, at_piece) == (way, piece):
                kind(part).wait()
        products(0, way, piece)
        if number > 0:
            first_piece(*order[number - 1])
    first_piece(*order[-1])
    tiny_swap.wait_recv()
    tiny_sum_s[...] = tiny_s[...] + tiny_take_s[...]
    tiny_go_s[0] = tiny_sum_s[block(0, 0)]
    tiny_ring(0).start()

    def group_step(group, carry):
        @pl.when(group < RING // 2)
        def _():
            for way, piece in order:
                products(group, way, piece)

        top = jnp.minimum(2 * group + 1, RING)
        return lax.fori_loop(2 * group - 1, top, reduce_step, carry)

    lax.fori_loop(1, RING // 2 + 1, group_step, 0)

    def round_step(step, carry):
        tiny_round_wait(step - 1)

        @pl.when(step < RING - 1)
        def _():
            tiny_round(step).start()

        for piece in range(PIECES):
            for way in range(2):
                round_wait(way, step - 1, piece)

                @pl.when(step < RING - 1)
                def _():
                    round_copy(way, step, piece).start()

                share_copy(way, step, piece).start()
        return carry

    lax.fori_loop(1, RING, round_step, 0)

    for part in range(D // 128):
        small_out[:, part * 128 : part * 128 + 128] = tiny_own_s[part]
    tiny_swap.wait_send()

    def finish(step, carry):
        for way in range(2):
            for piece in range(PIECES):
                give(way, step, piece).wait_send()
                share_wait(way, step, piece)
                share_copy(way, step, piece).wait_send()

                @pl.when(step < RING - 1)
                def _():
                    ring_copy(way, step, piece).wait_send()
                    round_copy(way, step, piece).wait_send()

        @pl.when(step < RING - 1)
        def _():
            tiny_ring(step).wait_send()
            tiny_round(step).wait_send()

        return carry

    lax.fori_loop(0, RING, finish, 0)
    for way in range(2):
        for piece in range(PIECES):
            own_copy(way, piece).wait()


def run_sums(left, right, small):
    rows = right.shape[1]
    anywhere = pl.BlockSpec(memory_space=pl.ANY)
    vectors = pl.BlockSpec(memory_space=pltpu.VMEM)

    def pieces(*lead, dtype=BF16):
        return pltpu.VMEM((*lead, PIECE, D), dtype)

    dma = pltpu.SemaphoreType.DMA
    scratch = [
        pltpu.VMEM(left.shape, BF16), pltpu.VMEM(right.shape, BF16),
        pieces(4, 2, PIECES, dtype=F32), pieces(2, RING, PIECES), pieces(2, RING, PIECES),
        pieces(2, RING - 1, PIECES), pieces(2, PIECES),
        pltpu.VMEM((RING, 16, 128), F32), pltpu.VMEM((RING, 16, 128), F32), pltpu.VMEM((RING, 16, 128), F32),
        pltpu.VMEM((RING - 1, 16, 128), F32), pltpu.VMEM((RING - 1, 16, 128), F32), pltpu.VMEM((RING, 16, 128), F32),
        dma((16,)), dma((2, RING, PIECES)), dma((2, RING, PIECES)),
        dma((2, RING - 1, PIECES)), dma((2, RING - 1, PIECES)), dma((2, PIECES)),
        dma((2, RING - 1, PIECES)), dma((2, RING - 1, PIECES)), dma((2, RING, PIECES)), dma((2, RING, PIECES)),
        dma((2,)), dma((RING - 1,)), dma((RING - 1,)), dma((RING - 1,)), dma((RING - 1,)),
    ]
    return pl.pallas_call(
        sums_kernel,
        out_shape=(jax.ShapeDtypeStruct((12, D, D), BF16), jax.ShapeDtypeStruct((16, D), F32)),
        in_specs=[anywhere, anywhere, vectors],
        out_specs=[anywhere, vectors],
        scratch_shapes=scratch,
        compiler_params=pltpu.CompilerParams(
            collective_id=1, has_side_effects=True, vmem_limit_bytes=60 * 1024 * 1024
        ),
        cost_estimate=pl.CostEstimate(flops=rows * 2 * 7077888, bytes_accessed=70000000, transcendentals=0),
    )(left, right, small)


def plain_sums(left, right, small):
    panels = [dot(left[row : row + D], right[number]).astype(BF16) for row, number in PANELS]
    return lax.psum(jnp.stack(panels), "dp"), lax.psum(small, "dp")


SLOTS = 4
CUT = D // 2


def widen_kernel(
    grads, small, query_out, key_out, value_out, out_out, up_out, down_out,
    bias_out, up_bias_out, gain_out, shift_out, low_s, wide_s, in_sem, out_sem,
):
    jobs = []
    for panel in range(12):
        for half in range(2):
            rows = pl.ds(half * CUT, CUT)
            if panel < 4:
                target = (query_out, key_out, value_out, out_out)[panel].at[0, rows]
            elif panel < 8:
                target = up_out.at[0, rows, pl.ds((panel - 4) * D, D)]
            else:
                target = down_out.at[0, pl.ds((panel - 8) * D + half * CUT, CUT)]
            jobs.append((grads.at[panel, rows], target))

    def fetch(number):
        return pltpu.make_async_copy(jobs[number][0], low_s.at[number % SLOTS], in_sem.at[number % SLOTS])

    def store(number):
        return pltpu.make_async_copy(wide_s.at[number % SLOTS], jobs[number][1], out_sem.at[number % SLOTS])

    for number in range(SLOTS):
        fetch(number).start()
    bias_out[0] = small[0:4]
    for panel in range(FF // D):
        up_bias_out[:, panel * D : (panel + 1) * D] = small[4 + panel : 5 + panel]
    gain_out[0] = small[8:10]
    shift_out[0] = small[10:12]
    for number in range(len(jobs)):
        slot = number % SLOTS
        fetch(number).wait()
        if number >= SLOTS:
            store(number - SLOTS).wait()

        def turn(step, carry):
            part = pl.ds(pl.multiple_of(step * SUB, SUB), SUB)
            wide_s[slot, part, :] = low_s[slot, part, :].astype(F32)
            return carry

        lax.fori_loop(0, CUT // SUB, turn, 0, unroll=4)
        store(number).start()
        if number + SLOTS < len(jobs):
            fetch(number + SLOTS).start()
    for number in range(len(jobs) - SLOTS, len(jobs)):
        store(number).wait()


def widen(grads, small):
    anywhere = pl.BlockSpec(memory_space=pl.ANY)
    vectors = pl.BlockSpec(memory_space=pltpu.VMEM)
    square = jax.ShapeDtypeStruct((1, D, D), F32)
    return pl.pallas_call(
        widen_kernel,
        out_shape=(
            square, square, square, square,
            jax.ShapeDtypeStruct((1, D, FF), F32), jax.ShapeDtypeStruct((1, FF, D), F32),
            jax.ShapeDtypeStruct((1, 4, D), F32), jax.ShapeDtypeStruct((1, FF), F32),
            jax.ShapeDtypeStruct((1, 2, D), F32), jax.ShapeDtypeStruct((1, 2, D), F32),
        ),
        in_specs=[anywhere, vectors],
        out_specs=[anywhere] * 6 + [vectors] * 4,
        scratch_shapes=[
            pltpu.VMEM((SLOTS, CUT, D), BF16), pltpu.VMEM((SLOTS, CUT, D), F32),
            pltpu.SemaphoreType.DMA((SLOTS,)), pltpu.SemaphoreType.DMA((SLOTS,)),
        ],
        compiler_params=pltpu.CompilerParams(vmem_limit_bytes=60 * 1024 * 1024),
        cost_estimate=pl.CostEstimate(flops=7077888, bytes_accessed=42467328, transcendentals=0),
    )(grads, small)


def per_device(grid, tokens, cotangent, lengths, spans, *weights):
    act, dx, left, right, small = run_layers(tokens, cotangent, lengths, spans, *weights)
    grads, small = (run_sums if grid else plain_sums)(left, right, small)
    return (act[None], dx[None], *widen(grads, small))


def solution(mesh):
    in_specs = (
        P("dp", None), P("dp", None), P("dp"), P("dp", None),
        P("section", None, None), P("section", None, None), P("section", None, None),
        P("section", None, None), P("section", None, None), P("section", None, None),
        P("section", None, None), P("section", None), P("section", None, None), P("section", None, None),
    )
    out_specs = (
        P("section", "dp", None), P("section", "dp", None),
        P("section", None, None), P("section", None, None), P("section", None, None),
        P("section", None, None), P("section", None, None), P("section", None, None),
        P("section", None, None), P("section", None), P("section", None, None), P("section", None, None),
    )
    part = functools.partial(per_device, mesh.shape["dp"] == 2 * RING)
    return jax.shard_map(part, mesh=mesh, in_specs=in_specs, out_specs=out_specs, check_vma=False)
```

```python
import functools

import jax
import jax.numpy as jnp
from jax import lax
from jax.experimental import pallas as pl
from jax.experimental.pallas import tpu as pltpu
from jax.sharding import PartitionSpec as P

D = 768
HEADS = 12
HEAD_DIM = 64
PAIRS = HEADS // 2
FF = 3072
LENGTH = 160
LEAST = 96
CHAINS_MB = 2
ROWS = CHAINS_MB * LENGTH
SUB = 32
WIDE = 512

F32 = jnp.float32
BF16 = jnp.bfloat16
MESH = pl.DeviceIdType.MESH


def dot(left, right):
    return jnp.dot(left, right, preferred_element_type=F32)


def dot_t(left, right):
    return lax.dot_general(left, right, (((1,), (1,)), ((), ())), preferred_element_type=F32)


def t_dot(left, right):
    return lax.dot_general(left, right, (((0,), (0,)), ((), ())), preferred_element_type=F32)


def fold(block):
    return jnp.sum(block.reshape(-1, 8, block.shape[-1]), axis=0)


def gelu_parts(u):
    t = pl.reciprocal(1.0 + 0.23164189 * jnp.abs(u), approx=True)
    gauss = jnp.exp2(u * u * -0.7213475204444817)
    poly = t * (
        0.127414796 + t * (-0.142248368 + t * (0.7107068705 + t * (-0.7265760135 + t * 0.5307027145)))
    )
    tail = poly * gauss
    cdf = jnp.where(u >= 0, 1.0 - tail, tail)
    return u * cdf, cdf + (u * 0.3989422804014327) * gauss


def layers_kernel(
    micro_count,
    tokens, cotangent, lengths, spans,
    wq, wk, wv, wo, w1, w2, bias_in, up_bias_in, gains_in, shifts_in,
    act_out, dx_out, left_out, right_out, small_out,
    wq_s, wk_s, wv_s, wo_s, w1_s, w2_s,
    h_s, q_s, k_s, v_s, p_s, o_s, n_s, xa_s, xb_s, z_s, g_s, inva_s, invb_s,
    y_s, dy_s, df_s, da_s, do_s, dx_s, wide_s, turn_s, acc_s, accu_s,
    w_sem, in_sem, out_sem, turn_sem, fwd_send, fwd_recv, bwd_send, bwd_recv,
):
    section = lax.axis_index("section")
    other = 1 - section
    first = section == 0
    last = section == 1

    barrier = pltpu.get_barrier_semaphore()
    pl.semaphore_signal(barrier, inc=1, device_id={"section": other}, device_id_type=MESH)

    weight_pairs = ((wq, wq_s), (wk, wk_s), (wv, wv_s), (wo, wo_s), (w1, w1_s), (w2, w2_s))

    def weight_copy(index):
        source, target = weight_pairs[index]
        return pltpu.make_async_copy(source.at[0], target, w_sem.at[index])

    def rows_of(index):
        return pl.ds(pl.multiple_of(index * ROWS, ROWS), ROWS)

    def entry_copy(index):
        return pltpu.make_async_copy(tokens.at[rows_of(index)], h_s.at[rows_of(index)], in_sem.at[index])

    def cot_copy(index):
        return pltpu.make_async_copy(cotangent.at[rows_of(index)], dy_s.at[rows_of(index)], in_sem.at[index])

    def forward_send(index):
        return pltpu.make_async_remote_copy(
            src_ref=y_s.at[rows_of(index)],
            dst_ref=h_s.at[rows_of(index)],
            send_sem=fwd_send.at[index],
            recv_sem=fwd_recv.at[index],
            device_id={"section": other},
            device_id_type=MESH,
        )

    def backward_send(index):
        return pltpu.make_async_remote_copy(
            src_ref=y_s.at[rows_of(index)],
            dst_ref=dy_s.at[rows_of(index)],
            send_sem=bwd_send.at[index],
            recv_sem=bwd_recv.at[index],
            device_id={"section": other},
            device_id_type=MESH,
        )

    backward_outs = ((q_s, 0), (k_s, 1), (v_s, 2), (da_s, 3), (df_s, 8))

    def act_copy(index):
        return pltpu.make_async_copy(y_s.at[rows_of(index)], act_out.at[rows_of(index)], out_sem.at[0, index])

    def dx_copy(index):
        return pltpu.make_async_copy(dx_s.at[rows_of(index)], dx_out.at[rows_of(index)], out_sem.at[1, index])

    def right_copies(index):
        for slot, (source, place) in enumerate(backward_outs):
            yield pltpu.make_async_copy(
                source.at[rows_of(index)], right_out.at[place, rows_of(index)], out_sem.at[2 + slot, index]
            )
        for panel in range(FF // D):
            yield pltpu.make_async_copy(
                g_s.at[rows_of(index), pl.ds(panel * D, D)],
                right_out.at[4 + panel, rows_of(index)],
                out_sem.at[7 + panel, index],
            )

    def turn_copy(slot, row):
        return pltpu.make_async_copy(
            turn_s.at[slot], left_out.at[pl.ds(pl.multiple_of(row, 128), 128)], turn_sem.at[slot]
        )

    def transpose_all():
        done = 0
        for source, tiles in ((h_s, D // 128), (o_s, D // 128), (n_s, D // 128), (z_s, FF // 128)):

            def tile_step(tile, carry, source=source, done=done):
                number = tile + done
                slot = lax.rem(number, 2)

                @pl.when(number >= 2)
                def _():
                    turn_copy(slot, (number - 2) * 128).wait()

                turn_s[slot] = source[:, pl.ds(pl.multiple_of(tile * 128, 128), 128)].T
                turn_copy(slot, number * 128).start()
                return carry

            lax.fori_loop(0, tiles, tile_step, 0)
            done += tiles
        for number in (done - 2, done - 1):
            turn_copy(number % 2, number * 128).wait()

    @pl.when(first)
    def _():
        for index in range(micro_count):
            entry_copy(index).start()

    @pl.when(last)
    def _():
        for index in range(micro_count):
            cot_copy(index).start()

    for index in range(6):
        weight_copy(index).start()

    acc_s[...] = jnp.zeros_like(acc_s)
    accu_s[...] = jnp.zeros_like(accu_s)

    bias = bias_in[0].astype(F32)
    gains = gains_in[0].astype(F32)
    shifts = shifts_in[0].astype(F32)
    low_half = lax.broadcasted_iota(jnp.int32, (1, 8, 128), 2) < HEAD_DIM
    keep_low = jnp.where(lax.broadcasted_iota(jnp.int32, (1, 16, 128), 2) < HEAD_DIM, 1.0, 0.0)
    keep_high = (1.0 - keep_low).astype(BF16)
    keep_low = keep_low.astype(BF16)

    def stacked(pair_block):
        tiles = pair_block.reshape(-1, 16, 128)
        return jnp.concatenate([tiles * keep_low, tiles * keep_high], axis=0).reshape(2 * LENGTH, 128)

    def merged(tall):
        tiles = tall.reshape(2, LENGTH // 8, 8, 128)
        return jnp.where(low_half, tiles[0], tiles[1]).reshape(LENGTH, 128)

    pl.semaphore_wait(barrier, 1)

    def forward(index, carry):
        base = index * ROWS
        rows = rows_of(index)

        @pl.when(first)
        def _():
            entry_copy(index).wait()
            for chain in range(CHAINS_MB):
                number = index * CHAINS_MB + chain
                start, stop = spans[0, number], spans[1, number]
                spot = lax.broadcasted_iota(jnp.int32, (LENGTH, D), 0)
                here = pl.ds(pl.multiple_of(base + chain * LENGTH, LENGTH), LENGTH)
                keep = (spot < start) | (spot >= stop)
                h_s[here, :] = jnp.where(keep, h_s[here, :].astype(F32), 0.0).astype(BF16)

        @pl.when(last)
        def _():
            forward_send(index).wait_recv()

        @pl.when(index == 0)
        def _():
            for number in range(3):
                weight_copy(number).wait()

        for weight, bias_row, target in ((wq_s, 0, q_s), (wk_s, None, k_s), (wv_s, 1, v_s)):
            block = dot(h_s[rows, :], weight[...])
            if bias_row is not None:
                block = block + bias[bias_row : bias_row + 1]
            if target is q_s:
                block = block * 0.125
            target[rows, :] = block.astype(BF16)

        def chain_step(chain, carry):
            here = pl.ds(pl.multiple_of(base + chain * LENGTH, LENGTH), LENGTH)
            number = index * CHAINS_MB + chain
            spot = lax.broadcasted_iota(jnp.int32, (LENGTH - LEAST, 2 * LENGTH), 0) + LEAST
            penalty = jnp.where(spot < lengths[number], 0.0, -1000000000.0)
            for pair in range(PAIRS):
                lanes = slice(pair * 128, pair * 128 + 128)
                scores = dot_t(k_s[here, lanes], stacked(q_s[here, lanes]))
                scores = jnp.concatenate([scores[:LEAST], scores[LEAST:] + penalty], axis=0)
                raised = jnp.exp(scores - jnp.max(scores, axis=0, keepdims=True))
                attend = (raised * (1.0 / jnp.sum(raised, axis=0, keepdims=True))).astype(BF16)
                p_s[number, pair] = attend
                o_s[here, lanes] = merged(t_dot(attend, v_s[here, lanes])).astype(BF16)
            return carry

        lax.fori_loop(0, CHAINS_MB, chain_step, 0)

        @pl.when(index == 0)
        def _():
            weight_copy(3).wait()

        wide_s[...] = dot(o_s[rows, :], wo_s[...])

        def first_norm(step, carry):
            part = pl.ds(pl.multiple_of(step * SUB, SUB), SUB)
            here = pl.ds(pl.multiple_of(base + step * SUB, SUB), SUB)
            r = h_s[here, :].astype(F32) + wide_s[part, :] + bias[2:3]
            centered = r - jnp.mean(r, axis=-1, keepdims=True)
            inv = lax.rsqrt(jnp.mean(centered * centered, axis=-1, keepdims=True) + 1e-05)
            hat = centered * inv
            normed = hat * gains[0:1] + shifts[0:1]
            xa_s[here, :] = hat.astype(BF16)
            inva_s[here, :] = jnp.broadcast_to(inv, (SUB, 128))
            n_s[here, :] = normed.astype(BF16)
            wide_s[part, :] = normed
            return carry

        lax.fori_loop(0, ROWS // SUB, first_norm, 0, unroll=5)

        @pl.when(index == 0)
        def _():
            weight_copy(4).wait()
            weight_copy(5).wait()

        def lift(n0):
            return dot(n_s[rows, :], w1_s[:, n0 : n0 + WIDE])

        following = lift(0)
        for n0 in range(0, FF, WIDE):
            block = following
            if n0 + WIDE < FF:
                following = lift(n0 + WIDE)
            up_bias = up_bias_in[0:1, n0 : n0 + WIDE].astype(F32)
            for r0 in range(0, ROWS, SUB):
                here = pl.ds(pl.multiple_of(base + r0, SUB), SUB)
                act, slope = gelu_parts(block[r0 : r0 + SUB] + up_bias)
                z_s[here, n0 : n0 + WIDE] = act.astype(BF16)
                g_s[here, n0 : n0 + WIDE] = slope.astype(BF16)

        wide_s[...] += dot(z_s[rows, :], w2_s[...])

        def second_norm(step, carry):
            part = pl.ds(pl.multiple_of(step * SUB, SUB), SUB)
            here = pl.ds(pl.multiple_of(base + step * SUB, SUB), SUB)
            r = wide_s[part, :] + bias[3:4]
            centered = r - jnp.mean(r, axis=-1, keepdims=True)
            inv = lax.rsqrt(jnp.mean(centered * centered, axis=-1, keepdims=True) + 1e-05)
            hat = centered * inv
            xb_s[here, :] = hat.astype(BF16)
            invb_s[here, :] = jnp.broadcast_to(inv, (SUB, 128))
            y_s[here, :] = (hat * gains[1:2] + shifts[1:2]).astype(BF16)
            return carry

        lax.fori_loop(0, ROWS // SUB, second_norm, 0, unroll=5)

        @pl.when(first)
        def _():
            forward_send(index).start()

        act_copy(index).start()
        return carry

    lax.fori_loop(0, micro_count, forward, 0)

    def forward_done(index, carry):
        @pl.when(first)
        def _():
            forward_send(index).wait_send()

        act_copy(index).wait()
        return carry

    lax.fori_loop(0, micro_count, forward_done, 0)

    @pl.when(first)
    def _():
        transpose_all()

    def backward(index, carry):
        base = index * ROWS
        rows = rows_of(index)

        @pl.when(first)
        def _():
            backward_send(index).wait_recv()

        @pl.when(last)
        def _():
            cot_copy(index).wait()

        def second_back(step, carry):
            part = pl.ds(pl.multiple_of(step * SUB, SUB), SUB)
            here = pl.ds(pl.multiple_of(base + step * SUB, SUB), SUB)
            dy = dy_s[here, :].astype(F32)
            hat = xb_s[here, :].astype(F32)
            acc_s[9] += fold(dy * hat)
            acc_s[11] += fold(dy)
            scaled = dy * gains[1:2]
            mean_plain = jnp.mean(scaled, axis=-1, keepdims=True)
            mean_hat = jnp.mean(scaled * hat, axis=-1, keepdims=True)
            grad = (scaled - mean_plain - hat * mean_hat) * invb_s[here, 0:1]
            wide_s[part, :] = grad
            df_s[here, :] = grad.astype(BF16)
            acc_s[3] += fold(grad)
            return carry

        lax.fori_loop(0, ROWS // SUB, second_back, 0, unroll=5)

        def drop(n0):
            return dot_t(df_s[rows, :], w2_s[n0 : n0 + WIDE, :])

        following = drop(0)
        for n0 in range(0, FF, WIDE):
            block = following
            if n0 + WIDE < FF:
                following = drop(n0 + WIDE)
            sums = jnp.zeros((8, WIDE), F32)
            for r0 in range(0, ROWS, SUB):
                here = pl.ds(pl.multiple_of(base + r0, SUB), SUB)
                part = block[r0 : r0 + SUB] * g_s[here, n0 : n0 + WIDE].astype(F32)
                g_s[here, n0 : n0 + WIDE] = part.astype(BF16)
                sums = sums + fold(part)
            accu_s[:, n0 : n0 + WIDE] += sums

        wide_s[...] += dot_t(g_s[rows, :], w1_s[...])

        def first_back(step, carry):
            part = pl.ds(pl.multiple_of(step * SUB, SUB), SUB)
            here = pl.ds(pl.multiple_of(base + step * SUB, SUB), SUB)
            dn = wide_s[part, :]
            hat = xa_s[here, :].astype(F32)
            acc_s[8] += fold(dn * hat)
            acc_s[10] += fold(dn)
            scaled = dn * gains[0:1]
            mean_plain = jnp.mean(scaled, axis=-1, keepdims=True)
            mean_hat = jnp.mean(scaled * hat, axis=-1, keepdims=True)
            grad = (scaled - mean_plain - hat * mean_hat) * inva_s[here, 0:1]
            wide_s[part, :] = grad
            da_s[here, :] = grad.astype(BF16)
            acc_s[2] += fold(grad)
            return carry

        lax.fori_loop(0, ROWS // SUB, first_back, 0, unroll=5)

        do_s[...] = dot_t(da_s[rows, :], wo_s[...]).astype(BF16)

        def chain_step(chain, carry):
            here = pl.ds(pl.multiple_of(base + chain * LENGTH, LENGTH), LENGTH)
            near = pl.ds(pl.multiple_of(chain * LENGTH, LENGTH), LENGTH)
            number = index * CHAINS_MB + chain
            for pair in range(PAIRS):
                lanes = slice(pair * 128, pair * 128 + 128)
                query, key_rows, value = q_s[here, lanes], k_s[here, lanes], v_s[here, lanes]
                grad_mix = do_s[near, lanes]
                attend = p_s[number, pair]
                grad_tall = stacked(grad_mix)
                grad_attend = dot_t(value, grad_tall)
                attend_wide = attend.astype(F32)
                weighted = attend_wide * grad_attend
                delta = jnp.sum(weighted, axis=0, keepdims=True) / jnp.sum(attend_wide, axis=0, keepdims=True)
                grad_scores = (weighted - attend_wide * delta).astype(BF16)
                dv = dot(attend, grad_tall)
                dk = dot(grad_scores, stacked(query))
                dq = merged(t_dot(grad_scores, key_rows)) * 0.125
                q_s[here, lanes] = dq.astype(BF16)
                k_s[here, lanes] = dk.astype(BF16)
                v_s[here, lanes] = dv.astype(BF16)
                acc_s[0, :, lanes] += fold(dq)
                acc_s[1, :, lanes] += fold(dv)
            return carry

        lax.fori_loop(0, CHAINS_MB, chain_step, 0)

        for source, weight in ((q_s, wq_s), (k_s, wk_s), (v_s, wv_s)):
            wide_s[...] += dot_t(source[rows, :], weight[...])

        @pl.when(last)
        def _():
            low = wide_s[...].astype(BF16)
            y_s[rows, :] = low
            dx_s[rows, :] = low.astype(F32)
            backward_send(index).start()

        @pl.when(first)
        def _():
            for chain in range(CHAINS_MB):
                number = index * CHAINS_MB + chain
                start, stop = spans[0, number], spans[1, number]
                spot = lax.broadcasted_iota(jnp.int32, (LENGTH, D), 0)
                here = pl.ds(pl.multiple_of(base + chain * LENGTH, LENGTH), LENGTH)
                keep = (spot < start) | (spot >= stop)
                dx_s[here, :] = jnp.where(keep, wide_s[chain * LENGTH : (chain + 1) * LENGTH, :], 0.0)

        dx_copy(index).start()
        for copy in right_copies(index):
            copy.start()
        return carry

    lax.fori_loop(0, micro_count, backward, 0)

    @pl.when(last)
    def _():
        transpose_all()

    for number in range(12):
        if 4 <= number < 8:
            panel = accu_s[:, (number - 4) * D : (number - 3) * D]
        else:
            panel = acc_s[number]
        small_out[number : number + 1, :] = jnp.sum(panel, axis=0, keepdims=True)
    small_out[12:16, :] = jnp.zeros((4, D), F32)

    def backward_done(index, carry):
        @pl.when(last)
        def _():
            backward_send(index).wait_send()

        dx_copy(index).wait()
        for copy in right_copies(index):
            copy.wait()
        return carry

    lax.fori_loop(0, micro_count, backward_done, 0)


def run_layers(tokens, cotangent, lengths, spans, *weights):
    rows = tokens.shape[0]
    micro_count = rows // ROWS
    chains = rows // LENGTH
    anywhere = pl.BlockSpec(memory_space=pl.ANY)
    scalars = pl.BlockSpec(memory_space=pltpu.SMEM)
    vectors = pl.BlockSpec(memory_space=pltpu.VMEM)
    out_shape = (
        jax.ShapeDtypeStruct((rows, D), BF16),
        jax.ShapeDtypeStruct((rows, D), F32),
        jax.ShapeDtypeStruct((3 * D + FF, rows), BF16),
        jax.ShapeDtypeStruct((9, rows, D), BF16),
        jax.ShapeDtypeStruct((16, D), F32),
    )

    def vm(count, width=D, dtype=BF16):
        return pltpu.VMEM((count, width), dtype)

    scratch = [
        vm(D), vm(D), vm(D), vm(D), vm(D, FF), vm(FF),
        vm(rows), vm(rows), vm(rows), vm(rows),
        pltpu.VMEM((chains, PAIRS, LENGTH, 2 * LENGTH), BF16),
        vm(rows), vm(rows), vm(rows), vm(rows), vm(rows, FF), vm(rows, FF),
        vm(rows, 128, F32), vm(rows, 128, F32),
        vm(rows), vm(rows), vm(rows), vm(rows), vm(ROWS), vm(rows, D, F32),
        vm(ROWS, D, F32), pltpu.VMEM((2, 128, rows), BF16), pltpu.VMEM((12, 8, D), F32), vm(8, FF, F32),
        pltpu.SemaphoreType.DMA((6,)),
        pltpu.SemaphoreType.DMA((micro_count,)),
        pltpu.SemaphoreType.DMA((11, micro_count)),
        pltpu.SemaphoreType.DMA((2,)),
        pltpu.SemaphoreType.DMA((micro_count,)),
        pltpu.SemaphoreType.DMA((micro_count,)),
        pltpu.SemaphoreType.DMA((micro_count,)),
        pltpu.SemaphoreType.DMA((micro_count,)),
    ]
    return pl.pallas_call(
        functools.partial(layers_kernel, micro_count),
        out_shape=out_shape,
        in_specs=[anywhere, anywhere, scalars, scalars] + [anywhere] * 6 + [vectors] * 4,
        out_specs=[anywhere] * 4 + [vectors],
        scratch_shapes=scratch,
        compiler_params=pltpu.CompilerParams(
            collective_id=0, has_side_effects=True, vmem_limit_bytes=60 * 1024 * 1024
        ),
        cost_estimate=pl.CostEstimate(
            flops=rows * 2 * 2 * 2 * 7077888, bytes_accessed=60000000, transcendentals=rows * FF * 2
        ),
    )(tokens, cotangent, lengths, spans.T, *weights)


RING = 8
PIECES = 3
PIECE = D // RING
PANELS = (
    (0, 0), (0, 1), (0, 2), (D, 3), (2 * D, 4), (2 * D, 5),
    (2 * D, 6), (2 * D, 7), (3 * D, 8), (4 * D, 8), (5 * D, 8), (6 * D, 8),
)


def sums_kernel(
    left, right, small_in, grads_out, small_out,
    left_s, right_s, total_s, give_s, take_s, ring_s, own_s,
    tiny_s, tiny_take_s, tiny_sum_s, tiny_go_s, tiny_ring_s, tiny_own_s,
    load_sem, give_sem, take_sem, ring_send, ring_recv, own_sem, round_send, round_recv, share_send, share_recv,
    tiny_sem, tiny_ring_send, tiny_ring_recv, tiny_round_send, tiny_round_recv,
):
    me = lax.axis_index("dp")
    core = lax.rem(me, 2)
    high = lax.rem(lax.div(me, 2), 2)
    depth = lax.div(me, 4)
    place = depth + high * (7 - 2 * depth)

    def device(spot, on_core):
        row = lax.div(spot, 4)
        return {"dp": 4 * (spot + row * (7 - 2 * spot)) + 2 * row + on_core}

    ahead = device(lax.rem(place + 1, RING), core)
    behind = device(lax.rem(place + RING - 1, RING), core)
    beside = device(place, 1 - core)
    targets = (ahead, behind)

    barrier = pltpu.get_barrier_semaphore()
    for peer in (ahead, behind, beside):
        pl.semaphore_signal(barrier, inc=1, device_id=peer, device_id_type=MESH)

    def block(way, step):
        return lax.rem(place - step + RING, RING) if way == 0 else lax.rem(place + step, RING)

    def late_block(way, step):
        return lax.rem(place + 1 - step + RING, RING) if way == 0 else lax.rem(place + RING - 1 + step, RING)

    def load_left(part):
        return pltpu.make_async_copy(left.at[pl.ds(part * D, D)], left_s.at[pl.ds(part * D, D)], load_sem.at[part])

    def load_right(part):
        return pltpu.make_async_copy(right.at[part], right_s.at[part], load_sem.at[7 + part])

    def remote(source, target, send, recv, peer):
        return pltpu.make_async_remote_copy(
            src_ref=source, dst_ref=target, send_sem=send, recv_sem=recv, device_id=peer, device_id_type=MESH
        )

    def give(way, step, piece):
        return remote(
            give_s.at[way, step, piece], take_s.at[way, step, piece],
            give_sem.at[way, step, piece], take_sem.at[way, step, piece], beside,
        )

    def ring_copy(way, step, piece):
        return remote(
            take_s.at[way, step, piece], ring_s.at[way, step, piece],
            ring_send.at[way, step, piece], ring_recv.at[way, step, piece], targets[way],
        )

    def region(way, spot, piece, on_core):
        rows = pl.ds(pl.multiple_of(spot * PIECE, PIECE), PIECE)
        return grads_out.at[6 * way + 3 * on_core + piece, rows]

    def own_copy(way, piece):
        return pltpu.make_async_copy(
            own_s.at[way, piece], region(way, late_block(way, 0), piece, core), own_sem.at[way, piece]
        )

    def round_copy(way, step, piece, source=None):
        target = region(way, late_block(way, step), piece, core)
        return remote(
            target if source is None else source, target,
            round_send.at[way, step, piece], round_recv.at[way, step, piece], targets[way],
        )

    def round_wait(way, step, piece):
        target = region(way, late_block(way, step + 1), piece, core)
        remote(
            target, target, round_send.at[way, step, piece], round_recv.at[way, step, piece], targets[way]
        ).wait_recv()

    def share_copy(way, step, piece, source=None):
        target = region(way, late_block(way, step), piece, core)
        return remote(
            target if source is None else source, target,
            share_send.at[way, step, piece], share_recv.at[way, step, piece], beside,
        )

    def share_wait(way, step, piece):
        target = region(way, late_block(way, step), piece, 1 - core)
        remote(
            target, target, share_send.at[way, step, piece], share_recv.at[way, step, piece], beside
        ).wait_recv()

    tiny_swap = remote(tiny_s, tiny_take_s, tiny_sem.at[0], tiny_sem.at[1], beside)

    def tiny_ring(step):
        return remote(
            tiny_go_s.at[step], tiny_ring_s.at[step], tiny_ring_send.at[step], tiny_ring_recv.at[step], ahead
        )

    def tiny_round(step):
        spot = late_block(0, step)
        return remote(
            tiny_own_s.at[spot], tiny_own_s.at[spot], tiny_round_send.at[step], tiny_round_recv.at[step], ahead
        )

    def tiny_round_wait(step):
        spot = late_block(0, step + 1)
        remote(
            tiny_own_s.at[spot], tiny_own_s.at[spot], tiny_round_send.at[step], tiny_round_recv.at[step], ahead
        ).wait_recv()

    loads = []
    for piece in range(PIECES):
        for way in range(2):
            for half in range(2):
                first_row, number = PANELS[6 * way + 3 * half + piece]
                for kind, part in ((load_right, number), (load_left, first_row // D)):
                    if (kind, part) not in [entry[:2] for entry in loads]:
                        loads.append((kind, part, way, piece))
    for kind, part, _, _ in loads:
        kind(part).start()

    for part in range(RING):
        if part * 128 < D:
            tiny_s[part] = small_in[:, part * 128 : part * 128 + 128]
        else:
            tiny_s[part] = jnp.zeros((16, 128), F32)

    pl.semaphore_wait(barrier, 3)
    tiny_swap.start()

    def products(group, way, piece):
        near, far = PANELS[6 * way + piece], PANELS[6 * way + 3 + piece]
        for mine in (False, True):
            pick = core if mine else 1 - core
            first_row = near[0] + pick * (far[0] - near[0])
            number = near[1] + pick * (far[1] - near[1])
            blocks = []
            for step in (2 * group, 2 * group + 1):
                start = pl.multiple_of(first_row + block(way, step) * PIECE, PIECE)
                blocks.append(left_s[pl.ds(start, PIECE), :])
            tall = jnp.concatenate(blocks, axis=0)
            product = dot(tall, right_s[number])
            for half in range(2):
                step = 2 * group + half
                part = product[half * PIECE : (half + 1) * PIECE]
                if mine:
                    total_s[lax.rem(step, 4), way, piece] = part
                else:
                    give_s[way, step, piece] = part.astype(BF16)
            if not mine:
                give(way, 2 * group, piece).start()
                give(way, 2 * group + 1, piece).start()

    def add_piece(step, way, piece, target):
        slot = lax.rem(step, 4)
        for r0 in range(0, PIECE, SUB):
            part = slice(r0, r0 + SUB)
            whole = total_s[slot, way, piece, part] + take_s[way, step, piece, part].astype(F32)
            target[part] = whole.astype(BF16)

    def reduce_step(step, carry):
        slot = lax.rem(step, 4)
        spot = block(0, step)

        @pl.when(step < RING - 1)
        def _():
            tiny_ring(step - 1).wait_recv()
            tiny_go_s[step] = tiny_sum_s[spot] + tiny_ring_s[step - 1]
            tiny_ring(step).start()

        @pl.when(step == RING - 1)
        def _():
            tiny_ring(step - 1).wait_recv()
            tiny_own_s[spot] = tiny_sum_s[spot] + tiny_ring_s[step - 1]
            tiny_round(0).start()

        for piece in range(PIECES):
            for way in range(2):
                give(way, step, piece).wait_recv()
                ring_copy(way, step - 1, piece).wait_recv()
                for r0 in range(0, PIECE, SUB):
                    part = slice(r0, r0 + SUB)
                    total_s[slot, way, piece, part] += ring_s[way, step - 1, piece, part].astype(F32)

                @pl.when(step < RING - 1)
                def _():
                    add_piece(step, way, piece, take_s.at[way, step, piece])
                    ring_copy(way, step, piece).start()

                @pl.when(step == RING - 1)
                def _():
                    add_piece(step, way, piece, own_s.at[way, piece])
                    round_copy(way, 0, piece, own_s.at[way, piece]).start()
                    share_copy(way, 0, piece, own_s.at[way, piece]).start()
                    own_copy(way, piece).start()
        return carry

    def first_piece(way, piece):
        give(way, 0, piece).wait_recv()
        add_piece(0, way, piece, take_s.at[way, 0, piece])
        ring_copy(way, 0, piece).start()

    order = [(way, piece) for piece in range(PIECES) for way in range(2)]
    for number, (way, piece) in enumerate(order):
        for kind, part, at_way, at_piece in loads:
            if (at_way, at_piece) == (way, piece):
                kind(part).wait()
        products(0, way, piece)
        if number > 0:
            first_piece(*order[number - 1])
    first_piece(*order[-1])
    tiny_swap.wait_recv()
    tiny_sum_s[...] = tiny_s[...] + tiny_take_s[...]
    tiny_go_s[0] = tiny_sum_s[block(0, 0)]
    tiny_ring(0).start()

    def group_step(group, carry):
        @pl.when(group < RING // 2)
        def _():
            for way, piece in order:
                products(group, way, piece)

        top = jnp.minimum(2 * group + 1, RING)
        return lax.fori_loop(2 * group - 1, top, reduce_step, carry)

    lax.fori_loop(1, RING // 2 + 1, group_step, 0)

    def round_step(step, carry):
        tiny_round_wait(step - 1)

        @pl.when(step < RING - 1)
        def _():
            tiny_round(step).start()

        for piece in range(PIECES):
            for way in range(2):
                round_wait(way, step - 1, piece)

                @pl.when(step < RING - 1)
                def _():
                    round_copy(way, step, piece).start()

                share_copy(way, step, piece).start()
        return carry

    lax.fori_loop(1, RING, round_step, 0)

    for part in range(D // 128):
        small_out[:, part * 128 : part * 128 + 128] = tiny_own_s[part]
    tiny_swap.wait_send()

    def finish(step, carry):
        for way in range(2):
            for piece in range(PIECES):
                give(way, step, piece).wait_send()
                share_wait(way, step, piece)
                share_copy(way, step, piece).wait_send()

                @pl.when(step < RING - 1)
                def _():
                    ring_copy(way, step, piece).wait_send()
                    round_copy(way, step, piece).wait_send()

        @pl.when(step < RING - 1)
        def _():
            tiny_ring(step).wait_send()
            tiny_round(step).wait_send()

        return carry

    lax.fori_loop(0, RING, finish, 0)
    for way in range(2):
        for piece in range(PIECES):
            own_copy(way, piece).wait()


def run_sums(left, right, small):
    rows = right.shape[1]
    anywhere = pl.BlockSpec(memory_space=pl.ANY)
    vectors = pl.BlockSpec(memory_space=pltpu.VMEM)

    def pieces(*lead, dtype=BF16):
        return pltpu.VMEM((*lead, PIECE, D), dtype)

    dma = pltpu.SemaphoreType.DMA
    scratch = [
        pltpu.VMEM(left.shape, BF16), pltpu.VMEM(right.shape, BF16),
        pieces(4, 2, PIECES, dtype=F32), pieces(2, RING, PIECES), pieces(2, RING, PIECES),
        pieces(2, RING - 1, PIECES), pieces(2, PIECES),
        pltpu.VMEM((RING, 16, 128), F32), pltpu.VMEM((RING, 16, 128), F32), pltpu.VMEM((RING, 16, 128), F32),
        pltpu.VMEM((RING - 1, 16, 128), F32), pltpu.VMEM((RING - 1, 16, 128), F32), pltpu.VMEM((RING, 16, 128), F32),
        dma((16,)), dma((2, RING, PIECES)), dma((2, RING, PIECES)),
        dma((2, RING - 1, PIECES)), dma((2, RING - 1, PIECES)), dma((2, PIECES)),
        dma((2, RING - 1, PIECES)), dma((2, RING - 1, PIECES)), dma((2, RING, PIECES)), dma((2, RING, PIECES)),
        dma((2,)), dma((RING - 1,)), dma((RING - 1,)), dma((RING - 1,)), dma((RING - 1,)),
    ]
    return pl.pallas_call(
        sums_kernel,
        out_shape=(jax.ShapeDtypeStruct((12, D, D), BF16), jax.ShapeDtypeStruct((16, D), F32)),
        in_specs=[anywhere, anywhere, vectors],
        out_specs=[anywhere, vectors],
        scratch_shapes=scratch,
        compiler_params=pltpu.CompilerParams(
            collective_id=1, has_side_effects=True, vmem_limit_bytes=60 * 1024 * 1024
        ),
        cost_estimate=pl.CostEstimate(flops=rows * 2 * 7077888, bytes_accessed=70000000, transcendentals=0),
    )(left, right, small)


def plain_sums(left, right, small):
    panels = [dot(left[row : row + D], right[number]).astype(BF16) for row, number in PANELS]
    return lax.psum(jnp.stack(panels), "dp"), lax.psum(small, "dp")


SLOTS = 8
CUT = D // 2


def widen_kernel(
    act, dx, grads, small, act_out, dx_out, query_out, key_out, value_out, out_out, up_out, down_out,
    bias_out, up_bias_out, gain_out, shift_out, low_s, wide_s, in_sem, out_sem, move_sem,
):
    moves = [
        pltpu.make_async_copy(act, act_out.at[0], move_sem.at[0]),
        pltpu.make_async_copy(dx, dx_out.at[0], move_sem.at[1]),
    ]
    jobs = []
    for panel in range(12):
        for half in range(2):
            rows = pl.ds(half * CUT, CUT)
            if panel < 4:
                target = (query_out, key_out, value_out, out_out)[panel].at[0, rows]
            elif panel < 8:
                target = up_out.at[0, rows, pl.ds((panel - 4) * D, D)]
            else:
                target = down_out.at[0, pl.ds((panel - 8) * D + half * CUT, CUT)]
            jobs.append((grads.at[panel, rows], target))

    def fetch(number):
        return pltpu.make_async_copy(jobs[number][0], low_s.at[number % SLOTS], in_sem.at[number % SLOTS])

    def store(number):
        return pltpu.make_async_copy(wide_s.at[number % SLOTS], jobs[number][1], out_sem.at[number % SLOTS])

    for number in range(SLOTS):
        fetch(number).start()
    for move in moves:
        move.start()
    bias_out[0] = small[0:4]
    for panel in range(FF // D):
        up_bias_out[:, panel * D : (panel + 1) * D] = small[4 + panel : 5 + panel]
    gain_out[0] = small[8:10]
    shift_out[0] = small[10:12]
    for number in range(len(jobs)):
        slot = number % SLOTS
        fetch(number).wait()
        if number >= SLOTS:
            store(number - SLOTS).wait()

        def turn(step, carry):
            part = pl.ds(pl.multiple_of(step * SUB, SUB), SUB)
            wide_s[slot, part, :] = low_s[slot, part, :].astype(F32)
            return carry

        lax.fori_loop(0, CUT // SUB, turn, 0, unroll=4)
        store(number).start()
        if number + SLOTS < len(jobs):
            fetch(number + SLOTS).start()
    for number in range(len(jobs) - SLOTS, len(jobs)):
        store(number).wait()
    for move in moves:
        move.wait()


def widen(act, dx, grads, small):
    anywhere = pl.BlockSpec(memory_space=pl.ANY)
    vectors = pl.BlockSpec(memory_space=pltpu.VMEM)
    square = jax.ShapeDtypeStruct((1, D, D), F32)
    return pl.pallas_call(
        widen_kernel,
        out_shape=(
            jax.ShapeDtypeStruct((1, *act.shape), BF16), jax.ShapeDtypeStruct((1, *dx.shape), F32),
            square, square, square, square,
            jax.ShapeDtypeStruct((1, D, FF), F32), jax.ShapeDtypeStruct((1, FF, D), F32),
            jax.ShapeDtypeStruct((1, 4, D), F32), jax.ShapeDtypeStruct((1, FF), F32),
            jax.ShapeDtypeStruct((1, 2, D), F32), jax.ShapeDtypeStruct((1, 2, D), F32),
        ),
        in_specs=[anywhere, anywhere, anywhere, vectors],
        out_specs=[anywhere] * 8 + [vectors] * 4,
        scratch_shapes=[
            pltpu.VMEM((SLOTS, CUT, D), BF16), pltpu.VMEM((SLOTS, CUT, D), F32),
            pltpu.SemaphoreType.DMA((SLOTS,)), pltpu.SemaphoreType.DMA((SLOTS,)), pltpu.SemaphoreType.DMA((2,)),
        ],
        compiler_params=pltpu.CompilerParams(vmem_limit_bytes=60 * 1024 * 1024),
        cost_estimate=pl.CostEstimate(flops=7077888, bytes_accessed=42467328, transcendentals=0),
    )(act, dx, grads, small)


def per_device(grid, tokens, cotangent, lengths, spans, *weights):
    act, dx, left, right, small = run_layers(tokens, cotangent, lengths, spans, *weights)
    grads, small = (run_sums if grid else plain_sums)(left, right, small)
    return widen(act, dx, grads, small)


def solution(mesh):
    in_specs = (
        P("dp", None), P("dp", None), P("dp"), P("dp", None),
        P("section", None, None), P("section", None, None), P("section", None, None),
        P("section", None, None), P("section", None, None), P("section", None, None),
        P("section", None, None), P("section", None), P("section", None, None), P("section", None, None),
    )
    out_specs = (
        P("section", "dp", None), P("section", "dp", None),
        P("section", None, None), P("section", None, None), P("section", None, None),
        P("section", None, None), P("section", None, None), P("section", None, None),
        P("section", None, None), P("section", None), P("section", None, None), P("section", None, None),
    )
    part = functools.partial(per_device, mesh.shape["dp"] == 2 * RING)
    return jax.shard_map(part, mesh=mesh, in_specs=in_specs, out_specs=out_specs, check_vma=False)
```

```python
import functools

import jax
import jax.numpy as jnp
from jax import lax
from jax.experimental import pallas as pl
from jax.experimental.pallas import tpu as pltpu
from jax.sharding import PartitionSpec as P

D = 768
HEADS = 12
HEAD_DIM = 64
PAIRS = HEADS // 2
FF = 3072
LENGTH = 160
LEAST = 96
CHAINS_MB = 2
ROWS = CHAINS_MB * LENGTH
SUB = 32
WIDE = 512
TURN = 256

F32 = jnp.float32
BF16 = jnp.bfloat16
MESH = pl.DeviceIdType.MESH


def dot(left, right):
    return jnp.dot(left, right, preferred_element_type=F32)


def dot_t(left, right):
    return lax.dot_general(left, right, (((1,), (1,)), ((), ())), preferred_element_type=F32)


def turned(eye, block):
    return dot_t(eye, block).astype(BF16)


def fold(block):
    return jnp.sum(block.reshape(-1, 8, block.shape[-1]), axis=0)


def gelu_parts(u):
    t = pl.reciprocal(1.0 + 0.23164189 * jnp.abs(u), approx=True)
    gauss = jnp.exp2(u * u * -0.7213475204444817)
    poly = t * (
        0.127414796 + t * (-0.142248368 + t * (0.7107068705 + t * (-0.7265760135 + t * 0.5307027145)))
    )
    tail = poly * gauss
    cdf = jnp.where(u >= 0, 1.0 - tail, tail)
    return u * cdf, cdf + (u * 0.3989422804014327) * gauss


def layers_kernel(
    micro_count,
    tokens, cotangent, lengths, spans,
    wq, wk, wv, wo, w1, w2, bias_in, up_bias_in, gains_in, shifts_in,
    act_out, dx_out, left_out, right_out, small_out,
    wq_s, wk_s, wv_s, wo_s, w1_s, w2_s,
    h_s, q_s, k_s, v_s, p_s, o_s, n_s, xa_s, xb_s, z_s, g_s, inva_s, invb_s,
    y_s, dy_s, df_s, da_s, do_s, dx_s, wide_s, turn_s, eye_s, acc_s, accu_s,
    w_sem, in_sem, out_sem, turn_sem, fwd_send, fwd_recv, bwd_send, bwd_recv,
):
    section = lax.axis_index("section")
    other = 1 - section
    first = section == 0
    last = section == 1

    barrier = pltpu.get_barrier_semaphore()
    pl.semaphore_signal(barrier, inc=1, device_id={"section": other}, device_id_type=MESH)

    weight_pairs = ((wq, wq_s), (wk, wk_s), (wv, wv_s), (wo, wo_s), (w1, w1_s), (w2, w2_s))

    def weight_copy(index):
        source, target = weight_pairs[index]
        return pltpu.make_async_copy(source.at[0], target, w_sem.at[index])

    def rows_of(index):
        return pl.ds(pl.multiple_of(index * ROWS, ROWS), ROWS)

    def entry_copy(index):
        return pltpu.make_async_copy(tokens.at[rows_of(index)], h_s.at[rows_of(index)], in_sem.at[index])

    def cot_copy(index):
        return pltpu.make_async_copy(cotangent.at[rows_of(index)], dy_s.at[rows_of(index)], in_sem.at[index])

    def forward_send(index):
        return pltpu.make_async_remote_copy(
            src_ref=y_s.at[rows_of(index)],
            dst_ref=h_s.at[rows_of(index)],
            send_sem=fwd_send.at[index],
            recv_sem=fwd_recv.at[index],
            device_id={"section": other},
            device_id_type=MESH,
        )

    def backward_send(index):
        return pltpu.make_async_remote_copy(
            src_ref=y_s.at[rows_of(index)],
            dst_ref=dy_s.at[rows_of(index)],
            send_sem=bwd_send.at[index],
            recv_sem=bwd_recv.at[index],
            device_id={"section": other},
            device_id_type=MESH,
        )

    backward_outs = ((q_s, 0), (k_s, 1), (v_s, 2), (da_s, 3), (df_s, 8))

    def act_copy(index):
        return pltpu.make_async_copy(y_s.at[rows_of(index)], act_out.at[rows_of(index)], out_sem.at[0, index])

    def dx_copy(index):
        return pltpu.make_async_copy(dx_s.at[rows_of(index)], dx_out.at[rows_of(index)], out_sem.at[1, index])

    def right_copies(index):
        for slot, (source, place) in enumerate(backward_outs):
            yield pltpu.make_async_copy(
                source.at[rows_of(index)], right_out.at[place, rows_of(index)], out_sem.at[2 + slot, index]
            )
        for panel in range(FF // D):
            yield pltpu.make_async_copy(
                g_s.at[rows_of(index), pl.ds(panel * D, D)],
                right_out.at[4 + panel, rows_of(index)],
                out_sem.at[7 + panel, index],
            )

    def turn_copy(slot, row):
        return pltpu.make_async_copy(
            turn_s.at[slot], left_out.at[pl.ds(pl.multiple_of(row, TURN), TURN)], turn_sem.at[slot]
        )

    def transpose_all():
        done = 0
        for source, tiles in ((h_s, D // TURN), (o_s, D // TURN), (n_s, D // TURN), (z_s, FF // TURN)):

            def tile_step(tile, carry, source=source, done=done):
                number = tile + done
                slot = lax.rem(number, 2)

                @pl.when(number >= 2)
                def _():
                    turn_copy(slot, (number - 2) * TURN).wait()

                block = source[:, pl.ds(pl.multiple_of(tile * TURN, TURN), TURN)]
                turn_s[slot] = turned(eye_s[:TURN, :TURN], block)
                turn_copy(slot, number * TURN).start()
                return carry

            lax.fori_loop(0, tiles, tile_step, 0)
            done += tiles
        for number in (done - 2, done - 1):
            turn_copy(number % 2, number * TURN).wait()

    @pl.when(first)
    def _():
        for index in range(micro_count):
            entry_copy(index).start()

    @pl.when(last)
    def _():
        for index in range(micro_count):
            cot_copy(index).start()

    for index in range(6):
        weight_copy(index).start()

    across = lax.broadcasted_iota(jnp.int32, (2 * LENGTH, 2 * LENGTH), 0)
    along = lax.broadcasted_iota(jnp.int32, (2 * LENGTH, 2 * LENGTH), 1)
    eye_s[...] = jnp.where(across == along, 1.0, 0.0).astype(BF16)
    acc_s[...] = jnp.zeros_like(acc_s)
    accu_s[...] = jnp.zeros_like(accu_s)

    bias = bias_in[0].astype(F32)
    gains = gains_in[0].astype(F32)
    shifts = shifts_in[0].astype(F32)
    low_half = lax.broadcasted_iota(jnp.int32, (1, 8, 128), 2) < HEAD_DIM
    keep_low = jnp.where(lax.broadcasted_iota(jnp.int32, (1, 16, 128), 2) < HEAD_DIM, 1.0, 0.0)
    keep_high = (1.0 - keep_low).astype(BF16)
    keep_low = keep_low.astype(BF16)

    def stacked(pair_block):
        tiles = pair_block.reshape(-1, 16, 128)
        return jnp.concatenate([tiles * keep_low, tiles * keep_high], axis=0).reshape(2 * LENGTH, 128)

    def merged(tall):
        tiles = tall.reshape(2, LENGTH // 8, 8, 128)
        return jnp.where(low_half, tiles[0], tiles[1]).reshape(LENGTH, 128)

    pl.semaphore_wait(barrier, 1)

    def forward(index, carry):
        base = index * ROWS
        rows = rows_of(index)

        @pl.when(first)
        def _():
            entry_copy(index).wait()
            for chain in range(CHAINS_MB):
                number = index * CHAINS_MB + chain
                start, stop = spans[0, number], spans[1, number]
                spot = lax.broadcasted_iota(jnp.int32, (LENGTH, D), 0)
                here = pl.ds(pl.multiple_of(base + chain * LENGTH, LENGTH), LENGTH)
                keep = (spot < start) | (spot >= stop)
                h_s[here, :] = jnp.where(keep, h_s[here, :].astype(F32), 0.0).astype(BF16)

        @pl.when(last)
        def _():
            forward_send(index).wait_recv()

        @pl.when(index == 0)
        def _():
            for number in range(3):
                weight_copy(number).wait()

        for weight, bias_row, target in ((wq_s, 0, q_s), (wk_s, None, k_s), (wv_s, 1, v_s)):
            block = dot(h_s[rows, :], weight[...])
            if bias_row is not None:
                block = block + bias[bias_row : bias_row + 1]
            if target is q_s:
                block = block * 0.125
            target[rows, :] = block.astype(BF16)

        def chain_step(chain, carry):
            here = pl.ds(pl.multiple_of(base + chain * LENGTH, LENGTH), LENGTH)
            number = index * CHAINS_MB + chain
            spot = lax.broadcasted_iota(jnp.int32, (LENGTH - LEAST, 2 * LENGTH), 0) + LEAST
            penalty = jnp.where(spot < lengths[number], 0.0, -1000000000.0)
            for pair in range(PAIRS):
                lanes = slice(pair * 128, pair * 128 + 128)
                scores = dot_t(k_s[here, lanes], stacked(q_s[here, lanes]))
                scores = jnp.concatenate([scores[:LEAST], scores[LEAST:] + penalty], axis=0)
                raised = jnp.exp(scores - jnp.max(scores, axis=0, keepdims=True))
                attend = (raised * (1.0 / jnp.sum(raised, axis=0, keepdims=True))).astype(BF16)
                p_s[number, pair] = attend
                o_s[here, lanes] = merged(dot(turned(eye_s[...], attend), v_s[here, lanes])).astype(BF16)
            return carry

        lax.fori_loop(0, CHAINS_MB, chain_step, 0)

        @pl.when(index == 0)
        def _():
            weight_copy(3).wait()

        wide_s[...] = dot(o_s[rows, :], wo_s[...])

        def first_norm(step, carry):
            part = pl.ds(pl.multiple_of(step * SUB, SUB), SUB)
            here = pl.ds(pl.multiple_of(base + step * SUB, SUB), SUB)
            r = h_s[here, :].astype(F32) + wide_s[part, :] + bias[2:3]
            centered = r - jnp.mean(r, axis=-1, keepdims=True)
            inv = lax.rsqrt(jnp.mean(centered * centered, axis=-1, keepdims=True) + 1e-05)
            hat = centered * inv
            normed = hat * gains[0:1] + shifts[0:1]
            xa_s[here, :] = hat.astype(BF16)
            inva_s[here, :] = jnp.broadcast_to(inv, (SUB, 128))
            n_s[here, :] = normed.astype(BF16)
            wide_s[part, :] = normed
            return carry

        lax.fori_loop(0, ROWS // SUB, first_norm, 0, unroll=5)

        @pl.when(index == 0)
        def _():
            weight_copy(4).wait()
            weight_copy(5).wait()

        def lift(n0):
            return dot(n_s[rows, :], w1_s[:, n0 : n0 + WIDE])

        following = lift(0)
        for n0 in range(0, FF, WIDE):
            block = following
            if n0 + WIDE < FF:
                following = lift(n0 + WIDE)
            up_bias = up_bias_in[0:1, n0 : n0 + WIDE].astype(F32)
            for r0 in range(0, ROWS, SUB):
                here = pl.ds(pl.multiple_of(base + r0, SUB), SUB)
                act, slope = gelu_parts(block[r0 : r0 + SUB] + up_bias)
                z_s[here, n0 : n0 + WIDE] = act.astype(BF16)
                g_s[here, n0 : n0 + WIDE] = slope.astype(BF16)

        wide_s[...] += dot(z_s[rows, :], w2_s[...])

        def second_norm(step, carry):
            part = pl.ds(pl.multiple_of(step * SUB, SUB), SUB)
            here = pl.ds(pl.multiple_of(base + step * SUB, SUB), SUB)
            r = wide_s[part, :] + bias[3:4]
            centered = r - jnp.mean(r, axis=-1, keepdims=True)
            inv = lax.rsqrt(jnp.mean(centered * centered, axis=-1, keepdims=True) + 1e-05)
            hat = centered * inv
            xb_s[here, :] = hat.astype(BF16)
            invb_s[here, :] = jnp.broadcast_to(inv, (SUB, 128))
            y_s[here, :] = (hat * gains[1:2] + shifts[1:2]).astype(BF16)
            return carry

        lax.fori_loop(0, ROWS // SUB, second_norm, 0, unroll=5)

        @pl.when(first)
        def _():
            forward_send(index).start()

        act_copy(index).start()
        return carry

    lax.fori_loop(0, micro_count, forward, 0)

    def forward_done(index, carry):
        @pl.when(first)
        def _():
            forward_send(index).wait_send()

        act_copy(index).wait()
        return carry

    lax.fori_loop(0, micro_count, forward_done, 0)

    @pl.when(first)
    def _():
        transpose_all()

    def backward(index, carry):
        base = index * ROWS
        rows = rows_of(index)

        @pl.when(first)
        def _():
            backward_send(index).wait_recv()

        @pl.when(last)
        def _():
            cot_copy(index).wait()

        def second_back(step, carry):
            part = pl.ds(pl.multiple_of(step * SUB, SUB), SUB)
            here = pl.ds(pl.multiple_of(base + step * SUB, SUB), SUB)
            dy = dy_s[here, :].astype(F32)
            hat = xb_s[here, :].astype(F32)
            acc_s[9] += fold(dy * hat)
            acc_s[11] += fold(dy)
            scaled = dy * gains[1:2]
            mean_plain = jnp.mean(scaled, axis=-1, keepdims=True)
            mean_hat = jnp.mean(scaled * hat, axis=-1, keepdims=True)
            grad = (scaled - mean_plain - hat * mean_hat) * invb_s[here, 0:1]
            wide_s[part, :] = grad
            df_s[here, :] = grad.astype(BF16)
            acc_s[3] += fold(grad)
            return carry

        lax.fori_loop(0, ROWS // SUB, second_back, 0, unroll=5)

        def drop(n0):
            return dot_t(df_s[rows, :], w2_s[n0 : n0 + WIDE, :])

        following = drop(0)
        for n0 in range(0, FF, WIDE):
            block = following
            if n0 + WIDE < FF:
                following = drop(n0 + WIDE)
            sums = jnp.zeros((8, WIDE), F32)
            for r0 in range(0, ROWS, SUB):
                here = pl.ds(pl.multiple_of(base + r0, SUB), SUB)
                part = block[r0 : r0 + SUB] * g_s[here, n0 : n0 + WIDE].astype(F32)
                g_s[here, n0 : n0 + WIDE] = part.astype(BF16)
                sums = sums + fold(part)
            accu_s[:, n0 : n0 + WIDE] += sums

        wide_s[...] += dot_t(g_s[rows, :], w1_s[...])

        def first_back(step, carry):
            part = pl.ds(pl.multiple_of(step * SUB, SUB), SUB)
            here = pl.ds(pl.multiple_of(base + step * SUB, SUB), SUB)
            dn = wide_s[part, :]
            hat = xa_s[here, :].astype(F32)
            acc_s[8] += fold(dn * hat)
            acc_s[10] += fold(dn)
            scaled = dn * gains[0:1]
            mean_plain = jnp.mean(scaled, axis=-1, keepdims=True)
            mean_hat = jnp.mean(scaled * hat, axis=-1, keepdims=True)
            grad = (scaled - mean_plain - hat * mean_hat) * inva_s[here, 0:1]
            wide_s[part, :] = grad
            da_s[here, :] = grad.astype(BF16)
            acc_s[2] += fold(grad)
            return carry

        lax.fori_loop(0, ROWS // SUB, first_back, 0, unroll=5)

        do_s[...] = dot_t(da_s[rows, :], wo_s[...]).astype(BF16)

        def chain_step(chain, carry):
            here = pl.ds(pl.multiple_of(base + chain * LENGTH, LENGTH), LENGTH)
            near = pl.ds(pl.multiple_of(chain * LENGTH, LENGTH), LENGTH)
            number = index * CHAINS_MB + chain
            for pair in range(PAIRS):
                lanes = slice(pair * 128, pair * 128 + 128)
                query, key_rows, value = q_s[here, lanes], k_s[here, lanes], v_s[here, lanes]
                grad_mix = do_s[near, lanes]
                attend = p_s[number, pair]
                grad_tall = stacked(grad_mix)
                grad_attend = dot_t(value, grad_tall)
                attend_wide = attend.astype(F32)
                weighted = attend_wide * grad_attend
                delta = jnp.sum(weighted, axis=0, keepdims=True) / jnp.sum(attend_wide, axis=0, keepdims=True)
                grad_scores = (weighted - attend_wide * delta).astype(BF16)
                dv = dot(attend, grad_tall)
                dk = dot(grad_scores, stacked(query))
                dq = merged(dot(turned(eye_s[...], grad_scores), key_rows)) * 0.125
                q_s[here, lanes] = dq.astype(BF16)
                k_s[here, lanes] = dk.astype(BF16)
                v_s[here, lanes] = dv.astype(BF16)
                acc_s[0, :, lanes] += fold(dq)
                acc_s[1, :, lanes] += fold(dv)
            return carry

        lax.fori_loop(0, CHAINS_MB, chain_step, 0)

        for source, weight in ((q_s, wq_s), (k_s, wk_s), (v_s, wv_s)):
            wide_s[...] += dot_t(source[rows, :], weight[...])

        @pl.when(last)
        def _():
            low = wide_s[...].astype(BF16)
            y_s[rows, :] = low
            dx_s[rows, :] = low.astype(F32)
            backward_send(index).start()

        @pl.when(first)
        def _():
            for chain in range(CHAINS_MB):
                number = index * CHAINS_MB + chain
                start, stop = spans[0, number], spans[1, number]
                spot = lax.broadcasted_iota(jnp.int32, (LENGTH, D), 0)
                here = pl.ds(pl.multiple_of(base + chain * LENGTH, LENGTH), LENGTH)
                keep = (spot < start) | (spot >= stop)
                dx_s[here, :] = jnp.where(keep, wide_s[chain * LENGTH : (chain + 1) * LENGTH, :], 0.0)

        dx_copy(index).start()
        for copy in right_copies(index):
            copy.start()
        return carry

    lax.fori_loop(0, micro_count, backward, 0)

    @pl.when(last)
    def _():
        transpose_all()

    for number in range(12):
        if 4 <= number < 8:
            panel = accu_s[:, (number - 4) * D : (number - 3) * D]
        else:
            panel = acc_s[number]
        small_out[number : number + 1, :] = jnp.sum(panel, axis=0, keepdims=True)
    small_out[12:16, :] = jnp.zeros((4, D), F32)

    def backward_done(index, carry):
        @pl.when(last)
        def _():
            backward_send(index).wait_send()

        dx_copy(index).wait()
        for copy in right_copies(index):
            copy.wait()
        return carry

    lax.fori_loop(0, micro_count, backward_done, 0)


def run_layers(tokens, cotangent, lengths, spans, *weights):
    rows = tokens.shape[0]
    micro_count = rows // ROWS
    chains = rows // LENGTH
    anywhere = pl.BlockSpec(memory_space=pl.ANY)
    scalars = pl.BlockSpec(memory_space=pltpu.SMEM)
    vectors = pl.BlockSpec(memory_space=pltpu.VMEM)
    out_shape = (
        jax.ShapeDtypeStruct((rows, D), BF16),
        jax.ShapeDtypeStruct((rows, D), F32),
        jax.ShapeDtypeStruct((3 * D + FF, rows), BF16),
        jax.ShapeDtypeStruct((9, rows, D), BF16),
        jax.ShapeDtypeStruct((16, D), F32),
    )

    def vm(count, width=D, dtype=BF16):
        return pltpu.VMEM((count, width), dtype)

    scratch = [
        vm(D), vm(D), vm(D), vm(D), vm(D, FF), vm(FF),
        vm(rows), vm(rows), vm(rows), vm(rows),
        pltpu.VMEM((chains, PAIRS, LENGTH, 2 * LENGTH), BF16),
        vm(rows), vm(rows), vm(rows), vm(rows), vm(rows, FF), vm(rows, FF),
        vm(rows, 128, F32), vm(rows, 128, F32),
        vm(rows), vm(rows), vm(rows), vm(rows), vm(ROWS), vm(rows, D, F32),
        vm(ROWS, D, F32), pltpu.VMEM((2, TURN, rows), BF16), pltpu.VMEM((2 * LENGTH, 2 * LENGTH), BF16), pltpu.VMEM((12, 8, D), F32), vm(8, FF, F32),
        pltpu.SemaphoreType.DMA((6,)),
        pltpu.SemaphoreType.DMA((micro_count,)),
        pltpu.SemaphoreType.DMA((11, micro_count)),
        pltpu.SemaphoreType.DMA((2,)),
        pltpu.SemaphoreType.DMA((micro_count,)),
        pltpu.SemaphoreType.DMA((micro_count,)),
        pltpu.SemaphoreType.DMA((micro_count,)),
        pltpu.SemaphoreType.DMA((micro_count,)),
    ]
    return pl.pallas_call(
        functools.partial(layers_kernel, micro_count),
        out_shape=out_shape,
        in_specs=[anywhere, anywhere, scalars, scalars] + [anywhere] * 6 + [vectors] * 4,
        out_specs=[anywhere] * 4 + [vectors],
        scratch_shapes=scratch,
        compiler_params=pltpu.CompilerParams(
            collective_id=0, has_side_effects=True, vmem_limit_bytes=60 * 1024 * 1024
        ),
        cost_estimate=pl.CostEstimate(
            flops=rows * 2 * 2 * 2 * 7077888, bytes_accessed=60000000, transcendentals=rows * FF * 2
        ),
    )(tokens, cotangent, lengths, spans.T, *weights)


RING = 8
PIECES = 3
PIECE = D // RING
PANELS = (
    (0, 0), (0, 1), (0, 2), (D, 3), (2 * D, 4), (2 * D, 5),
    (2 * D, 6), (2 * D, 7), (3 * D, 8), (4 * D, 8), (5 * D, 8), (6 * D, 8),
)


def sums_kernel(
    left, right, small_in, grads_out, small_out,
    left_s, right_s, total_s, give_s, take_s, ring_s, own_s, late_s,
    tiny_s, tiny_take_s, tiny_sum_s, tiny_go_s, tiny_ring_s, tiny_own_s,
    load_sem, give_sem, take_sem, ring_send, ring_recv, own_sem, round_send, round_recv, share_send, share_recv,
    tiny_sem, tiny_ring_send, tiny_ring_recv, tiny_round_send, tiny_round_recv,
):
    me = lax.axis_index("dp")
    core = lax.rem(me, 2)
    high = lax.rem(lax.div(me, 2), 2)
    depth = lax.div(me, 4)
    place = depth + high * (7 - 2 * depth)

    def device(spot, on_core):
        row = lax.div(spot, 4)
        return {"dp": 4 * (spot + row * (7 - 2 * spot)) + 2 * row + on_core}

    ahead = device(lax.rem(place + 1, RING), core)
    behind = device(lax.rem(place + RING - 1, RING), core)
    beside = device(place, 1 - core)
    targets = (ahead, behind)

    barrier = pltpu.get_barrier_semaphore()
    for peer in (ahead, behind, beside):
        pl.semaphore_signal(barrier, inc=1, device_id=peer, device_id_type=MESH)

    def block(way, step):
        return lax.rem(place - step + RING, RING) if way == 0 else lax.rem(place + step, RING)

    def late_block(way, step):
        return lax.rem(place + 1 - step + RING, RING) if way == 0 else lax.rem(place + RING - 1 + step, RING)

    def load_left(part):
        return pltpu.make_async_copy(left.at[pl.ds(part * D, D)], left_s.at[pl.ds(part * D, D)], load_sem.at[part])

    def load_right(part):
        return pltpu.make_async_copy(right.at[part], right_s.at[part], load_sem.at[7 + part])

    def remote(source, target, send, recv, peer):
        return pltpu.make_async_remote_copy(
            src_ref=source, dst_ref=target, send_sem=send, recv_sem=recv, device_id=peer, device_id_type=MESH
        )

    def give(way, step, piece):
        return remote(
            give_s.at[way, lax.rem(step, 4), piece], take_s.at[way, step, piece],
            give_sem.at[way, step, piece], take_sem.at[way, step, piece], beside,
        )

    def ring_copy(way, step, piece):
        return remote(
            take_s.at[way, step, piece], ring_s.at[way, step, piece],
            ring_send.at[way, step, piece], ring_recv.at[way, step, piece], targets[way],
        )

    def region(way, spot, piece, on_core):
        rows = pl.ds(pl.multiple_of(spot * PIECE, PIECE), PIECE)
        return grads_out.at[6 * way + 3 * on_core + piece, rows]

    def settled(way, step, piece):
        return own_s.at[way, piece] if isinstance(step, int) and step == 0 else late_s.at[way, step - 1, piece]

    def own_copy(way, step, piece):
        target = region(way, late_block(way, step), piece, core)
        return pltpu.make_async_copy(settled(way, step, piece), target, own_sem.at[way, step, piece])

    def round_copy(way, step, piece):
        return remote(
            settled(way, step, piece), late_s.at[way, step, piece],
            round_send.at[way, step, piece], round_recv.at[way, step, piece], targets[way],
        )

    def arrival(way, step, piece):
        target = late_s.at[way, step, piece]
        return remote(
            target, target, round_send.at[way, step, piece], round_recv.at[way, step, piece], targets[way]
        )

    def share_copy(way, step, piece):
        return remote(
            settled(way, step, piece), region(way, late_block(way, step), piece, core),
            share_send.at[way, step, piece], share_recv.at[way, step, piece], beside,
        )

    def share_wait(way, step, piece):
        target = region(way, late_block(way, step), piece, 1 - core)
        remote(
            target, target, share_send.at[way, step, piece], share_recv.at[way, step, piece], beside
        ).wait_recv()

    tiny_swap = remote(tiny_s, tiny_take_s, tiny_sem.at[0], tiny_sem.at[1], beside)

    def tiny_ring(step):
        return remote(
            tiny_go_s.at[step], tiny_ring_s.at[step], tiny_ring_send.at[step], tiny_ring_recv.at[step], ahead
        )

    def tiny_round(step):
        spot = late_block(0, step)
        return remote(
            tiny_own_s.at[spot], tiny_own_s.at[spot], tiny_round_send.at[step], tiny_round_recv.at[step], ahead
        )

    def tiny_round_wait(step):
        spot = late_block(0, step + 1)
        remote(
            tiny_own_s.at[spot], tiny_own_s.at[spot], tiny_round_send.at[step], tiny_round_recv.at[step], ahead
        ).wait_recv()

    loads = []
    for piece in range(PIECES):
        for way in range(2):
            for half in range(2):
                first_row, number = PANELS[6 * way + 3 * half + piece]
                for kind, part in ((load_right, number), (load_left, first_row // D)):
                    if (kind, part) not in [entry[:2] for entry in loads]:
                        loads.append((kind, part, way, piece))
    for kind, part, _, _ in loads:
        kind(part).start()

    for part in range(RING):
        if part * 128 < D:
            tiny_s[part] = small_in[:, part * 128 : part * 128 + 128]
        else:
            tiny_s[part] = jnp.zeros((16, 128), F32)

    pl.semaphore_wait(barrier, 3)
    tiny_swap.start()

    def products(group, way, piece):
        near, far = PANELS[6 * way + piece], PANELS[6 * way + 3 + piece]

        @pl.when(group >= 2)
        def _():
            give(way, 2 * group - 4, piece).wait_send()
            give(way, 2 * group - 3, piece).wait_send()

        for mine in (False, True):
            pick = core if mine else 1 - core
            first_row = near[0] + pick * (far[0] - near[0])
            number = near[1] + pick * (far[1] - near[1])
            blocks = []
            for step in (2 * group, 2 * group + 1):
                start = pl.multiple_of(first_row + block(way, step) * PIECE, PIECE)
                blocks.append(left_s[pl.ds(start, PIECE), :])
            tall = jnp.concatenate(blocks, axis=0)
            product = dot(tall, right_s[number])
            for half in range(2):
                step = 2 * group + half
                part = product[half * PIECE : (half + 1) * PIECE]
                if mine:
                    total_s[lax.rem(step, 4), way, piece] = part
                else:
                    give_s[way, lax.rem(step, 4), piece] = part.astype(BF16)
            if not mine:
                give(way, 2 * group, piece).start()
                give(way, 2 * group + 1, piece).start()

    def add_piece(step, way, piece, target):
        slot = lax.rem(step, 4)
        for r0 in range(0, PIECE, SUB):
            part = slice(r0, r0 + SUB)
            whole = total_s[slot, way, piece, part] + take_s[way, step, piece, part].astype(F32)
            target[part] = whole.astype(BF16)

    def reduce_step(step, carry):
        slot = lax.rem(step, 4)
        spot = block(0, step)

        @pl.when(step < RING - 1)
        def _():
            tiny_ring(step - 1).wait_recv()
            tiny_go_s[step] = tiny_sum_s[spot] + tiny_ring_s[step - 1]
            tiny_ring(step).start()

        @pl.when(step == RING - 1)
        def _():
            tiny_ring(step - 1).wait_recv()
            tiny_own_s[spot] = tiny_sum_s[spot] + tiny_ring_s[step - 1]
            tiny_round(0).start()

        for piece in range(PIECES):
            for way in range(2):
                give(way, step, piece).wait_recv()
                ring_copy(way, step - 1, piece).wait_recv()
                for r0 in range(0, PIECE, SUB):
                    part = slice(r0, r0 + SUB)
                    total_s[slot, way, piece, part] += ring_s[way, step - 1, piece, part].astype(F32)

                @pl.when(step < RING - 1)
                def _():
                    add_piece(step, way, piece, take_s.at[way, step, piece])
                    ring_copy(way, step, piece).start()

                @pl.when(step == RING - 1)
                def _():
                    add_piece(step, way, piece, own_s.at[way, piece])
                    round_copy(way, 0, piece).start()
                    share_copy(way, 0, piece).start()
                    own_copy(way, 0, piece).start()
        return carry

    def first_piece(way, piece):
        give(way, 0, piece).wait_recv()
        add_piece(0, way, piece, take_s.at[way, 0, piece])
        ring_copy(way, 0, piece).start()

    order = [(way, piece) for piece in range(PIECES) for way in range(2)]
    for number, (way, piece) in enumerate(order):
        for kind, part, at_way, at_piece in loads:
            if (at_way, at_piece) == (way, piece):
                kind(part).wait()
        products(0, way, piece)
        if number > 0:
            first_piece(*order[number - 1])
    first_piece(*order[-1])
    tiny_swap.wait_recv()
    tiny_sum_s[...] = tiny_s[...] + tiny_take_s[...]
    tiny_go_s[0] = tiny_sum_s[block(0, 0)]
    tiny_ring(0).start()

    def group_step(group, carry):
        @pl.when(group < RING // 2)
        def _():
            for way, piece in order:
                products(group, way, piece)

        top = jnp.minimum(2 * group + 1, RING)
        return lax.fori_loop(2 * group - 1, top, reduce_step, carry)

    lax.fori_loop(1, RING // 2 + 1, group_step, 0)

    def round_step(step, carry):
        tiny_round_wait(step - 1)

        @pl.when(step < RING - 1)
        def _():
            tiny_round(step).start()

        for piece in range(PIECES):
            for way in range(2):
                arrival(way, step - 1, piece).wait_recv()

                @pl.when(step < RING - 1)
                def _():
                    round_copy(way, step, piece).start()

                share_copy(way, step, piece).start()
                own_copy(way, step, piece).start()
        return carry

    lax.fori_loop(1, RING, round_step, 0)

    for part in range(D // 128):
        small_out[:, part * 128 : part * 128 + 128] = tiny_own_s[part]
    tiny_swap.wait_send()

    for way in range(2):
        for piece in range(PIECES):
            share_copy(way, 0, piece).wait_send()
            own_copy(way, 0, piece).wait()
            share_wait(way, 0, piece)
            round_copy(way, 0, piece).wait_send()
            ring_copy(way, 0, piece).wait_send()
    tiny_ring(0).wait_send()
    tiny_round(0).wait_send()

    def finish(step, carry):
        for way in range(2):
            for piece in range(PIECES):
                share_copy(way, step, piece).wait_send()
                own_copy(way, step, piece).wait()
                share_wait(way, step, piece)

                @pl.when(step >= RING // 2)
                def _():
                    give(way, step, piece).wait_send()

                @pl.when(step < RING - 1)
                def _():
                    ring_copy(way, step, piece).wait_send()
                    round_copy(way, step, piece).wait_send()

        @pl.when(step < RING - 1)
        def _():
            tiny_ring(step).wait_send()
            tiny_round(step).wait_send()

        return carry

    lax.fori_loop(1, RING, finish, 0)


def run_sums(left, right, small):
    rows = right.shape[1]
    anywhere = pl.BlockSpec(memory_space=pl.ANY)
    vectors = pl.BlockSpec(memory_space=pltpu.VMEM)

    def pieces(*lead, dtype=BF16):
        return pltpu.VMEM((*lead, PIECE, D), dtype)

    dma = pltpu.SemaphoreType.DMA
    scratch = [
        pltpu.VMEM(left.shape, BF16), pltpu.VMEM(right.shape, BF16),
        pieces(4, 2, PIECES, dtype=F32), pieces(2, 4, PIECES), pieces(2, RING, PIECES),
        pieces(2, RING - 1, PIECES), pieces(2, PIECES), pieces(2, RING - 1, PIECES),
        pltpu.VMEM((RING, 16, 128), F32), pltpu.VMEM((RING, 16, 128), F32), pltpu.VMEM((RING, 16, 128), F32),
        pltpu.VMEM((RING - 1, 16, 128), F32), pltpu.VMEM((RING - 1, 16, 128), F32), pltpu.VMEM((RING, 16, 128), F32),
        dma((16,)), dma((2, RING, PIECES)), dma((2, RING, PIECES)),
        dma((2, RING - 1, PIECES)), dma((2, RING - 1, PIECES)), dma((2, RING, PIECES)),
        dma((2, RING - 1, PIECES)), dma((2, RING - 1, PIECES)), dma((2, RING, PIECES)), dma((2, RING, PIECES)),
        dma((2,)), dma((RING - 1,)), dma((RING - 1,)), dma((RING - 1,)), dma((RING - 1,)),
    ]
    return pl.pallas_call(
        sums_kernel,
        out_shape=(jax.ShapeDtypeStruct((12, D, D), BF16), jax.ShapeDtypeStruct((16, D), F32)),
        in_specs=[anywhere, anywhere, vectors],
        out_specs=[anywhere, vectors],
        scratch_shapes=scratch,
        compiler_params=pltpu.CompilerParams(
            collective_id=1, has_side_effects=True, vmem_limit_bytes=60 * 1024 * 1024
        ),
        cost_estimate=pl.CostEstimate(flops=rows * 2 * 7077888, bytes_accessed=70000000, transcendentals=0),
    )(left, right, small)


def plain_sums(left, right, small):
    panels = [dot(left[row : row + D], right[number]).astype(BF16) for row, number in PANELS]
    return lax.psum(jnp.stack(panels), "dp"), lax.psum(small, "dp")


SLOTS = 8
CUT = D // 2


def widen_kernel(
    act, dx, grads, small, act_out, dx_out, query_out, key_out, value_out, out_out, up_out, down_out,
    bias_out, up_bias_out, gain_out, shift_out, low_s, wide_s, act_s, dx_s, in_sem, out_sem, move_sem,
):
    moves_in = [
        pltpu.make_async_copy(act, act_s, move_sem.at[0]), pltpu.make_async_copy(dx, dx_s, move_sem.at[1])
    ]
    moves_out = [
        pltpu.make_async_copy(act_s, act_out.at[0], move_sem.at[0]),
        pltpu.make_async_copy(dx_s, dx_out.at[0], move_sem.at[1]),
    ]
    jobs = []
    for panel in range(12):
        for half in range(2):
            rows = pl.ds(half * CUT, CUT)
            if panel < 4:
                target = (query_out, key_out, value_out, out_out)[panel].at[0, rows]
            elif panel < 8:
                target = up_out.at[0, rows, pl.ds((panel - 4) * D, D)]
            else:
                target = down_out.at[0, pl.ds((panel - 8) * D + half * CUT, CUT)]
            jobs.append((grads.at[panel, rows], target))

    def fetch(number):
        return pltpu.make_async_copy(jobs[number][0], low_s.at[number % SLOTS], in_sem.at[number % SLOTS])

    def store(number):
        return pltpu.make_async_copy(wide_s.at[number % SLOTS], jobs[number][1], out_sem.at[number % SLOTS])

    for number in range(SLOTS):
        fetch(number).start()
    for move in moves_in:
        move.start()
    bias_out[0] = small[0:4]
    for panel in range(FF // D):
        up_bias_out[:, panel * D : (panel + 1) * D] = small[4 + panel : 5 + panel]
    gain_out[0] = small[8:10]
    shift_out[0] = small[10:12]
    for number in range(len(jobs)):
        slot = number % SLOTS
        fetch(number).wait()
        if number >= SLOTS:
            store(number - SLOTS).wait()

        def turn(step, carry):
            part = pl.ds(pl.multiple_of(step * SUB, SUB), SUB)
            wide_s[slot, part, :] = low_s[slot, part, :].astype(F32)
            return carry

        lax.fori_loop(0, CUT // SUB, turn, 0, unroll=4)
        store(number).start()
        if number == SLOTS:
            for move_in, move_out in zip(moves_in, moves_out):
                move_in.wait()
                move_out.start()
        if number + SLOTS < len(jobs):
            fetch(number + SLOTS).start()
    for number in range(len(jobs) - SLOTS, len(jobs)):
        store(number).wait()
    for move in moves_out:
        move.wait()


def widen(act, dx, grads, small):
    anywhere = pl.BlockSpec(memory_space=pl.ANY)
    vectors = pl.BlockSpec(memory_space=pltpu.VMEM)
    square = jax.ShapeDtypeStruct((1, D, D), F32)
    return pl.pallas_call(
        widen_kernel,
        out_shape=(
            jax.ShapeDtypeStruct((1, *act.shape), BF16), jax.ShapeDtypeStruct((1, *dx.shape), F32),
            square, square, square, square,
            jax.ShapeDtypeStruct((1, D, FF), F32), jax.ShapeDtypeStruct((1, FF, D), F32),
            jax.ShapeDtypeStruct((1, 4, D), F32), jax.ShapeDtypeStruct((1, FF), F32),
            jax.ShapeDtypeStruct((1, 2, D), F32), jax.ShapeDtypeStruct((1, 2, D), F32),
        ),
        in_specs=[anywhere, anywhere, anywhere, vectors],
        out_specs=[anywhere] * 8 + [vectors] * 4,
        scratch_shapes=[
            pltpu.VMEM((SLOTS, CUT, D), BF16), pltpu.VMEM((SLOTS, CUT, D), F32),
            pltpu.VMEM(act.shape, BF16), pltpu.VMEM(dx.shape, F32),
            pltpu.SemaphoreType.DMA((SLOTS,)), pltpu.SemaphoreType.DMA((SLOTS,)), pltpu.SemaphoreType.DMA((2,)),
        ],
        compiler_params=pltpu.CompilerParams(vmem_limit_bytes=60 * 1024 * 1024),
        cost_estimate=pl.CostEstimate(flops=7077888, bytes_accessed=42467328, transcendentals=0),
    )(act, dx, grads, small)


def per_device(grid, tokens, cotangent, lengths, spans, *weights):
    act, dx, left, right, small = run_layers(tokens, cotangent, lengths, spans, *weights)
    grads, small = (run_sums if grid else plain_sums)(left, right, small)
    return widen(act, dx, grads, small)


def solution(mesh):
    in_specs = (
        P("dp", None), P("dp", None), P("dp"), P("dp", None),
        P("section", None, None), P("section", None, None), P("section", None, None),
        P("section", None, None), P("section", None, None), P("section", None, None),
        P("section", None, None), P("section", None), P("section", None, None), P("section", None, None),
    )
    out_specs = (
        P("section", "dp", None), P("section", "dp", None),
        P("section", None, None), P("section", None, None), P("section", None, None),
        P("section", None, None), P("section", None, None), P("section", None, None),
        P("section", None, None), P("section", None), P("section", None, None), P("section", None, None),
    )
    part = functools.partial(per_device, mesh.shape["dp"] == 2 * RING)
    return jax.shard_map(part, mesh=mesh, in_specs=in_specs, out_specs=out_specs, check_vma=False)
```

```python
import functools

import jax
import jax.numpy as jnp
from jax import lax
from jax.experimental import pallas as pl
from jax.experimental.pallas import tpu as pltpu
from jax.sharding import PartitionSpec as P

D = 768
HEADS = 12
HEAD_DIM = 64
PAIRS = HEADS // 2
FF = 3072
LENGTH = 160
LEAST = 96
CHAINS_MB = 2
ROWS = CHAINS_MB * LENGTH
SUB = 32
WIDE = 512

F32 = jnp.float32
BF16 = jnp.bfloat16
MESH = pl.DeviceIdType.MESH


def dot(left, right):
    return jnp.dot(left, right, preferred_element_type=F32)


def dot_t(left, right):
    return lax.dot_general(left, right, (((1,), (1,)), ((), ())), preferred_element_type=F32)


def t_dot(left, right):
    return lax.dot_general(left, right, (((0,), (0,)), ((), ())), preferred_element_type=F32)


def fold(block):
    return jnp.sum(block.reshape(-1, 8, block.shape[-1]), axis=0)


def gelu_parts(u):
    t = pl.reciprocal(1.0 + 0.23164189 * jnp.abs(u), approx=True)
    gauss = jnp.exp2(u * u * -0.7213475204444817)
    poly = t * (
        0.127414796 + t * (-0.142248368 + t * (0.7107068705 + t * (-0.7265760135 + t * 0.5307027145)))
    )
    tail = poly * gauss
    cdf = jnp.where(u >= 0, 1.0 - tail, tail)
    return u * cdf, cdf + (u * 0.3989422804014327) * gauss


def layers_kernel(
    micro_count,
    tokens, cotangent, lengths, spans,
    wq, wk, wv, wo, w1, w2, bias_in, up_bias_in, gains_in, shifts_in,
    act_out, dx_out, left_out, right_out, small_out,
    wq_s, wk_s, wv_s, wo_s, w1_s, w2_s,
    h_s, q_s, k_s, v_s, p_s, o_s, n_s, xa_s, xb_s, z_s, g_s, inva_s, invb_s,
    y_s, dy_s, df_s, da_s, do_s, dx_s, wide_s, turn_s, acc_s, accu_s,
    w_sem, in_sem, out_sem, turn_sem, fwd_send, fwd_recv, bwd_send, bwd_recv,
):
    section = lax.axis_index("section")
    other = 1 - section
    first = section == 0
    last = section == 1

    barrier = pltpu.get_barrier_semaphore()
    pl.semaphore_signal(barrier, inc=1, device_id={"section": other}, device_id_type=MESH)

    weight_pairs = ((wq, wq_s), (wk, wk_s), (wv, wv_s), (wo, wo_s), (w1, w1_s), (w2, w2_s))

    def weight_copy(index):
        source, target = weight_pairs[index]
        return pltpu.make_async_copy(source.at[0], target, w_sem.at[index])

    def rows_of(index):
        return pl.ds(pl.multiple_of(index * ROWS, ROWS), ROWS)

    def entry_copy(index):
        return pltpu.make_async_copy(tokens.at[rows_of(index)], h_s.at[rows_of(index)], in_sem.at[index])

    def cot_copy(index):
        return pltpu.make_async_copy(cotangent.at[rows_of(index)], dy_s.at[rows_of(index)], in_sem.at[index])

    def forward_send(index):
        return pltpu.make_async_remote_copy(
            src_ref=y_s.at[rows_of(index)],
            dst_ref=h_s.at[rows_of(index)],
            send_sem=fwd_send.at[index],
            recv_sem=fwd_recv.at[index],
            device_id={"section": other},
            device_id_type=MESH,
        )

    def backward_send(index):
        return pltpu.make_async_remote_copy(
            src_ref=y_s.at[rows_of(index)],
            dst_ref=dy_s.at[rows_of(index)],
            send_sem=bwd_send.at[index],
            recv_sem=bwd_recv.at[index],
            device_id={"section": other},
            device_id_type=MESH,
        )

    backward_outs = ((q_s, 0), (k_s, 1), (v_s, 2), (da_s, 3), (df_s, 8))

    def act_copy(index):
        return pltpu.make_async_copy(y_s.at[rows_of(index)], act_out.at[rows_of(index)], out_sem.at[0, index])

    def dx_copy(index):
        return pltpu.make_async_copy(dx_s.at[rows_of(index)], dx_out.at[rows_of(index)], out_sem.at[1, index])

    def right_copies(index):
        for slot, (source, place) in enumerate(backward_outs):
            yield pltpu.make_async_copy(
                source.at[rows_of(index)], right_out.at[place, rows_of(index)], out_sem.at[2 + slot, index]
            )
        for panel in range(FF // D):
            yield pltpu.make_async_copy(
                g_s.at[rows_of(index), pl.ds(panel * D, D)],
                right_out.at[4 + panel, rows_of(index)],
                out_sem.at[7 + panel, index],
            )

    def turn_copy(slot, row):
        return pltpu.make_async_copy(
            turn_s.at[slot], left_out.at[pl.ds(pl.multiple_of(row, 128), 128)], turn_sem.at[slot]
        )

    def transpose_all():
        done = 0
        for source, tiles in ((h_s, D // 128), (o_s, D // 128), (n_s, D // 128), (z_s, FF // 128)):

            def tile_step(tile, carry, source=source, done=done):
                number = tile + done
                slot = lax.rem(number, 2)

                @pl.when(number >= 2)
                def _():
                    turn_copy(slot, (number - 2) * 128).wait()

                turn_s[slot] = source[:, pl.ds(pl.multiple_of(tile * 128, 128), 128)].T
                turn_copy(slot, number * 128).start()
                return carry

            lax.fori_loop(0, tiles, tile_step, 0)
            done += tiles
        for number in (done - 2, done - 1):
            turn_copy(number % 2, number * 128).wait()

    @pl.when(first)
    def _():
        for index in range(micro_count):
            entry_copy(index).start()

    @pl.when(last)
    def _():
        for index in range(micro_count):
            cot_copy(index).start()

    for index in range(6):
        weight_copy(index).start()

    acc_s[...] = jnp.zeros_like(acc_s)
    accu_s[...] = jnp.zeros_like(accu_s)

    bias = bias_in[0].astype(F32)
    gains = gains_in[0].astype(F32)
    shifts = shifts_in[0].astype(F32)
    low_half = lax.broadcasted_iota(jnp.int32, (1, 8, 128), 2) < HEAD_DIM
    keep_low = jnp.where(lax.broadcasted_iota(jnp.int32, (1, 16, 128), 2) < HEAD_DIM, 1.0, 0.0)
    keep_high = (1.0 - keep_low).astype(BF16)
    keep_low = keep_low.astype(BF16)

    def stacked(pair_block):
        tiles = pair_block.reshape(-1, 16, 128)
        return jnp.concatenate([tiles * keep_low, tiles * keep_high], axis=0).reshape(2 * LENGTH, 128)

    def merged(tall):
        tiles = tall.reshape(2, LENGTH // 8, 8, 128)
        return jnp.where(low_half, tiles[0], tiles[1]).reshape(LENGTH, 128)

    pl.semaphore_wait(barrier, 1)

    def forward(index, carry):
        base = index * ROWS
        rows = rows_of(index)

        @pl.when(first)
        def _():
            entry_copy(index).wait()
            for chain in range(CHAINS_MB):
                number = index * CHAINS_MB + chain
                start, stop = spans[0, number], spans[1, number]
                spot = lax.broadcasted_iota(jnp.int32, (LENGTH, D), 0)
                here = pl.ds(pl.multiple_of(base + chain * LENGTH, LENGTH), LENGTH)
                keep = (spot < start) | (spot >= stop)
                h_s[here, :] = jnp.where(keep, h_s[here, :].astype(F32), 0.0).astype(BF16)

        @pl.when(last)
        def _():
            forward_send(index).wait_recv()

        @pl.when(index == 0)
        def _():
            for number in range(3):
                weight_copy(number).wait()

        for weight, bias_row, target in ((wq_s, 0, q_s), (wk_s, None, k_s), (wv_s, 1, v_s)):
            block = dot(h_s[rows, :], weight[...])
            if bias_row is not None:
                block = block + bias[bias_row : bias_row + 1]
            if target is q_s:
                block = block * 0.125
            target[rows, :] = block.astype(BF16)

        def chain_step(chain, carry):
            here = pl.ds(pl.multiple_of(base + chain * LENGTH, LENGTH), LENGTH)
            number = index * CHAINS_MB + chain
            spot = lax.broadcasted_iota(jnp.int32, (LENGTH - LEAST, 2 * LENGTH), 0) + LEAST
            penalty = jnp.where(spot < lengths[number], 0.0, -1000000000.0)
            lanes = [slice(pair * 128, pair * 128 + 128) for pair in range(PAIRS)]
            scores = [dot_t(k_s[here, lane], stacked(q_s[here, lane])) for lane in lanes]
            attends = []
            for pair in range(PAIRS):
                held = jnp.concatenate([scores[pair][:LEAST], scores[pair][LEAST:] + penalty], axis=0)
                raised = jnp.exp(held - jnp.max(held, axis=0, keepdims=True))
                attends.append((raised * (1.0 / jnp.sum(raised, axis=0, keepdims=True))).astype(BF16))
                p_s[number, pair] = attends[pair]
            mixes = [t_dot(attends[pair], v_s[here, lanes[pair]]) for pair in range(PAIRS)]
            for pair in range(PAIRS):
                o_s[here, lanes[pair]] = merged(mixes[pair]).astype(BF16)
            return carry

        lax.fori_loop(0, CHAINS_MB, chain_step, 0)

        @pl.when(index == 0)
        def _():
            weight_copy(3).wait()

        wide_s[...] = dot(o_s[rows, :], wo_s[...])

        def first_norm(step, carry):
            part = pl.ds(pl.multiple_of(step * SUB, SUB), SUB)
            here = pl.ds(pl.multiple_of(base + step * SUB, SUB), SUB)
            r = h_s[here, :].astype(F32) + wide_s[part, :] + bias[2:3]
            centered = r - jnp.mean(r, axis=-1, keepdims=True)
            inv = lax.rsqrt(jnp.mean(centered * centered, axis=-1, keepdims=True) + 1e-05)
            hat = centered * inv
            normed = hat * gains[0:1] + shifts[0:1]
            xa_s[here, :] = hat.astype(BF16)
            inva_s[here, :] = jnp.broadcast_to(inv, (SUB, 128))
            n_s[here, :] = normed.astype(BF16)
            wide_s[part, :] = normed
            return carry

        lax.fori_loop(0, ROWS // SUB, first_norm, 0, unroll=5)

        @pl.when(index == 0)
        def _():
            weight_copy(4).wait()
            weight_copy(5).wait()

        def lift(n0):
            return dot(n_s[rows, :], w1_s[:, n0 : n0 + WIDE])

        following = lift(0)
        for n0 in range(0, FF, WIDE):
            block = following
            if n0 + WIDE < FF:
                following = lift(n0 + WIDE)
            up_bias = up_bias_in[0:1, n0 : n0 + WIDE].astype(F32)
            for r0 in range(0, ROWS, SUB):
                here = pl.ds(pl.multiple_of(base + r0, SUB), SUB)
                act, slope = gelu_parts(block[r0 : r0 + SUB] + up_bias)
                z_s[here, n0 : n0 + WIDE] = act.astype(BF16)
                g_s[here, n0 : n0 + WIDE] = slope.astype(BF16)

        wide_s[...] += dot(z_s[rows, :], w2_s[...])

        def second_norm(step, carry):
            part = pl.ds(pl.multiple_of(step * SUB, SUB), SUB)
            here = pl.ds(pl.multiple_of(base + step * SUB, SUB), SUB)
            r = wide_s[part, :] + bias[3:4]
            centered = r - jnp.mean(r, axis=-1, keepdims=True)
            inv = lax.rsqrt(jnp.mean(centered * centered, axis=-1, keepdims=True) + 1e-05)
            hat = centered * inv
            xb_s[here, :] = hat.astype(BF16)
            invb_s[here, :] = jnp.broadcast_to(inv, (SUB, 128))
            y_s[here, :] = (hat * gains[1:2] + shifts[1:2]).astype(BF16)
            return carry

        lax.fori_loop(0, ROWS // SUB, second_norm, 0, unroll=5)

        @pl.when(first)
        def _():
            forward_send(index).start()

        act_copy(index).start()
        return carry

    lax.fori_loop(0, micro_count, forward, 0)

    def forward_done(index, carry):
        @pl.when(first)
        def _():
            forward_send(index).wait_send()

        act_copy(index).wait()
        return carry

    lax.fori_loop(0, micro_count, forward_done, 0)

    @pl.when(first)
    def _():
        transpose_all()

    def backward(index, carry):
        base = index * ROWS
        rows = rows_of(index)

        @pl.when(first)
        def _():
            backward_send(index).wait_recv()

        @pl.when(last)
        def _():
            cot_copy(index).wait()

        def second_back(step, carry):
            part = pl.ds(pl.multiple_of(step * SUB, SUB), SUB)
            here = pl.ds(pl.multiple_of(base + step * SUB, SUB), SUB)
            dy = dy_s[here, :].astype(F32)
            hat = xb_s[here, :].astype(F32)
            acc_s[9] += fold(dy * hat)
            acc_s[11] += fold(dy)
            scaled = dy * gains[1:2]
            mean_plain = jnp.mean(scaled, axis=-1, keepdims=True)
            mean_hat = jnp.mean(scaled * hat, axis=-1, keepdims=True)
            grad = (scaled - mean_plain - hat * mean_hat) * invb_s[here, 0:1]
            wide_s[part, :] = grad
            df_s[here, :] = grad.astype(BF16)
            acc_s[3] += fold(grad)
            return carry

        lax.fori_loop(0, ROWS // SUB, second_back, 0, unroll=5)

        def drop(n0):
            return dot_t(df_s[rows, :], w2_s[n0 : n0 + WIDE, :])

        following = drop(0)
        for n0 in range(0, FF, WIDE):
            block = following
            if n0 + WIDE < FF:
                following = drop(n0 + WIDE)
            sums = jnp.zeros((8, WIDE), F32)
            for r0 in range(0, ROWS, SUB):
                here = pl.ds(pl.multiple_of(base + r0, SUB), SUB)
                part = block[r0 : r0 + SUB] * g_s[here, n0 : n0 + WIDE].astype(F32)
                g_s[here, n0 : n0 + WIDE] = part.astype(BF16)
                sums = sums + fold(part)
            accu_s[:, n0 : n0 + WIDE] += sums

        wide_s[...] += dot_t(g_s[rows, :], w1_s[...])

        def first_back(step, carry):
            part = pl.ds(pl.multiple_of(step * SUB, SUB), SUB)
            here = pl.ds(pl.multiple_of(base + step * SUB, SUB), SUB)
            dn = wide_s[part, :]
            hat = xa_s[here, :].astype(F32)
            acc_s[8] += fold(dn * hat)
            acc_s[10] += fold(dn)
            scaled = dn * gains[0:1]
            mean_plain = jnp.mean(scaled, axis=-1, keepdims=True)
            mean_hat = jnp.mean(scaled * hat, axis=-1, keepdims=True)
            grad = (scaled - mean_plain - hat * mean_hat) * inva_s[here, 0:1]
            wide_s[part, :] = grad
            da_s[here, :] = grad.astype(BF16)
            acc_s[2] += fold(grad)
            return carry

        lax.fori_loop(0, ROWS // SUB, first_back, 0, unroll=5)

        do_s[...] = dot_t(da_s[rows, :], wo_s[...]).astype(BF16)

        def chain_step(chain, carry):
            here = pl.ds(pl.multiple_of(base + chain * LENGTH, LENGTH), LENGTH)
            near = pl.ds(pl.multiple_of(chain * LENGTH, LENGTH), LENGTH)
            number = index * CHAINS_MB + chain
            pairs = range(PAIRS)
            lanes = [slice(pair * 128, pair * 128 + 128) for pair in pairs]
            grad_talls = [stacked(do_s[near, lane]) for lane in lanes]
            grad_attends = [dot_t(v_s[here, lanes[pair]], grad_talls[pair]) for pair in pairs]
            dvs = [dot(p_s[number, pair], grad_talls[pair]) for pair in pairs]
            grad_scores = []
            for pair in pairs:
                attend = p_s[number, pair].astype(F32)
                weighted = attend * grad_attends[pair]
                delta = jnp.sum(weighted, axis=0, keepdims=True) / jnp.sum(attend, axis=0, keepdims=True)
                grad_scores.append((weighted - attend * delta).astype(BF16))
            dks = [dot(grad_scores[pair], stacked(q_s[here, lanes[pair]])) for pair in pairs]
            dqs = [t_dot(grad_scores[pair], k_s[here, lanes[pair]]) for pair in pairs]
            for pair in pairs:
                dq = merged(dqs[pair]) * 0.125
                q_s[here, lanes[pair]] = dq.astype(BF16)
                k_s[here, lanes[pair]] = dks[pair].astype(BF16)
                v_s[here, lanes[pair]] = dvs[pair].astype(BF16)
                acc_s[0, :, lanes[pair]] += fold(dq)
                acc_s[1, :, lanes[pair]] += fold(dvs[pair])
            return carry

        lax.fori_loop(0, CHAINS_MB, chain_step, 0)

        for source, weight in ((q_s, wq_s), (k_s, wk_s), (v_s, wv_s)):
            wide_s[...] += dot_t(source[rows, :], weight[...])

        @pl.when(last)
        def _():
            low = wide_s[...].astype(BF16)
            y_s[rows, :] = low
            dx_s[rows, :] = low.astype(F32)
            backward_send(index).start()

        @pl.when(first)
        def _():
            for chain in range(CHAINS_MB):
                number = index * CHAINS_MB + chain
                start, stop = spans[0, number], spans[1, number]
                spot = lax.broadcasted_iota(jnp.int32, (LENGTH, D), 0)
                here = pl.ds(pl.multiple_of(base + chain * LENGTH, LENGTH), LENGTH)
                keep = (spot < start) | (spot >= stop)
                dx_s[here, :] = jnp.where(keep, wide_s[chain * LENGTH : (chain + 1) * LENGTH, :], 0.0)

        dx_copy(index).start()
        for copy in right_copies(index):
            copy.start()
        return carry

    lax.fori_loop(0, micro_count, backward, 0)

    @pl.when(last)
    def _():
        transpose_all()

    for number in range(12):
        if 4 <= number < 8:
            panel = accu_s[:, (number - 4) * D : (number - 3) * D]
        else:
            panel = acc_s[number]
        small_out[number : number + 1, :] = jnp.sum(panel, axis=0, keepdims=True)
    small_out[12:16, :] = jnp.zeros((4, D), F32)

    def backward_done(index, carry):
        @pl.when(last)
        def _():
            backward_send(index).wait_send()

        dx_copy(index).wait()
        for copy in right_copies(index):
            copy.wait()
        return carry

    lax.fori_loop(0, micro_count, backward_done, 0)


def run_layers(tokens, cotangent, lengths, spans, *weights):
    rows = tokens.shape[0]
    micro_count = rows // ROWS
    chains = rows // LENGTH
    anywhere = pl.BlockSpec(memory_space=pl.ANY)
    scalars = pl.BlockSpec(memory_space=pltpu.SMEM)
    vectors = pl.BlockSpec(memory_space=pltpu.VMEM)
    out_shape = (
        jax.ShapeDtypeStruct((rows, D), BF16),
        jax.ShapeDtypeStruct((rows, D), F32),
        jax.ShapeDtypeStruct((3 * D + FF, rows), BF16),
        jax.ShapeDtypeStruct((9, rows, D), BF16),
        jax.ShapeDtypeStruct((16, D), F32),
    )

    def vm(count, width=D, dtype=BF16):
        return pltpu.VMEM((count, width), dtype)

    scratch = [
        vm(D), vm(D), vm(D), vm(D), vm(D, FF), vm(FF),
        vm(rows), vm(rows), vm(rows), vm(rows),
        pltpu.VMEM((chains, PAIRS, LENGTH, 2 * LENGTH), BF16),
        vm(rows), vm(rows), vm(rows), vm(rows), vm(rows, FF), vm(rows, FF),
        vm(rows, 128, F32), vm(rows, 128, F32),
        vm(rows), vm(rows), vm(rows), vm(rows), vm(ROWS), vm(rows, D, F32),
        vm(ROWS, D, F32), pltpu.VMEM((2, 128, rows), BF16), pltpu.VMEM((12, 8, D), F32), vm(8, FF, F32),
        pltpu.SemaphoreType.DMA((6,)),
        pltpu.SemaphoreType.DMA((micro_count,)),
        pltpu.SemaphoreType.DMA((11, micro_count)),
        pltpu.SemaphoreType.DMA((2,)),
        pltpu.SemaphoreType.DMA((micro_count,)),
        pltpu.SemaphoreType.DMA((micro_count,)),
        pltpu.SemaphoreType.DMA((micro_count,)),
        pltpu.SemaphoreType.DMA((micro_count,)),
    ]
    return pl.pallas_call(
        functools.partial(layers_kernel, micro_count),
        out_shape=out_shape,
        in_specs=[anywhere, anywhere, scalars, scalars] + [anywhere] * 6 + [vectors] * 4,
        out_specs=[anywhere] * 4 + [vectors],
        scratch_shapes=scratch,
        compiler_params=pltpu.CompilerParams(
            collective_id=0, has_side_effects=True, vmem_limit_bytes=60 * 1024 * 1024
        ),
        cost_estimate=pl.CostEstimate(
            flops=rows * 2 * 2 * 2 * 7077888, bytes_accessed=60000000, transcendentals=rows * FF * 2
        ),
    )(tokens, cotangent, lengths, spans.T, *weights)


RING = 8
PIECES = 3
PIECE = D // RING
PANELS = (
    (0, 0), (0, 1), (0, 2), (D, 3), (2 * D, 4), (2 * D, 5),
    (2 * D, 6), (2 * D, 7), (3 * D, 8), (4 * D, 8), (5 * D, 8), (6 * D, 8),
)


def sums_kernel(
    left, right, small_in, grads_out, small_out,
    left_s, right_s, total_s, give_s, take_s, ring_s, own_s,
    tiny_s, tiny_take_s, tiny_sum_s, tiny_go_s, tiny_ring_s, tiny_own_s,
    load_sem, give_sem, take_sem, ring_send, ring_recv, own_sem, round_send, round_recv, share_send, share_recv,
    tiny_sem, tiny_ring_send, tiny_ring_recv, tiny_round_send, tiny_round_recv,
):
    me = lax.axis_index("dp")
    core = lax.rem(me, 2)
    high = lax.rem(lax.div(me, 2), 2)
    depth = lax.div(me, 4)
    place = depth + high * (7 - 2 * depth)

    def device(spot, on_core):
        row = lax.div(spot, 4)
        return {"dp": 4 * (spot + row * (7 - 2 * spot)) + 2 * row + on_core}

    ahead = device(lax.rem(place + 1, RING), core)
    behind = device(lax.rem(place + RING - 1, RING), core)
    beside = device(place, 1 - core)
    targets = (ahead, behind)

    barrier = pltpu.get_barrier_semaphore()
    for peer in (ahead, behind, beside):
        pl.semaphore_signal(barrier, inc=1, device_id=peer, device_id_type=MESH)

    def block(way, step):
        return lax.rem(place - step + RING, RING) if way == 0 else lax.rem(place + step, RING)

    def late_block(way, step):
        return lax.rem(place + 1 - step + RING, RING) if way == 0 else lax.rem(place + RING - 1 + step, RING)

    def load_left(part):
        return pltpu.make_async_copy(left.at[pl.ds(part * D, D)], left_s.at[pl.ds(part * D, D)], load_sem.at[part])

    def load_right(part):
        return pltpu.make_async_copy(right.at[part], right_s.at[part], load_sem.at[7 + part])

    def remote(source, target, send, recv, peer):
        return pltpu.make_async_remote_copy(
            src_ref=source, dst_ref=target, send_sem=send, recv_sem=recv, device_id=peer, device_id_type=MESH
        )

    def give(way, step, piece):
        return remote(
            give_s.at[way, step, piece], take_s.at[way, step, piece],
            give_sem.at[way, step, piece], take_sem.at[way, step, piece], beside,
        )

    def ring_copy(way, step, piece):
        return remote(
            take_s.at[way, step, piece], ring_s.at[way, step, piece],
            ring_send.at[way, step, piece], ring_recv.at[way, step, piece], targets[way],
        )

    def region(way, spot, piece, on_core):
        rows = pl.ds(pl.multiple_of(spot * PIECE, PIECE), PIECE)
        return grads_out.at[6 * way + 3 * on_core + piece, rows]

    def own_copy(way, piece):
        return pltpu.make_async_copy(
            own_s.at[way, piece], region(way, late_block(way, 0), piece, core), own_sem.at[way, piece]
        )

    def round_copy(way, step, piece, source=None):
        target = region(way, late_block(way, step), piece, core)
        return remote(
            target if source is None else source, target,
            round_send.at[way, step, piece], round_recv.at[way, step, piece], targets[way],
        )

    def round_wait(way, step, piece):
        target = region(way, late_block(way, step + 1), piece, core)
        remote(
            target, target, round_send.at[way, step, piece], round_recv.at[way, step, piece], targets[way]
        ).wait_recv()

    def share_copy(way, step, piece, source=None):
        target = region(way, late_block(way, step), piece, core)
        return remote(
            target if source is None else source, target,
            share_send.at[way, step, piece], share_recv.at[way, step, piece], beside,
        )

    def share_wait(way, step, piece):
        target = region(way, late_block(way, step), piece, 1 - core)
        remote(
            target, target, share_send.at[way, step, piece], share_recv.at[way, step, piece], beside
        ).wait_recv()

    tiny_swap = remote(tiny_s, tiny_take_s, tiny_sem.at[0], tiny_sem.at[1], beside)

    def tiny_ring(step):
        return remote(
            tiny_go_s.at[step], tiny_ring_s.at[step], tiny_ring_send.at[step], tiny_ring_recv.at[step], ahead
        )

    def tiny_round(step):
        spot = late_block(0, step)
        return remote(
            tiny_own_s.at[spot], tiny_own_s.at[spot], tiny_round_send.at[step], tiny_round_recv.at[step], ahead
        )

    def tiny_round_wait(step):
        spot = late_block(0, step + 1)
        remote(
            tiny_own_s.at[spot], tiny_own_s.at[spot], tiny_round_send.at[step], tiny_round_recv.at[step], ahead
        ).wait_recv()

    loads = []
    for piece in range(PIECES):
        for way in range(2):
            for half in range(2):
                first_row, number = PANELS[6 * way + 3 * half + piece]
                for kind, part in ((load_right, number), (load_left, first_row // D)):
                    if (kind, part) not in [entry[:2] for entry in loads]:
                        loads.append((kind, part, way, piece))
    for kind, part, _, _ in loads:
        kind(part).start()

    for part in range(RING):
        if part * 128 < D:
            tiny_s[part] = small_in[:, part * 128 : part * 128 + 128]
        else:
            tiny_s[part] = jnp.zeros((16, 128), F32)

    pl.semaphore_wait(barrier, 3)
    tiny_swap.start()

    def product(group, way, piece, pick):
        near, far = PANELS[6 * way + piece], PANELS[6 * way + 3 + piece]
        first_row = near[0] + pick * (far[0] - near[0])
        number = near[1] + pick * (far[1] - near[1])
        blocks = []
        for step in (2 * group, 2 * group + 1):
            start = pl.multiple_of(first_row + block(way, step) * PIECE, PIECE)
            blocks.append(left_s[pl.ds(start, PIECE), :])
        return dot(jnp.concatenate(blocks, axis=0), right_s[number])

    def keep_product(group, way, piece, both):
        total_s[lax.rem(2 * group, 4), way, piece] = both[:PIECE]
        total_s[lax.rem(2 * group + 1, 4), way, piece] = both[PIECE:]

    def give_product(group, way, piece, both):
        give_s[way, 2 * group, piece] = both[:PIECE].astype(BF16)
        give_s[way, 2 * group + 1, piece] = both[PIECE:].astype(BF16)
        give(way, 2 * group, piece).start()
        give(way, 2 * group + 1, piece).start()

    def add_piece(step, way, piece, target):
        slot = lax.rem(step, 4)
        for r0 in range(0, PIECE, SUB):
            part = slice(r0, r0 + SUB)
            whole = total_s[slot, way, piece, part] + take_s[way, step, piece, part].astype(F32)
            target[part] = whole.astype(BF16)

    def reduce_step(step, carry):
        slot = lax.rem(step, 4)
        spot = block(0, step)

        @pl.when(step < RING - 1)
        def _():
            tiny_ring(step - 1).wait_recv()
            tiny_go_s[step] = tiny_sum_s[spot] + tiny_ring_s[step - 1]
            tiny_ring(step).start()

        @pl.when(step == RING - 1)
        def _():
            tiny_ring(step - 1).wait_recv()
            tiny_own_s[spot] = tiny_sum_s[spot] + tiny_ring_s[step - 1]
            tiny_round(0).start()

        for piece in range(PIECES):
            for way in range(2):
                give(way, step, piece).wait_recv()
                ring_copy(way, step - 1, piece).wait_recv()
                for r0 in range(0, PIECE, SUB):
                    part = slice(r0, r0 + SUB)
                    total_s[slot, way, piece, part] += ring_s[way, step - 1, piece, part].astype(F32)

                @pl.when(step < RING - 1)
                def _():
                    add_piece(step, way, piece, take_s.at[way, step, piece])
                    ring_copy(way, step, piece).start()

                @pl.when(step == RING - 1)
                def _():
                    add_piece(step, way, piece, own_s.at[way, piece])
                    round_copy(way, 0, piece, own_s.at[way, piece]).start()
                    share_copy(way, 0, piece, own_s.at[way, piece]).start()
                    own_copy(way, piece).start()

                @pl.when(step < RING - 2)
                def _():
                    odd = lax.rem(step, 2)
                    group = lax.div(step, 2) + 1
                    both = product(group, way, piece, odd * core + (1 - odd) * (1 - core))

                    @pl.when(odd == 1)
                    def _():
                        keep_product(group, way, piece, both)

                    @pl.when(odd == 0)
                    def _():
                        give_product(group, way, piece, both)

        return carry

    def first_piece(way, piece):
        give(way, 0, piece).wait_recv()
        add_piece(0, way, piece, take_s.at[way, 0, piece])
        ring_copy(way, 0, piece).start()

    order = [(way, piece) for piece in range(PIECES) for way in range(2)]
    for number, (way, piece) in enumerate(order):
        for kind, part, at_way, at_piece in loads:
            if (at_way, at_piece) == (way, piece):
                kind(part).wait()
        give_product(0, way, piece, product(0, way, piece, 1 - core))
        keep_product(0, way, piece, product(0, way, piece, core))
        if number > 0:
            first_piece(*order[number - 1])
    first_piece(*order[-1])
    for way, piece in order:
        give_product(1, way, piece, product(1, way, piece, 1 - core))
    tiny_swap.wait_recv()
    tiny_sum_s[...] = tiny_s[...] + tiny_take_s[...]
    tiny_go_s[0] = tiny_sum_s[block(0, 0)]
    tiny_ring(0).start()

    lax.fori_loop(1, RING, reduce_step, 0)

    def round_step(step, carry):
        tiny_round_wait(step - 1)

        @pl.when(step < RING - 1)
        def _():
            tiny_round(step).start()

        for piece in range(PIECES):
            for way in range(2):
                round_wait(way, step - 1, piece)

                @pl.when(step < RING - 1)
                def _():
                    round_copy(way, step, piece).start()

                share_copy(way, step, piece).start()
        return carry

    lax.fori_loop(1, RING, round_step, 0)

    for part in range(D // 128):
        small_out[:, part * 128 : part * 128 + 128] = tiny_own_s[part]
    tiny_swap.wait_send()

    def finish(step, carry):
        for way in range(2):
            for piece in range(PIECES):
                give(way, step, piece).wait_send()
                share_wait(way, step, piece)
                share_copy(way, step, piece).wait_send()

                @pl.when(step < RING - 1)
                def _():
                    ring_copy(way, step, piece).wait_send()
                    round_copy(way, step, piece).wait_send()

        @pl.when(step < RING - 1)
        def _():
            tiny_ring(step).wait_send()
            tiny_round(step).wait_send()

        return carry

    lax.fori_loop(0, RING, finish, 0)
    for way in range(2):
        for piece in range(PIECES):
            own_copy(way, piece).wait()


def run_sums(left, right, small):
    rows = right.shape[1]
    anywhere = pl.BlockSpec(memory_space=pl.ANY)
    vectors = pl.BlockSpec(memory_space=pltpu.VMEM)

    def pieces(*lead, dtype=BF16):
        return pltpu.VMEM((*lead, PIECE, D), dtype)

    dma = pltpu.SemaphoreType.DMA
    scratch = [
        pltpu.VMEM(left.shape, BF16), pltpu.VMEM(right.shape, BF16),
        pieces(4, 2, PIECES, dtype=F32), pieces(2, RING, PIECES), pieces(2, RING, PIECES),
        pieces(2, RING - 1, PIECES), pieces(2, PIECES),
        pltpu.VMEM((RING, 16, 128), F32), pltpu.VMEM((RING, 16, 128), F32), pltpu.VMEM((RING, 16, 128), F32),
        pltpu.VMEM((RING - 1, 16, 128), F32), pltpu.VMEM((RING - 1, 16, 128), F32), pltpu.VMEM((RING, 16, 128), F32),
        dma((16,)), dma((2, RING, PIECES)), dma((2, RING, PIECES)),
        dma((2, RING - 1, PIECES)), dma((2, RING - 1, PIECES)), dma((2, PIECES)),
        dma((2, RING - 1, PIECES)), dma((2, RING - 1, PIECES)), dma((2, RING, PIECES)), dma((2, RING, PIECES)),
        dma((2,)), dma((RING - 1,)), dma((RING - 1,)), dma((RING - 1,)), dma((RING - 1,)),
    ]
    return pl.pallas_call(
        sums_kernel,
        out_shape=(jax.ShapeDtypeStruct((12, D, D), BF16), jax.ShapeDtypeStruct((16, D), F32)),
        in_specs=[anywhere, anywhere, vectors],
        out_specs=[anywhere, vectors],
        scratch_shapes=scratch,
        compiler_params=pltpu.CompilerParams(
            collective_id=1, has_side_effects=True, vmem_limit_bytes=60 * 1024 * 1024
        ),
        cost_estimate=pl.CostEstimate(flops=rows * 2 * 7077888, bytes_accessed=70000000, transcendentals=0),
    )(left, right, small)


def plain_sums(left, right, small):
    panels = [dot(left[row : row + D], right[number]).astype(BF16) for row, number in PANELS]
    return lax.psum(jnp.stack(panels), "dp"), lax.psum(small, "dp")


SLOTS = 8
CUT = D // 2


def widen_kernel(
    act, dx, grads, small, act_out, dx_out, query_out, key_out, value_out, out_out, up_out, down_out,
    bias_out, up_bias_out, gain_out, shift_out, low_s, wide_s, act_s, dx_s, in_sem, out_sem, move_sem,
):
    moves_in = [
        pltpu.make_async_copy(act, act_s, move_sem.at[0]), pltpu.make_async_copy(dx, dx_s, move_sem.at[1])
    ]
    moves_out = [
        pltpu.make_async_copy(act_s, act_out.at[0], move_sem.at[0]),
        pltpu.make_async_copy(dx_s, dx_out.at[0], move_sem.at[1]),
    ]
    jobs = []
    for panel in range(12):
        for half in range(2):
            rows = pl.ds(half * CUT, CUT)
            if panel < 4:
                target = (query_out, key_out, value_out, out_out)[panel].at[0, rows]
            elif panel < 8:
                target = up_out.at[0, rows, pl.ds((panel - 4) * D, D)]
            else:
                target = down_out.at[0, pl.ds((panel - 8) * D + half * CUT, CUT)]
            jobs.append((grads.at[panel, rows], target))

    def fetch(number):
        return pltpu.make_async_copy(jobs[number][0], low_s.at[number % SLOTS], in_sem.at[number % SLOTS])

    def store(number):
        return pltpu.make_async_copy(wide_s.at[number % SLOTS], jobs[number][1], out_sem.at[number % SLOTS])

    for number in range(SLOTS):
        fetch(number).start()
    for move in moves_in:
        move.start()
    bias_out[0] = small[0:4]
    for panel in range(FF // D):
        up_bias_out[:, panel * D : (panel + 1) * D] = small[4 + panel : 5 + panel]
    gain_out[0] = small[8:10]
    shift_out[0] = small[10:12]
    for number in range(len(jobs)):
        slot = number % SLOTS
        fetch(number).wait()
        if number >= SLOTS:
            store(number - SLOTS).wait()

        def turn(step, carry):
            part = pl.ds(pl.multiple_of(step * SUB, SUB), SUB)
            wide_s[slot, part, :] = low_s[slot, part, :].astype(F32)
            return carry

        lax.fori_loop(0, CUT // SUB, turn, 0, unroll=4)
        store(number).start()
        if number == SLOTS:
            for move_in, move_out in zip(moves_in, moves_out):
                move_in.wait()
                move_out.start()
        if number + SLOTS < len(jobs):
            fetch(number + SLOTS).start()
    for number in range(len(jobs) - SLOTS, len(jobs)):
        store(number).wait()
    for move in moves_out:
        move.wait()


def widen(act, dx, grads, small):
    anywhere = pl.BlockSpec(memory_space=pl.ANY)
    vectors = pl.BlockSpec(memory_space=pltpu.VMEM)
    square = jax.ShapeDtypeStruct((1, D, D), F32)
    return pl.pallas_call(
        widen_kernel,
        out_shape=(
            jax.ShapeDtypeStruct((1, *act.shape), BF16), jax.ShapeDtypeStruct((1, *dx.shape), F32),
            square, square, square, square,
            jax.ShapeDtypeStruct((1, D, FF), F32), jax.ShapeDtypeStruct((1, FF, D), F32),
            jax.ShapeDtypeStruct((1, 4, D), F32), jax.ShapeDtypeStruct((1, FF), F32),
            jax.ShapeDtypeStruct((1, 2, D), F32), jax.ShapeDtypeStruct((1, 2, D), F32),
        ),
        in_specs=[anywhere, anywhere, anywhere, vectors],
        out_specs=[anywhere] * 8 + [vectors] * 4,
        scratch_shapes=[
            pltpu.VMEM((SLOTS, CUT, D), BF16), pltpu.VMEM((SLOTS, CUT, D), F32),
            pltpu.VMEM(act.shape, BF16), pltpu.VMEM(dx.shape, F32),
            pltpu.SemaphoreType.DMA((SLOTS,)), pltpu.SemaphoreType.DMA((SLOTS,)), pltpu.SemaphoreType.DMA((2,)),
        ],
        compiler_params=pltpu.CompilerParams(vmem_limit_bytes=60 * 1024 * 1024),
        cost_estimate=pl.CostEstimate(flops=7077888, bytes_accessed=42467328, transcendentals=0),
    )(act, dx, grads, small)


def per_device(grid, tokens, cotangent, lengths, spans, *weights):
    act, dx, left, right, small = run_layers(tokens, cotangent, lengths, spans, *weights)
    grads, small = (run_sums if grid else plain_sums)(left, right, small)
    return widen(act, dx, grads, small)


def solution(mesh):
    in_specs = (
        P("dp", None), P("dp", None), P("dp"), P("dp", None),
        P("section", None, None), P("section", None, None), P("section", None, None),
        P("section", None, None), P("section", None, None), P("section", None, None),
        P("section", None, None), P("section", None), P("section", None, None), P("section", None, None),
    )
    out_specs = (
        P("section", "dp", None), P("section", "dp", None),
        P("section", None, None), P("section", None, None), P("section", None, None),
        P("section", None, None), P("section", None, None), P("section", None, None),
        P("section", None, None), P("section", None), P("section", None, None), P("section", None, None),
    )
    part = functools.partial(per_device, mesh.shape["dp"] == 2 * RING)
    return jax.shard_map(part, mesh=mesh, in_specs=in_specs, out_specs=out_specs, check_vma=False)
```

```python
import functools

import jax
import jax.numpy as jnp
from jax import lax
from jax.experimental import pallas as pl
from jax.experimental.pallas import tpu as pltpu
from jax.sharding import PartitionSpec as P

D = 768
HEADS = 12
HEAD_DIM = 64
PAIRS = HEADS // 2
FF = 3072
LENGTH = 160
LEAST = 96
CHAINS_MB = 1
ROWS = CHAINS_MB * LENGTH
SUB = 32
WIDE = 512

F32 = jnp.float32
BF16 = jnp.bfloat16
MESH = pl.DeviceIdType.MESH


def dot(left, right):
    return jnp.dot(left, right, preferred_element_type=F32)


def dot_t(left, right):
    return lax.dot_general(left, right, (((1,), (1,)), ((), ())), preferred_element_type=F32)


def t_dot(left, right):
    return lax.dot_general(left, right, (((0,), (0,)), ((), ())), preferred_element_type=F32)


def fold(block):
    return jnp.sum(block.reshape(-1, 8, block.shape[-1]), axis=0)


def gelu_parts(u):
    t = pl.reciprocal(1.0 + 0.23164189 * jnp.abs(u), approx=True)
    gauss = jnp.exp2(u * u * -0.7213475204444817)
    poly = t * (
        0.127414796 + t * (-0.142248368 + t * (0.7107068705 + t * (-0.7265760135 + t * 0.5307027145)))
    )
    tail = poly * gauss
    cdf = jnp.where(u >= 0, 1.0 - tail, tail)
    return u * cdf, cdf + (u * 0.3989422804014327) * gauss


def layers_kernel(
    micro_count,
    tokens, cotangent, lengths, spans,
    wq, wk, wv, wo, w1, w2, bias_in, up_bias_in, gains_in, shifts_in,
    act_out, dx_out, left_out, right_out, small_out,
    wq_s, wk_s, wv_s, wo_s, w1_s, w2_s,
    h_s, q_s, k_s, v_s, p_s, o_s, n_s, xa_s, xb_s, z_s, g_s, inva_s, invb_s,
    y_s, dy_s, df_s, da_s, do_s, dx_s, wide_s, turn_s, acc_s, accu_s,
    w_sem, in_sem, out_sem, turn_sem, fwd_send, fwd_recv, bwd_send, bwd_recv,
):
    section = lax.axis_index("section")
    other = 1 - section
    first = section == 0
    last = section == 1

    barrier = pltpu.get_barrier_semaphore()
    pl.semaphore_signal(barrier, inc=1, device_id={"section": other}, device_id_type=MESH)

    weight_pairs = ((wq, wq_s), (wk, wk_s), (wv, wv_s), (wo, wo_s), (w1, w1_s), (w2, w2_s))

    def weight_copy(index):
        source, target = weight_pairs[index]
        return pltpu.make_async_copy(source.at[0], target, w_sem.at[index])

    def rows_of(index):
        return pl.ds(pl.multiple_of(index * ROWS, ROWS), ROWS)

    def entry_copy(index):
        return pltpu.make_async_copy(tokens.at[rows_of(index)], h_s.at[rows_of(index)], in_sem.at[index])

    def cot_copy(index):
        return pltpu.make_async_copy(cotangent.at[rows_of(index)], dy_s.at[rows_of(index)], in_sem.at[index])

    def forward_send(index):
        return pltpu.make_async_remote_copy(
            src_ref=y_s.at[rows_of(index)],
            dst_ref=h_s.at[rows_of(index)],
            send_sem=fwd_send.at[index],
            recv_sem=fwd_recv.at[index],
            device_id={"section": other},
            device_id_type=MESH,
        )

    def backward_send(index):
        return pltpu.make_async_remote_copy(
            src_ref=y_s.at[rows_of(index)],
            dst_ref=dy_s.at[rows_of(index)],
            send_sem=bwd_send.at[index],
            recv_sem=bwd_recv.at[index],
            device_id={"section": other},
            device_id_type=MESH,
        )

    backward_outs = ((q_s, 0), (k_s, 1), (v_s, 2), (da_s, 3), (df_s, 8))

    def act_copy(index):
        return pltpu.make_async_copy(y_s.at[rows_of(index)], act_out.at[rows_of(index)], out_sem.at[0, index])

    def dx_copy(index):
        return pltpu.make_async_copy(dx_s.at[rows_of(index)], dx_out.at[rows_of(index)], out_sem.at[1, index])

    def right_copies(index):
        for slot, (source, place) in enumerate(backward_outs):
            yield pltpu.make_async_copy(
                source.at[rows_of(index)], right_out.at[place, rows_of(index)], out_sem.at[2 + slot, index]
            )
        for panel in range(FF // D):
            yield pltpu.make_async_copy(
                g_s.at[rows_of(index), pl.ds(panel * D, D)],
                right_out.at[4 + panel, rows_of(index)],
                out_sem.at[7 + panel, index],
            )

    def turn_copy(slot, row):
        return pltpu.make_async_copy(
            turn_s.at[slot], left_out.at[pl.ds(pl.multiple_of(row, 128), 128)], turn_sem.at[slot]
        )

    def transpose_all():
        done = 0
        for source, tiles in ((h_s, D // 128), (o_s, D // 128), (n_s, D // 128), (z_s, FF // 128)):

            def tile_step(tile, carry, source=source, done=done):
                number = tile + done
                slot = lax.rem(number, 2)

                @pl.when(number >= 2)
                def _():
                    turn_copy(slot, (number - 2) * 128).wait()

                turn_s[slot] = source[:, pl.ds(pl.multiple_of(tile * 128, 128), 128)].T
                turn_copy(slot, number * 128).start()
                return carry

            lax.fori_loop(0, tiles, tile_step, 0)
            done += tiles
        for number in (done - 2, done - 1):
            turn_copy(number % 2, number * 128).wait()

    @pl.when(first)
    def _():
        for index in range(micro_count):
            entry_copy(index).start()

    @pl.when(last)
    def _():
        for index in range(micro_count):
            cot_copy(index).start()

    for index in range(6):
        weight_copy(index).start()

    acc_s[...] = jnp.zeros_like(acc_s)
    accu_s[...] = jnp.zeros_like(accu_s)

    bias = bias_in[0].astype(F32)
    gains = gains_in[0].astype(F32)
    shifts = shifts_in[0].astype(F32)
    low_half = lax.broadcasted_iota(jnp.int32, (1, 8, 128), 2) < HEAD_DIM
    keep_low = jnp.where(lax.broadcasted_iota(jnp.int32, (1, 16, 128), 2) < HEAD_DIM, 1.0, 0.0)
    keep_high = (1.0 - keep_low).astype(BF16)
    keep_low = keep_low.astype(BF16)

    def stacked(pair_block):
        tiles = pair_block.reshape(-1, 16, 128)
        return jnp.concatenate([tiles * keep_low, tiles * keep_high], axis=0).reshape(2 * LENGTH, 128)

    def merged(tall):
        tiles = tall.reshape(2, LENGTH // 8, 8, 128)
        return jnp.where(low_half, tiles[0], tiles[1]).reshape(LENGTH, 128)

    pl.semaphore_wait(barrier, 1)

    def forward(index, carry):
        base = index * ROWS
        rows = rows_of(index)

        @pl.when(first)
        def _():
            entry_copy(index).wait()
            for chain in range(CHAINS_MB):
                number = index * CHAINS_MB + chain
                start, stop = spans[0, number], spans[1, number]
                spot = lax.broadcasted_iota(jnp.int32, (LENGTH, D), 0)
                here = pl.ds(pl.multiple_of(base + chain * LENGTH, LENGTH), LENGTH)
                keep = (spot < start) | (spot >= stop)
                h_s[here, :] = jnp.where(keep, h_s[here, :].astype(F32), 0.0).astype(BF16)

        @pl.when(last)
        def _():
            forward_send(index).wait_recv()

        @pl.when(index == 0)
        def _():
            for number in range(3):
                weight_copy(number).wait()

        for weight, bias_row, target in ((wq_s, 0, q_s), (wk_s, None, k_s), (wv_s, 1, v_s)):
            block = dot(h_s[rows, :], weight[...])
            if bias_row is not None:
                block = block + bias[bias_row : bias_row + 1]
            if target is q_s:
                block = block * 0.125
            target[rows, :] = block.astype(BF16)

        def chain_step(chain, carry):
            here = pl.ds(pl.multiple_of(base + chain * LENGTH, LENGTH), LENGTH)
            number = index * CHAINS_MB + chain
            spot = lax.broadcasted_iota(jnp.int32, (LENGTH - LEAST, 2 * LENGTH), 0) + LEAST
            penalty = jnp.where(spot < lengths[number], 0.0, -1000000000.0)
            lanes = [slice(pair * 128, pair * 128 + 128) for pair in range(PAIRS)]
            scores = [dot_t(k_s[here, lane], stacked(q_s[here, lane])) for lane in lanes]
            attends = []
            for pair in range(PAIRS):
                held = jnp.concatenate([scores[pair][:LEAST], scores[pair][LEAST:] + penalty], axis=0)
                raised = jnp.exp(held - jnp.max(held, axis=0, keepdims=True))
                attends.append((raised * (1.0 / jnp.sum(raised, axis=0, keepdims=True))).astype(BF16))
                p_s[number, pair] = attends[pair]
            mixes = [t_dot(attends[pair], v_s[here, lanes[pair]]) for pair in range(PAIRS)]
            for pair in range(PAIRS):
                o_s[here, lanes[pair]] = merged(mixes[pair]).astype(BF16)
            return carry

        lax.fori_loop(0, CHAINS_MB, chain_step, 0)

        @pl.when(index == 0)
        def _():
            weight_copy(3).wait()

        wide_s[...] = dot(o_s[rows, :], wo_s[...])

        def first_norm(step, carry):
            part = pl.ds(pl.multiple_of(step * SUB, SUB), SUB)
            here = pl.ds(pl.multiple_of(base + step * SUB, SUB), SUB)
            r = h_s[here, :].astype(F32) + wide_s[part, :] + bias[2:3]
            centered = r - jnp.mean(r, axis=-1, keepdims=True)
            inv = lax.rsqrt(jnp.mean(centered * centered, axis=-1, keepdims=True) + 1e-05)
            hat = centered * inv
            normed = hat * gains[0:1] + shifts[0:1]
            xa_s[here, :] = hat.astype(BF16)
            inva_s[here, :] = jnp.broadcast_to(inv, (SUB, 128))
            n_s[here, :] = normed.astype(BF16)
            wide_s[part, :] = normed
            return carry

        lax.fori_loop(0, ROWS // SUB, first_norm, 0, unroll=5)

        @pl.when(index == 0)
        def _():
            weight_copy(4).wait()
            weight_copy(5).wait()

        def lift(n0):
            return dot(n_s[rows, :], w1_s[:, n0 : n0 + WIDE])

        following = lift(0)
        for n0 in range(0, FF, WIDE):
            block = following
            if n0 + WIDE < FF:
                following = lift(n0 + WIDE)
            up_bias = up_bias_in[0:1, n0 : n0 + WIDE].astype(F32)
            for r0 in range(0, ROWS, SUB):
                here = pl.ds(pl.multiple_of(base + r0, SUB), SUB)
                act, slope = gelu_parts(block[r0 : r0 + SUB] + up_bias)
                z_s[here, n0 : n0 + WIDE] = act.astype(BF16)
                g_s[here, n0 : n0 + WIDE] = slope.astype(BF16)

        wide_s[...] += dot(z_s[rows, :], w2_s[...])

        def second_norm(step, carry):
            part = pl.ds(pl.multiple_of(step * SUB, SUB), SUB)
            here = pl.ds(pl.multiple_of(base + step * SUB, SUB), SUB)
            r = wide_s[part, :] + bias[3:4]
            centered = r - jnp.mean(r, axis=-1, keepdims=True)
            inv = lax.rsqrt(jnp.mean(centered * centered, axis=-1, keepdims=True) + 1e-05)
            hat = centered * inv
            xb_s[here, :] = hat.astype(BF16)
            invb_s[here, :] = jnp.broadcast_to(inv, (SUB, 128))
            y_s[here, :] = (hat * gains[1:2] + shifts[1:2]).astype(BF16)
            return carry

        lax.fori_loop(0, ROWS // SUB, second_norm, 0, unroll=5)

        @pl.when(first)
        def _():
            forward_send(index).start()

        act_copy(index).start()
        return carry

    lax.fori_loop(0, micro_count, forward, 0)

    def forward_done(index, carry):
        @pl.when(first)
        def _():
            forward_send(index).wait_send()

        act_copy(index).wait()
        return carry

    lax.fori_loop(0, micro_count, forward_done, 0)

    @pl.when(first)
    def _():
        transpose_all()

    def backward(index, carry):
        base = index * ROWS
        rows = rows_of(index)

        @pl.when(first)
        def _():
            backward_send(index).wait_recv()

        @pl.when(last)
        def _():
            cot_copy(index).wait()

        def second_back(step, carry):
            part = pl.ds(pl.multiple_of(step * SUB, SUB), SUB)
            here = pl.ds(pl.multiple_of(base + step * SUB, SUB), SUB)
            dy = dy_s[here, :].astype(F32)
            hat = xb_s[here, :].astype(F32)
            acc_s[9] += fold(dy * hat)
            acc_s[11] += fold(dy)
            scaled = dy * gains[1:2]
            mean_plain = jnp.mean(scaled, axis=-1, keepdims=True)
            mean_hat = jnp.mean(scaled * hat, axis=-1, keepdims=True)
            grad = (scaled - mean_plain - hat * mean_hat) * invb_s[here, 0:1]
            wide_s[part, :] = grad
            df_s[here, :] = grad.astype(BF16)
            acc_s[3] += fold(grad)
            return carry

        lax.fori_loop(0, ROWS // SUB, second_back, 0, unroll=5)

        def drop(n0):
            return dot_t(df_s[rows, :], w2_s[n0 : n0 + WIDE, :])

        following = drop(0)
        for n0 in range(0, FF, WIDE):
            block = following
            if n0 + WIDE < FF:
                following = drop(n0 + WIDE)
            sums = jnp.zeros((8, WIDE), F32)
            for r0 in range(0, ROWS, SUB):
                here = pl.ds(pl.multiple_of(base + r0, SUB), SUB)
                part = block[r0 : r0 + SUB] * g_s[here, n0 : n0 + WIDE].astype(F32)
                g_s[here, n0 : n0 + WIDE] = part.astype(BF16)
                sums = sums + fold(part)
            accu_s[:, n0 : n0 + WIDE] += sums

        wide_s[...] += dot_t(g_s[rows, :], w1_s[...])

        def first_back(step, carry):
            part = pl.ds(pl.multiple_of(step * SUB, SUB), SUB)
            here = pl.ds(pl.multiple_of(base + step * SUB, SUB), SUB)
            dn = wide_s[part, :]
            hat = xa_s[here, :].astype(F32)
            acc_s[8] += fold(dn * hat)
            acc_s[10] += fold(dn)
            scaled = dn * gains[0:1]
            mean_plain = jnp.mean(scaled, axis=-1, keepdims=True)
            mean_hat = jnp.mean(scaled * hat, axis=-1, keepdims=True)
            grad = (scaled - mean_plain - hat * mean_hat) * inva_s[here, 0:1]
            wide_s[part, :] = grad
            da_s[here, :] = grad.astype(BF16)
            acc_s[2] += fold(grad)
            return carry

        lax.fori_loop(0, ROWS // SUB, first_back, 0, unroll=5)

        do_s[...] = dot_t(da_s[rows, :], wo_s[...]).astype(BF16)

        def chain_step(chain, carry):
            here = pl.ds(pl.multiple_of(base + chain * LENGTH, LENGTH), LENGTH)
            near = pl.ds(pl.multiple_of(chain * LENGTH, LENGTH), LENGTH)
            number = index * CHAINS_MB + chain
            pairs = range(PAIRS)
            lanes = [slice(pair * 128, pair * 128 + 128) for pair in pairs]
            grad_talls = [stacked(do_s[near, lane]) for lane in lanes]
            grad_attends = [dot_t(v_s[here, lanes[pair]], grad_talls[pair]) for pair in pairs]
            dvs = [dot(p_s[number, pair], grad_talls[pair]) for pair in pairs]
            grad_scores = []
            for pair in pairs:
                attend = p_s[number, pair].astype(F32)
                weighted = attend * grad_attends[pair]
                delta = jnp.sum(weighted, axis=0, keepdims=True) / jnp.sum(attend, axis=0, keepdims=True)
                grad_scores.append((weighted - attend * delta).astype(BF16))
            dks = [dot(grad_scores[pair], stacked(q_s[here, lanes[pair]])) for pair in pairs]
            dqs = [t_dot(grad_scores[pair], k_s[here, lanes[pair]]) for pair in pairs]
            for pair in pairs:
                dq = merged(dqs[pair]) * 0.125
                q_s[here, lanes[pair]] = dq.astype(BF16)
                k_s[here, lanes[pair]] = dks[pair].astype(BF16)
                v_s[here, lanes[pair]] = dvs[pair].astype(BF16)
                acc_s[0, :, lanes[pair]] += fold(dq)
                acc_s[1, :, lanes[pair]] += fold(dvs[pair])
            return carry

        lax.fori_loop(0, CHAINS_MB, chain_step, 0)

        for source, weight in ((q_s, wq_s), (k_s, wk_s), (v_s, wv_s)):
            wide_s[...] += dot_t(source[rows, :], weight[...])

        @pl.when(last)
        def _():
            low = wide_s[...].astype(BF16)
            y_s[rows, :] = low
            dx_s[rows, :] = low.astype(F32)
            backward_send(index).start()

        @pl.when(first)
        def _():
            for chain in range(CHAINS_MB):
                number = index * CHAINS_MB + chain
                start, stop = spans[0, number], spans[1, number]
                spot = lax.broadcasted_iota(jnp.int32, (LENGTH, D), 0)
                here = pl.ds(pl.multiple_of(base + chain * LENGTH, LENGTH), LENGTH)
                keep = (spot < start) | (spot >= stop)
                dx_s[here, :] = jnp.where(keep, wide_s[chain * LENGTH : (chain + 1) * LENGTH, :], 0.0)

        dx_copy(index).start()
        for copy in right_copies(index):
            copy.start()
        return carry

    lax.fori_loop(0, micro_count, backward, 0)

    @pl.when(last)
    def _():
        transpose_all()

    for number in range(12):
        if 4 <= number < 8:
            panel = accu_s[:, (number - 4) * D : (number - 3) * D]
        else:
            panel = acc_s[number]
        small_out[number : number + 1, :] = jnp.sum(panel, axis=0, keepdims=True)
    small_out[12:16, :] = jnp.zeros((4, D), F32)

    def backward_done(index, carry):
        @pl.when(last)
        def _():
            backward_send(index).wait_send()

        dx_copy(index).wait()
        for copy in right_copies(index):
            copy.wait()
        return carry

    lax.fori_loop(0, micro_count, backward_done, 0)


def run_layers(tokens, cotangent, lengths, spans, *weights):
    rows = tokens.shape[0]
    micro_count = rows // ROWS
    chains = rows // LENGTH
    anywhere = pl.BlockSpec(memory_space=pl.ANY)
    scalars = pl.BlockSpec(memory_space=pltpu.SMEM)
    vectors = pl.BlockSpec(memory_space=pltpu.VMEM)
    out_shape = (
        jax.ShapeDtypeStruct((rows, D), BF16),
        jax.ShapeDtypeStruct((rows, D), F32),
        jax.ShapeDtypeStruct((3 * D + FF, rows), BF16),
        jax.ShapeDtypeStruct((9, rows, D), BF16),
        jax.ShapeDtypeStruct((16, D), F32),
    )

    def vm(count, width=D, dtype=BF16):
        return pltpu.VMEM((count, width), dtype)

    scratch = [
        vm(D), vm(D), vm(D), vm(D), vm(D, FF), vm(FF),
        vm(rows), vm(rows), vm(rows), vm(rows),
        pltpu.VMEM((chains, PAIRS, LENGTH, 2 * LENGTH), BF16),
        vm(rows), vm(rows), vm(rows), vm(rows), vm(rows, FF), vm(rows, FF),
        vm(rows, 128, F32), vm(rows, 128, F32),
        vm(rows), vm(rows), vm(rows), vm(rows), vm(ROWS), vm(rows, D, F32),
        vm(ROWS, D, F32), pltpu.VMEM((2, 128, rows), BF16), pltpu.VMEM((12, 8, D), F32), vm(8, FF, F32),
        pltpu.SemaphoreType.DMA((6,)),
        pltpu.SemaphoreType.DMA((micro_count,)),
        pltpu.SemaphoreType.DMA((11, micro_count)),
        pltpu.SemaphoreType.DMA((2,)),
        pltpu.SemaphoreType.DMA((micro_count,)),
        pltpu.SemaphoreType.DMA((micro_count,)),
        pltpu.SemaphoreType.DMA((micro_count,)),
        pltpu.SemaphoreType.DMA((micro_count,)),
    ]
    return pl.pallas_call(
        functools.partial(layers_kernel, micro_count),
        out_shape=out_shape,
        in_specs=[anywhere, anywhere, scalars, scalars] + [anywhere] * 6 + [vectors] * 4,
        out_specs=[anywhere] * 4 + [vectors],
        scratch_shapes=scratch,
        compiler_params=pltpu.CompilerParams(
            collective_id=0, has_side_effects=True, vmem_limit_bytes=60 * 1024 * 1024
        ),
        cost_estimate=pl.CostEstimate(
            flops=rows * 2 * 2 * 2 * 7077888, bytes_accessed=60000000, transcendentals=rows * FF * 2
        ),
    )(tokens, cotangent, lengths, spans.T, *weights)


RING = 8
PIECES = 3
PIECE = D // RING
PANELS = (
    (0, 0), (0, 1), (0, 2), (D, 3), (2 * D, 4), (2 * D, 5),
    (2 * D, 6), (2 * D, 7), (3 * D, 8), (4 * D, 8), (5 * D, 8), (6 * D, 8),
)


def sums_kernel(
    left, right, small_in, grads_out, small_out,
    left_s, right_s, total_s, give_s, take_s, ring_s, own_s,
    tiny_s, tiny_take_s, tiny_sum_s, tiny_go_s, tiny_ring_s, tiny_own_s,
    load_sem, give_sem, take_sem, ring_send, ring_recv, own_sem, round_send, round_recv, share_send, share_recv,
    tiny_sem, tiny_ring_send, tiny_ring_recv, tiny_round_send, tiny_round_recv,
):
    me = lax.axis_index("dp")
    core = lax.rem(me, 2)
    high = lax.rem(lax.div(me, 2), 2)
    depth = lax.div(me, 4)
    place = depth + high * (7 - 2 * depth)

    def device(spot, on_core):
        row = lax.div(spot, 4)
        return {"dp": 4 * (spot + row * (7 - 2 * spot)) + 2 * row + on_core}

    ahead = device(lax.rem(place + 1, RING), core)
    behind = device(lax.rem(place + RING - 1, RING), core)
    beside = device(place, 1 - core)
    targets = (ahead, behind)

    barrier = pltpu.get_barrier_semaphore()
    for peer in (ahead, behind, beside):
        pl.semaphore_signal(barrier, inc=1, device_id=peer, device_id_type=MESH)

    def block(way, step):
        return lax.rem(place - step + RING, RING) if way == 0 else lax.rem(place + step, RING)

    def late_block(way, step):
        return lax.rem(place + 1 - step + RING, RING) if way == 0 else lax.rem(place + RING - 1 + step, RING)

    def load_left(part):
        return pltpu.make_async_copy(left.at[pl.ds(part * D, D)], left_s.at[pl.ds(part * D, D)], load_sem.at[part])

    def load_right(part):
        return pltpu.make_async_copy(right.at[part], right_s.at[part], load_sem.at[7 + part])

    def remote(source, target, send, recv, peer):
        return pltpu.make_async_remote_copy(
            src_ref=source, dst_ref=target, send_sem=send, recv_sem=recv, device_id=peer, device_id_type=MESH
        )

    def give(way, step, piece):
        return remote(
            give_s.at[way, step, piece], take_s.at[way, step, piece],
            give_sem.at[way, step, piece], take_sem.at[way, step, piece], beside,
        )

    def ring_copy(way, step, piece):
        return remote(
            take_s.at[way, step, piece], ring_s.at[way, step, piece],
            ring_send.at[way, step, piece], ring_recv.at[way, step, piece], targets[way],
        )

    def region(way, spot, piece, on_core):
        rows = pl.ds(pl.multiple_of(spot * PIECE, PIECE), PIECE)
        return grads_out.at[6 * way + 3 * on_core + piece, rows]

    def own_copy(way, piece):
        return pltpu.make_async_copy(
            own_s.at[way, piece], region(way, late_block(way, 0), piece, core), own_sem.at[way, piece]
        )

    def round_copy(way, step, piece, source=None):
        target = region(way, late_block(way, step), piece, core)
        return remote(
            target if source is None else source, target,
            round_send.at[way, step, piece], round_recv.at[way, step, piece], targets[way],
        )

    def round_wait(way, step, piece):
        target = region(way, late_block(way, step + 1), piece, core)
        remote(
            target, target, round_send.at[way, step, piece], round_recv.at[way, step, piece], targets[way]
        ).wait_recv()

    def share_copy(way, step, piece, source=None):
        target = region(way, late_block(way, step), piece, core)
        return remote(
            target if source is None else source, target,
            share_send.at[way, step, piece], share_recv.at[way, step, piece], beside,
        )

    def share_wait(way, step, piece):
        target = region(way, late_block(way, step), piece, 1 - core)
        remote(
            target, target, share_send.at[way, step, piece], share_recv.at[way, step, piece], beside
        ).wait_recv()

    tiny_swap = remote(tiny_s, tiny_take_s, tiny_sem.at[0], tiny_sem.at[1], beside)

    def tiny_ring(step):
        return remote(
            tiny_go_s.at[step], tiny_ring_s.at[step], tiny_ring_send.at[step], tiny_ring_recv.at[step], ahead
        )

    def tiny_round(step):
        spot = late_block(0, step)
        return remote(
            tiny_own_s.at[spot], tiny_own_s.at[spot], tiny_round_send.at[step], tiny_round_recv.at[step], ahead
        )

    def tiny_round_wait(step):
        spot = late_block(0, step + 1)
        remote(
            tiny_own_s.at[spot], tiny_own_s.at[spot], tiny_round_send.at[step], tiny_round_recv.at[step], ahead
        ).wait_recv()

    loads = []
    for piece in range(PIECES):
        for way in range(2):
            for half in range(2):
                first_row, number = PANELS[6 * way + 3 * half + piece]
                for kind, part in ((load_right, number), (load_left, first_row // D)):
                    if (kind, part) not in [entry[:2] for entry in loads]:
                        loads.append((kind, part, way, piece))
    for kind, part, _, _ in loads:
        kind(part).start()

    for part in range(RING):
        if part * 128 < D:
            tiny_s[part] = small_in[:, part * 128 : part * 128 + 128]
        else:
            tiny_s[part] = jnp.zeros((16, 128), F32)

    pl.semaphore_wait(barrier, 3)
    tiny_swap.start()

    def product(group, way, piece, pick):
        near, far = PANELS[6 * way + piece], PANELS[6 * way + 3 + piece]
        first_row = near[0] + pick * (far[0] - near[0])
        number = near[1] + pick * (far[1] - near[1])
        blocks = []
        for step in (2 * group, 2 * group + 1):
            start = pl.multiple_of(first_row + block(way, step) * PIECE, PIECE)
            blocks.append(left_s[pl.ds(start, PIECE), :])
        return dot(jnp.concatenate(blocks, axis=0), right_s[number])

    def keep_product(group, way, piece, both):
        total_s[lax.rem(2 * group, 4), way, piece] = both[:PIECE]
        total_s[lax.rem(2 * group + 1, 4), way, piece] = both[PIECE:]

    def give_product(group, way, piece, both):
        give_s[way, 2 * group, piece] = both[:PIECE].astype(BF16)
        give_s[way, 2 * group + 1, piece] = both[PIECE:].astype(BF16)
        give(way, 2 * group, piece).start()
        give(way, 2 * group + 1, piece).start()

    def add_piece(step, way, piece, target):
        slot = lax.rem(step, 4)
        for r0 in range(0, PIECE, SUB):
            part = slice(r0, r0 + SUB)
            whole = total_s[slot, way, piece, part] + take_s[way, step, piece, part].astype(F32)
            target[part] = whole.astype(BF16)

    def reduce_step(step, carry):
        slot = lax.rem(step, 4)
        spot = block(0, step)

        @pl.when(step < RING - 1)
        def _():
            tiny_ring(step - 1).wait_recv()
            tiny_go_s[step] = tiny_sum_s[spot] + tiny_ring_s[step - 1]
            tiny_ring(step).start()

        @pl.when(step == RING - 1)
        def _():
            tiny_ring(step - 1).wait_recv()
            tiny_own_s[spot] = tiny_sum_s[spot] + tiny_ring_s[step - 1]
            tiny_round(0).start()

        for piece in range(PIECES):
            for way in range(2):
                give(way, step, piece).wait_recv()
                ring_copy(way, step - 1, piece).wait_recv()
                for r0 in range(0, PIECE, SUB):
                    part = slice(r0, r0 + SUB)
                    total_s[slot, way, piece, part] += ring_s[way, step - 1, piece, part].astype(F32)

                @pl.when(step < RING - 1)
                def _():
                    add_piece(step, way, piece, take_s.at[way, step, piece])
                    ring_copy(way, step, piece).start()

                @pl.when(step == RING - 1)
                def _():
                    add_piece(step, way, piece, own_s.at[way, piece])
                    round_copy(way, 0, piece, own_s.at[way, piece]).start()
                    share_copy(way, 0, piece, own_s.at[way, piece]).start()
                    own_copy(way, piece).start()

                @pl.when(step < RING - 2)
                def _():
                    odd = lax.rem(step, 2)
                    group = lax.div(step, 2) + 1
                    both = product(group, way, piece, odd * core + (1 - odd) * (1 - core))

                    @pl.when(odd == 1)
                    def _():
                        keep_product(group, way, piece, both)

                    @pl.when(odd == 0)
                    def _():
                        give_product(group, way, piece, both)

        return carry

    def first_piece(way, piece):
        give(way, 0, piece).wait_recv()
        add_piece(0, way, piece, take_s.at[way, 0, piece])
        ring_copy(way, 0, piece).start()

    order = [(way, piece) for piece in range(PIECES) for way in range(2)]
    for number, (way, piece) in enumerate(order):
        for kind, part, at_way, at_piece in loads:
            if (at_way, at_piece) == (way, piece):
                kind(part).wait()
        give_product(0, way, piece, product(0, way, piece, 1 - core))
        keep_product(0, way, piece, product(0, way, piece, core))
        if number > 0:
            first_piece(*order[number - 1])
    first_piece(*order[-1])
    for way, piece in order:
        give_product(1, way, piece, product(1, way, piece, 1 - core))
    tiny_swap.wait_recv()
    tiny_sum_s[...] = tiny_s[...] + tiny_take_s[...]
    tiny_go_s[0] = tiny_sum_s[block(0, 0)]
    tiny_ring(0).start()

    lax.fori_loop(1, RING, reduce_step, 0)

    def round_step(step, carry):
        tiny_round_wait(step - 1)

        @pl.when(step < RING - 1)
        def _():
            tiny_round(step).start()

        for piece in range(PIECES):
            for way in range(2):
                round_wait(way, step - 1, piece)

                @pl.when(step < RING - 1)
                def _():
                    round_copy(way, step, piece).start()

                share_copy(way, step, piece).start()
        return carry

    lax.fori_loop(1, RING, round_step, 0)

    for part in range(D // 128):
        small_out[:, part * 128 : part * 128 + 128] = tiny_own_s[part]
    tiny_swap.wait_send()

    def finish(step, carry):
        for way in range(2):
            for piece in range(PIECES):
                give(way, step, piece).wait_send()
                share_wait(way, step, piece)
                share_copy(way, step, piece).wait_send()

                @pl.when(step < RING - 1)
                def _():
                    ring_copy(way, step, piece).wait_send()
                    round_copy(way, step, piece).wait_send()

        @pl.when(step < RING - 1)
        def _():
            tiny_ring(step).wait_send()
            tiny_round(step).wait_send()

        return carry

    lax.fori_loop(0, RING, finish, 0)
    for way in range(2):
        for piece in range(PIECES):
            own_copy(way, piece).wait()


def run_sums(left, right, small):
    rows = right.shape[1]
    anywhere = pl.BlockSpec(memory_space=pl.ANY)
    vectors = pl.BlockSpec(memory_space=pltpu.VMEM)

    def pieces(*lead, dtype=BF16):
        return pltpu.VMEM((*lead, PIECE, D), dtype)

    dma = pltpu.SemaphoreType.DMA
    scratch = [
        pltpu.VMEM(left.shape, BF16), pltpu.VMEM(right.shape, BF16),
        pieces(4, 2, PIECES, dtype=F32), pieces(2, RING, PIECES), pieces(2, RING, PIECES),
        pieces(2, RING - 1, PIECES), pieces(2, PIECES),
        pltpu.VMEM((RING, 16, 128), F32), pltpu.VMEM((RING, 16, 128), F32), pltpu.VMEM((RING, 16, 128), F32),
        pltpu.VMEM((RING - 1, 16, 128), F32), pltpu.VMEM((RING - 1, 16, 128), F32), pltpu.VMEM((RING, 16, 128), F32),
        dma((16,)), dma((2, RING, PIECES)), dma((2, RING, PIECES)),
        dma((2, RING - 1, PIECES)), dma((2, RING - 1, PIECES)), dma((2, PIECES)),
        dma((2, RING - 1, PIECES)), dma((2, RING - 1, PIECES)), dma((2, RING, PIECES)), dma((2, RING, PIECES)),
        dma((2,)), dma((RING - 1,)), dma((RING - 1,)), dma((RING - 1,)), dma((RING - 1,)),
    ]
    return pl.pallas_call(
        sums_kernel,
        out_shape=(jax.ShapeDtypeStruct((12, D, D), BF16), jax.ShapeDtypeStruct((16, D), F32)),
        in_specs=[anywhere, anywhere, vectors],
        out_specs=[anywhere, vectors],
        scratch_shapes=scratch,
        compiler_params=pltpu.CompilerParams(
            collective_id=1, has_side_effects=True, vmem_limit_bytes=60 * 1024 * 1024
        ),
        cost_estimate=pl.CostEstimate(flops=rows * 2 * 7077888, bytes_accessed=70000000, transcendentals=0),
    )(left, right, small)


def plain_sums(left, right, small):
    panels = [dot(left[row : row + D], right[number]).astype(BF16) for row, number in PANELS]
    return lax.psum(jnp.stack(panels), "dp"), lax.psum(small, "dp")


SLOTS = 8
CUT = D // 2


def widen_kernel(
    act, dx, grads, small, act_out, dx_out, query_out, key_out, value_out, out_out, up_out, down_out,
    bias_out, up_bias_out, gain_out, shift_out, low_s, wide_s, act_s, dx_s, in_sem, out_sem, move_sem,
):
    moves_in = [
        pltpu.make_async_copy(act, act_s, move_sem.at[0]), pltpu.make_async_copy(dx, dx_s, move_sem.at[1])
    ]
    moves_out = [
        pltpu.make_async_copy(act_s, act_out.at[0], move_sem.at[0]),
        pltpu.make_async_copy(dx_s, dx_out.at[0], move_sem.at[1]),
    ]
    jobs = []
    for panel in range(12):
        for half in range(2):
            rows = pl.ds(half * CUT, CUT)
            if panel < 4:
                target = (query_out, key_out, value_out, out_out)[panel].at[0, rows]
            elif panel < 8:
                target = up_out.at[0, rows, pl.ds((panel - 4) * D, D)]
            else:
                target = down_out.at[0, pl.ds((panel - 8) * D + half * CUT, CUT)]
            jobs.append((grads.at[panel, rows], target))

    def fetch(number):
        return pltpu.make_async_copy(jobs[number][0], low_s.at[number % SLOTS], in_sem.at[number % SLOTS])

    def store(number):
        return pltpu.make_async_copy(wide_s.at[number % SLOTS], jobs[number][1], out_sem.at[number % SLOTS])

    for number in range(SLOTS):
        fetch(number).start()
    for move in moves_in:
        move.start()
    bias_out[0] = small[0:4]
    for panel in range(FF // D):
        up_bias_out[:, panel * D : (panel + 1) * D] = small[4 + panel : 5 + panel]
    gain_out[0] = small[8:10]
    shift_out[0] = small[10:12]
    for number in range(len(jobs)):
        slot = number % SLOTS
        fetch(number).wait()
        if number >= SLOTS:
            store(number - SLOTS).wait()

        def turn(step, carry):
            part = pl.ds(pl.multiple_of(step * SUB, SUB), SUB)
            wide_s[slot, part, :] = low_s[slot, part, :].astype(F32)
            return carry

        lax.fori_loop(0, CUT // SUB, turn, 0, unroll=4)
        store(number).start()
        if number == SLOTS:
            for move_in, move_out in zip(moves_in, moves_out):
                move_in.wait()
                move_out.start()
        if number + SLOTS < len(jobs):
            fetch(number + SLOTS).start()
    for number in range(len(jobs) - SLOTS, len(jobs)):
        store(number).wait()
    for move in moves_out:
        move.wait()


def widen(act, dx, grads, small):
    anywhere = pl.BlockSpec(memory_space=pl.ANY)
    vectors = pl.BlockSpec(memory_space=pltpu.VMEM)
    square = jax.ShapeDtypeStruct((1, D, D), F32)
    return pl.pallas_call(
        widen_kernel,
        out_shape=(
            jax.ShapeDtypeStruct((1, *act.shape), BF16), jax.ShapeDtypeStruct((1, *dx.shape), F32),
            square, square, square, square,
            jax.ShapeDtypeStruct((1, D, FF), F32), jax.ShapeDtypeStruct((1, FF, D), F32),
            jax.ShapeDtypeStruct((1, 4, D), F32), jax.ShapeDtypeStruct((1, FF), F32),
            jax.ShapeDtypeStruct((1, 2, D), F32), jax.ShapeDtypeStruct((1, 2, D), F32),
        ),
        in_specs=[anywhere, anywhere, anywhere, vectors],
        out_specs=[anywhere] * 8 + [vectors] * 4,
        scratch_shapes=[
            pltpu.VMEM((SLOTS, CUT, D), BF16), pltpu.VMEM((SLOTS, CUT, D), F32),
            pltpu.VMEM(act.shape, BF16), pltpu.VMEM(dx.shape, F32),
            pltpu.SemaphoreType.DMA((SLOTS,)), pltpu.SemaphoreType.DMA((SLOTS,)), pltpu.SemaphoreType.DMA((2,)),
        ],
        compiler_params=pltpu.CompilerParams(vmem_limit_bytes=60 * 1024 * 1024),
        cost_estimate=pl.CostEstimate(flops=7077888, bytes_accessed=42467328, transcendentals=0),
    )(act, dx, grads, small)


def per_device(grid, tokens, cotangent, lengths, spans, *weights):
    act, dx, left, right, small = run_layers(tokens, cotangent, lengths, spans, *weights)
    grads, small = (run_sums if grid else plain_sums)(left, right, small)
    return widen(act, dx, grads, small)


def solution(mesh):
    in_specs = (
        P("dp", None), P("dp", None), P("dp"), P("dp", None),
        P("section", None, None), P("section", None, None), P("section", None, None),
        P("section", None, None), P("section", None, None), P("section", None, None),
        P("section", None, None), P("section", None), P("section", None, None), P("section", None, None),
    )
    out_specs = (
        P("section", "dp", None), P("section", "dp", None),
        P("section", None, None), P("section", None, None), P("section", None, None),
        P("section", None, None), P("section", None, None), P("section", None, None),
        P("section", None, None), P("section", None), P("section", None, None), P("section", None, None),
    )
    part = functools.partial(per_device, mesh.shape["dp"] == 2 * RING)
    return jax.shard_map(part, mesh=mesh, in_specs=in_specs, out_specs=out_specs, check_vma=False)
```

```python
import functools

import jax
import jax.numpy as jnp
from jax import lax
from jax.experimental import pallas as pl
from jax.experimental.pallas import tpu as pltpu
from jax.sharding import PartitionSpec as P

D = 768
HEADS = 12
HEAD_DIM = 64
PAIRS = HEADS // 2
FF = 3072
LENGTH = 160
LEAST = 96
ROWS = LENGTH
SUB = 32
WIDE = 512
PART = 256

F32 = jnp.float32
BF16 = jnp.bfloat16
MESH = pl.DeviceIdType.MESH


def dot(left, right):
    return jnp.dot(left, right, preferred_element_type=F32)


def dot_t(left, right):
    return lax.dot_general(left, right, (((1,), (1,)), ((), ())), preferred_element_type=F32)


def t_dot(left, right):
    return lax.dot_general(left, right, (((0,), (0,)), ((), ())), preferred_element_type=F32)


def fold(block):
    return jnp.sum(block.reshape(-1, 8, block.shape[-1]), axis=0)


def gelu_parts(u):
    t = pl.reciprocal(1.0 + 0.23164189 * jnp.abs(u), approx=True)
    gauss = jnp.exp2(u * u * -0.7213475204444817)
    poly = t * (
        0.127414796 + t * (-0.142248368 + t * (0.7107068705 + t * (-0.7265760135 + t * 0.5307027145)))
    )
    tail = poly * gauss
    cdf = jnp.where(u >= 0, 1.0 - tail, tail)
    return u * cdf, cdf + (u * 0.3989422804014327) * gauss


def layers_kernel(
    micro_count,
    tokens, cotangent, lengths, spans,
    wq, wk, wv, wo, w1, w2, bias_in, up_bias_in, gains_in, shifts_in,
    act_out, dx_out, left_out, right_out, small_out,
    wq_s, wk_s, wv_s, wo_s, w1_s, w2_s,
    h_s, q_s, k_s, v_s, p_s, o_s, n_s, xa_s, xb_s, z_s, g_s, inva_s, invb_s,
    y_s, dy_s, df_s, da_s, dx_s, wide_s, turn_s, acc_s, accu_s,
    w_sem, in_sem, out_sem, turn_sem, fwd_send, fwd_recv, bwd_send, bwd_recv,
):
    section = lax.axis_index("section")
    other = 1 - section
    first = section == 0
    last = section == 1

    barrier = pltpu.get_barrier_semaphore()
    pl.semaphore_signal(barrier, inc=1, device_id={"section": other}, device_id_type=MESH)

    weight_pairs = ((wq, wq_s), (wk, wk_s), (wv, wv_s), (wo, wo_s), (w1, w1_s), (w2, w2_s))

    def weight_copy(index):
        source, target = weight_pairs[index]
        return pltpu.make_async_copy(source.at[0], target, w_sem.at[index])

    def rows_of(index):
        return pl.ds(pl.multiple_of(index * ROWS, ROWS), ROWS)

    def entry_copy(index):
        return pltpu.make_async_copy(tokens.at[rows_of(index)], h_s.at[rows_of(index)], in_sem.at[index])

    def cot_copy(index):
        return pltpu.make_async_copy(cotangent.at[rows_of(index)], dy_s.at[rows_of(index)], in_sem.at[index])

    def forward_send(index):
        return pltpu.make_async_remote_copy(
            src_ref=y_s.at[rows_of(index)],
            dst_ref=h_s.at[rows_of(index)],
            send_sem=fwd_send.at[index],
            recv_sem=fwd_recv.at[index],
            device_id={"section": other},
            device_id_type=MESH,
        )

    def backward_send(index):
        return pltpu.make_async_remote_copy(
            src_ref=y_s.at[rows_of(index)],
            dst_ref=dy_s.at[rows_of(index)],
            send_sem=bwd_send.at[index],
            recv_sem=bwd_recv.at[index],
            device_id={"section": other},
            device_id_type=MESH,
        )

    backward_outs = ((q_s, 0), (k_s, 1), (v_s, 2), (da_s, 3), (df_s, 8))

    def act_copy(index):
        return pltpu.make_async_copy(y_s.at[rows_of(index)], act_out.at[rows_of(index)], out_sem.at[0, index])

    def dx_copy(index):
        return pltpu.make_async_copy(dx_s.at[rows_of(index)], dx_out.at[rows_of(index)], out_sem.at[1, index])

    def right_copies(index):
        for slot, (source, place) in enumerate(backward_outs):
            yield pltpu.make_async_copy(
                source.at[rows_of(index)], right_out.at[place, rows_of(index)], out_sem.at[2 + slot, index]
            )
        for panel in range(FF // D):
            yield pltpu.make_async_copy(
                g_s.at[rows_of(index), pl.ds(panel * D, D)],
                right_out.at[4 + panel, rows_of(index)],
                out_sem.at[7 + panel, index],
            )

    def turn_copy(slot, row):
        return pltpu.make_async_copy(
            turn_s.at[slot], left_out.at[pl.ds(pl.multiple_of(row, 128), 128)], turn_sem.at[slot]
        )

    def transpose_all():
        done = 0
        for source, tiles in ((h_s, D // 128), (o_s, D // 128), (n_s, D // 128), (z_s, FF // 128)):

            def tile_step(tile, carry, source=source, done=done):
                number = tile + done
                slot = lax.rem(number, 2)

                @pl.when(number >= 2)
                def _():
                    turn_copy(slot, (number - 2) * 128).wait()

                turn_s[slot] = source[:, pl.ds(pl.multiple_of(tile * 128, 128), 128)].T
                turn_copy(slot, number * 128).start()
                return carry

            lax.fori_loop(0, tiles, tile_step, 0)
            done += tiles
        for number in (done - 2, done - 1):
            turn_copy(number % 2, number * 128).wait()

    @pl.when(first)
    def _():
        for index in range(micro_count):
            entry_copy(index).start()

    @pl.when(last)
    def _():
        for index in range(micro_count):
            cot_copy(index).start()

    for index in range(6):
        weight_copy(index).start()

    acc_s[...] = jnp.zeros_like(acc_s)
    accu_s[...] = jnp.zeros_like(accu_s)

    bias = bias_in[0].astype(F32)
    gains = gains_in[0].astype(F32)
    shifts = shifts_in[0].astype(F32)
    low_half = lax.broadcasted_iota(jnp.int32, (1, 8, 128), 2) < HEAD_DIM
    keep_low = jnp.where(lax.broadcasted_iota(jnp.int32, (1, 16, 128), 2) < HEAD_DIM, 1.0, 0.0)
    keep_high = (1.0 - keep_low).astype(BF16)
    keep_low = keep_low.astype(BF16)

    def stacked(pair_block):
        tiles = pair_block.reshape(-1, 16, 128)
        return jnp.concatenate([tiles * keep_low, tiles * keep_high], axis=0).reshape(2 * LENGTH, 128)

    def merged(tall):
        tiles = tall.reshape(2, LENGTH // 8, 8, 128)
        return jnp.where(low_half, tiles[0], tiles[1]).reshape(LENGTH, 128)

    pl.semaphore_wait(barrier, 1)

    blocks = [slice(r0, r0 + SUB) for r0 in range(0, ROWS, SUB)]
    columns = [slice(c0, c0 + PART) for c0 in range(0, D, PART)]
    panels = [slice(n0, n0 + WIDE) for n0 in range(0, FF, WIDE)]
    halves = [slice(0, 128), slice(128, 256)]
    count, chunks = len(columns), len(panels)

    def forward(index, carry):
        base = index * ROWS
        rows = rows_of(index)

        def at(block):
            return pl.ds(pl.multiple_of(base + block.start, SUB), SUB)

        @pl.when(first)
        def _():
            entry_copy(index).wait()
            start, stop = spans[0, index], spans[1, index]
            spot = lax.broadcasted_iota(jnp.int32, (LENGTH, D), 0)
            keep = (spot < start) | (spot >= stop)
            h_s[rows, :] = jnp.where(keep, h_s[rows, :].astype(F32), 0.0).astype(BF16)

        @pl.when(last)
        def _():
            forward_send(index).wait_recv()

        @pl.when(index == 0)
        def _():
            for number in range(4):
                weight_copy(number).wait()

        hidden = h_s[rows, :]

        def project(column):
            query = ((dot(hidden, wq_s[:, column]) + bias[0:1, column]) * 0.125).astype(BF16)
            key_rows = dot(hidden, wk_s[:, column]).astype(BF16)
            value = (dot(hidden, wv_s[:, column]) + bias[1:2, column]).astype(BF16)
            q_s[rows, column] = query
            k_s[rows, column] = key_rows
            v_s[rows, column] = value
            return query, key_rows, value

        spot = lax.broadcasted_iota(jnp.int32, (LENGTH - LEAST, 2 * LENGTH), 0) + LEAST
        penalty = jnp.where(spot < lengths[index], 0.0, -1000000000.0)
        projected, attends = {}, {}
        attended = None
        for step in range(count + 2):
            if step < count:
                projected[step] = project(columns[step])
            spot = step - 1
            if 0 <= spot < count:
                query, key_rows, _ = projected[spot]
                scores = [dot_t(key_rows[:, half], stacked(query[:, half])) for half in halves]
                held = [
                    jnp.concatenate([score[:LEAST], score[LEAST:] + penalty], axis=0) for score in scores
                ]
                raised = [jnp.exp(score - jnp.max(score, axis=0, keepdims=True)) for score in held]
                attends[spot] = [
                    (part * (1.0 / jnp.sum(part, axis=0, keepdims=True))).astype(BF16) for part in raised
                ]
                for half in range(2):
                    p_s[index, 2 * spot + half] = attends[spot][half]
            spot = step - 2
            if 0 <= spot:
                value = projected[spot][2]
                mixes = [t_dot(attends[spot][half], value[:, halves[half]]) for half in range(2)]
                mixture = jnp.concatenate([merged(mix).astype(BF16) for mix in mixes], axis=1)
                o_s[rows, columns[spot]] = mixture
                product = dot(mixture, wo_s[columns[spot], :])
                attended = product if attended is None else attended + product

        for block in blocks:
            r = h_s[at(block), :].astype(F32) + attended[block] + bias[2:3]
            centered = r - jnp.mean(r, axis=-1, keepdims=True)
            inv = lax.rsqrt(jnp.mean(centered * centered, axis=-1, keepdims=True) + 1e-05)
            hat = centered * inv
            normed = hat * gains[0:1] + shifts[0:1]
            xa_s[at(block), :] = hat.astype(BF16)
            inva_s[at(block), :] = jnp.broadcast_to(inv, (SUB, 128))
            n_s[at(block), :] = normed.astype(BF16)
            wide_s[block, :] = normed

        @pl.when(index == 0)
        def _():
            weight_copy(4).wait()
            weight_copy(5).wait()

        normed_low = n_s[rows, :]
        lifted = {}
        outer = None
        for step in range(chunks + 2):
            if step < chunks:
                lifted[step] = dot(normed_low, w1_s[:, panels[step]])
            spot = step - 1
            if 0 <= spot < chunks:
                up_bias = up_bias_in[0:1, panels[spot]].astype(F32)
                for block in blocks:
                    act, slope = gelu_parts(lifted[spot][block] + up_bias)
                    z_s[at(block), panels[spot]] = act.astype(BF16)
                    g_s[at(block), panels[spot]] = slope.astype(BF16)
            spot = step - 2
            if 0 <= spot:
                product = dot(z_s[rows, panels[spot]], w2_s[panels[spot], :])
                outer = product if outer is None else outer + product

        for block in blocks:
            r = wide_s[block, :] + outer[block] + bias[3:4]
            centered = r - jnp.mean(r, axis=-1, keepdims=True)
            inv = lax.rsqrt(jnp.mean(centered * centered, axis=-1, keepdims=True) + 1e-05)
            hat = centered * inv
            xb_s[at(block), :] = hat.astype(BF16)
            invb_s[at(block), :] = jnp.broadcast_to(inv, (SUB, 128))
            y_s[at(block), :] = (hat * gains[1:2] + shifts[1:2]).astype(BF16)

        @pl.when(first)
        def _():
            forward_send(index).start()

        act_copy(index).start()
        return carry

    lax.fori_loop(0, micro_count, forward, 0)

    def forward_done(index, carry):
        @pl.when(first)
        def _():
            forward_send(index).wait_send()

        act_copy(index).wait()
        return carry

    lax.fori_loop(0, micro_count, forward_done, 0)

    @pl.when(first)
    def _():
        transpose_all()

    def backward(index, carry):
        base = index * ROWS
        rows = rows_of(index)

        def at(block):
            return pl.ds(pl.multiple_of(base + block.start, SUB), SUB)

        @pl.when(first)
        def _():
            backward_send(index).wait_recv()

        @pl.when(last)
        def _():
            cot_copy(index).wait()

        for block in blocks:
            dy = dy_s[at(block), :].astype(F32)
            hat = xb_s[at(block), :].astype(F32)
            acc_s[9] += fold(dy * hat)
            acc_s[11] += fold(dy)
            scaled = dy * gains[1:2]
            mean_plain = jnp.mean(scaled, axis=-1, keepdims=True)
            mean_hat = jnp.mean(scaled * hat, axis=-1, keepdims=True)
            grad = (scaled - mean_plain - hat * mean_hat) * invb_s[at(block), 0:1]
            wide_s[block, :] = grad
            df_s[at(block), :] = grad.astype(BF16)
            acc_s[3] += fold(grad)

        outer_low = df_s[rows, :]
        dropped = {}
        total = None
        for step in range(chunks + 2):
            if step < chunks:
                dropped[step] = dot_t(outer_low, w2_s[panels[step], :])
            spot = step - 1
            if 0 <= spot < chunks:
                sums = jnp.zeros((8, WIDE), F32)
                for block in blocks:
                    part = dropped[spot][block] * g_s[at(block), panels[spot]].astype(F32)
                    g_s[at(block), panels[spot]] = part.astype(BF16)
                    sums = sums + fold(part)
                accu_s[:, panels[spot]] += sums
            spot = step - 2
            if 0 <= spot:
                product = dot_t(g_s[rows, panels[spot]], w1_s[:, panels[spot]])
                total = product if total is None else total + product

        for block in blocks:
            dn = wide_s[block, :] + total[block]
            hat = xa_s[at(block), :].astype(F32)
            acc_s[8] += fold(dn * hat)
            acc_s[10] += fold(dn)
            scaled = dn * gains[0:1]
            mean_plain = jnp.mean(scaled, axis=-1, keepdims=True)
            mean_hat = jnp.mean(scaled * hat, axis=-1, keepdims=True)
            grad = (scaled - mean_plain - hat * mean_hat) * inva_s[at(block), 0:1]
            wide_s[block, :] = grad
            da_s[at(block), :] = grad.astype(BF16)
            acc_s[2] += fold(grad)

        attended_low = da_s[rows, :]
        mixed, scored, values_back = {}, {}, {}
        total = None
        for step in range(count + 2):
            if step < count:
                mixed[step] = dot_t(attended_low, wo_s[columns[step], :]).astype(BF16)
            spot = step - 1
            if 0 <= spot < count:
                value = v_s[rows, columns[spot]]
                talls = [stacked(mixed[spot][:, half]) for half in halves]
                grad_attends = [dot_t(value[:, halves[half]], talls[half]) for half in range(2)]
                values_back[spot] = [dot(p_s[index, 2 * spot + half], talls[half]) for half in range(2)]
                scored[spot] = []
                for half in range(2):
                    attend = p_s[index, 2 * spot + half].astype(F32)
                    weighted = attend * grad_attends[half]
                    delta = jnp.sum(weighted, axis=0, keepdims=True) / jnp.sum(attend, axis=0, keepdims=True)
                    scored[spot].append((weighted - attend * delta).astype(BF16))
            spot = step - 2
            if 0 <= spot:
                column = columns[spot]
                query, key_rows = q_s[rows, column], k_s[rows, column]
                dk = [dot(scored[spot][half], stacked(query[:, halves[half]])) for half in range(2)]
                dq = [merged(t_dot(scored[spot][half], key_rows[:, halves[half]])) for half in range(2)]
                dq, dk = jnp.concatenate(dq, axis=1) * 0.125, jnp.concatenate(dk, axis=1)
                dv = jnp.concatenate(values_back[spot], axis=1)
                acc_s[0, :, column] += fold(dq)
                acc_s[1, :, column] += fold(dv)
                dq, dk, dv = dq.astype(BF16), dk.astype(BF16), dv.astype(BF16)
                q_s[rows, column] = dq
                k_s[rows, column] = dk
                v_s[rows, column] = dv
                for grad, weight in ((dq, wq_s), (dk, wk_s), (dv, wv_s)):
                    product = dot_t(grad, weight[:, column])
                    total = product if total is None else total + product

        @pl.when(last)
        def _():
            low = (wide_s[...] + total).astype(BF16)
            y_s[rows, :] = low
            dx_s[rows, :] = low.astype(F32)
            backward_send(index).start()

        @pl.when(first)
        def _():
            start, stop = spans[0, index], spans[1, index]
            spot = lax.broadcasted_iota(jnp.int32, (LENGTH, D), 0)
            keep = (spot < start) | (spot >= stop)
            dx_s[rows, :] = jnp.where(keep, wide_s[...] + total, 0.0)

        dx_copy(index).start()
        for copy in right_copies(index):
            copy.start()
        return carry

    lax.fori_loop(0, micro_count, backward, 0)

    @pl.when(last)
    def _():
        transpose_all()

    for number in range(12):
        if 4 <= number < 8:
            panel = accu_s[:, (number - 4) * D : (number - 3) * D]
        else:
            panel = acc_s[number]
        small_out[number : number + 1, :] = jnp.sum(panel, axis=0, keepdims=True)
    small_out[12:16, :] = jnp.zeros((4, D), F32)

    def backward_done(index, carry):
        @pl.when(last)
        def _():
            backward_send(index).wait_send()

        dx_copy(index).wait()
        for copy in right_copies(index):
            copy.wait()
        return carry

    lax.fori_loop(0, micro_count, backward_done, 0)


def run_layers(tokens, cotangent, lengths, spans, *weights):
    rows = tokens.shape[0]
    micro_count = rows // ROWS
    anywhere = pl.BlockSpec(memory_space=pl.ANY)
    scalars = pl.BlockSpec(memory_space=pltpu.SMEM)
    vectors = pl.BlockSpec(memory_space=pltpu.VMEM)
    out_shape = (
        jax.ShapeDtypeStruct((rows, D), BF16),
        jax.ShapeDtypeStruct((rows, D), F32),
        jax.ShapeDtypeStruct((3 * D + FF, rows), BF16),
        jax.ShapeDtypeStruct((9, rows, D), BF16),
        jax.ShapeDtypeStruct((16, D), F32),
    )

    def vm(count, width=D, dtype=BF16):
        return pltpu.VMEM((count, width), dtype)

    scratch = [
        vm(D), vm(D), vm(D), vm(D), vm(D, FF), vm(FF),
        vm(rows), vm(rows), vm(rows), vm(rows),
        pltpu.VMEM((micro_count, PAIRS, LENGTH, 2 * LENGTH), BF16),
        vm(rows), vm(rows), vm(rows), vm(rows), vm(rows, FF), vm(rows, FF),
        vm(rows, 128, F32), vm(rows, 128, F32),
        vm(rows), vm(rows), vm(rows), vm(rows), vm(rows, D, F32),
        vm(ROWS, D, F32), pltpu.VMEM((2, 128, rows), BF16), pltpu.VMEM((12, 8, D), F32), vm(8, FF, F32),
        pltpu.SemaphoreType.DMA((6,)),
        pltpu.SemaphoreType.DMA((micro_count,)),
        pltpu.SemaphoreType.DMA((11, micro_count)),
        pltpu.SemaphoreType.DMA((2,)),
        pltpu.SemaphoreType.DMA((micro_count,)),
        pltpu.SemaphoreType.DMA((micro_count,)),
        pltpu.SemaphoreType.DMA((micro_count,)),
        pltpu.SemaphoreType.DMA((micro_count,)),
    ]
    return pl.pallas_call(
        functools.partial(layers_kernel, micro_count),
        out_shape=out_shape,
        in_specs=[anywhere, anywhere, scalars, scalars] + [anywhere] * 6 + [vectors] * 4,
        out_specs=[anywhere] * 4 + [vectors],
        scratch_shapes=scratch,
        compiler_params=pltpu.CompilerParams(
            collective_id=0, has_side_effects=True, vmem_limit_bytes=60 * 1024 * 1024
        ),
        cost_estimate=pl.CostEstimate(
            flops=rows * 2 * 2 * 2 * 7077888, bytes_accessed=60000000, transcendentals=rows * FF * 2
        ),
    )(tokens, cotangent, lengths, spans.T, *weights)


RING = 8
PIECES = 3
PIECE = D // RING
PANELS = (
    (0, 0), (0, 1), (0, 2), (D, 3), (2 * D, 4), (2 * D, 5),
    (2 * D, 6), (2 * D, 7), (3 * D, 8), (4 * D, 8), (5 * D, 8), (6 * D, 8),
)


def sums_kernel(
    left, right, small_in, grads_out, small_out,
    left_s, right_s, total_s, give_s, take_s, ring_s, own_s,
    tiny_s, tiny_take_s, tiny_sum_s, tiny_go_s, tiny_ring_s, tiny_own_s,
    load_sem, give_sem, take_sem, ring_send, ring_recv, own_sem, round_send, round_recv, share_send, share_recv,
    tiny_sem, tiny_ring_send, tiny_ring_recv, tiny_round_send, tiny_round_recv,
):
    me = lax.axis_index("dp")
    core = lax.rem(me, 2)
    high = lax.rem(lax.div(me, 2), 2)
    depth = lax.div(me, 4)
    place = depth + high * (7 - 2 * depth)

    def device(spot, on_core):
        row = lax.div(spot, 4)
        return {"dp": 4 * (spot + row * (7 - 2 * spot)) + 2 * row + on_core}

    ahead = device(lax.rem(place + 1, RING), core)
    behind = device(lax.rem(place + RING - 1, RING), core)
    beside = device(place, 1 - core)
    targets = (ahead, behind)

    barrier = pltpu.get_barrier_semaphore()
    for peer in (ahead, behind, beside):
        pl.semaphore_signal(barrier, inc=1, device_id=peer, device_id_type=MESH)

    def block(way, step):
        return lax.rem(place - step + RING, RING) if way == 0 else lax.rem(place + step, RING)

    def late_block(way, step):
        return lax.rem(place + 1 - step + RING, RING) if way == 0 else lax.rem(place + RING - 1 + step, RING)

    def load_left(part):
        return pltpu.make_async_copy(left.at[pl.ds(part * D, D)], left_s.at[pl.ds(part * D, D)], load_sem.at[part])

    def load_right(part):
        return pltpu.make_async_copy(right.at[part], right_s.at[part], load_sem.at[7 + part])

    def remote(source, target, send, recv, peer):
        return pltpu.make_async_remote_copy(
            src_ref=source, dst_ref=target, send_sem=send, recv_sem=recv, device_id=peer, device_id_type=MESH
        )

    def give(way, step, piece):
        return remote(
            give_s.at[way, step, piece], take_s.at[way, step, piece],
            give_sem.at[way, step, piece], take_sem.at[way, step, piece], beside,
        )

    def ring_copy(way, step, piece):
        return remote(
            take_s.at[way, step, piece], ring_s.at[way, step, piece],
            ring_send.at[way, step, piece], ring_recv.at[way, step, piece], targets[way],
        )

    def region(way, spot, piece, on_core):
        rows = pl.ds(pl.multiple_of(spot * PIECE, PIECE), PIECE)
        return grads_out.at[6 * way + 3 * on_core + piece, rows]

    def own_copy(way, piece):
        return pltpu.make_async_copy(
            own_s.at[way, piece], region(way, late_block(way, 0), piece, core), own_sem.at[way, piece]
        )

    def round_copy(way, step, piece, source=None):
        target = region(way, late_block(way, step), piece, core)
        return remote(
            target if source is None else source, target,
            round_send.at[way, step, piece], round_recv.at[way, step, piece], targets[way],
        )

    def round_wait(way, step, piece):
        target = region(way, late_block(way, step + 1), piece, core)
        remote(
            target, target, round_send.at[way, step, piece], round_recv.at[way, step, piece], targets[way]
        ).wait_recv()

    def share_copy(way, step, piece, source=None):
        target = region(way, late_block(way, step), piece, core)
        return remote(
            target if source is None else source, target,
            share_send.at[way, step, piece], share_recv.at[way, step, piece], beside,
        )

    def share_wait(way, step, piece):
        target = region(way, late_block(way, step), piece, 1 - core)
        remote(
            target, target, share_send.at[way, step, piece], share_recv.at[way, step, piece], beside
        ).wait_recv()

    tiny_swap = remote(tiny_s, tiny_take_s, tiny_sem.at[0], tiny_sem.at[1], beside)

    def tiny_ring(step):
        return remote(
            tiny_go_s.at[step], tiny_ring_s.at[step], tiny_ring_send.at[step], tiny_ring_recv.at[step], ahead
        )

    def tiny_round(step):
        spot = late_block(0, step)
        return remote(
            tiny_own_s.at[spot], tiny_own_s.at[spot], tiny_round_send.at[step], tiny_round_recv.at[step], ahead
        )

    def tiny_round_wait(step):
        spot = late_block(0, step + 1)
        remote(
            tiny_own_s.at[spot], tiny_own_s.at[spot], tiny_round_send.at[step], tiny_round_recv.at[step], ahead
        ).wait_recv()

    loads = []
    for piece in range(PIECES):
        for way in range(2):
            for half in range(2):
                first_row, number = PANELS[6 * way + 3 * half + piece]
                for kind, part in ((load_right, number), (load_left, first_row // D)):
                    if (kind, part) not in [entry[:2] for entry in loads]:
                        loads.append((kind, part, way, piece))
    for kind, part, _, _ in loads:
        kind(part).start()

    for part in range(RING):
        if part * 128 < D:
            tiny_s[part] = small_in[:, part * 128 : part * 128 + 128]
        else:
            tiny_s[part] = jnp.zeros((16, 128), F32)

    pl.semaphore_wait(barrier, 3)
    tiny_swap.start()

    def product(group, way, piece, pick):
        near, far = PANELS[6 * way + piece], PANELS[6 * way + 3 + piece]
        first_row = near[0] + pick * (far[0] - near[0])
        number = near[1] + pick * (far[1] - near[1])
        blocks = []
        for step in (2 * group, 2 * group + 1):
            start = pl.multiple_of(first_row + block(way, step) * PIECE, PIECE)
            blocks.append(left_s[pl.ds(start, PIECE), :])
        return dot(jnp.concatenate(blocks, axis=0), right_s[number])

    def keep_product(group, way, piece, both):
        total_s[lax.rem(2 * group, 4), way, piece] = both[:PIECE]
        total_s[lax.rem(2 * group + 1, 4), way, piece] = both[PIECE:]

    def give_product(group, way, piece, both):
        give_s[way, 2 * group, piece] = both[:PIECE].astype(BF16)
        give_s[way, 2 * group + 1, piece] = both[PIECE:].astype(BF16)
        give(way, 2 * group, piece).start()
        give(way, 2 * group + 1, piece).start()

    def add_piece(step, way, piece, target):
        slot = lax.rem(step, 4)
        for r0 in range(0, PIECE, SUB):
            part = slice(r0, r0 + SUB)
            whole = total_s[slot, way, piece, part] + take_s[way, step, piece, part].astype(F32)
            target[part] = whole.astype(BF16)

    def reduce_step(step, carry):
        slot = lax.rem(step, 4)
        spot = block(0, step)

        @pl.when(step < RING - 1)
        def _():
            tiny_ring(step - 1).wait_recv()
            tiny_go_s[step] = tiny_sum_s[spot] + tiny_ring_s[step - 1]
            tiny_ring(step).start()

        @pl.when(step == RING - 1)
        def _():
            tiny_ring(step - 1).wait_recv()
            tiny_own_s[spot] = tiny_sum_s[spot] + tiny_ring_s[step - 1]
            tiny_round(0).start()

        for piece in range(PIECES):
            for way in range(2):
                give(way, step, piece).wait_recv()
                ring_copy(way, step - 1, piece).wait_recv()
                for r0 in range(0, PIECE, SUB):
                    part = slice(r0, r0 + SUB)
                    total_s[slot, way, piece, part] += ring_s[way, step - 1, piece, part].astype(F32)

                @pl.when(step < RING - 1)
                def _():
                    add_piece(step, way, piece, take_s.at[way, step, piece])
                    ring_copy(way, step, piece).start()

                @pl.when(step == RING - 1)
                def _():
                    add_piece(step, way, piece, own_s.at[way, piece])
                    round_copy(way, 0, piece, own_s.at[way, piece]).start()
                    share_copy(way, 0, piece, own_s.at[way, piece]).start()
                    own_copy(way, piece).start()

                @pl.when(step < RING - 2)
                def _():
                    odd = lax.rem(step, 2)
                    group = lax.div(step, 2) + 1
                    both = product(group, way, piece, odd * core + (1 - odd) * (1 - core))

                    @pl.when(odd == 1)
                    def _():
                        keep_product(group, way, piece, both)

                    @pl.when(odd == 0)
                    def _():
                        give_product(group, way, piece, both)

        return carry

    def first_piece(way, piece):
        give(way, 0, piece).wait_recv()
        add_piece(0, way, piece, take_s.at[way, 0, piece])
        ring_copy(way, 0, piece).start()

    order = [(way, piece) for piece in range(PIECES) for way in range(2)]
    for number, (way, piece) in enumerate(order):
        for kind, part, at_way, at_piece in loads:
            if (at_way, at_piece) == (way, piece):
                kind(part).wait()
        give_product(0, way, piece, product(0, way, piece, 1 - core))
        keep_product(0, way, piece, product(0, way, piece, core))
        if number > 0:
            first_piece(*order[number - 1])
    first_piece(*order[-1])
    for way, piece in order:
        give_product(1, way, piece, product(1, way, piece, 1 - core))
    tiny_swap.wait_recv()
    tiny_sum_s[...] = tiny_s[...] + tiny_take_s[...]
    tiny_go_s[0] = tiny_sum_s[block(0, 0)]
    tiny_ring(0).start()

    lax.fori_loop(1, RING, reduce_step, 0)

    def round_step(step, carry):
        tiny_round_wait(step - 1)

        @pl.when(step < RING - 1)
        def _():
            tiny_round(step).start()

        for piece in range(PIECES):
            for way in range(2):
                round_wait(way, step - 1, piece)

                @pl.when(step < RING - 1)
                def _():
                    round_copy(way, step, piece).start()

                share_copy(way, step, piece).start()
        return carry

    lax.fori_loop(1, RING, round_step, 0)

    for part in range(D // 128):
        small_out[:, part * 128 : part * 128 + 128] = tiny_own_s[part]
    tiny_swap.wait_send()

    def finish(step, carry):
        for way in range(2):
            for piece in range(PIECES):
                give(way, step, piece).wait_send()
                share_wait(way, step, piece)
                share_copy(way, step, piece).wait_send()

                @pl.when(step < RING - 1)
                def _():
                    ring_copy(way, step, piece).wait_send()
                    round_copy(way, step, piece).wait_send()

        @pl.when(step < RING - 1)
        def _():
            tiny_ring(step).wait_send()
            tiny_round(step).wait_send()

        return carry

    lax.fori_loop(0, RING, finish, 0)
    for way in range(2):
        for piece in range(PIECES):
            own_copy(way, piece).wait()


def run_sums(left, right, small):
    rows = right.shape[1]
    anywhere = pl.BlockSpec(memory_space=pl.ANY)
    vectors = pl.BlockSpec(memory_space=pltpu.VMEM)

    def pieces(*lead, dtype=BF16):
        return pltpu.VMEM((*lead, PIECE, D), dtype)

    dma = pltpu.SemaphoreType.DMA
    scratch = [
        pltpu.VMEM(left.shape, BF16), pltpu.VMEM(right.shape, BF16),
        pieces(4, 2, PIECES, dtype=F32), pieces(2, RING, PIECES), pieces(2, RING, PIECES),
        pieces(2, RING - 1, PIECES), pieces(2, PIECES),
        pltpu.VMEM((RING, 16, 128), F32), pltpu.VMEM((RING, 16, 128), F32), pltpu.VMEM((RING, 16, 128), F32),
        pltpu.VMEM((RING - 1, 16, 128), F32), pltpu.VMEM((RING - 1, 16, 128), F32), pltpu.VMEM((RING, 16, 128), F32),
        dma((16,)), dma((2, RING, PIECES)), dma((2, RING, PIECES)),
        dma((2, RING - 1, PIECES)), dma((2, RING - 1, PIECES)), dma((2, PIECES)),
        dma((2, RING - 1, PIECES)), dma((2, RING - 1, PIECES)), dma((2, RING, PIECES)), dma((2, RING, PIECES)),
        dma((2,)), dma((RING - 1,)), dma((RING - 1,)), dma((RING - 1,)), dma((RING - 1,)),
    ]
    return pl.pallas_call(
        sums_kernel,
        out_shape=(jax.ShapeDtypeStruct((12, D, D), BF16), jax.ShapeDtypeStruct((16, D), F32)),
        in_specs=[anywhere, anywhere, vectors],
        out_specs=[anywhere, vectors],
        scratch_shapes=scratch,
        compiler_params=pltpu.CompilerParams(
            collective_id=1, has_side_effects=True, vmem_limit_bytes=60 * 1024 * 1024
        ),
        cost_estimate=pl.CostEstimate(flops=rows * 2 * 7077888, bytes_accessed=70000000, transcendentals=0),
    )(left, right, small)


def plain_sums(left, right, small):
    panels = [dot(left[row : row + D], right[number]).astype(BF16) for row, number in PANELS]
    return lax.psum(jnp.stack(panels), "dp"), lax.psum(small, "dp")


SLOTS = 8
CUT = D // 2


def widen_kernel(
    act, dx, grads, small, act_out, dx_out, query_out, key_out, value_out, out_out, up_out, down_out,
    bias_out, up_bias_out, gain_out, shift_out, low_s, wide_s, act_s, dx_s, in_sem, out_sem, move_sem,
):
    moves_in = [
        pltpu.make_async_copy(act, act_s, move_sem.at[0]), pltpu.make_async_copy(dx, dx_s, move_sem.at[1])
    ]
    moves_out = [
        pltpu.make_async_copy(act_s, act_out.at[0], move_sem.at[0]),
        pltpu.make_async_copy(dx_s, dx_out.at[0], move_sem.at[1]),
    ]
    jobs = []
    for panel in range(12):
        for half in range(2):
            rows = pl.ds(half * CUT, CUT)
            if panel < 4:
                target = (query_out, key_out, value_out, out_out)[panel].at[0, rows]
            elif panel < 8:
                target = up_out.at[0, rows, pl.ds((panel - 4) * D, D)]
            else:
                target = down_out.at[0, pl.ds((panel - 8) * D + half * CUT, CUT)]
            jobs.append((grads.at[panel, rows], target))

    def fetch(number):
        return pltpu.make_async_copy(jobs[number][0], low_s.at[number % SLOTS], in_sem.at[number % SLOTS])

    def store(number):
        return pltpu.make_async_copy(wide_s.at[number % SLOTS], jobs[number][1], out_sem.at[number % SLOTS])

    for number in range(SLOTS):
        fetch(number).start()
    for move in moves_in:
        move.start()
    bias_out[0] = small[0:4]
    for panel in range(FF // D):
        up_bias_out[:, panel * D : (panel + 1) * D] = small[4 + panel : 5 + panel]
    gain_out[0] = small[8:10]
    shift_out[0] = small[10:12]
    for number in range(len(jobs)):
        slot = number % SLOTS
        fetch(number).wait()
        if number >= SLOTS:
            store(number - SLOTS).wait()

        def turn(step, carry):
            part = pl.ds(pl.multiple_of(step * SUB, SUB), SUB)
            wide_s[slot, part, :] = low_s[slot, part, :].astype(F32)
            return carry

        lax.fori_loop(0, CUT // SUB, turn, 0, unroll=4)
        store(number).start()
        if number == SLOTS:
            for move_in, move_out in zip(moves_in, moves_out):
                move_in.wait()
                move_out.start()
        if number + SLOTS < len(jobs):
            fetch(number + SLOTS).start()
    for number in range(len(jobs) - SLOTS, len(jobs)):
        store(number).wait()
    for move in moves_out:
        move.wait()


def widen(act, dx, grads, small):
    anywhere = pl.BlockSpec(memory_space=pl.ANY)
    vectors = pl.BlockSpec(memory_space=pltpu.VMEM)
    square = jax.ShapeDtypeStruct((1, D, D), F32)
    return pl.pallas_call(
        widen_kernel,
        out_shape=(
            jax.ShapeDtypeStruct((1, *act.shape), BF16), jax.ShapeDtypeStruct((1, *dx.shape), F32),
            square, square, square, square,
            jax.ShapeDtypeStruct((1, D, FF), F32), jax.ShapeDtypeStruct((1, FF, D), F32),
            jax.ShapeDtypeStruct((1, 4, D), F32), jax.ShapeDtypeStruct((1, FF), F32),
            jax.ShapeDtypeStruct((1, 2, D), F32), jax.ShapeDtypeStruct((1, 2, D), F32),
        ),
        in_specs=[anywhere, anywhere, anywhere, vectors],
        out_specs=[anywhere] * 8 + [vectors] * 4,
        scratch_shapes=[
            pltpu.VMEM((SLOTS, CUT, D), BF16), pltpu.VMEM((SLOTS, CUT, D), F32),
            pltpu.VMEM(act.shape, BF16), pltpu.VMEM(dx.shape, F32),
            pltpu.SemaphoreType.DMA((SLOTS,)), pltpu.SemaphoreType.DMA((SLOTS,)), pltpu.SemaphoreType.DMA((2,)),
        ],
        compiler_params=pltpu.CompilerParams(vmem_limit_bytes=60 * 1024 * 1024),
        cost_estimate=pl.CostEstimate(flops=7077888, bytes_accessed=42467328, transcendentals=0),
    )(act, dx, grads, small)


def per_device(grid, tokens, cotangent, lengths, spans, *weights):
    act, dx, left, right, small = run_layers(tokens, cotangent, lengths, spans, *weights)
    grads, small = (run_sums if grid else plain_sums)(left, right, small)
    return widen(act, dx, grads, small)


def solution(mesh):
    in_specs = (
        P("dp", None), P("dp", None), P("dp"), P("dp", None),
        P("section", None, None), P("section", None, None), P("section", None, None),
        P("section", None, None), P("section", None, None), P("section", None, None),
        P("section", None, None), P("section", None), P("section", None, None), P("section", None, None),
    )
    out_specs = (
        P("section", "dp", None), P("section", "dp", None),
        P("section", None, None), P("section", None, None), P("section", None, None),
        P("section", None, None), P("section", None, None), P("section", None, None),
        P("section", None, None), P("section", None), P("section", None, None), P("section", None, None),
    )
    part = functools.partial(per_device, mesh.shape["dp"] == 2 * RING)
    return jax.shard_map(part, mesh=mesh, in_specs=in_specs, out_specs=out_specs, check_vma=False)
```

```python
import functools

import jax
import jax.numpy as jnp
from jax import lax
from jax.experimental import pallas as pl
from jax.experimental.pallas import tpu as pltpu
from jax.sharding import PartitionSpec as P

D = 768
HEADS = 12
HEAD_DIM = 64
PAIRS = HEADS // 2
FF = 3072
LENGTH = 160
LEAST = 96
ROWS = LENGTH
SUB = 32
WIDE = 768
TURN = 256
PART = 256

F32 = jnp.float32
BF16 = jnp.bfloat16
MESH = pl.DeviceIdType.MESH


def dot(left, right):
    return jnp.dot(left, right, preferred_element_type=F32)


def dot_t(left, right):
    return lax.dot_general(left, right, (((1,), (1,)), ((), ())), preferred_element_type=F32)


def t_dot(left, right):
    return lax.dot_general(left, right, (((0,), (0,)), ((), ())), preferred_element_type=F32)


def fold(block):
    return jnp.sum(block.reshape(-1, 8, block.shape[-1]), axis=0)


def gelu_parts(u):
    t = pl.reciprocal(1.0 + 0.23164189 * jnp.abs(u), approx=True)
    gauss = jnp.exp2(u * u * -0.7213475204444817)
    poly = t * (
        0.127414796 + t * (-0.142248368 + t * (0.7107068705 + t * (-0.7265760135 + t * 0.5307027145)))
    )
    tail = poly * gauss
    cdf = jnp.where(u >= 0, 1.0 - tail, tail)
    return u * cdf, cdf + (u * 0.3989422804014327) * gauss


def layers_kernel(
    micro_count,
    tokens, cotangent, lengths, spans,
    wq, wk, wv, wo, w1, w2, bias_in, up_bias_in, gains_in, shifts_in,
    act_out, dx_out, left_out, right_out, small_out,
    wx_s, wo_s, w1_s, w2_s,
    h_s, x_s, p_s, o_s, n_s, xa_s, xb_s, z_s, g_s, inva_s, invb_s,
    y_s, dy_s, df_s, da_s, dx_s, wide_s, turn_s, acc_s, accu_s,
    w_sem, in_sem, out_sem, turn_sem, fwd_send, fwd_recv, bwd_send, bwd_recv,
):
    section = lax.axis_index("section")
    other = 1 - section
    first = section == 0
    last = section == 1

    barrier = pltpu.get_barrier_semaphore()
    pl.semaphore_signal(barrier, inc=1, device_id={"section": other}, device_id_type=MESH)

    columns = [slice(c0, c0 + PART) for c0 in range(0, D, PART)]
    places = [slice(3 * c0, 3 * (c0 + PART)) for c0 in range(0, D, PART)]
    weight_copies = []
    for column, place in zip(columns, places):
        for number, source in enumerate((wq, wk, wv)):
            target = wx_s.at[:, pl.ds(place.start + number * PART, PART)]
            weight_copies.append((source.at[0, :, pl.ds(column.start, PART)], target))
    for source, target in ((wo, wo_s), (w1, w1_s), (w2, w2_s)):
        weight_copies.append((source.at[0], target))
    weight_copies = [
        pltpu.make_async_copy(source, target, w_sem.at[number])
        for number, (source, target) in enumerate(weight_copies)
    ]

    def rows_of(index):
        return pl.ds(pl.multiple_of(index * ROWS, ROWS), ROWS)

    def entry_copy(index):
        return pltpu.make_async_copy(tokens.at[rows_of(index)], h_s.at[rows_of(index)], in_sem.at[index])

    def cot_copy(index):
        return pltpu.make_async_copy(cotangent.at[rows_of(index)], dy_s.at[rows_of(index)], in_sem.at[index])

    def forward_send(index):
        return pltpu.make_async_remote_copy(
            src_ref=y_s.at[rows_of(index)],
            dst_ref=h_s.at[rows_of(index)],
            send_sem=fwd_send.at[index],
            recv_sem=fwd_recv.at[index],
            device_id={"section": other},
            device_id_type=MESH,
        )

    def backward_send(index):
        return pltpu.make_async_remote_copy(
            src_ref=y_s.at[rows_of(index)],
            dst_ref=dy_s.at[rows_of(index)],
            send_sem=bwd_send.at[index],
            recv_sem=bwd_recv.at[index],
            device_id={"section": other},
            device_id_type=MESH,
        )

    backward_outs = ((da_s, 3), (df_s, 8))

    def act_copy(index):
        return pltpu.make_async_copy(y_s.at[rows_of(index)], act_out.at[rows_of(index)], out_sem.at[0, index])

    def dx_copy(index):
        return pltpu.make_async_copy(dx_s.at[rows_of(index)], dx_out.at[rows_of(index)], out_sem.at[1, index])

    def right_copies(index):
        for slot, (source, place) in enumerate(backward_outs):
            yield pltpu.make_async_copy(
                source.at[rows_of(index)], right_out.at[place, rows_of(index)], out_sem.at[2 + slot, index]
            )
        for spot, (column, place) in enumerate(zip(columns, places)):
            for number in range(3):
                yield pltpu.make_async_copy(
                    x_s.at[rows_of(index), pl.ds(place.start + number * PART, PART)],
                    right_out.at[number, rows_of(index), pl.ds(column.start, PART)],
                    out_sem.at[8 + 3 * spot + number, index],
                )
        for panel in range(FF // D):
            yield pltpu.make_async_copy(
                g_s.at[rows_of(index), pl.ds(panel * D, D)],
                right_out.at[4 + panel, rows_of(index)],
                out_sem.at[4 + panel, index],
            )

    def turn_copy(slot, row):
        return pltpu.make_async_copy(
            turn_s.at[slot], left_out.at[pl.ds(pl.multiple_of(row, TURN), TURN)], turn_sem.at[slot]
        )

    def transpose_all():
        done = 0
        for source, tiles in ((h_s, D // TURN), (o_s, D // TURN), (n_s, D // TURN), (z_s, FF // TURN)):

            def tile_step(tile, carry, source=source, done=done):
                number = tile + done
                slot = lax.rem(number, 2)

                @pl.when(number >= 2)
                def _():
                    turn_copy(slot, (number - 2) * TURN).wait()

                turn_s[slot] = source[:, pl.ds(pl.multiple_of(tile * TURN, TURN), TURN)].T
                turn_copy(slot, number * TURN).start()
                return carry

            lax.fori_loop(0, tiles, tile_step, 0)
            done += tiles
        for number in (done - 2, done - 1):
            turn_copy(number % 2, number * TURN).wait()

    @pl.when(first)
    def _():
        for index in range(micro_count):
            entry_copy(index).start()

    @pl.when(last)
    def _():
        for index in range(micro_count):
            cot_copy(index).start()

    for copy in weight_copies:
        copy.start()

    acc_s[...] = jnp.zeros_like(acc_s)
    accu_s[...] = jnp.zeros_like(accu_s)

    bias = bias_in[0].astype(F32)
    gains = gains_in[0].astype(F32)
    shifts = shifts_in[0].astype(F32)
    low_half = lax.broadcasted_iota(jnp.int32, (1, 8, 128), 2) < HEAD_DIM
    keep_low = jnp.where(lax.broadcasted_iota(jnp.int32, (1, 16, 128), 2) < HEAD_DIM, 1.0, 0.0)
    keep_high = (1.0 - keep_low).astype(BF16)
    keep_low = keep_low.astype(BF16)

    def stacked(pair_block):
        tiles = pair_block.reshape(-1, 16, 128)
        return jnp.concatenate([tiles * keep_low, tiles * keep_high], axis=0).reshape(2 * LENGTH, 128)

    def merged(tall):
        tiles = tall.reshape(2, LENGTH // 8, 8, 128)
        return jnp.where(low_half, tiles[0], tiles[1]).reshape(LENGTH, 128)

    pl.semaphore_wait(barrier, 1)

    blocks = [slice(r0, r0 + SUB) for r0 in range(0, ROWS, SUB)]
    panels = [slice(n0, n0 + WIDE) for n0 in range(0, FF, WIDE)]
    halves = [slice(0, 128), slice(128, 256)]
    count, chunks = len(columns), len(panels)

    def forward(index, carry):
        base = index * ROWS
        rows = rows_of(index)

        def at(block):
            return pl.ds(pl.multiple_of(base + block.start, SUB), SUB)

        @pl.when(first)
        def _():
            entry_copy(index).wait()
            start, stop = spans[0, index], spans[1, index]
            spot = lax.broadcasted_iota(jnp.int32, (LENGTH, D), 0)
            keep = (spot < start) | (spot >= stop)
            h_s[rows, :] = jnp.where(keep, h_s[rows, :].astype(F32), 0.0).astype(BF16)

        @pl.when(last)
        def _():
            forward_send(index).wait_recv()

        @pl.when(index == 0)
        def _():
            for copy in weight_copies[:10]:
                copy.wait()

        hidden = h_s[rows, :]

        def project(spot):
            both = dot(hidden, wx_s[:, places[spot]])
            query = ((both[:, :PART] + bias[0:1, columns[spot]]) * 0.125).astype(BF16)
            key_rows = both[:, PART : 2 * PART].astype(BF16)
            value = (both[:, 2 * PART :] + bias[1:2, columns[spot]]).astype(BF16)
            x_s[rows, places[spot]] = jnp.concatenate([query, key_rows, value], axis=1)
            return query, key_rows, value

        spot = lax.broadcasted_iota(jnp.int32, (LENGTH - LEAST, 2 * LENGTH), 0) + LEAST
        penalty = jnp.where(spot < lengths[index], 0.0, -1000000000.0)
        projected, attends = {}, {}
        attended = None
        for step in range(count + 2):
            if step < count:
                projected[step] = project(step)
            spot = step - 1
            if 0 <= spot < count:
                query, key_rows, _ = projected[spot]
                scores = [dot_t(key_rows[:, half], stacked(query[:, half])) for half in halves]
                held = [
                    jnp.concatenate([score[:LEAST], score[LEAST:] + penalty], axis=0) for score in scores
                ]
                raised = [jnp.exp(score - jnp.max(score, axis=0, keepdims=True)) for score in held]
                attends[spot] = [
                    (part * (1.0 / jnp.sum(part, axis=0, keepdims=True))).astype(BF16) for part in raised
                ]
                for half in range(2):
                    p_s[index, 2 * spot + half] = attends[spot][half]
            spot = step - 2
            if 0 <= spot:
                value = projected[spot][2]
                mixes = [t_dot(attends[spot][half], value[:, halves[half]]) for half in range(2)]
                mixture = jnp.concatenate([merged(mix).astype(BF16) for mix in mixes], axis=1)
                o_s[rows, columns[spot]] = mixture
                product = dot(mixture, wo_s[columns[spot], :])
                attended = product if attended is None else attended + product

        for block in blocks:
            r = h_s[at(block), :].astype(F32) + attended[block] + bias[2:3]
            centered = r - jnp.mean(r, axis=-1, keepdims=True)
            inv = lax.rsqrt(jnp.mean(centered * centered, axis=-1, keepdims=True) + 1e-05)
            hat = centered * inv
            normed = hat * gains[0:1] + shifts[0:1]
            xa_s[at(block), :] = hat.astype(BF16)
            inva_s[at(block), :] = jnp.broadcast_to(inv, (SUB, 128))
            n_s[at(block), :] = normed.astype(BF16)
            wide_s[block, :] = normed

        @pl.when(index == 0)
        def _():
            for copy in weight_copies[10:]:
                copy.wait()

        normed_low = n_s[rows, :]
        lifted = {}
        outer = None
        for step in range(chunks + 2):
            if step < chunks:
                lifted[step] = dot(normed_low, w1_s[:, panels[step]])
            spot = step - 1
            if 0 <= spot < chunks:
                up_bias = up_bias_in[0:1, panels[spot]].astype(F32)
                for block in blocks:
                    act, slope = gelu_parts(lifted[spot][block] + up_bias)
                    z_s[at(block), panels[spot]] = act.astype(BF16)
                    g_s[at(block), panels[spot]] = slope.astype(BF16)
            spot = step - 2
            if 0 <= spot:
                product = dot(z_s[rows, panels[spot]], w2_s[panels[spot], :])
                outer = product if outer is None else outer + product

        for block in blocks:
            r = wide_s[block, :] + outer[block] + bias[3:4]
            centered = r - jnp.mean(r, axis=-1, keepdims=True)
            inv = lax.rsqrt(jnp.mean(centered * centered, axis=-1, keepdims=True) + 1e-05)
            hat = centered * inv
            xb_s[at(block), :] = hat.astype(BF16)
            invb_s[at(block), :] = jnp.broadcast_to(inv, (SUB, 128))
            y_s[at(block), :] = (hat * gains[1:2] + shifts[1:2]).astype(BF16)

        @pl.when(first)
        def _():
            forward_send(index).start()

        act_copy(index).start()
        return carry

    lax.fori_loop(0, micro_count, forward, 0)

    def forward_done(index, carry):
        @pl.when(first)
        def _():
            forward_send(index).wait_send()

        act_copy(index).wait()
        return carry

    lax.fori_loop(0, micro_count, forward_done, 0)

    @pl.when(first)
    def _():
        transpose_all()

    def backward(index, carry):
        base = index * ROWS
        rows = rows_of(index)

        def at(block):
            return pl.ds(pl.multiple_of(base + block.start, SUB), SUB)

        @pl.when(first)
        def _():
            backward_send(index).wait_recv()

        @pl.when(last)
        def _():
            cot_copy(index).wait()

        for block in blocks:
            dy = dy_s[at(block), :].astype(F32)
            hat = xb_s[at(block), :].astype(F32)
            acc_s[9] += fold(dy * hat)
            acc_s[11] += fold(dy)
            scaled = dy * gains[1:2]
            mean_plain = jnp.mean(scaled, axis=-1, keepdims=True)
            mean_hat = jnp.mean(scaled * hat, axis=-1, keepdims=True)
            grad = (scaled - mean_plain - hat * mean_hat) * invb_s[at(block), 0:1]
            wide_s[block, :] = grad
            df_s[at(block), :] = grad.astype(BF16)
            acc_s[3] += fold(grad)

        outer_low = df_s[rows, :]
        dropped = {}
        total = None
        for step in range(chunks + 2):
            if step < chunks:
                dropped[step] = dot_t(outer_low, w2_s[panels[step], :])
            spot = step - 1
            if 0 <= spot < chunks:
                sums = jnp.zeros((8, WIDE), F32)
                for block in blocks:
                    part = dropped[spot][block] * g_s[at(block), panels[spot]].astype(F32)
                    g_s[at(block), panels[spot]] = part.astype(BF16)
                    sums = sums + fold(part)
                accu_s[:, panels[spot]] += sums
            spot = step - 2
            if 0 <= spot:
                product = dot_t(g_s[rows, panels[spot]], w1_s[:, panels[spot]])
                total = product if total is None else total + product

        for block in blocks:
            dn = wide_s[block, :] + total[block]
            hat = xa_s[at(block), :].astype(F32)
            acc_s[8] += fold(dn * hat)
            acc_s[10] += fold(dn)
            scaled = dn * gains[0:1]
            mean_plain = jnp.mean(scaled, axis=-1, keepdims=True)
            mean_hat = jnp.mean(scaled * hat, axis=-1, keepdims=True)
            grad = (scaled - mean_plain - hat * mean_hat) * inva_s[at(block), 0:1]
            wide_s[block, :] = grad
            da_s[at(block), :] = grad.astype(BF16)
            acc_s[2] += fold(grad)

        attended_low = da_s[rows, :]
        mixed, scored, values_back = {}, {}, {}
        total = None
        for step in range(count + 2):
            if step < count:
                mixed[step] = dot_t(attended_low, wo_s[columns[step], :]).astype(BF16)
            spot = step - 1
            if 0 <= spot < count:
                value = x_s[rows, places[spot]][:, 2 * PART :]
                talls = [stacked(mixed[spot][:, half]) for half in halves]
                grad_attends = [dot_t(value[:, halves[half]], talls[half]) for half in range(2)]
                values_back[spot] = [dot(p_s[index, 2 * spot + half], talls[half]) for half in range(2)]
                scored[spot] = []
                for half in range(2):
                    attend = p_s[index, 2 * spot + half].astype(F32)
                    weighted = attend * grad_attends[half]
                    delta = jnp.sum(weighted, axis=0, keepdims=True) / jnp.sum(attend, axis=0, keepdims=True)
                    scored[spot].append((weighted - attend * delta).astype(BF16))
            spot = step - 2
            if 0 <= spot:
                column = columns[spot]
                whole = x_s[rows, places[spot]]
                query, key_rows = whole[:, :PART], whole[:, PART : 2 * PART]
                dk = [dot(scored[spot][half], stacked(query[:, halves[half]])) for half in range(2)]
                dq = [merged(t_dot(scored[spot][half], key_rows[:, halves[half]])) for half in range(2)]
                dq, dk = jnp.concatenate(dq, axis=1) * 0.125, jnp.concatenate(dk, axis=1)
                dv = jnp.concatenate(values_back[spot], axis=1)
                acc_s[0, :, column] += fold(dq)
                acc_s[1, :, column] += fold(dv)
                grads = jnp.concatenate([dq.astype(BF16), dk.astype(BF16), dv.astype(BF16)], axis=1)
                x_s[rows, places[spot]] = grads
                product = dot_t(grads, wx_s[:, places[spot]])
                total = product if total is None else total + product

        @pl.when(last)
        def _():
            low = (wide_s[...] + total).astype(BF16)
            y_s[rows, :] = low
            dx_s[rows, :] = low.astype(F32)
            backward_send(index).start()

        @pl.when(first)
        def _():
            start, stop = spans[0, index], spans[1, index]
            spot = lax.broadcasted_iota(jnp.int32, (LENGTH, D), 0)
            keep = (spot < start) | (spot >= stop)
            dx_s[rows, :] = jnp.where(keep, wide_s[...] + total, 0.0)

        dx_copy(index).start()
        for copy in right_copies(index):
            copy.start()
        return carry

    lax.fori_loop(0, micro_count, backward, 0)

    @pl.when(last)
    def _():
        transpose_all()

    for number in range(12):
        if 4 <= number < 8:
            panel = accu_s[:, (number - 4) * D : (number - 3) * D]
        else:
            panel = acc_s[number]
        small_out[number : number + 1, :] = jnp.sum(panel, axis=0, keepdims=True)
    small_out[12:16, :] = jnp.zeros((4, D), F32)

    def backward_done(index, carry):
        @pl.when(last)
        def _():
            backward_send(index).wait_send()

        dx_copy(index).wait()
        for copy in right_copies(index):
            copy.wait()
        return carry

    lax.fori_loop(0, micro_count, backward_done, 0)


def run_layers(tokens, cotangent, lengths, spans, *weights):
    rows = tokens.shape[0]
    micro_count = rows // ROWS
    anywhere = pl.BlockSpec(memory_space=pl.ANY)
    scalars = pl.BlockSpec(memory_space=pltpu.SMEM)
    vectors = pl.BlockSpec(memory_space=pltpu.VMEM)
    out_shape = (
        jax.ShapeDtypeStruct((rows, D), BF16),
        jax.ShapeDtypeStruct((rows, D), F32),
        jax.ShapeDtypeStruct((3 * D + FF, rows), BF16),
        jax.ShapeDtypeStruct((9, rows, D), BF16),
        jax.ShapeDtypeStruct((16, D), F32),
    )

    def vm(count, width=D, dtype=BF16):
        return pltpu.VMEM((count, width), dtype)

    scratch = [
        vm(D, 3 * D), vm(D), vm(D, FF), vm(FF),
        vm(rows), vm(rows, 3 * D),
        pltpu.VMEM((micro_count, PAIRS, LENGTH, 2 * LENGTH), BF16),
        vm(rows), vm(rows), vm(rows), vm(rows), vm(rows, FF), vm(rows, FF),
        vm(rows, 128, F32), vm(rows, 128, F32),
        vm(rows), vm(rows), vm(rows), vm(rows), vm(rows, D, F32),
        vm(ROWS, D, F32), pltpu.VMEM((2, TURN, rows), BF16), pltpu.VMEM((12, 8, D), F32), vm(8, FF, F32),
        pltpu.SemaphoreType.DMA((12,)),
        pltpu.SemaphoreType.DMA((micro_count,)),
        pltpu.SemaphoreType.DMA((17, micro_count)),
        pltpu.SemaphoreType.DMA((2,)),
        pltpu.SemaphoreType.DMA((micro_count,)),
        pltpu.SemaphoreType.DMA((micro_count,)),
        pltpu.SemaphoreType.DMA((micro_count,)),
        pltpu.SemaphoreType.DMA((micro_count,)),
    ]
    return pl.pallas_call(
        functools.partial(layers_kernel, micro_count),
        out_shape=out_shape,
        in_specs=[anywhere, anywhere, scalars, scalars] + [anywhere] * 6 + [vectors] * 4,
        out_specs=[anywhere] * 4 + [vectors],
        scratch_shapes=scratch,
        compiler_params=pltpu.CompilerParams(
            collective_id=0, has_side_effects=True, vmem_limit_bytes=60 * 1024 * 1024
        ),
        cost_estimate=pl.CostEstimate(
            flops=rows * 2 * 2 * 2 * 7077888, bytes_accessed=60000000, transcendentals=rows * FF * 2
        ),
    )(tokens, cotangent, lengths, spans.T, *weights)


RING = 8
PIECES = 3
PIECE = D // RING
PANELS = (
    (0, 0), (0, 1), (0, 2), (D, 3), (2 * D, 4), (2 * D, 5),
    (2 * D, 6), (2 * D, 7), (3 * D, 8), (4 * D, 8), (5 * D, 8), (6 * D, 8),
)


def sums_kernel(
    left, right, small_in, grads_out, small_out,
    left_s, right_s, total_s, give_s, take_s, ring_s, own_s,
    tiny_s, tiny_take_s, tiny_sum_s, tiny_go_s, tiny_ring_s, tiny_own_s,
    load_sem, give_sem, take_sem, ring_send, ring_recv, own_sem, round_send, round_recv, share_send, share_recv,
    tiny_sem, tiny_ring_send, tiny_ring_recv, tiny_round_send, tiny_round_recv,
):
    me = lax.axis_index("dp")
    core = lax.rem(me, 2)
    high = lax.rem(lax.div(me, 2), 2)
    depth = lax.div(me, 4)
    place = depth + high * (7 - 2 * depth)

    def device(spot, on_core):
        row = lax.div(spot, 4)
        return {"dp": 4 * (spot + row * (7 - 2 * spot)) + 2 * row + on_core}

    ahead = device(lax.rem(place + 1, RING), core)
    behind = device(lax.rem(place + RING - 1, RING), core)
    beside = device(place, 1 - core)
    targets = (ahead, behind)

    barrier = pltpu.get_barrier_semaphore()
    for peer in (ahead, behind, beside):
        pl.semaphore_signal(barrier, inc=1, device_id=peer, device_id_type=MESH)

    def block(way, step):
        return lax.rem(place - step + RING, RING) if way == 0 else lax.rem(place + step, RING)

    def late_block(way, step):
        return lax.rem(place + 1 - step + RING, RING) if way == 0 else lax.rem(place + RING - 1 + step, RING)

    def load_left(part):
        return pltpu.make_async_copy(left.at[pl.ds(part * D, D)], left_s.at[pl.ds(part * D, D)], load_sem.at[part])

    def load_right(part):
        return pltpu.make_async_copy(right.at[part], right_s.at[part], load_sem.at[7 + part])

    def remote(source, target, send, recv, peer):
        return pltpu.make_async_remote_copy(
            src_ref=source, dst_ref=target, send_sem=send, recv_sem=recv, device_id=peer, device_id_type=MESH
        )

    def give(way, step, piece):
        return remote(
            give_s.at[way, step, piece], take_s.at[way, step, piece],
            give_sem.at[way, step, piece], take_sem.at[way, step, piece], beside,
        )

    def ring_copy(way, step, piece):
        return remote(
            take_s.at[way, step, piece], ring_s.at[way, step, piece],
            ring_send.at[way, step, piece], ring_recv.at[way, step, piece], targets[way],
        )

    def region(way, spot, piece, on_core):
        rows = pl.ds(pl.multiple_of(spot * PIECE, PIECE), PIECE)
        return grads_out.at[6 * way + 3 * on_core + piece, rows]

    def own_copy(way, piece):
        return pltpu.make_async_copy(
            own_s.at[way, piece], region(way, late_block(way, 0), piece, core), own_sem.at[way, piece]
        )

    def round_copy(way, step, piece, source=None):
        target = region(way, late_block(way, step), piece, core)
        return remote(
            target if source is None else source, target,
            round_send.at[way, step, piece], round_recv.at[way, step, piece], targets[way],
        )

    def round_wait(way, step, piece):
        target = region(way, late_block(way, step + 1), piece, core)
        remote(
            target, target, round_send.at[way, step, piece], round_recv.at[way, step, piece], targets[way]
        ).wait_recv()

    def share_copy(way, step, piece, source=None):
        target = region(way, late_block(way, step), piece, core)
        return remote(
            target if source is None else source, target,
            share_send.at[way, step, piece], share_recv.at[way, step, piece], beside,
        )

    def share_wait(way, step, piece):
        target = region(way, late_block(way, step), piece, 1 - core)
        remote(
            target, target, share_send.at[way, step, piece], share_recv.at[way, step, piece], beside
        ).wait_recv()

    tiny_swap = remote(tiny_s, tiny_take_s, tiny_sem.at[0], tiny_sem.at[1], beside)

    def tiny_ring(step):
        return remote(
            tiny_go_s.at[step], tiny_ring_s.at[step], tiny_ring_send.at[step], tiny_ring_recv.at[step], ahead
        )

    def tiny_round(step):
        spot = late_block(0, step)
        return remote(
            tiny_own_s.at[spot], tiny_own_s.at[spot], tiny_round_send.at[step], tiny_round_recv.at[step], ahead
        )

    def tiny_round_wait(step):
        spot = late_block(0, step + 1)
        remote(
            tiny_own_s.at[spot], tiny_own_s.at[spot], tiny_round_send.at[step], tiny_round_recv.at[step], ahead
        ).wait_recv()

    loads = []
    for piece in range(PIECES):
        for way in range(2):
            for half in range(2):
                first_row, number = PANELS[6 * way + 3 * half + piece]
                for kind, part in ((load_right, number), (load_left, first_row // D)):
                    if (kind, part) not in [entry[:2] for entry in loads]:
                        loads.append((kind, part, way, piece))
    for kind, part, _, _ in loads:
        kind(part).start()

    for part in range(RING):
        if part * 128 < D:
            tiny_s[part] = small_in[:, part * 128 : part * 128 + 128]
        else:
            tiny_s[part] = jnp.zeros((16, 128), F32)

    pl.semaphore_wait(barrier, 3)
    tiny_swap.start()

    def product(group, way, piece, pick):
        near, far = PANELS[6 * way + piece], PANELS[6 * way + 3 + piece]
        first_row = near[0] + pick * (far[0] - near[0])
        number = near[1] + pick * (far[1] - near[1])
        blocks = []
        for step in (2 * group, 2 * group + 1):
            start = pl.multiple_of(first_row + block(way, step) * PIECE, PIECE)
            blocks.append(left_s[pl.ds(start, PIECE), :])
        return dot(jnp.concatenate(blocks, axis=0), right_s[number])

    def keep_product(group, way, piece, both):
        total_s[lax.rem(2 * group, 4), way, piece] = both[:PIECE]
        total_s[lax.rem(2 * group + 1, 4), way, piece] = both[PIECE:]

    def give_product(group, way, piece, both):
        give_s[way, 2 * group, piece] = both[:PIECE].astype(BF16)
        give_s[way, 2 * group + 1, piece] = both[PIECE:].astype(BF16)
        give(way, 2 * group, piece).start()
        give(way, 2 * group + 1, piece).start()

    def add_piece(step, way, piece, target):
        slot = lax.rem(step, 4)
        for r0 in range(0, PIECE, SUB):
            part = slice(r0, r0 + SUB)
            whole = total_s[slot, way, piece, part] + take_s[way, step, piece, part].astype(F32)
            target[part] = whole.astype(BF16)

    def reduce_step(step, carry):
        slot = lax.rem(step, 4)
        spot = block(0, step)

        @pl.when(step < RING - 1)
        def _():
            tiny_ring(step - 1).wait_recv()
            tiny_go_s[step] = tiny_sum_s[spot] + tiny_ring_s[step - 1]
            tiny_ring(step).start()

        @pl.when(step == RING - 1)
        def _():
            tiny_ring(step - 1).wait_recv()
            tiny_own_s[spot] = tiny_sum_s[spot] + tiny_ring_s[step - 1]
            tiny_round(0).start()

        for piece in range(PIECES):
            for way in range(2):
                give(way, step, piece).wait_recv()
                ring_copy(way, step - 1, piece).wait_recv()
                for r0 in range(0, PIECE, SUB):
                    part = slice(r0, r0 + SUB)
                    total_s[slot, way, piece, part] += ring_s[way, step - 1, piece, part].astype(F32)

                @pl.when(step < RING - 1)
                def _():
                    add_piece(step, way, piece, take_s.at[way, step, piece])
                    ring_copy(way, step, piece).start()

                @pl.when(step == RING - 1)
                def _():
                    add_piece(step, way, piece, own_s.at[way, piece])
                    round_copy(way, 0, piece, own_s.at[way, piece]).start()
                    share_copy(way, 0, piece, own_s.at[way, piece]).start()
                    own_copy(way, piece).start()

                @pl.when(step < RING - 2)
                def _():
                    odd = lax.rem(step, 2)
                    group = lax.div(step, 2) + 1
                    both = product(group, way, piece, odd * core + (1 - odd) * (1 - core))

                    @pl.when(odd == 1)
                    def _():
                        keep_product(group, way, piece, both)

                    @pl.when(odd == 0)
                    def _():
                        give_product(group, way, piece, both)

        return carry

    def first_piece(way, piece):
        give(way, 0, piece).wait_recv()
        add_piece(0, way, piece, take_s.at[way, 0, piece])
        ring_copy(way, 0, piece).start()

    order = [(way, piece) for piece in range(PIECES) for way in range(2)]
    for number, (way, piece) in enumerate(order):
        for kind, part, at_way, at_piece in loads:
            if (at_way, at_piece) == (way, piece):
                kind(part).wait()
        give_product(0, way, piece, product(0, way, piece, 1 - core))
        keep_product(0, way, piece, product(0, way, piece, core))
        if number > 0:
            first_piece(*order[number - 1])
    first_piece(*order[-1])
    for way, piece in order:
        give_product(1, way, piece, product(1, way, piece, 1 - core))
    tiny_swap.wait_recv()
    tiny_sum_s[...] = tiny_s[...] + tiny_take_s[...]
    tiny_go_s[0] = tiny_sum_s[block(0, 0)]
    tiny_ring(0).start()

    lax.fori_loop(1, RING, reduce_step, 0)

    def round_step(step, carry):
        tiny_round_wait(step - 1)

        @pl.when(step < RING - 1)
        def _():
            tiny_round(step).start()

        for piece in range(PIECES):
            for way in range(2):
                round_wait(way, step - 1, piece)

                @pl.when(step < RING - 1)
                def _():
                    round_copy(way, step, piece).start()

                share_copy(way, step, piece).start()
        return carry

    lax.fori_loop(1, RING, round_step, 0)

    for part in range(D // 128):
        small_out[:, part * 128 : part * 128 + 128] = tiny_own_s[part]
    tiny_swap.wait_send()

    def finish(step, carry):
        for way in range(2):
            for piece in range(PIECES):
                give(way, step, piece).wait_send()
                share_wait(way, step, piece)
                share_copy(way, step, piece).wait_send()

                @pl.when(step < RING - 1)
                def _():
                    ring_copy(way, step, piece).wait_send()
                    round_copy(way, step, piece).wait_send()

        @pl.when(step < RING - 1)
        def _():
            tiny_ring(step).wait_send()
            tiny_round(step).wait_send()

        return carry

    lax.fori_loop(0, RING, finish, 0)
    for way in range(2):
        for piece in range(PIECES):
            own_copy(way, piece).wait()


def run_sums(left, right, small):
    rows = right.shape[1]
    anywhere = pl.BlockSpec(memory_space=pl.ANY)
    vectors = pl.BlockSpec(memory_space=pltpu.VMEM)

    def pieces(*lead, dtype=BF16):
        return pltpu.VMEM((*lead, PIECE, D), dtype)

    dma = pltpu.SemaphoreType.DMA
    scratch = [
        pltpu.VMEM(left.shape, BF16), pltpu.VMEM(right.shape, BF16),
        pieces(4, 2, PIECES, dtype=F32), pieces(2, RING, PIECES), pieces(2, RING, PIECES),
        pieces(2, RING - 1, PIECES), pieces(2, PIECES),
        pltpu.VMEM((RING, 16, 128), F32), pltpu.VMEM((RING, 16, 128), F32), pltpu.VMEM((RING, 16, 128), F32),
        pltpu.VMEM((RING - 1, 16, 128), F32), pltpu.VMEM((RING - 1, 16, 128), F32), pltpu.VMEM((RING, 16, 128), F32),
        dma((16,)), dma((2, RING, PIECES)), dma((2, RING, PIECES)),
        dma((2, RING - 1, PIECES)), dma((2, RING - 1, PIECES)), dma((2, PIECES)),
        dma((2, RING - 1, PIECES)), dma((2, RING - 1, PIECES)), dma((2, RING, PIECES)), dma((2, RING, PIECES)),
        dma((2,)), dma((RING - 1,)), dma((RING - 1,)), dma((RING - 1,)), dma((RING - 1,)),
    ]
    return pl.pallas_call(
        sums_kernel,
        out_shape=(jax.ShapeDtypeStruct((12, D, D), BF16), jax.ShapeDtypeStruct((16, D), F32)),
        in_specs=[anywhere, anywhere, vectors],
        out_specs=[anywhere, vectors],
        scratch_shapes=scratch,
        compiler_params=pltpu.CompilerParams(
            collective_id=1, has_side_effects=True, vmem_limit_bytes=60 * 1024 * 1024
        ),
        cost_estimate=pl.CostEstimate(flops=rows * 2 * 7077888, bytes_accessed=70000000, transcendentals=0),
    )(left, right, small)


def plain_sums(left, right, small):
    panels = [dot(left[row : row + D], right[number]).astype(BF16) for row, number in PANELS]
    return lax.psum(jnp.stack(panels), "dp"), lax.psum(small, "dp")


SLOTS = 6
CUT = D


def widen_kernel(
    act, dx, grads, small, act_out, dx_out, query_out, key_out, value_out, out_out, up_out, down_out,
    bias_out, up_bias_out, gain_out, shift_out, low_s, wide_s, act_s, dx_s, in_sem, out_sem, move_sem,
):
    moves_in = [
        pltpu.make_async_copy(act, act_s, move_sem.at[0]), pltpu.make_async_copy(dx, dx_s, move_sem.at[1])
    ]
    moves_out = [
        pltpu.make_async_copy(act_s, act_out.at[0], move_sem.at[0]),
        pltpu.make_async_copy(dx_s, dx_out.at[0], move_sem.at[1]),
    ]
    jobs = []
    for panel in range(12):
        for half in range(D // CUT):
            rows = pl.ds(half * CUT, CUT)
            if panel < 4:
                target = (query_out, key_out, value_out, out_out)[panel].at[0, rows]
            elif panel < 8:
                target = up_out.at[0, rows, pl.ds((panel - 4) * D, D)]
            else:
                target = down_out.at[0, pl.ds((panel - 8) * D + half * CUT, CUT)]
            jobs.append((grads.at[panel, rows], target))

    def fetch(number):
        return pltpu.make_async_copy(jobs[number][0], low_s.at[number % SLOTS], in_sem.at[number % SLOTS])

    def store(number):
        return pltpu.make_async_copy(wide_s.at[number % SLOTS], jobs[number][1], out_sem.at[number % SLOTS])

    for number in range(SLOTS):
        fetch(number).start()
    for move in moves_in:
        move.start()
    bias_out[0] = small[0:4]
    for panel in range(FF // D):
        up_bias_out[:, panel * D : (panel + 1) * D] = small[4 + panel : 5 + panel]
    gain_out[0] = small[8:10]
    shift_out[0] = small[10:12]
    for number in range(len(jobs)):
        slot = number % SLOTS
        fetch(number).wait()
        if number >= SLOTS:
            store(number - SLOTS).wait()

        def turn(step, carry):
            part = pl.ds(pl.multiple_of(step * SUB, SUB), SUB)
            wide_s[slot, part, :] = low_s[slot, part, :].astype(F32)
            return carry

        lax.fori_loop(0, CUT // SUB, turn, 0, unroll=4)
        store(number).start()
        if number == 1:
            for move_in, move_out in zip(moves_in, moves_out):
                move_in.wait()
                move_out.start()
        if number + SLOTS < len(jobs):
            fetch(number + SLOTS).start()
    for number in range(len(jobs) - SLOTS, len(jobs)):
        store(number).wait()
    for move in moves_out:
        move.wait()


def widen(act, dx, grads, small):
    anywhere = pl.BlockSpec(memory_space=pl.ANY)
    vectors = pl.BlockSpec(memory_space=pltpu.VMEM)
    square = jax.ShapeDtypeStruct((1, D, D), F32)
    return pl.pallas_call(
        widen_kernel,
        out_shape=(
            jax.ShapeDtypeStruct((1, *act.shape), BF16), jax.ShapeDtypeStruct((1, *dx.shape), F32),
            square, square, square, square,
            jax.ShapeDtypeStruct((1, D, FF), F32), jax.ShapeDtypeStruct((1, FF, D), F32),
            jax.ShapeDtypeStruct((1, 4, D), F32), jax.ShapeDtypeStruct((1, FF), F32),
            jax.ShapeDtypeStruct((1, 2, D), F32), jax.ShapeDtypeStruct((1, 2, D), F32),
        ),
        in_specs=[anywhere, anywhere, anywhere, vectors],
        out_specs=[anywhere] * 8 + [vectors] * 4,
        scratch_shapes=[
            pltpu.VMEM((SLOTS, CUT, D), BF16), pltpu.VMEM((SLOTS, CUT, D), F32),
            pltpu.VMEM(act.shape, BF16), pltpu.VMEM(dx.shape, F32),
            pltpu.SemaphoreType.DMA((SLOTS,)), pltpu.SemaphoreType.DMA((SLOTS,)), pltpu.SemaphoreType.DMA((2,)),
        ],
        compiler_params=pltpu.CompilerParams(vmem_limit_bytes=60 * 1024 * 1024),
        cost_estimate=pl.CostEstimate(flops=7077888, bytes_accessed=42467328, transcendentals=0),
    )(act, dx, grads, small)


def per_device(grid, tokens, cotangent, lengths, spans, *weights):
    act, dx, left, right, small = run_layers(tokens, cotangent, lengths, spans, *weights)
    grads, small = (run_sums if grid else plain_sums)(left, right, small)
    return widen(act, dx, grads, small)


def solution(mesh):
    in_specs = (
        P("dp", None), P("dp", None), P("dp"), P("dp", None),
        P("section", None, None), P("section", None, None), P("section", None, None),
        P("section", None, None), P("section", None, None), P("section", None, None),
        P("section", None, None), P("section", None), P("section", None, None), P("section", None, None),
    )
    out_specs = (
        P("section", "dp", None), P("section", "dp", None),
        P("section", None, None), P("section", None, None), P("section", None, None),
        P("section", None, None), P("section", None, None), P("section", None, None),
        P("section", None, None), P("section", None), P("section", None, None), P("section", None, None),
    )
    part = functools.partial(per_device, mesh.shape["dp"] == 2 * RING)
    return jax.shard_map(part, mesh=mesh, in_specs=in_specs, out_specs=out_specs, check_vma=False)
```

```python
import functools
import itertools

import jax
import jax.numpy as jnp
from jax import lax
from jax.experimental import pallas as pl
from jax.experimental.pallas import tpu as pltpu
from jax.sharding import PartitionSpec as P

D = 768
HEADS = 12
HEAD_DIM = 64
PAIRS = HEADS // 2
FF = 3072
LENGTH = 160
LEAST = 96
ROWS = LENGTH
SUB = 32
WIDE = 512
TURN = 256
PART = 256

F32 = jnp.float32
BF16 = jnp.bfloat16
MESH = pl.DeviceIdType.MESH


def dot(left, right):
    return jnp.dot(left, right, preferred_element_type=F32)


def dot_t(left, right):
    return lax.dot_general(left, right, (((1,), (1,)), ((), ())), preferred_element_type=F32)


def t_dot(left, right):
    return lax.dot_general(left, right, (((0,), (0,)), ((), ())), preferred_element_type=F32)


def alternate(*lists):
    for group in itertools.zip_longest(*lists):
        for step in group:
            if step is not None:
                step()


def fold(block):
    return jnp.sum(block.reshape(-1, 8, block.shape[-1]), axis=0)


def gelu_parts(u):
    t = pl.reciprocal(1.0 + 0.23164189 * jnp.abs(u), approx=True)
    gauss = jnp.exp2(u * u * -0.7213475204444817)
    poly = t * (
        0.127414796 + t * (-0.142248368 + t * (0.7107068705 + t * (-0.7265760135 + t * 0.5307027145)))
    )
    tail = poly * gauss
    cdf = jnp.where(u >= 0, 1.0 - tail, tail)
    return u * cdf, cdf + (u * 0.3989422804014327) * gauss


def layers_kernel(
    micro_count,
    tokens, cotangent, lengths, spans,
    wq, wk, wv, wo, w1, w2, bias_in, up_bias_in, gains_in, shifts_in,
    act_out, dx_out, left_out, right_out, small_out,
    wx_s, wo_s, w1_s, w2_s,
    h_s, x_s, p_s, o_s, n_s, xa_s, xb_s, z_s, g_s, inva_s, invb_s,
    y_s, dy_s, df_s, da_s, dx_s, wide_s, turn_s, acc_s, accu_s,
    w_sem, in_sem, out_sem, turn_sem, fwd_send, fwd_recv, bwd_send, bwd_recv,
):
    section = lax.axis_index("section")
    other = 1 - section
    first = section == 0
    last = section == 1

    barrier = pltpu.get_barrier_semaphore()
    pl.semaphore_signal(barrier, inc=1, device_id={"section": other}, device_id_type=MESH)

    columns = [slice(c0, c0 + PART) for c0 in range(0, D, PART)]
    places = [slice(3 * c0, 3 * (c0 + PART)) for c0 in range(0, D, PART)]
    weight_copies = []
    for column, place in zip(columns, places):
        for number, source in enumerate((wq, wk, wv)):
            target = wx_s.at[:, pl.ds(place.start + number * PART, PART)]
            weight_copies.append((source.at[0, :, pl.ds(column.start, PART)], target))
    for source, target in ((wo, wo_s), (w1, w1_s), (w2, w2_s)):
        weight_copies.append((source.at[0], target))
    weight_copies = [
        pltpu.make_async_copy(source, target, w_sem.at[number])
        for number, (source, target) in enumerate(weight_copies)
    ]

    def rows_of(index):
        return pl.ds(pl.multiple_of(index * ROWS, ROWS), ROWS)

    def entry_copy(index):
        return pltpu.make_async_copy(tokens.at[rows_of(index)], h_s.at[rows_of(index)], in_sem.at[index])

    def cot_copy(index):
        return pltpu.make_async_copy(cotangent.at[rows_of(index)], dy_s.at[rows_of(index)], in_sem.at[index])

    def forward_send(index):
        return pltpu.make_async_remote_copy(
            src_ref=y_s.at[rows_of(index)],
            dst_ref=h_s.at[rows_of(index)],
            send_sem=fwd_send.at[index],
            recv_sem=fwd_recv.at[index],
            device_id={"section": other},
            device_id_type=MESH,
        )

    def backward_send(index):
        return pltpu.make_async_remote_copy(
            src_ref=y_s.at[rows_of(index)],
            dst_ref=dy_s.at[rows_of(index)],
            send_sem=bwd_send.at[index],
            recv_sem=bwd_recv.at[index],
            device_id={"section": other},
            device_id_type=MESH,
        )

    backward_outs = ((da_s, 3), (df_s, 8))

    def act_copy(index):
        return pltpu.make_async_copy(y_s.at[rows_of(index)], act_out.at[rows_of(index)], out_sem.at[0, index])

    def dx_copy(index):
        return pltpu.make_async_copy(dx_s.at[rows_of(index)], dx_out.at[rows_of(index)], out_sem.at[1, index])

    def right_copies(index):
        for slot, (source, place) in enumerate(backward_outs):
            yield pltpu.make_async_copy(
                source.at[rows_of(index)], right_out.at[place, rows_of(index)], out_sem.at[2 + slot, index]
            )
        for spot, (column, place) in enumerate(zip(columns, places)):
            for number in range(3):
                yield pltpu.make_async_copy(
                    x_s.at[rows_of(index), pl.ds(place.start + number * PART, PART)],
                    right_out.at[number, rows_of(index), pl.ds(column.start, PART)],
                    out_sem.at[8 + 3 * spot + number, index],
                )
        for panel in range(FF // D):
            yield pltpu.make_async_copy(
                g_s.at[rows_of(index), pl.ds(panel * D, D)],
                right_out.at[4 + panel, rows_of(index)],
                out_sem.at[4 + panel, index],
            )

    def turn_copy(slot, row):
        return pltpu.make_async_copy(
            turn_s.at[slot], left_out.at[pl.ds(pl.multiple_of(row, TURN), TURN)], turn_sem.at[slot]
        )

    def transpose_all():
        done = 0
        for source, tiles in ((h_s, D // TURN), (o_s, D // TURN), (n_s, D // TURN), (z_s, FF // TURN)):

            def tile_step(tile, carry, source=source, done=done):
                number = tile + done
                slot = lax.rem(number, 2)

                @pl.when(number >= 2)
                def _():
                    turn_copy(slot, (number - 2) * TURN).wait()

                turn_s[slot] = source[:, pl.ds(pl.multiple_of(tile * TURN, TURN), TURN)].T
                turn_copy(slot, number * TURN).start()
                return carry

            lax.fori_loop(0, tiles, tile_step, 0)
            done += tiles
        for number in (done - 2, done - 1):
            turn_copy(number % 2, number * TURN).wait()

    @pl.when(first)
    def _():
        for index in range(micro_count):
            entry_copy(index).start()

    @pl.when(last)
    def _():
        for index in range(micro_count):
            cot_copy(index).start()

    for copy in weight_copies:
        copy.start()

    acc_s[...] = jnp.zeros_like(acc_s)
    accu_s[...] = jnp.zeros_like(accu_s)

    bias = bias_in[0].astype(F32)
    gains = gains_in[0].astype(F32)
    shifts = shifts_in[0].astype(F32)
    low_half = lax.broadcasted_iota(jnp.int32, (1, 8, 128), 2) < HEAD_DIM
    keep_low = jnp.where(lax.broadcasted_iota(jnp.int32, (1, 16, 128), 2) < HEAD_DIM, 1.0, 0.0)
    keep_high = (1.0 - keep_low).astype(BF16)
    keep_low = keep_low.astype(BF16)

    def stacked(pair_block):
        tiles = pair_block.reshape(-1, 16, 128)
        return jnp.concatenate([tiles * keep_low, tiles * keep_high], axis=0).reshape(2 * LENGTH, 128)

    def merged(tall):
        tiles = tall.reshape(2, LENGTH // 8, 8, 128)
        return jnp.where(low_half, tiles[0], tiles[1]).reshape(LENGTH, 128)

    pl.semaphore_wait(barrier, 1)

    blocks = [slice(r0, r0 + SUB) for r0 in range(0, ROWS, SUB)]
    panels = [slice(n0, n0 + WIDE) for n0 in range(0, FF, WIDE)]
    halves = [slice(0, 128), slice(128, 256)]
    count, chunks = len(columns), len(panels)

    def forward(index, carry):
        base = index * ROWS
        rows = rows_of(index)

        def at(block):
            return pl.ds(pl.multiple_of(base + block.start, SUB), SUB)

        @pl.when(first)
        def _():
            entry_copy(index).wait()
            start, stop = spans[0, index], spans[1, index]
            spot = lax.broadcasted_iota(jnp.int32, (LENGTH, D), 0)
            keep = (spot < start) | (spot >= stop)
            h_s[rows, :] = jnp.where(keep, h_s[rows, :].astype(F32), 0.0).astype(BF16)

        @pl.when(last)
        def _():
            forward_send(index).wait_recv()

        @pl.when(index == 0)
        def _():
            for copy in weight_copies[:10]:
                copy.wait()

        hidden = h_s[rows, :]

        spot = lax.broadcasted_iota(jnp.int32, (LENGTH - LEAST, 2 * LENGTH), 0) + LEAST
        penalty = jnp.where(spot < lengths[index], 0.0, -1000000000.0)
        projected, attends, scores, sums = {}, {}, {}, {}

        def project(spot, number):
            place = slice(places[spot].start + number * PART, places[spot].start + (number + 1) * PART)
            part = dot(hidden, wx_s[:, place])
            if number == 0:
                part = (part + bias[0:1, columns[spot]]) * 0.125
            elif number == 2:
                part = part + bias[1:2, columns[spot]]
            projected[spot, number] = part.astype(BF16)
            x_s[rows, place] = projected[spot, number]

        def score(spot, half):
            query, key_rows = projected[spot, 0], projected[spot, 1]
            scores[spot, half] = dot_t(key_rows[:, halves[half]], stacked(query[:, halves[half]]))

        def soften(spot, half):
            held = scores[spot, half]
            held = jnp.concatenate([held[:LEAST], held[LEAST:] + penalty], axis=0)
            raised = jnp.exp(held - jnp.max(held, axis=0, keepdims=True))
            attend = (raised * (1.0 / jnp.sum(raised, axis=0, keepdims=True))).astype(BF16)
            attends[spot, half] = attend
            p_s[index, 2 * spot + half] = attend

        def mix(spot):
            value = projected[spot, 2]
            mixes = [merged(t_dot(attends[spot, half], value[:, halves[half]])) for half in range(2)]
            o_s[rows, columns[spot]] = jnp.concatenate([part.astype(BF16) for part in mixes], axis=1)

        def outward(spot, column):
            product = dot(o_s[rows, columns[spot]], wo_s[columns[spot], columns[column]])
            sums[column] = product if spot == 0 else sums[column] + product

        for step in range(count + 2):
            left, right = [], []
            if step < count:
                left += [functools.partial(project, step, number) for number in range(3)]
            if 0 <= step - 2:
                left += [functools.partial(mix, step - 2)]
                left += [functools.partial(outward, step - 2, column) for column in range(count)]
            if 0 <= step - 1 < count:
                score(step - 1, 0)
                score(step - 1, 1)
                right += [functools.partial(soften, step - 1, half) for half in range(2)]
            alternate(left, right)
        attended = jnp.concatenate([sums[column] for column in range(count)], axis=1)

        for block in blocks:
            r = h_s[at(block), :].astype(F32) + attended[block] + bias[2:3]
            centered = r - jnp.mean(r, axis=-1, keepdims=True)
            inv = lax.rsqrt(jnp.mean(centered * centered, axis=-1, keepdims=True) + 1e-05)
            hat = centered * inv
            normed = hat * gains[0:1] + shifts[0:1]
            xa_s[at(block), :] = hat.astype(BF16)
            inva_s[at(block), :] = jnp.broadcast_to(inv, (SUB, 128))
            n_s[at(block), :] = normed.astype(BF16)
            wide_s[block, :] = normed

        @pl.when(index == 0)
        def _():
            for copy in weight_copies[10:]:
                copy.wait()

        normed_low = n_s[rows, :]
        lifted, sums = {}, {}

        def lift(spot, part):
            start = panels[spot].start + part * PART
            lifted[spot, part] = dot(normed_low, w1_s[:, start : start + PART])

        def bend(spot, block):
            for part in range(WIDE // PART):
                start = panels[spot].start + part * PART
                up_bias = up_bias_in[0:1, start : start + PART].astype(F32)
                act, slope = gelu_parts(lifted[spot, part][block] + up_bias)
                z_s[at(block), start : start + PART] = act.astype(BF16)
                g_s[at(block), start : start + PART] = slope.astype(BF16)

        def lower(spot, column):
            product = dot(z_s[rows, panels[spot]], w2_s[panels[spot], columns[column]])
            sums[column] = product if spot == 0 else sums[column] + product

        for step in range(chunks + 2):
            left, right = [], []
            if step < chunks:
                left += [functools.partial(lift, step, part) for part in range(WIDE // PART)]
            if 0 <= step - 2:
                left += [functools.partial(lower, step - 2, column) for column in range(count)]
            if 0 <= step - 1 < chunks:
                right += [functools.partial(bend, step - 1, block) for block in blocks]
            alternate(left, right)
        outer = jnp.concatenate([sums[column] for column in range(count)], axis=1)

        for block in blocks:
            r = wide_s[block, :] + outer[block] + bias[3:4]
            centered = r - jnp.mean(r, axis=-1, keepdims=True)
            inv = lax.rsqrt(jnp.mean(centered * centered, axis=-1, keepdims=True) + 1e-05)
            hat = centered * inv
            xb_s[at(block), :] = hat.astype(BF16)
            invb_s[at(block), :] = jnp.broadcast_to(inv, (SUB, 128))
            y_s[at(block), :] = (hat * gains[1:2] + shifts[1:2]).astype(BF16)

        @pl.when(first)
        def _():
            forward_send(index).start()

        act_copy(index).start()
        return carry

    lax.fori_loop(0, micro_count, forward, 0)

    def forward_done(index, carry):
        @pl.when(first)
        def _():
            forward_send(index).wait_send()

        act_copy(index).wait()
        return carry

    lax.fori_loop(0, micro_count, forward_done, 0)

    @pl.when(first)
    def _():
        transpose_all()

    def backward(index, carry):
        base = index * ROWS
        rows = rows_of(index)

        def at(block):
            return pl.ds(pl.multiple_of(base + block.start, SUB), SUB)

        @pl.when(first)
        def _():
            backward_send(index).wait_recv()

        @pl.when(last)
        def _():
            cot_copy(index).wait()

        for block in blocks:
            dy = dy_s[at(block), :].astype(F32)
            hat = xb_s[at(block), :].astype(F32)
            acc_s[9] += fold(dy * hat)
            acc_s[11] += fold(dy)
            scaled = dy * gains[1:2]
            mean_plain = jnp.mean(scaled, axis=-1, keepdims=True)
            mean_hat = jnp.mean(scaled * hat, axis=-1, keepdims=True)
            grad = (scaled - mean_plain - hat * mean_hat) * invb_s[at(block), 0:1]
            wide_s[block, :] = grad
            df_s[at(block), :] = grad.astype(BF16)
            acc_s[3] += fold(grad)

        outer_low = df_s[rows, :]
        dropped, sums, folds = {}, {}, {}

        def drop(spot, part):
            start = panels[spot].start + part * PART
            dropped[spot, part] = dot_t(outer_low, w2_s[start : start + PART, :])

        def unbend(spot, block):
            for part in range(WIDE // PART):
                start = panels[spot].start + part * PART
                grad = dropped[spot, part][block] * g_s[at(block), start : start + PART].astype(F32)
                g_s[at(block), start : start + PART] = grad.astype(BF16)
                folds[spot, part] = folds.get((spot, part), 0.0) + fold(grad)
                if block is blocks[-1]:
                    accu_s[:, start : start + PART] += folds[spot, part]

        def back(spot, column):
            product = dot_t(g_s[rows, panels[spot]], w1_s[columns[column], panels[spot]])
            sums[column] = product if spot == 0 else sums[column] + product

        for step in range(chunks + 2):
            left, right = [], []
            if step < chunks:
                left += [functools.partial(drop, step, part) for part in range(WIDE // PART)]
            if 0 <= step - 2:
                left += [functools.partial(back, step - 2, column) for column in range(count)]
            if 0 <= step - 1 < chunks:
                right += [functools.partial(unbend, step - 1, block) for block in blocks]
            alternate(left, right)
        total = jnp.concatenate([sums[column] for column in range(count)], axis=1)

        for block in blocks:
            dn = wide_s[block, :] + total[block]
            hat = xa_s[at(block), :].astype(F32)
            acc_s[8] += fold(dn * hat)
            acc_s[10] += fold(dn)
            scaled = dn * gains[0:1]
            mean_plain = jnp.mean(scaled, axis=-1, keepdims=True)
            mean_hat = jnp.mean(scaled * hat, axis=-1, keepdims=True)
            grad = (scaled - mean_plain - hat * mean_hat) * inva_s[at(block), 0:1]
            wide_s[block, :] = grad
            da_s[at(block), :] = grad.astype(BF16)
            acc_s[2] += fold(grad)

        attended_low = da_s[rows, :]
        mixed, talls, grad_attends, values_back, scored, grads, sums = {}, {}, {}, {}, {}, {}, {}

        def unmix(spot):
            mixed[spot] = dot_t(attended_low, wo_s[columns[spot], :]).astype(BF16)

        def attend_back(spot, half):
            value = x_s[rows, places[spot]][:, 2 * PART :]
            talls[spot, half] = stacked(mixed[spot][:, halves[half]])
            grad_attends[spot, half] = dot_t(value[:, halves[half]], talls[spot, half])

        def value_back(spot, half):
            values_back[spot, half] = dot(p_s[index, 2 * spot + half], talls[spot, half])

        def score_back(spot, half):
            attend = p_s[index, 2 * spot + half].astype(F32)
            weighted = attend * grad_attends[spot, half]
            delta = jnp.sum(weighted, axis=0, keepdims=True) / jnp.sum(attend, axis=0, keepdims=True)
            scored[spot, half] = (weighted - attend * delta).astype(BF16)

        def pair_back(spot, half):
            whole = x_s[rows, places[spot]]
            query, key_rows = whole[:, :PART][:, halves[half]], whole[:, PART : 2 * PART][:, halves[half]]
            dk = dot(scored[spot, half], stacked(query))
            dq = merged(t_dot(scored[spot, half], key_rows)) * 0.125
            grads[spot, half] = (dq, dk, values_back[spot, half])

        def keep_back(spot):
            dq, dk, dv = [
                jnp.concatenate([grads[spot, half][number] for half in range(2)], axis=1) for number in range(3)
            ]
            acc_s[0, :, columns[spot]] += fold(dq)
            acc_s[1, :, columns[spot]] += fold(dv)
            x_s[rows, places[spot]] = jnp.concatenate(
                [dq.astype(BF16), dk.astype(BF16), dv.astype(BF16)], axis=1
            )

        def inward(spot, column):
            product = dot_t(x_s[rows, places[spot]], wx_s[columns[column], places[spot]])
            sums[column] = product if spot == 0 else sums[column] + product

        for step in range(count + 3):
            left, right = [], []
            if step < count:
                left += [functools.partial(unmix, step)]
            if 0 <= step - 3:
                left += [functools.partial(inward, step - 3, column) for column in range(count)]
            if 0 <= step - 1 < count:
                attend_back(step - 1, 0)
                attend_back(step - 1, 1)
                left += [functools.partial(value_back, step - 1, half) for half in range(2)]
                right += [functools.partial(score_back, step - 1, half) for half in range(2)]
            if 0 <= step - 2 < count:
                left += [functools.partial(pair_back, step - 2, half) for half in range(2)]
                left += [functools.partial(keep_back, step - 2)]
            alternate(left, right)
        total = jnp.concatenate([sums[column] for column in range(count)], axis=1)

        @pl.when(last)
        def _():
            low = (wide_s[...] + total).astype(BF16)
            y_s[rows, :] = low
            dx_s[rows, :] = low.astype(F32)
            backward_send(index).start()

        @pl.when(first)
        def _():
            start, stop = spans[0, index], spans[1, index]
            spot = lax.broadcasted_iota(jnp.int32, (LENGTH, D), 0)
            keep = (spot < start) | (spot >= stop)
            dx_s[rows, :] = jnp.where(keep, wide_s[...] + total, 0.0)

        dx_copy(index).start()
        for copy in right_copies(index):
            copy.start()
        return carry

    lax.fori_loop(0, micro_count, backward, 0)

    @pl.when(last)
    def _():
        transpose_all()

    for number in range(12):
        if 4 <= number < 8:
            panel = accu_s[:, (number - 4) * D : (number - 3) * D]
        else:
            panel = acc_s[number]
        small_out[number : number + 1, :] = jnp.sum(panel, axis=0, keepdims=True)
    small_out[12:16, :] = jnp.zeros((4, D), F32)

    def backward_done(index, carry):
        @pl.when(last)
        def _():
            backward_send(index).wait_send()

        dx_copy(index).wait()
        for copy in right_copies(index):
            copy.wait()
        return carry

    lax.fori_loop(0, micro_count, backward_done, 0)


def run_layers(tokens, cotangent, lengths, spans, *weights):
    rows = tokens.shape[0]
    micro_count = rows // ROWS
    anywhere = pl.BlockSpec(memory_space=pl.ANY)
    scalars = pl.BlockSpec(memory_space=pltpu.SMEM)
    vectors = pl.BlockSpec(memory_space=pltpu.VMEM)
    out_shape = (
        jax.ShapeDtypeStruct((rows, D), BF16),
        jax.ShapeDtypeStruct((rows, D), F32),
        jax.ShapeDtypeStruct((3 * D + FF, rows), BF16),
        jax.ShapeDtypeStruct((9, rows, D), BF16),
        jax.ShapeDtypeStruct((16, D), F32),
    )

    def vm(count, width=D, dtype=BF16):
        return pltpu.VMEM((count, width), dtype)

    scratch = [
        vm(D, 3 * D), vm(D), vm(D, FF), vm(FF),
        vm(rows), vm(rows, 3 * D),
        pltpu.VMEM((micro_count, PAIRS, LENGTH, 2 * LENGTH), BF16),
        vm(rows), vm(rows), vm(rows), vm(rows), vm(rows, FF), vm(rows, FF),
        vm(rows, 128, F32), vm(rows, 128, F32),
        vm(rows), vm(rows), vm(rows), vm(rows), vm(rows, D, F32),
        vm(ROWS, D, F32), pltpu.VMEM((2, TURN, rows), BF16), pltpu.VMEM((12, 8, D), F32), vm(8, FF, F32),
        pltpu.SemaphoreType.DMA((12,)),
        pltpu.SemaphoreType.DMA((micro_count,)),
        pltpu.SemaphoreType.DMA((17, micro_count)),
        pltpu.SemaphoreType.DMA((2,)),
        pltpu.SemaphoreType.DMA((micro_count,)),
        pltpu.SemaphoreType.DMA((micro_count,)),
        pltpu.SemaphoreType.DMA((micro_count,)),
        pltpu.SemaphoreType.DMA((micro_count,)),
    ]
    return pl.pallas_call(
        functools.partial(layers_kernel, micro_count),
        out_shape=out_shape,
        in_specs=[anywhere, anywhere, scalars, scalars] + [anywhere] * 6 + [vectors] * 4,
        out_specs=[anywhere] * 4 + [vectors],
        scratch_shapes=scratch,
        compiler_params=pltpu.CompilerParams(
            collective_id=0, has_side_effects=True, vmem_limit_bytes=60 * 1024 * 1024
        ),
        cost_estimate=pl.CostEstimate(
            flops=rows * 2 * 2 * 2 * 7077888, bytes_accessed=60000000, transcendentals=rows * FF * 2
        ),
    )(tokens, cotangent, lengths, spans.T, *weights)


RING = 8
PIECES = 3
PIECE = D // RING
PANELS = (
    (0, 0), (0, 1), (0, 2), (D, 3), (2 * D, 4), (2 * D, 5),
    (2 * D, 6), (2 * D, 7), (3 * D, 8), (4 * D, 8), (5 * D, 8), (6 * D, 8),
)


def sums_kernel(
    left, right, small_in, grads_out, small_out,
    left_s, right_s, total_s, give_s, take_s, ring_s, own_s,
    tiny_s, tiny_take_s, tiny_sum_s, tiny_go_s, tiny_ring_s, tiny_own_s,
    load_sem, give_sem, take_sem, ring_send, ring_recv, own_sem, round_send, round_recv, share_send, share_recv,
    tiny_sem, tiny_ring_send, tiny_ring_recv, tiny_round_send, tiny_round_recv,
):
    me = lax.axis_index("dp")
    core = lax.rem(me, 2)
    high = lax.rem(lax.div(me, 2), 2)
    depth = lax.div(me, 4)
    place = depth + high * (7 - 2 * depth)

    def device(spot, on_core):
        row = lax.div(spot, 4)
        return {"dp": 4 * (spot + row * (7 - 2 * spot)) + 2 * row + on_core}

    ahead = device(lax.rem(place + 1, RING), core)
    behind = device(lax.rem(place + RING - 1, RING), core)
    beside = device(place, 1 - core)
    targets = (ahead, behind)

    barrier = pltpu.get_barrier_semaphore()
    for peer in (ahead, behind, beside):
        pl.semaphore_signal(barrier, inc=1, device_id=peer, device_id_type=MESH)

    def block(way, step):
        return lax.rem(place - step + RING, RING) if way == 0 else lax.rem(place + step, RING)

    def late_block(way, step):
        return lax.rem(place + 1 - step + RING, RING) if way == 0 else lax.rem(place + RING - 1 + step, RING)

    def load_left(part):
        return pltpu.make_async_copy(left.at[pl.ds(part * D, D)], left_s.at[pl.ds(part * D, D)], load_sem.at[part])

    def load_right(part):
        return pltpu.make_async_copy(right.at[part], right_s.at[part], load_sem.at[7 + part])

    def remote(source, target, send, recv, peer):
        return pltpu.make_async_remote_copy(
            src_ref=source, dst_ref=target, send_sem=send, recv_sem=recv, device_id=peer, device_id_type=MESH
        )

    def give(way, step, piece):
        return remote(
            give_s.at[way, step, piece], take_s.at[way, step, piece],
            give_sem.at[way, step, piece], take_sem.at[way, step, piece], beside,
        )

    def ring_copy(way, step, piece):
        return remote(
            take_s.at[way, step, piece], ring_s.at[way, step, piece],
            ring_send.at[way, step, piece], ring_recv.at[way, step, piece], targets[way],
        )

    def region(way, spot, piece, on_core):
        rows = pl.ds(pl.multiple_of(spot * PIECE, PIECE), PIECE)
        return grads_out.at[6 * way + 3 * on_core + piece, rows]

    def own_copy(way, piece):
        return pltpu.make_async_copy(
            own_s.at[way, piece], region(way, late_block(way, 0), piece, core), own_sem.at[way, piece]
        )

    def round_copy(way, step, piece, source=None):
        target = region(way, late_block(way, step), piece, core)
        return remote(
            target if source is None else source, target,
            round_send.at[way, step, piece], round_recv.at[way, step, piece], targets[way],
        )

    def round_wait(way, step, piece):
        target = region(way, late_block(way, step + 1), piece, core)
        remote(
            target, target, round_send.at[way, step, piece], round_recv.at[way, step, piece], targets[way]
        ).wait_recv()

    def share_copy(way, step, piece, source=None):
        target = region(way, late_block(way, step), piece, core)
        return remote(
            target if source is None else source, target,
            share_send.at[way, step, piece], share_recv.at[way, step, piece], beside,
        )

    def share_wait(way, step, piece):
        target = region(way, late_block(way, step), piece, 1 - core)
        remote(
            target, target, share_send.at[way, step, piece], share_recv.at[way, step, piece], beside
        ).wait_recv()

    tiny_swap = remote(tiny_s, tiny_take_s, tiny_sem.at[0], tiny_sem.at[1], beside)

    def tiny_ring(step):
        return remote(
            tiny_go_s.at[step], tiny_ring_s.at[step], tiny_ring_send.at[step], tiny_ring_recv.at[step], ahead
        )

    def tiny_round(step):
        spot = late_block(0, step)
        return remote(
            tiny_own_s.at[spot], tiny_own_s.at[spot], tiny_round_send.at[step], tiny_round_recv.at[step], ahead
        )

    def tiny_round_wait(step):
        spot = late_block(0, step + 1)
        remote(
            tiny_own_s.at[spot], tiny_own_s.at[spot], tiny_round_send.at[step], tiny_round_recv.at[step], ahead
        ).wait_recv()

    loads = []
    for piece in range(PIECES):
        for way in range(2):
            for half in range(2):
                first_row, number = PANELS[6 * way + 3 * half + piece]
                for kind, part in ((load_right, number), (load_left, first_row // D)):
                    if (kind, part) not in [entry[:2] for entry in loads]:
                        loads.append((kind, part, way, piece))
    for kind, part, _, _ in loads:
        kind(part).start()

    for part in range(RING):
        if part * 128 < D:
            tiny_s[part] = small_in[:, part * 128 : part * 128 + 128]
        else:
            tiny_s[part] = jnp.zeros((16, 128), F32)

    pl.semaphore_wait(barrier, 3)
    tiny_swap.start()

    def product(group, way, piece, pick):
        near, far = PANELS[6 * way + piece], PANELS[6 * way + 3 + piece]
        first_row = near[0] + pick * (far[0] - near[0])
        number = near[1] + pick * (far[1] - near[1])
        blocks = []
        for step in (2 * group, 2 * group + 1):
            start = pl.multiple_of(first_row + block(way, step) * PIECE, PIECE)
            blocks.append(left_s[pl.ds(start, PIECE), :])
        return dot(jnp.concatenate(blocks, axis=0), right_s[number])

    def keep_product(group, way, piece, both):
        total_s[lax.rem(2 * group, 4), way, piece] = both[:PIECE]
        total_s[lax.rem(2 * group + 1, 4), way, piece] = both[PIECE:]

    def give_product(group, way, piece, both):
        give_s[way, 2 * group, piece] = both[:PIECE].astype(BF16)
        give_s[way, 2 * group + 1, piece] = both[PIECE:].astype(BF16)
        give(way, 2 * group, piece).start()
        give(way, 2 * group + 1, piece).start()

    def add_piece(step, way, piece, target):
        slot = lax.rem(step, 4)
        for r0 in range(0, PIECE, SUB):
            part = slice(r0, r0 + SUB)
            whole = total_s[slot, way, piece, part] + take_s[way, step, piece, part].astype(F32)
            target[part] = whole.astype(BF16)

    def reduce_step(step, carry):
        slot = lax.rem(step, 4)
        spot = block(0, step)

        @pl.when(step < RING - 1)
        def _():
            tiny_ring(step - 1).wait_recv()
            tiny_go_s[step] = tiny_sum_s[spot] + tiny_ring_s[step - 1]
            tiny_ring(step).start()

        @pl.when(step == RING - 1)
        def _():
            tiny_ring(step - 1).wait_recv()
            tiny_own_s[spot] = tiny_sum_s[spot] + tiny_ring_s[step - 1]
            tiny_round(0).start()

        for piece in range(PIECES):
            for way in range(2):
                give(way, step, piece).wait_recv()
                ring_copy(way, step - 1, piece).wait_recv()
                for r0 in range(0, PIECE, SUB):
                    part = slice(r0, r0 + SUB)
                    total_s[slot, way, piece, part] += ring_s[way, step - 1, piece, part].astype(F32)

                @pl.when(step < RING - 1)
                def _():
                    add_piece(step, way, piece, take_s.at[way, step, piece])
                    ring_copy(way, step, piece).start()

                @pl.when(step == RING - 1)
                def _():
                    add_piece(step, way, piece, own_s.at[way, piece])
                    round_copy(way, 0, piece, own_s.at[way, piece]).start()
                    share_copy(way, 0, piece, own_s.at[way, piece]).start()
                    own_copy(way, piece).start()

                @pl.when(step < RING - 2)
                def _():
                    odd = lax.rem(step, 2)
                    group = lax.div(step, 2) + 1
                    both = product(group, way, piece, odd * core + (1 - odd) * (1 - core))

                    @pl.when(odd == 1)
                    def _():
                        keep_product(group, way, piece, both)

                    @pl.when(odd == 0)
                    def _():
                        give_product(group, way, piece, both)

        return carry

    def first_piece(way, piece):
        give(way, 0, piece).wait_recv()
        add_piece(0, way, piece, take_s.at[way, 0, piece])
        ring_copy(way, 0, piece).start()

    order = [(way, piece) for piece in range(PIECES) for way in range(2)]
    for number, (way, piece) in enumerate(order):
        for kind, part, at_way, at_piece in loads:
            if (at_way, at_piece) == (way, piece):
                kind(part).wait()
        give_product(0, way, piece, product(0, way, piece, 1 - core))
        keep_product(0, way, piece, product(0, way, piece, core))
        if number > 0:
            first_piece(*order[number - 1])
    first_piece(*order[-1])
    for way, piece in order:
        give_product(1, way, piece, product(1, way, piece, 1 - core))
    tiny_swap.wait_recv()
    tiny_sum_s[...] = tiny_s[...] + tiny_take_s[...]
    tiny_go_s[0] = tiny_sum_s[block(0, 0)]
    tiny_ring(0).start()

    lax.fori_loop(1, RING, reduce_step, 0)

    def round_step(step, carry):
        tiny_round_wait(step - 1)

        @pl.when(step < RING - 1)
        def _():
            tiny_round(step).start()

        for piece in range(PIECES):
            for way in range(2):
                round_wait(way, step - 1, piece)

                @pl.when(step < RING - 1)
                def _():
                    round_copy(way, step, piece).start()

                share_copy(way, step, piece).start()
        return carry

    lax.fori_loop(1, RING, round_step, 0)

    for part in range(D // 128):
        small_out[:, part * 128 : part * 128 + 128] = tiny_own_s[part]
    tiny_swap.wait_send()

    def finish(step, carry):
        for way in range(2):
            for piece in range(PIECES):
                give(way, step, piece).wait_send()
                share_wait(way, step, piece)
                share_copy(way, step, piece).wait_send()

                @pl.when(step < RING - 1)
                def _():
                    ring_copy(way, step, piece).wait_send()
                    round_copy(way, step, piece).wait_send()

        @pl.when(step < RING - 1)
        def _():
            tiny_ring(step).wait_send()
            tiny_round(step).wait_send()

        return carry

    lax.fori_loop(0, RING, finish, 0)
    for way in range(2):
        for piece in range(PIECES):
            own_copy(way, piece).wait()


def run_sums(left, right, small):
    rows = right.shape[1]
    anywhere = pl.BlockSpec(memory_space=pl.ANY)
    vectors = pl.BlockSpec(memory_space=pltpu.VMEM)

    def pieces(*lead, dtype=BF16):
        return pltpu.VMEM((*lead, PIECE, D), dtype)

    dma = pltpu.SemaphoreType.DMA
    scratch = [
        pltpu.VMEM(left.shape, BF16), pltpu.VMEM(right.shape, BF16),
        pieces(4, 2, PIECES, dtype=F32), pieces(2, RING, PIECES), pieces(2, RING, PIECES),
        pieces(2, RING - 1, PIECES), pieces(2, PIECES),
        pltpu.VMEM((RING, 16, 128), F32), pltpu.VMEM((RING, 16, 128), F32), pltpu.VMEM((RING, 16, 128), F32),
        pltpu.VMEM((RING - 1, 16, 128), F32), pltpu.VMEM((RING - 1, 16, 128), F32), pltpu.VMEM((RING, 16, 128), F32),
        dma((16,)), dma((2, RING, PIECES)), dma((2, RING, PIECES)),
        dma((2, RING - 1, PIECES)), dma((2, RING - 1, PIECES)), dma((2, PIECES)),
        dma((2, RING - 1, PIECES)), dma((2, RING - 1, PIECES)), dma((2, RING, PIECES)), dma((2, RING, PIECES)),
        dma((2,)), dma((RING - 1,)), dma((RING - 1,)), dma((RING - 1,)), dma((RING - 1,)),
    ]
    return pl.pallas_call(
        sums_kernel,
        out_shape=(jax.ShapeDtypeStruct((12, D, D), BF16), jax.ShapeDtypeStruct((16, D), F32)),
        in_specs=[anywhere, anywhere, vectors],
        out_specs=[anywhere, vectors],
        scratch_shapes=scratch,
        compiler_params=pltpu.CompilerParams(
            collective_id=1, has_side_effects=True, vmem_limit_bytes=60 * 1024 * 1024
        ),
        cost_estimate=pl.CostEstimate(flops=rows * 2 * 7077888, bytes_accessed=70000000, transcendentals=0),
    )(left, right, small)


def plain_sums(left, right, small):
    panels = [dot(left[row : row + D], right[number]).astype(BF16) for row, number in PANELS]
    return lax.psum(jnp.stack(panels), "dp"), lax.psum(small, "dp")


SLOTS = 8
CUT = D // 2


def widen_kernel(
    act, dx, grads, small, act_out, dx_out, query_out, key_out, value_out, out_out, up_out, down_out,
    bias_out, up_bias_out, gain_out, shift_out, low_s, wide_s, act_s, dx_s, in_sem, out_sem, move_sem,
):
    moves_in = [
        pltpu.make_async_copy(act, act_s, move_sem.at[0]), pltpu.make_async_copy(dx, dx_s, move_sem.at[1])
    ]
    moves_out = [
        pltpu.make_async_copy(act_s, act_out.at[0], move_sem.at[0]),
        pltpu.make_async_copy(dx_s, dx_out.at[0], move_sem.at[1]),
    ]
    jobs = []
    for panel in range(12):
        for half in range(D // CUT):
            rows = pl.ds(half * CUT, CUT)
            if panel < 4:
                target = (query_out, key_out, value_out, out_out)[panel].at[0, rows]
            elif panel < 8:
                target = up_out.at[0, rows, pl.ds((panel - 4) * D, D)]
            else:
                target = down_out.at[0, pl.ds((panel - 8) * D + half * CUT, CUT)]
            jobs.append((grads.at[panel, rows], target))

    def fetch(number):
        return pltpu.make_async_copy(jobs[number][0], low_s.at[number % SLOTS], in_sem.at[number % SLOTS])

    def store(number):
        return pltpu.make_async_copy(wide_s.at[number % SLOTS], jobs[number][1], out_sem.at[number % SLOTS])

    for number in range(SLOTS):
        fetch(number).start()
    for move in moves_in:
        move.start()
    bias_out[0] = small[0:4]
    for panel in range(FF // D):
        up_bias_out[:, panel * D : (panel + 1) * D] = small[4 + panel : 5 + panel]
    gain_out[0] = small[8:10]
    shift_out[0] = small[10:12]
    for number in range(len(jobs)):
        slot = number % SLOTS
        fetch(number).wait()
        if number >= SLOTS:
            store(number - SLOTS).wait()

        def turn(step, carry):
            part = pl.ds(pl.multiple_of(step * SUB, SUB), SUB)
            wide_s[slot, part, :] = low_s[slot, part, :].astype(F32)
            return carry

        lax.fori_loop(0, CUT // SUB, turn, 0, unroll=4)
        store(number).start()
        if number == SLOTS:
            for move_in, move_out in zip(moves_in, moves_out):
                move_in.wait()
                move_out.start()
        if number + SLOTS < len(jobs):
            fetch(number + SLOTS).start()
    for number in range(len(jobs) - SLOTS, len(jobs)):
        store(number).wait()
    for move in moves_out:
        move.wait()


def widen(act, dx, grads, small):
    anywhere = pl.BlockSpec(memory_space=pl.ANY)
    vectors = pl.BlockSpec(memory_space=pltpu.VMEM)
    square = jax.ShapeDtypeStruct((1, D, D), F32)
    return pl.pallas_call(
        widen_kernel,
        out_shape=(
            jax.ShapeDtypeStruct((1, *act.shape), BF16), jax.ShapeDtypeStruct((1, *dx.shape), F32),
            square, square, square, square,
            jax.ShapeDtypeStruct((1, D, FF), F32), jax.ShapeDtypeStruct((1, FF, D), F32),
            jax.ShapeDtypeStruct((1, 4, D), F32), jax.ShapeDtypeStruct((1, FF), F32),
            jax.ShapeDtypeStruct((1, 2, D), F32), jax.ShapeDtypeStruct((1, 2, D), F32),
        ),
        in_specs=[anywhere, anywhere, anywhere, vectors],
        out_specs=[anywhere] * 8 + [vectors] * 4,
        scratch_shapes=[
            pltpu.VMEM((SLOTS, CUT, D), BF16), pltpu.VMEM((SLOTS, CUT, D), F32),
            pltpu.VMEM(act.shape, BF16), pltpu.VMEM(dx.shape, F32),
            pltpu.SemaphoreType.DMA((SLOTS,)), pltpu.SemaphoreType.DMA((SLOTS,)), pltpu.SemaphoreType.DMA((2,)),
        ],
        compiler_params=pltpu.CompilerParams(vmem_limit_bytes=60 * 1024 * 1024),
        cost_estimate=pl.CostEstimate(flops=7077888, bytes_accessed=42467328, transcendentals=0),
    )(act, dx, grads, small)


def per_device(grid, tokens, cotangent, lengths, spans, *weights):
    act, dx, left, right, small = run_layers(tokens, cotangent, lengths, spans, *weights)
    grads, small = (run_sums if grid else plain_sums)(left, right, small)
    return widen(act, dx, grads, small)


def solution(mesh):
    in_specs = (
        P("dp", None), P("dp", None), P("dp"), P("dp", None),
        P("section", None, None), P("section", None, None), P("section", None, None),
        P("section", None, None), P("section", None, None), P("section", None, None),
        P("section", None, None), P("section", None), P("section", None, None), P("section", None, None),
    )
    out_specs = (
        P("section", "dp", None), P("section", "dp", None),
        P("section", None, None), P("section", None, None), P("section", None, None),
        P("section", None, None), P("section", None, None), P("section", None, None),
        P("section", None, None), P("section", None), P("section", None, None), P("section", None, None),
    )
    part = functools.partial(per_device, mesh.shape["dp"] == 2 * RING)
    return jax.shard_map(part, mesh=mesh, in_specs=in_specs, out_specs=out_specs, check_vma=False)
```

```python
import functools

import jax
import jax.numpy as jnp
from jax import lax
from jax.experimental import pallas as pl
from jax.experimental.pallas import tpu as pltpu
from jax.sharding import PartitionSpec as P

D = 768
HEADS = 12
HEAD_DIM = 64
QUADS = HEADS // 4
FF = 3072
LENGTH = 160
LEAST = 96
ROWS = LENGTH
SUB = 32
WIDE = 512
TURN = 256
PART = 256

F32 = jnp.float32
BF16 = jnp.bfloat16
MESH = pl.DeviceIdType.MESH


def dot(left, right):
    return jnp.dot(left, right, preferred_element_type=F32)


def dot_t(left, right):
    return lax.dot_general(left, right, (((1,), (1,)), ((), ())), preferred_element_type=F32)


def fold(block):
    return jnp.sum(block.reshape(-1, 8, block.shape[-1]), axis=0)


def gelu_parts(u):
    t = pl.reciprocal(1.0 + 0.23164189 * jnp.abs(u), approx=True)
    gauss = jnp.exp2(u * u * -0.7213475204444817)
    poly = t * (
        0.127414796 + t * (-0.142248368 + t * (0.7107068705 + t * (-0.7265760135 + t * 0.5307027145)))
    )
    tail = poly * gauss
    cdf = jnp.where(u >= 0, 1.0 - tail, tail)
    return u * cdf, cdf + (u * 0.3989422804014327) * gauss


def layers_kernel(
    micro_count,
    tokens, cotangent, lengths, spans,
    wq, wk, wv, wo, w1, w2, bias_in, up_bias_in, gains_in, shifts_in,
    act_out, dx_out, left_out, right_out, small_out,
    wq_s, wk_s, wv_s, wo_s, w1_s, w2_s,
    h_s, q_s, k_s, v_s, p_s, o_s, n_s, xa_s, xb_s, z_s, g_s, inva_s, invb_s,
    y_s, dy_s, df_s, da_s, dx_s, wide_s, turn_s, acc_s, accu_s,
    w_sem, in_sem, out_sem, turn_sem, fwd_send, fwd_recv, bwd_send, bwd_recv,
):
    section = lax.axis_index("section")
    other = 1 - section
    first = section == 0
    last = section == 1

    barrier = pltpu.get_barrier_semaphore()
    pl.semaphore_signal(barrier, inc=1, device_id={"section": other}, device_id_type=MESH)

    weight_pairs = ((wq, wq_s), (wk, wk_s), (wv, wv_s), (wo, wo_s), (w1, w1_s), (w2, w2_s))

    def weight_copy(index):
        source, target = weight_pairs[index]
        return pltpu.make_async_copy(source.at[0], target, w_sem.at[index])

    def rows_of(index):
        return pl.ds(pl.multiple_of(index * ROWS, ROWS), ROWS)

    def entry_copy(index):
        return pltpu.make_async_copy(tokens.at[rows_of(index)], h_s.at[rows_of(index)], in_sem.at[index])

    def cot_copy(index):
        return pltpu.make_async_copy(cotangent.at[rows_of(index)], dy_s.at[rows_of(index)], in_sem.at[index])

    def forward_send(index):
        return pltpu.make_async_remote_copy(
            src_ref=y_s.at[rows_of(index)],
            dst_ref=h_s.at[rows_of(index)],
            send_sem=fwd_send.at[index],
            recv_sem=fwd_recv.at[index],
            device_id={"section": other},
            device_id_type=MESH,
        )

    def backward_send(index):
        return pltpu.make_async_remote_copy(
            src_ref=y_s.at[rows_of(index)],
            dst_ref=dy_s.at[rows_of(index)],
            send_sem=bwd_send.at[index],
            recv_sem=bwd_recv.at[index],
            device_id={"section": other},
            device_id_type=MESH,
        )

    backward_outs = ((q_s, 0), (k_s, 1), (v_s, 2), (da_s, 3), (df_s, 8))

    def act_copy(index):
        return pltpu.make_async_copy(y_s.at[rows_of(index)], act_out.at[rows_of(index)], out_sem.at[0, index])

    def dx_copy(index):
        return pltpu.make_async_copy(dx_s.at[rows_of(index)], dx_out.at[rows_of(index)], out_sem.at[1, index])

    def right_copies(index):
        for slot, (source, place) in enumerate(backward_outs):
            yield pltpu.make_async_copy(
                source.at[rows_of(index)], right_out.at[place, rows_of(index)], out_sem.at[2 + slot, index]
            )
        for panel in range(FF // D):
            yield pltpu.make_async_copy(
                g_s.at[rows_of(index), pl.ds(panel * D, D)],
                right_out.at[4 + panel, rows_of(index)],
                out_sem.at[7 + panel, index],
            )

    def turn_copy(slot, row):
        return pltpu.make_async_copy(
            turn_s.at[slot], left_out.at[pl.ds(pl.multiple_of(row, TURN), TURN)], turn_sem.at[slot]
        )

    def transpose_all():
        done = 0
        for source, tiles in ((h_s, D // TURN), (o_s, D // TURN), (n_s, D // TURN), (z_s, FF // TURN)):

            def tile_step(tile, carry, source=source, done=done):
                number = tile + done
                slot = lax.rem(number, 2)

                @pl.when(number >= 2)
                def _():
                    turn_copy(slot, (number - 2) * TURN).wait()

                turn_s[slot] = source[:, pl.ds(pl.multiple_of(tile * TURN, TURN), TURN)].T
                turn_copy(slot, number * TURN).start()
                return carry

            lax.fori_loop(0, tiles, tile_step, 0)
            done += tiles
        for number in (done - 2, done - 1):
            turn_copy(number % 2, number * TURN).wait()

    @pl.when(first)
    def _():
        for index in range(micro_count):
            entry_copy(index).start()

    @pl.when(last)
    def _():
        for index in range(micro_count):
            cot_copy(index).start()

    for index in range(6):
        weight_copy(index).start()

    acc_s[...] = jnp.zeros_like(acc_s)
    accu_s[...] = jnp.zeros_like(accu_s)

    bias = bias_in[0].astype(F32)
    gains = gains_in[0].astype(F32)
    shifts = shifts_in[0].astype(F32)
    low_half = lax.broadcasted_iota(jnp.int32, (1, 8, 128), 2) < HEAD_DIM
    lane = lax.broadcasted_iota(jnp.int32, (1, 16, PART), 2)
    keeps = [
        jnp.where((lane >= head * HEAD_DIM) & (lane < (head + 1) * HEAD_DIM), 1.0, 0.0).astype(BF16)
        for head in range(4)
    ]

    def stacked(quad_block):
        tiles = quad_block.reshape(-1, 16, PART)
        return jnp.concatenate([tiles * keep for keep in keeps], axis=0).reshape(4 * LENGTH, PART)

    def mixed_by(table, quad_block):
        tall = table.T
        parts = []
        for half in halves:
            start = 2 * LENGTH * (half.start // 128)
            tiles = dot(tall[start : start + 2 * LENGTH], quad_block[:, half]).reshape(2, LENGTH // 8, 8, 128)
            parts.append(jnp.where(low_half, tiles[0], tiles[1]).reshape(LENGTH, 128))
        return jnp.concatenate(parts, axis=1)

    pl.semaphore_wait(barrier, 1)

    blocks = [slice(r0, r0 + SUB) for r0 in range(0, ROWS, SUB)]
    columns = [slice(c0, c0 + PART) for c0 in range(0, D, PART)]
    panels = [slice(n0, n0 + WIDE) for n0 in range(0, FF, WIDE)]
    halves = [slice(0, 128), slice(128, 256)]
    count, chunks = len(columns), len(panels)

    def forward(index, carry):
        base = index * ROWS
        rows = rows_of(index)

        def at(block):
            return pl.ds(pl.multiple_of(base + block.start, SUB), SUB)

        @pl.when(first)
        def _():
            entry_copy(index).wait()
            start, stop = spans[0, index], spans[1, index]
            spot = lax.broadcasted_iota(jnp.int32, (LENGTH, D), 0)
            keep = (spot < start) | (spot >= stop)
            h_s[rows, :] = jnp.where(keep, h_s[rows, :].astype(F32), 0.0).astype(BF16)

        @pl.when(last)
        def _():
            forward_send(index).wait_recv()

        @pl.when(index == 0)
        def _():
            for number in range(4):
                weight_copy(number).wait()

        hidden = h_s[rows, :]

        def project(column):
            query = ((dot(hidden, wq_s[:, column]) + bias[0:1, column]) * 0.125).astype(BF16)
            key_rows = dot(hidden, wk_s[:, column]).astype(BF16)
            value = (dot(hidden, wv_s[:, column]) + bias[1:2, column]).astype(BF16)
            q_s[rows, column] = query
            k_s[rows, column] = key_rows
            v_s[rows, column] = value
            return query, key_rows, value

        spot = lax.broadcasted_iota(jnp.int32, (LENGTH - LEAST, 4 * LENGTH), 0) + LEAST
        penalty = jnp.where(spot < lengths[index], 0.0, -1000000000.0)
        projected, attends = {}, {}
        attended = None
        for step in range(count + 2):
            if step < count:
                projected[step] = project(columns[step])
            spot = step - 1
            if 0 <= spot < count:
                query, key_rows, _ = projected[spot]
                scores = dot_t(key_rows, stacked(query))
                held = jnp.concatenate([scores[:LEAST], scores[LEAST:] + penalty], axis=0)
                raised = jnp.exp(held - jnp.max(held, axis=0, keepdims=True))
                attends[spot] = (raised * (1.0 / jnp.sum(raised, axis=0, keepdims=True))).astype(BF16)
                p_s[index, spot] = attends[spot]
            spot = step - 2
            if 0 <= spot:
                mixture = mixed_by(attends[spot], projected[spot][2]).astype(BF16)
                o_s[rows, columns[spot]] = mixture
                product = dot(mixture, wo_s[columns[spot], :])
                attended = product if attended is None else attended + product

        for block in blocks:
            r = h_s[at(block), :].astype(F32) + attended[block] + bias[2:3]
            centered = r - jnp.mean(r, axis=-1, keepdims=True)
            inv = lax.rsqrt(jnp.mean(centered * centered, axis=-1, keepdims=True) + 1e-05)
            hat = centered * inv
            normed = hat * gains[0:1] + shifts[0:1]
            xa_s[at(block), :] = hat.astype(BF16)
            inva_s[at(block), :] = jnp.broadcast_to(inv, (SUB, 128))
            n_s[at(block), :] = normed.astype(BF16)
            wide_s[block, :] = normed

        @pl.when(index == 0)
        def _():
            weight_copy(4).wait()
            weight_copy(5).wait()

        normed_low = n_s[rows, :]
        lifted = {}
        outer = None
        for step in range(chunks + 2):
            if step < chunks:
                lifted[step] = dot(normed_low, w1_s[:, panels[step]])
            spot = step - 1
            if 0 <= spot < chunks:
                up_bias = up_bias_in[0:1, panels[spot]].astype(F32)
                for block in blocks:
                    act, slope = gelu_parts(lifted[spot][block] + up_bias)
                    z_s[at(block), panels[spot]] = act.astype(BF16)
                    g_s[at(block), panels[spot]] = slope.astype(BF16)
            spot = step - 2
            if 0 <= spot:
                product = dot(z_s[rows, panels[spot]], w2_s[panels[spot], :])
                outer = product if outer is None else outer + product

        for block in blocks:
            r = wide_s[block, :] + outer[block] + bias[3:4]
            centered = r - jnp.mean(r, axis=-1, keepdims=True)
            inv = lax.rsqrt(jnp.mean(centered * centered, axis=-1, keepdims=True) + 1e-05)
            hat = centered * inv
            xb_s[at(block), :] = hat.astype(BF16)
            invb_s[at(block), :] = jnp.broadcast_to(inv, (SUB, 128))
            y_s[at(block), :] = (hat * gains[1:2] + shifts[1:2]).astype(BF16)

        @pl.when(first)
        def _():
            forward_send(index).start()

        act_copy(index).start()
        return carry

    lax.fori_loop(0, micro_count, forward, 0)

    def forward_done(index, carry):
        @pl.when(first)
        def _():
            forward_send(index).wait_send()

        act_copy(index).wait()
        return carry

    lax.fori_loop(0, micro_count, forward_done, 0)

    @pl.when(first)
    def _():
        transpose_all()

    def backward(index, carry):
        base = index * ROWS
        rows = rows_of(index)

        def at(block):
            return pl.ds(pl.multiple_of(base + block.start, SUB), SUB)

        @pl.when(first)
        def _():
            backward_send(index).wait_recv()

        @pl.when(last)
        def _():
            cot_copy(index).wait()

        for block in blocks:
            dy = dy_s[at(block), :].astype(F32)
            hat = xb_s[at(block), :].astype(F32)
            acc_s[9] += fold(dy * hat)
            acc_s[11] += fold(dy)
            scaled = dy * gains[1:2]
            mean_plain = jnp.mean(scaled, axis=-1, keepdims=True)
            mean_hat = jnp.mean(scaled * hat, axis=-1, keepdims=True)
            grad = (scaled - mean_plain - hat * mean_hat) * invb_s[at(block), 0:1]
            wide_s[block, :] = grad
            df_s[at(block), :] = grad.astype(BF16)
            acc_s[3] += fold(grad)

        outer_low = df_s[rows, :]
        dropped = {}
        total = None
        for step in range(chunks + 2):
            if step < chunks:
                dropped[step] = dot_t(outer_low, w2_s[panels[step], :])
            spot = step - 1
            if 0 <= spot < chunks:
                sums = jnp.zeros((8, WIDE), F32)
                for block in blocks:
                    part = dropped[spot][block] * g_s[at(block), panels[spot]].astype(F32)
                    g_s[at(block), panels[spot]] = part.astype(BF16)
                    sums = sums + fold(part)
                accu_s[:, panels[spot]] += sums
            spot = step - 2
            if 0 <= spot:
                product = dot_t(g_s[rows, panels[spot]], w1_s[:, panels[spot]])
                total = product if total is None else total + product

        for block in blocks:
            dn = wide_s[block, :] + total[block]
            hat = xa_s[at(block), :].astype(F32)
            acc_s[8] += fold(dn * hat)
            acc_s[10] += fold(dn)
            scaled = dn * gains[0:1]
            mean_plain = jnp.mean(scaled, axis=-1, keepdims=True)
            mean_hat = jnp.mean(scaled * hat, axis=-1, keepdims=True)
            grad = (scaled - mean_plain - hat * mean_hat) * inva_s[at(block), 0:1]
            wide_s[block, :] = grad
            da_s[at(block), :] = grad.astype(BF16)
            acc_s[2] += fold(grad)

        attended_low = da_s[rows, :]
        mixed, scored, values_back = {}, {}, {}
        total = None
        for step in range(count + 2):
            if step < count:
                mixed[step] = dot_t(attended_low, wo_s[columns[step], :]).astype(BF16)
            spot = step - 1
            if 0 <= spot < count:
                tall = stacked(mixed[spot])
                grad_attend = dot_t(v_s[rows, columns[spot]], tall)
                values_back[spot] = dot(p_s[index, spot], tall)
                attend = p_s[index, spot].astype(F32)
                weighted = attend * grad_attend
                delta = jnp.sum(weighted, axis=0, keepdims=True) / jnp.sum(attend, axis=0, keepdims=True)
                scored[spot] = (weighted - attend * delta).astype(BF16)
            spot = step - 2
            if 0 <= spot:
                column = columns[spot]
                dk = dot(scored[spot], stacked(q_s[rows, column]))
                dq = mixed_by(scored[spot], k_s[rows, column]) * 0.125
                dv = values_back[spot]
                acc_s[0, :, column] += fold(dq)
                acc_s[1, :, column] += fold(dv)
                dq, dk, dv = dq.astype(BF16), dk.astype(BF16), dv.astype(BF16)
                q_s[rows, column] = dq
                k_s[rows, column] = dk
                v_s[rows, column] = dv
                for grad, weight in ((dq, wq_s), (dk, wk_s), (dv, wv_s)):
                    product = dot_t(grad, weight[:, column])
                    total = product if total is None else total + product

        @pl.when(last)
        def _():
            low = (wide_s[...] + total).astype(BF16)
            y_s[rows, :] = low
            dx_s[rows, :] = low.astype(F32)
            backward_send(index).start()

        @pl.when(first)
        def _():
            start, stop = spans[0, index], spans[1, index]
            spot = lax.broadcasted_iota(jnp.int32, (LENGTH, D), 0)
            keep = (spot < start) | (spot >= stop)
            dx_s[rows, :] = jnp.where(keep, wide_s[...] + total, 0.0)

        dx_copy(index).start()
        for copy in right_copies(index):
            copy.start()
        return carry

    lax.fori_loop(0, micro_count, backward, 0)

    @pl.when(last)
    def _():
        transpose_all()

    for number in range(12):
        if 4 <= number < 8:
            panel = accu_s[:, (number - 4) * D : (number - 3) * D]
        else:
            panel = acc_s[number]
        small_out[number : number + 1, :] = jnp.sum(panel, axis=0, keepdims=True)
    small_out[12:16, :] = jnp.zeros((4, D), F32)

    def backward_done(index, carry):
        @pl.when(last)
        def _():
            backward_send(index).wait_send()

        dx_copy(index).wait()
        for copy in right_copies(index):
            copy.wait()
        return carry

    lax.fori_loop(0, micro_count, backward_done, 0)


def run_layers(tokens, cotangent, lengths, spans, *weights):
    rows = tokens.shape[0]
    micro_count = rows // ROWS
    anywhere = pl.BlockSpec(memory_space=pl.ANY)
    scalars = pl.BlockSpec(memory_space=pltpu.SMEM)
    vectors = pl.BlockSpec(memory_space=pltpu.VMEM)
    out_shape = (
        jax.ShapeDtypeStruct((rows, D), BF16),
        jax.ShapeDtypeStruct((rows, D), F32),
        jax.ShapeDtypeStruct((3 * D + FF, rows), BF16),
        jax.ShapeDtypeStruct((9, rows, D), BF16),
        jax.ShapeDtypeStruct((16, D), F32),
    )

    def vm(count, width=D, dtype=BF16):
        return pltpu.VMEM((count, width), dtype)

    scratch = [
        vm(D), vm(D), vm(D), vm(D), vm(D, FF), vm(FF),
        vm(rows), vm(rows), vm(rows), vm(rows),
        pltpu.VMEM((micro_count, QUADS, LENGTH, 4 * LENGTH), BF16),
        vm(rows), vm(rows), vm(rows), vm(rows), vm(rows, FF), vm(rows, FF),
        vm(rows, 128, F32), vm(rows, 128, F32),
        vm(rows), vm(rows), vm(rows), vm(rows), vm(rows, D, F32),
        vm(ROWS, D, F32), pltpu.VMEM((2, TURN, rows), BF16), pltpu.VMEM((12, 8, D), F32), vm(8, FF, F32),
        pltpu.SemaphoreType.DMA((6,)),
        pltpu.SemaphoreType.DMA((micro_count,)),
        pltpu.SemaphoreType.DMA((11, micro_count)),
        pltpu.SemaphoreType.DMA((2,)),
        pltpu.SemaphoreType.DMA((micro_count,)),
        pltpu.SemaphoreType.DMA((micro_count,)),
        pltpu.SemaphoreType.DMA((micro_count,)),
        pltpu.SemaphoreType.DMA((micro_count,)),
    ]
    return pl.pallas_call(
        functools.partial(layers_kernel, micro_count),
        out_shape=out_shape,
        in_specs=[anywhere, anywhere, scalars, scalars] + [anywhere] * 6 + [vectors] * 4,
        out_specs=[anywhere] * 4 + [vectors],
        scratch_shapes=scratch,
        compiler_params=pltpu.CompilerParams(
            collective_id=0, has_side_effects=True, vmem_limit_bytes=60 * 1024 * 1024
        ),
        cost_estimate=pl.CostEstimate(
            flops=rows * 2 * 2 * 2 * 7077888, bytes_accessed=60000000, transcendentals=rows * FF * 2
        ),
    )(tokens, cotangent, lengths, spans.T, *weights)


RING = 8
PIECES = 3
PIECE = D // RING
PANELS = (
    (0, 0), (0, 1), (0, 2), (D, 3), (2 * D, 4), (2 * D, 5),
    (2 * D, 6), (2 * D, 7), (3 * D, 8), (4 * D, 8), (5 * D, 8), (6 * D, 8),
)


def sums_kernel(
    left, right, small_in, grads_out, small_out,
    left_s, right_s, total_s, give_s, take_s, ring_s, own_s,
    tiny_s, tiny_take_s, tiny_sum_s, tiny_go_s, tiny_ring_s, tiny_own_s,
    load_sem, give_sem, take_sem, ring_send, ring_recv, own_sem, round_send, round_recv, share_send, share_recv,
    tiny_sem, tiny_ring_send, tiny_ring_recv, tiny_round_send, tiny_round_recv,
):
    me = lax.axis_index("dp")
    core = lax.rem(me, 2)
    high = lax.rem(lax.div(me, 2), 2)
    depth = lax.div(me, 4)
    place = depth + high * (7 - 2 * depth)

    def device(spot, on_core):
        row = lax.div(spot, 4)
        return {"dp": 4 * (spot + row * (7 - 2 * spot)) + 2 * row + on_core}

    ahead = device(lax.rem(place + 1, RING), core)
    behind = device(lax.rem(place + RING - 1, RING), core)
    beside = device(place, 1 - core)
    targets = (ahead, behind)

    barrier = pltpu.get_barrier_semaphore()
    for peer in (ahead, behind, beside):
        pl.semaphore_signal(barrier, inc=1, device_id=peer, device_id_type=MESH)

    def block(way, step):
        return lax.rem(place - step + RING, RING) if way == 0 else lax.rem(place + step, RING)

    def late_block(way, step):
        return lax.rem(place + 1 - step + RING, RING) if way == 0 else lax.rem(place + RING - 1 + step, RING)

    def load_left(part):
        return pltpu.make_async_copy(left.at[pl.ds(part * D, D)], left_s.at[pl.ds(part * D, D)], load_sem.at[part])

    def load_right(part):
        return pltpu.make_async_copy(right.at[part], right_s.at[part], load_sem.at[7 + part])

    def remote(source, target, send, recv, peer):
        return pltpu.make_async_remote_copy(
            src_ref=source, dst_ref=target, send_sem=send, recv_sem=recv, device_id=peer, device_id_type=MESH
        )

    def give(way, step, piece):
        return remote(
            give_s.at[way, step, piece], take_s.at[way, step, piece],
            give_sem.at[way, step, piece], take_sem.at[way, step, piece], beside,
        )

    def ring_copy(way, step, piece):
        return remote(
            take_s.at[way, step, piece], ring_s.at[way, step, piece],
            ring_send.at[way, step, piece], ring_recv.at[way, step, piece], targets[way],
        )

    def region(way, spot, piece, on_core):
        rows = pl.ds(pl.multiple_of(spot * PIECE, PIECE), PIECE)
        return grads_out.at[6 * way + 3 * on_core + piece, rows]

    def own_copy(way, piece):
        return pltpu.make_async_copy(
            own_s.at[way, piece], region(way, late_block(way, 0), piece, core), own_sem.at[way, piece]
        )

    def round_copy(way, step, piece, source=None):
        target = region(way, late_block(way, step), piece, core)
        return remote(
            target if source is None else source, target,
            round_send.at[way, step, piece], round_recv.at[way, step, piece], targets[way],
        )

    def round_wait(way, step, piece):
        target = region(way, late_block(way, step + 1), piece, core)
        remote(
            target, target, round_send.at[way, step, piece], round_recv.at[way, step, piece], targets[way]
        ).wait_recv()

    def share_copy(way, step, piece, source=None):
        target = region(way, late_block(way, step), piece, core)
        return remote(
            target if source is None else source, target,
            share_send.at[way, step, piece], share_recv.at[way, step, piece], beside,
        )

    def share_wait(way, step, piece):
        target = region(way, late_block(way, step), piece, 1 - core)
        remote(
            target, target, share_send.at[way, step, piece], share_recv.at[way, step, piece], beside
        ).wait_recv()

    tiny_swap = remote(tiny_s, tiny_take_s, tiny_sem.at[0], tiny_sem.at[1], beside)

    def tiny_ring(step):
        return remote(
            tiny_go_s.at[step], tiny_ring_s.at[step], tiny_ring_send.at[step], tiny_ring_recv.at[step], ahead
        )

    def tiny_round(step):
        spot = late_block(0, step)
        return remote(
            tiny_own_s.at[spot], tiny_own_s.at[spot], tiny_round_send.at[step], tiny_round_recv.at[step], ahead
        )

    def tiny_round_wait(step):
        spot = late_block(0, step + 1)
        remote(
            tiny_own_s.at[spot], tiny_own_s.at[spot], tiny_round_send.at[step], tiny_round_recv.at[step], ahead
        ).wait_recv()

    loads = []
    for piece in range(PIECES):
        for way in range(2):
            for half in range(2):
                first_row, number = PANELS[6 * way + 3 * half + piece]
                for kind, part in ((load_right, number), (load_left, first_row // D)):
                    if (kind, part) not in [entry[:2] for entry in loads]:
                        loads.append((kind, part, way, piece))
    for kind, part, _, _ in loads:
        kind(part).start()

    for part in range(RING):
        if part * 128 < D:
            tiny_s[part] = small_in[:, part * 128 : part * 128 + 128]
        else:
            tiny_s[part] = jnp.zeros((16, 128), F32)

    pl.semaphore_wait(barrier, 3)
    tiny_swap.start()

    def product(group, way, piece, pick):
        near, far = PANELS[6 * way + piece], PANELS[6 * way + 3 + piece]
        first_row = near[0] + pick * (far[0] - near[0])
        number = near[1] + pick * (far[1] - near[1])
        blocks = []
        for step in (2 * group, 2 * group + 1):
            start = pl.multiple_of(first_row + block(way, step) * PIECE, PIECE)
            blocks.append(left_s[pl.ds(start, PIECE), :])
        return dot(jnp.concatenate(blocks, axis=0), right_s[number])

    def keep_product(group, way, piece, both):
        total_s[lax.rem(2 * group, 4), way, piece] = both[:PIECE]
        total_s[lax.rem(2 * group + 1, 4), way, piece] = both[PIECE:]

    def give_product(group, way, piece, both):
        give_s[way, 2 * group, piece] = both[:PIECE].astype(BF16)
        give_s[way, 2 * group + 1, piece] = both[PIECE:].astype(BF16)
        give(way, 2 * group, piece).start()
        give(way, 2 * group + 1, piece).start()

    def add_piece(step, way, piece, target):
        slot = lax.rem(step, 4)
        for r0 in range(0, PIECE, SUB):
            part = slice(r0, r0 + SUB)
            whole = total_s[slot, way, piece, part] + take_s[way, step, piece, part].astype(F32)
            target[part] = whole.astype(BF16)

    def reduce_step(step, carry):
        slot = lax.rem(step, 4)
        spot = block(0, step)

        @pl.when(step < RING - 1)
        def _():
            tiny_ring(step - 1).wait_recv()
            tiny_go_s[step] = tiny_sum_s[spot] + tiny_ring_s[step - 1]
            tiny_ring(step).start()

        @pl.when(step == RING - 1)
        def _():
            tiny_ring(step - 1).wait_recv()
            tiny_own_s[spot] = tiny_sum_s[spot] + tiny_ring_s[step - 1]
            tiny_round(0).start()

        for piece in range(PIECES):
            for way in range(2):
                give(way, step, piece).wait_recv()
                ring_copy(way, step - 1, piece).wait_recv()
                for r0 in range(0, PIECE, SUB):
                    part = slice(r0, r0 + SUB)
                    total_s[slot, way, piece, part] += ring_s[way, step - 1, piece, part].astype(F32)

                @pl.when(step < RING - 1)
                def _():
                    add_piece(step, way, piece, take_s.at[way, step, piece])
                    ring_copy(way, step, piece).start()

                @pl.when(step == RING - 1)
                def _():
                    add_piece(step, way, piece, own_s.at[way, piece])
                    round_copy(way, 0, piece, own_s.at[way, piece]).start()
                    share_copy(way, 0, piece, own_s.at[way, piece]).start()
                    own_copy(way, piece).start()

                @pl.when(step < RING - 2)
                def _():
                    odd = lax.rem(step, 2)
                    group = lax.div(step, 2) + 1
                    both = product(group, way, piece, odd * core + (1 - odd) * (1 - core))

                    @pl.when(odd == 1)
                    def _():
                        keep_product(group, way, piece, both)

                    @pl.when(odd == 0)
                    def _():
                        give_product(group, way, piece, both)

        return carry

    def first_piece(way, piece):
        give(way, 0, piece).wait_recv()
        add_piece(0, way, piece, take_s.at[way, 0, piece])
        ring_copy(way, 0, piece).start()

    order = [(way, piece) for piece in range(PIECES) for way in range(2)]
    for number, (way, piece) in enumerate(order):
        for kind, part, at_way, at_piece in loads:
            if (at_way, at_piece) == (way, piece):
                kind(part).wait()
        give_product(0, way, piece, product(0, way, piece, 1 - core))
        keep_product(0, way, piece, product(0, way, piece, core))
        if number > 0:
            first_piece(*order[number - 1])
    first_piece(*order[-1])
    for way, piece in order:
        give_product(1, way, piece, product(1, way, piece, 1 - core))
    tiny_swap.wait_recv()
    tiny_sum_s[...] = tiny_s[...] + tiny_take_s[...]
    tiny_go_s[0] = tiny_sum_s[block(0, 0)]
    tiny_ring(0).start()

    lax.fori_loop(1, RING, reduce_step, 0)

    def round_step(step, carry):
        tiny_round_wait(step - 1)

        @pl.when(step < RING - 1)
        def _():
            tiny_round(step).start()

        for piece in range(PIECES):
            for way in range(2):
                round_wait(way, step - 1, piece)

                @pl.when(step < RING - 1)
                def _():
                    round_copy(way, step, piece).start()

                share_copy(way, step, piece).start()
        return carry

    lax.fori_loop(1, RING, round_step, 0)

    for part in range(D // 128):
        small_out[:, part * 128 : part * 128 + 128] = tiny_own_s[part]
    tiny_swap.wait_send()

    def finish(step, carry):
        for way in range(2):
            for piece in range(PIECES):
                give(way, step, piece).wait_send()
                share_wait(way, step, piece)
                share_copy(way, step, piece).wait_send()

                @pl.when(step < RING - 1)
                def _():
                    ring_copy(way, step, piece).wait_send()
                    round_copy(way, step, piece).wait_send()

        @pl.when(step < RING - 1)
        def _():
            tiny_ring(step).wait_send()
            tiny_round(step).wait_send()

        return carry

    lax.fori_loop(0, RING, finish, 0)
    for way in range(2):
        for piece in range(PIECES):
            own_copy(way, piece).wait()


def run_sums(left, right, small):
    rows = right.shape[1]
    anywhere = pl.BlockSpec(memory_space=pl.ANY)
    vectors = pl.BlockSpec(memory_space=pltpu.VMEM)

    def pieces(*lead, dtype=BF16):
        return pltpu.VMEM((*lead, PIECE, D), dtype)

    dma = pltpu.SemaphoreType.DMA
    scratch = [
        pltpu.VMEM(left.shape, BF16), pltpu.VMEM(right.shape, BF16),
        pieces(4, 2, PIECES, dtype=F32), pieces(2, RING, PIECES), pieces(2, RING, PIECES),
        pieces(2, RING - 1, PIECES), pieces(2, PIECES),
        pltpu.VMEM((RING, 16, 128), F32), pltpu.VMEM((RING, 16, 128), F32), pltpu.VMEM((RING, 16, 128), F32),
        pltpu.VMEM((RING - 1, 16, 128), F32), pltpu.VMEM((RING - 1, 16, 128), F32), pltpu.VMEM((RING, 16, 128), F32),
        dma((16,)), dma((2, RING, PIECES)), dma((2, RING, PIECES)),
        dma((2, RING - 1, PIECES)), dma((2, RING - 1, PIECES)), dma((2, PIECES)),
        dma((2, RING - 1, PIECES)), dma((2, RING - 1, PIECES)), dma((2, RING, PIECES)), dma((2, RING, PIECES)),
        dma((2,)), dma((RING - 1,)), dma((RING - 1,)), dma((RING - 1,)), dma((RING - 1,)),
    ]
    return pl.pallas_call(
        sums_kernel,
        out_shape=(jax.ShapeDtypeStruct((12, D, D), BF16), jax.ShapeDtypeStruct((16, D), F32)),
        in_specs=[anywhere, anywhere, vectors],
        out_specs=[anywhere, vectors],
        scratch_shapes=scratch,
        compiler_params=pltpu.CompilerParams(
            collective_id=1, has_side_effects=True, vmem_limit_bytes=60 * 1024 * 1024
        ),
        cost_estimate=pl.CostEstimate(flops=rows * 2 * 7077888, bytes_accessed=70000000, transcendentals=0),
    )(left, right, small)


def plain_sums(left, right, small):
    panels = [dot(left[row : row + D], right[number]).astype(BF16) for row, number in PANELS]
    return lax.psum(jnp.stack(panels), "dp"), lax.psum(small, "dp")


SLOTS = 8
CUT = D // 2


def widen_kernel(
    act, dx, grads, small, act_out, dx_out, query_out, key_out, value_out, out_out, up_out, down_out,
    bias_out, up_bias_out, gain_out, shift_out, low_s, wide_s, act_s, dx_s, in_sem, out_sem, move_sem,
):
    moves_in = [
        pltpu.make_async_copy(act, act_s, move_sem.at[0]), pltpu.make_async_copy(dx, dx_s, move_sem.at[1])
    ]
    moves_out = [
        pltpu.make_async_copy(act_s, act_out.at[0], move_sem.at[0]),
        pltpu.make_async_copy(dx_s, dx_out.at[0], move_sem.at[1]),
    ]
    jobs = []
    for panel in range(12):
        for half in range(2):
            rows = pl.ds(half * CUT, CUT)
            if panel < 4:
                target = (query_out, key_out, value_out, out_out)[panel].at[0, rows]
            elif panel < 8:
                target = up_out.at[0, rows, pl.ds((panel - 4) * D, D)]
            else:
                target = down_out.at[0, pl.ds((panel - 8) * D + half * CUT, CUT)]
            jobs.append((grads.at[panel, rows], target))

    def fetch(number):
        return pltpu.make_async_copy(jobs[number][0], low_s.at[number % SLOTS], in_sem.at[number % SLOTS])

    def store(number):
        return pltpu.make_async_copy(wide_s.at[number % SLOTS], jobs[number][1], out_sem.at[number % SLOTS])

    for number in range(SLOTS):
        fetch(number).start()
    for move in moves_in:
        move.start()
    bias_out[0] = small[0:4]
    for panel in range(FF // D):
        up_bias_out[:, panel * D : (panel + 1) * D] = small[4 + panel : 5 + panel]
    gain_out[0] = small[8:10]
    shift_out[0] = small[10:12]
    for number in range(len(jobs)):
        slot = number % SLOTS
        fetch(number).wait()
        if number >= SLOTS:
            store(number - SLOTS).wait()

        def turn(step, carry):
            part = pl.ds(pl.multiple_of(step * SUB, SUB), SUB)
            wide_s[slot, part, :] = low_s[slot, part, :].astype(F32)
            return carry

        lax.fori_loop(0, CUT // SUB, turn, 0, unroll=4)
        store(number).start()
        if number == SLOTS:
            for move_in, move_out in zip(moves_in, moves_out):
                move_in.wait()
                move_out.start()
        if number + SLOTS < len(jobs):
            fetch(number + SLOTS).start()
    for number in range(len(jobs) - SLOTS, len(jobs)):
        store(number).wait()
    for move in moves_out:
        move.wait()


def widen(act, dx, grads, small):
    anywhere = pl.BlockSpec(memory_space=pl.ANY)
    vectors = pl.BlockSpec(memory_space=pltpu.VMEM)
    square = jax.ShapeDtypeStruct((1, D, D), F32)
    return pl.pallas_call(
        widen_kernel,
        out_shape=(
            jax.ShapeDtypeStruct((1, *act.shape), BF16), jax.ShapeDtypeStruct((1, *dx.shape), F32),
            square, square, square, square,
            jax.ShapeDtypeStruct((1, D, FF), F32), jax.ShapeDtypeStruct((1, FF, D), F32),
            jax.ShapeDtypeStruct((1, 4, D), F32), jax.ShapeDtypeStruct((1, FF), F32),
            jax.ShapeDtypeStruct((1, 2, D), F32), jax.ShapeDtypeStruct((1, 2, D), F32),
        ),
        in_specs=[anywhere, anywhere, anywhere, vectors],
        out_specs=[anywhere] * 8 + [vectors] * 4,
        scratch_shapes=[
            pltpu.VMEM((SLOTS, CUT, D), BF16), pltpu.VMEM((SLOTS, CUT, D), F32),
            pltpu.VMEM(act.shape, BF16), pltpu.VMEM(dx.shape, F32),
            pltpu.SemaphoreType.DMA((SLOTS,)), pltpu.SemaphoreType.DMA((SLOTS,)), pltpu.SemaphoreType.DMA((2,)),
        ],
        compiler_params=pltpu.CompilerParams(vmem_limit_bytes=60 * 1024 * 1024),
        cost_estimate=pl.CostEstimate(flops=7077888, bytes_accessed=42467328, transcendentals=0),
    )(act, dx, grads, small)


def per_device(grid, tokens, cotangent, lengths, spans, *weights):
    act, dx, left, right, small = run_layers(tokens, cotangent, lengths, spans, *weights)
    grads, small = (run_sums if grid else plain_sums)(left, right, small)
    return widen(act, dx, grads, small)


def solution(mesh):
    in_specs = (
        P("dp", None), P("dp", None), P("dp"), P("dp", None),
        P("section", None, None), P("section", None, None), P("section", None, None),
        P("section", None, None), P("section", None, None), P("section", None, None),
        P("section", None, None), P("section", None), P("section", None, None), P("section", None, None),
    )
    out_specs = (
        P("section", "dp", None), P("section", "dp", None),
        P("section", None, None), P("section", None, None), P("section", None, None),
        P("section", None, None), P("section", None, None), P("section", None, None),
        P("section", None, None), P("section", None), P("section", None, None), P("section", None, None),
    )
    part = functools.partial(per_device, mesh.shape["dp"] == 2 * RING)
    return jax.shard_map(part, mesh=mesh, in_specs=in_specs, out_specs=out_specs, check_vma=False)
```

```python
import functools

import jax
import jax.numpy as jnp
from jax import lax
from jax.experimental import pallas as pl
from jax.experimental.pallas import tpu as pltpu
from jax.sharding import PartitionSpec as P

D = 768
HEADS = 12
HEAD_DIM = 64
QUADS = HEADS // 4
FF = 3072
LENGTH = 160
LEAST = 96
ROWS = LENGTH
SUB = 32
WIDE = 512
TURN = 256
PART = 256

F32 = jnp.float32
BF16 = jnp.bfloat16
MESH = pl.DeviceIdType.MESH


def dot(left, right):
    return jnp.dot(left, right, preferred_element_type=F32)


def dot_t(left, right):
    return lax.dot_general(left, right, (((1,), (1,)), ((), ())), preferred_element_type=F32)


def fold(block):
    return jnp.sum(block.reshape(-1, 8, block.shape[-1]), axis=0)


def gelu_parts(u):
    t = pl.reciprocal(1.0 + 0.23164189 * jnp.abs(u), approx=True)
    gauss = jnp.exp2(u * u * -0.7213475204444817)
    poly = t * (
        0.127414796 + t * (-0.142248368 + t * (0.7107068705 + t * (-0.7265760135 + t * 0.5307027145)))
    )
    tail = poly * gauss
    cdf = jnp.where(u >= 0, 1.0 - tail, tail)
    return u * cdf, cdf + (u * 0.3989422804014327) * gauss


def layers_kernel(
    micro_count,
    tokens, cotangent, lengths, spans,
    wq, wk, wv, wo, w1, w2, bias_in, up_bias_in, gains_in, shifts_in,
    act_out, dx_out, left_out, right_out, small_out,
    wq_s, wk_s, wv_s, wo_s, w1_s, w2_s,
    h_s, q_s, k_s, v_s, p_s, o_s, n_s, xa_s, xb_s, z_s, g_s, inva_s, invb_s,
    y_s, dy_s, df_s, da_s, dx_s, wide_s, turn_s, acc_s, accu_s,
    w_sem, in_sem, out_sem, turn_sem, fwd_send, fwd_recv, bwd_send, bwd_recv,
):
    section = lax.axis_index("section")
    other = 1 - section
    first = section == 0
    last = section == 1

    barrier = pltpu.get_barrier_semaphore()
    pl.semaphore_signal(barrier, inc=1, device_id={"section": other}, device_id_type=MESH)

    weight_pairs = ((wq, wq_s), (wk, wk_s), (wv, wv_s), (wo, wo_s), (w1, w1_s), (w2, w2_s))

    def weight_copy(index):
        source, target = weight_pairs[index]
        return pltpu.make_async_copy(source.at[0], target, w_sem.at[index])

    def rows_of(index):
        return pl.ds(pl.multiple_of(index * ROWS, ROWS), ROWS)

    def entry_copy(index):
        return pltpu.make_async_copy(tokens.at[rows_of(index)], h_s.at[rows_of(index)], in_sem.at[index])

    def cot_copy(index):
        return pltpu.make_async_copy(cotangent.at[rows_of(index)], dy_s.at[rows_of(index)], in_sem.at[index])

    def forward_send(index):
        return pltpu.make_async_remote_copy(
            src_ref=y_s.at[rows_of(index)],
            dst_ref=h_s.at[rows_of(index)],
            send_sem=fwd_send.at[index],
            recv_sem=fwd_recv.at[index],
            device_id={"section": other},
            device_id_type=MESH,
        )

    def backward_send(index):
        return pltpu.make_async_remote_copy(
            src_ref=y_s.at[rows_of(index)],
            dst_ref=dy_s.at[rows_of(index)],
            send_sem=bwd_send.at[index],
            recv_sem=bwd_recv.at[index],
            device_id={"section": other},
            device_id_type=MESH,
        )

    backward_outs = ((q_s, 0), (k_s, 1), (v_s, 2), (da_s, 3), (df_s, 8))

    def act_copy(index):
        return pltpu.make_async_copy(y_s.at[rows_of(index)], act_out.at[rows_of(index)], out_sem.at[0, index])

    def dx_copy(index):
        return pltpu.make_async_copy(dx_s.at[rows_of(index)], dx_out.at[rows_of(index)], out_sem.at[1, index])

    def right_copies(index):
        for slot, (source, place) in enumerate(backward_outs):
            yield pltpu.make_async_copy(
                source.at[rows_of(index)], right_out.at[place, rows_of(index)], out_sem.at[2 + slot, index]
            )
        for panel in range(FF // D):
            yield pltpu.make_async_copy(
                g_s.at[rows_of(index), pl.ds(panel * D, D)],
                right_out.at[4 + panel, rows_of(index)],
                out_sem.at[7 + panel, index],
            )

    def turn_copy(slot, row):
        return pltpu.make_async_copy(
            turn_s.at[slot], left_out.at[pl.ds(pl.multiple_of(row, TURN), TURN)], turn_sem.at[slot]
        )

    def transpose_all():
        done = 0
        for source, tiles in ((h_s, D // TURN), (o_s, D // TURN), (n_s, D // TURN), (z_s, FF // TURN)):

            def tile_step(tile, carry, source=source, done=done):
                number = tile + done
                slot = lax.rem(number, 2)

                @pl.when(number >= 2)
                def _():
                    turn_copy(slot, (number - 2) * TURN).wait()

                turn_s[slot] = source[:, pl.ds(pl.multiple_of(tile * TURN, TURN), TURN)].T
                turn_copy(slot, number * TURN).start()
                return carry

            lax.fori_loop(0, tiles, tile_step, 0)
            done += tiles
        for number in (done - 2, done - 1):
            turn_copy(number % 2, number * TURN).wait()

    @pl.when(first)
    def _():
        for index in range(micro_count):
            entry_copy(index).start()

    @pl.when(last)
    def _():
        for index in range(micro_count):
            cot_copy(index).start()

    for index in range(6):
        weight_copy(index).start()

    acc_s[...] = jnp.zeros_like(acc_s)
    accu_s[...] = jnp.zeros_like(accu_s)

    bias = bias_in[0].astype(F32)
    gains = gains_in[0].astype(F32)
    shifts = shifts_in[0].astype(F32)
    low_half = lax.broadcasted_iota(jnp.int32, (1, 8, 128), 2) < HEAD_DIM
    lane = lax.broadcasted_iota(jnp.int32, (1, 16, PART), 2)
    keeps = [
        jnp.where((lane >= head * HEAD_DIM) & (lane < (head + 1) * HEAD_DIM), 1.0, 0.0).astype(BF16)
        for head in range(4)
    ]

    def stacked(quad_block):
        tiles = quad_block.reshape(-1, 16, PART)
        return jnp.concatenate([tiles * keep for keep in keeps], axis=0).reshape(4 * LENGTH, PART)

    def mixed_by(table, quad_block):
        tall = table.T
        parts = []
        for half in halves:
            start = 2 * LENGTH * (half.start // 128)
            tiles = dot(tall[start : start + 2 * LENGTH], quad_block[:, half]).reshape(2, LENGTH // 8, 8, 128)
            parts.append(jnp.where(low_half, tiles[0], tiles[1]).reshape(LENGTH, 128))
        return jnp.concatenate(parts, axis=1)

    pl.semaphore_wait(barrier, 1)

    blocks = [slice(r0, r0 + SUB) for r0 in range(0, ROWS, SUB)]
    columns = [slice(c0, c0 + PART) for c0 in range(0, D, PART)]
    panels = [slice(n0, n0 + WIDE) for n0 in range(0, FF, WIDE)]
    halves = [slice(0, 128), slice(128, 256)]
    count, chunks = len(columns), len(panels)

    def forward(index, carry):
        base = index * ROWS
        rows = rows_of(index)

        def at(block):
            return pl.ds(pl.multiple_of(base + block.start, SUB), SUB)

        @pl.when(first)
        def _():
            entry_copy(index).wait()
            start, stop = spans[0, index], spans[1, index]
            spot = lax.broadcasted_iota(jnp.int32, (LENGTH, D), 0)
            keep = (spot < start) | (spot >= stop)
            h_s[rows, :] = jnp.where(keep, h_s[rows, :].astype(F32), 0.0).astype(BF16)

        @pl.when(last)
        def _():
            forward_send(index).wait_recv()

        @pl.when(index == 0)
        def _():
            for number in range(4):
                weight_copy(number).wait()

        hidden = h_s[rows, :]

        def project(column):
            query = ((dot(hidden, wq_s[:, column]) + bias[0:1, column]) * 0.125).astype(BF16)
            key_rows = dot(hidden, wk_s[:, column]).astype(BF16)
            value = (dot(hidden, wv_s[:, column]) + bias[1:2, column]).astype(BF16)
            q_s[rows, column] = query
            k_s[rows, column] = key_rows
            v_s[rows, column] = value
            return query, key_rows, value

        spot = lax.broadcasted_iota(jnp.int32, (LENGTH - LEAST, 4 * LENGTH), 0) + LEAST
        penalty = jnp.where(spot < lengths[index], 0.0, -1000000000.0)
        projected, attends = {}, {}
        attended = None
        for step in range(count + 2):
            if step < count:
                projected[step] = project(columns[step])
            spot = step - 1
            if 0 <= spot < count:
                query, key_rows, _ = projected[spot]
                scores = dot_t(key_rows, stacked(query))
                held = jnp.concatenate([scores[:LEAST], scores[LEAST:] + penalty], axis=0)
                raised = jnp.exp(held - jnp.max(held, axis=0, keepdims=True))
                attends[spot] = (raised * (1.0 / jnp.sum(raised, axis=0, keepdims=True))).astype(BF16)
                p_s[index, spot] = attends[spot]
            spot = step - 2
            if 0 <= spot:
                mixture = mixed_by(attends[spot], projected[spot][2]).astype(BF16)
                o_s[rows, columns[spot]] = mixture
                product = dot(mixture, wo_s[columns[spot], :])
                attended = product if attended is None else attended + product

        for block in blocks:
            r = h_s[at(block), :].astype(F32) + attended[block] + bias[2:3]
            centered = r - jnp.mean(r, axis=-1, keepdims=True)
            inv = lax.rsqrt(jnp.mean(centered * centered, axis=-1, keepdims=True) + 1e-05)
            hat = centered * inv
            normed = hat * gains[0:1] + shifts[0:1]
            xa_s[at(block), :] = hat.astype(BF16)
            inva_s[at(block), :] = jnp.broadcast_to(inv, (SUB, 128))
            n_s[at(block), :] = normed.astype(BF16)
            wide_s[block, :] = normed

        @pl.when(index == 0)
        def _():
            weight_copy(4).wait()
            weight_copy(5).wait()

        normed_low = n_s[rows, :]
        lifted = {}
        outer = None
        for step in range(chunks + 2):
            if step < chunks:
                lifted[step] = dot(normed_low, w1_s[:, panels[step]])
            spot = step - 1
            if 0 <= spot < chunks:
                up_bias = up_bias_in[0:1, panels[spot]].astype(F32)
                for block in blocks:
                    act, slope = gelu_parts(lifted[spot][block] + up_bias)
                    z_s[at(block), panels[spot]] = act.astype(BF16)
                    g_s[at(block), panels[spot]] = slope.astype(BF16)
            spot = step - 2
            if 0 <= spot:
                product = dot(z_s[rows, panels[spot]], w2_s[panels[spot], :])
                outer = product if outer is None else outer + product

        for block in blocks:
            r = wide_s[block, :] + outer[block] + bias[3:4]
            centered = r - jnp.mean(r, axis=-1, keepdims=True)
            inv = lax.rsqrt(jnp.mean(centered * centered, axis=-1, keepdims=True) + 1e-05)
            hat = centered * inv
            xb_s[at(block), :] = hat.astype(BF16)
            invb_s[at(block), :] = jnp.broadcast_to(inv, (SUB, 128))
            y_s[at(block), :] = (hat * gains[1:2] + shifts[1:2]).astype(BF16)

        @pl.when(first)
        def _():
            forward_send(index).start()

        act_copy(index).start()
        return carry

    lax.fori_loop(0, micro_count, forward, 0)

    def forward_done(index, carry):
        @pl.when(first)
        def _():
            forward_send(index).wait_send()

        act_copy(index).wait()
        return carry

    lax.fori_loop(0, micro_count, forward_done, 0)

    @pl.when(first)
    def _():
        transpose_all()

    def backward(index, carry):
        base = index * ROWS
        rows = rows_of(index)

        def at(block):
            return pl.ds(pl.multiple_of(base + block.start, SUB), SUB)

        @pl.when(first)
        def _():
            backward_send(index).wait_recv()

        @pl.when(last)
        def _():
            cot_copy(index).wait()

        for block in blocks:
            dy = dy_s[at(block), :].astype(F32)
            hat = xb_s[at(block), :].astype(F32)
            acc_s[9] += fold(dy * hat)
            acc_s[11] += fold(dy)
            scaled = dy * gains[1:2]
            mean_plain = jnp.mean(scaled, axis=-1, keepdims=True)
            mean_hat = jnp.mean(scaled * hat, axis=-1, keepdims=True)
            grad = (scaled - mean_plain - hat * mean_hat) * invb_s[at(block), 0:1]
            wide_s[block, :] = grad
            df_s[at(block), :] = grad.astype(BF16)
            acc_s[3] += fold(grad)

        outer_low = df_s[rows, :]
        dropped = {}
        total = None
        for step in range(chunks + 2):
            if step < chunks:
                dropped[step] = dot_t(outer_low, w2_s[panels[step], :])
            spot = step - 1
            if 0 <= spot < chunks:
                sums = jnp.zeros((8, WIDE), F32)
                for block in blocks:
                    part = dropped[spot][block] * g_s[at(block), panels[spot]].astype(F32)
                    g_s[at(block), panels[spot]] = part.astype(BF16)
                    sums = sums + fold(part)
                accu_s[:, panels[spot]] += sums
            spot = step - 2
            if 0 <= spot:
                product = dot_t(g_s[rows, panels[spot]], w1_s[:, panels[spot]])
                total = product if total is None else total + product

        for block in blocks:
            dn = wide_s[block, :] + total[block]
            hat = xa_s[at(block), :].astype(F32)
            acc_s[8] += fold(dn * hat)
            acc_s[10] += fold(dn)
            scaled = dn * gains[0:1]
            mean_plain = jnp.mean(scaled, axis=-1, keepdims=True)
            mean_hat = jnp.mean(scaled * hat, axis=-1, keepdims=True)
            grad = (scaled - mean_plain - hat * mean_hat) * inva_s[at(block), 0:1]
            wide_s[block, :] = grad
            da_s[at(block), :] = grad.astype(BF16)
            acc_s[2] += fold(grad)

        attended_low = da_s[rows, :]
        mixed, scored, values_back = {}, {}, {}
        total = None
        for step in range(count + 2):
            if step < count:
                mixed[step] = dot_t(attended_low, wo_s[columns[step], :]).astype(BF16)
            spot = step - 1
            if 0 <= spot < count:
                tall = stacked(mixed[spot])
                grad_attend = dot_t(v_s[rows, columns[spot]], tall)
                values_back[spot] = dot(p_s[index, spot], tall)
                attend = p_s[index, spot].astype(F32)
                weighted = attend * grad_attend
                delta = jnp.sum(weighted, axis=0, keepdims=True) / jnp.sum(attend, axis=0, keepdims=True)
                scored[spot] = (weighted - attend * delta).astype(BF16)
            spot = step - 2
            if 0 <= spot:
                column = columns[spot]
                dk = dot(scored[spot], stacked(q_s[rows, column]))
                dq = mixed_by(scored[spot], k_s[rows, column]) * 0.125
                dv = values_back[spot]
                acc_s[0, :, column] += fold(dq)
                acc_s[1, :, column] += fold(dv)
                dq, dk, dv = dq.astype(BF16), dk.astype(BF16), dv.astype(BF16)
                q_s[rows, column] = dq
                k_s[rows, column] = dk
                v_s[rows, column] = dv
                for grad, weight in ((dq, wq_s), (dk, wk_s), (dv, wv_s)):
                    product = dot_t(grad, weight[:, column])
                    total = product if total is None else total + product

        @pl.when(last)
        def _():
            low = (wide_s[...] + total).astype(BF16)
            y_s[rows, :] = low
            dx_s[rows, :] = low.astype(F32)
            backward_send(index).start()

        @pl.when(first)
        def _():
            start, stop = spans[0, index], spans[1, index]
            spot = lax.broadcasted_iota(jnp.int32, (LENGTH, D), 0)
            keep = (spot < start) | (spot >= stop)
            dx_s[rows, :] = jnp.where(keep, wide_s[...] + total, 0.0)

        dx_copy(index).start()
        for copy in right_copies(index):
            copy.start()
        return carry

    lax.fori_loop(0, micro_count, backward, 0)

    @pl.when(last)
    def _():
        transpose_all()

    for number in range(12):
        if 4 <= number < 8:
            panel = accu_s[:, (number - 4) * D : (number - 3) * D]
        else:
            panel = acc_s[number]
        small_out[number : number + 1, :] = jnp.sum(panel, axis=0, keepdims=True)
    small_out[12:16, :] = jnp.zeros((4, D), F32)

    def backward_done(index, carry):
        @pl.when(last)
        def _():
            backward_send(index).wait_send()

        dx_copy(index).wait()
        for copy in right_copies(index):
            copy.wait()
        return carry

    lax.fori_loop(0, micro_count, backward_done, 0)


def run_layers(tokens, cotangent, lengths, spans, *weights):
    rows = tokens.shape[0]
    micro_count = rows // ROWS
    anywhere = pl.BlockSpec(memory_space=pl.ANY)
    scalars = pl.BlockSpec(memory_space=pltpu.SMEM)
    vectors = pl.BlockSpec(memory_space=pltpu.VMEM)
    out_shape = (
        jax.ShapeDtypeStruct((rows, D), BF16),
        jax.ShapeDtypeStruct((rows, D), F32),
        jax.ShapeDtypeStruct((3 * D + FF, rows), BF16),
        jax.ShapeDtypeStruct((9, rows, D), BF16),
        jax.ShapeDtypeStruct((16, D), F32),
    )

    def vm(count, width=D, dtype=BF16):
        return pltpu.VMEM((count, width), dtype)

    scratch = [
        vm(D), vm(D), vm(D), vm(D), vm(D, FF), vm(FF),
        vm(rows), vm(rows), vm(rows), vm(rows),
        pltpu.VMEM((micro_count, QUADS, LENGTH, 4 * LENGTH), BF16),
        vm(rows), vm(rows), vm(rows), vm(rows), vm(rows, FF), vm(rows, FF),
        vm(rows, 128, F32), vm(rows, 128, F32),
        vm(rows), vm(rows), vm(rows), vm(rows), vm(rows, D, F32),
        vm(ROWS, D, F32), pltpu.VMEM((2, TURN, rows), BF16), pltpu.VMEM((12, 8, D), F32), vm(8, FF, F32),
        pltpu.SemaphoreType.DMA((6,)),
        pltpu.SemaphoreType.DMA((micro_count,)),
        pltpu.SemaphoreType.DMA((11, micro_count)),
        pltpu.SemaphoreType.DMA((2,)),
        pltpu.SemaphoreType.DMA((micro_count,)),
        pltpu.SemaphoreType.DMA((micro_count,)),
        pltpu.SemaphoreType.DMA((micro_count,)),
        pltpu.SemaphoreType.DMA((micro_count,)),
    ]
    return pl.pallas_call(
        functools.partial(layers_kernel, micro_count),
        out_shape=out_shape,
        in_specs=[anywhere, anywhere, scalars, scalars] + [anywhere] * 6 + [vectors] * 4,
        out_specs=[anywhere] * 4 + [vectors],
        scratch_shapes=scratch,
        compiler_params=pltpu.CompilerParams(
            collective_id=0, has_side_effects=True, vmem_limit_bytes=60 * 1024 * 1024
        ),
        cost_estimate=pl.CostEstimate(
            flops=rows * 2 * 2 * 2 * 7077888, bytes_accessed=60000000, transcendentals=rows * FF * 2
        ),
    )(tokens, cotangent, lengths, spans.T, *weights)


RING = 8
PIECES = 3
PIECE = D // RING
PANELS = (
    (0, 0), (0, 1), (0, 2), (D, 3), (2 * D, 4), (2 * D, 5),
    (2 * D, 6), (2 * D, 7), (3 * D, 8), (4 * D, 8), (5 * D, 8), (6 * D, 8),
)


def sums_kernel(
    left, right, small_in, grads_out, small_out,
    left_s, right_s, total_s, give_s, take_s, ring_s,
    tiny_s, tiny_take_s, tiny_sum_s, tiny_go_s, tiny_ring_s, tiny_own_s,
    load_sem, give_sem, take_sem, ring_send, ring_recv, round_send, round_recv, share_send, share_recv,
    tiny_sem, tiny_ring_send, tiny_ring_recv, tiny_round_send, tiny_round_recv,
):
    me = lax.axis_index("dp")
    core = lax.rem(me, 2)
    high = lax.rem(lax.div(me, 2), 2)
    depth = lax.div(me, 4)
    place = depth + high * (7 - 2 * depth)

    def device(spot, on_core):
        row = lax.div(spot, 4)
        return {"dp": 4 * (spot + row * (7 - 2 * spot)) + 2 * row + on_core}

    ahead = device(lax.rem(place + 1, RING), core)
    behind = device(lax.rem(place + RING - 1, RING), core)
    beside = device(place, 1 - core)
    targets = (ahead, behind)

    barrier = pltpu.get_barrier_semaphore()
    for peer in (ahead, behind, beside):
        pl.semaphore_signal(barrier, inc=1, device_id=peer, device_id_type=MESH)

    def block(way, step):
        return lax.rem(place - step + RING, RING) if way == 0 else lax.rem(place + step, RING)

    def late_block(way, step):
        return lax.rem(place + 1 - step + RING, RING) if way == 0 else lax.rem(place + RING - 1 + step, RING)

    def load_left(part):
        return pltpu.make_async_copy(left.at[pl.ds(part * D, D)], left_s.at[pl.ds(part * D, D)], load_sem.at[part])

    def load_right(part):
        return pltpu.make_async_copy(right.at[part], right_s.at[part], load_sem.at[7 + part])

    def remote(source, target, send, recv, peer):
        return pltpu.make_async_remote_copy(
            src_ref=source, dst_ref=target, send_sem=send, recv_sem=recv, device_id=peer, device_id_type=MESH
        )

    def give(way, step, piece):
        return remote(
            give_s.at[way, lax.rem(step, 4), piece], take_s.at[way, step, piece],
            give_sem.at[way, step, piece], take_sem.at[way, step, piece], beside,
        )

    def ring_copy(way, step, piece):
        return remote(
            take_s.at[way, step, piece], ring_s.at[way, step, piece],
            ring_send.at[way, step, piece], ring_recv.at[way, step, piece], targets[way],
        )

    def region(way, spot, piece, on_core):
        rows = pl.ds(pl.multiple_of(spot * PIECE, PIECE), PIECE)
        return grads_out.at[6 * way + 3 * on_core + piece, rows]

    def round_copy(way, step, piece):
        target = region(way, late_block(way, step), piece, core)
        return remote(
            target, target, round_send.at[way, step, piece], round_recv.at[way, step, piece], targets[way]
        )

    def round_wait(way, step, piece):
        target = region(way, late_block(way, step + 1), piece, core)
        remote(
            target, target, round_send.at[way, step, piece], round_recv.at[way, step, piece], targets[way]
        ).wait_recv()

    def share_copy(way, step, piece):
        target = region(way, late_block(way, step), piece, core)
        return remote(
            target, target, share_send.at[way, step, piece], share_recv.at[way, step, piece], beside
        )

    def share_wait(way, step, piece):
        target = region(way, late_block(way, step), piece, 1 - core)
        remote(
            target, target, share_send.at[way, step, piece], share_recv.at[way, step, piece], beside
        ).wait_recv()

    tiny_swap = remote(tiny_s, tiny_take_s, tiny_sem.at[0], tiny_sem.at[1], beside)

    def tiny_ring(step):
        return remote(
            tiny_go_s.at[step], tiny_ring_s.at[step], tiny_ring_send.at[step], tiny_ring_recv.at[step], ahead
        )

    def tiny_round(step):
        spot = late_block(0, step)
        return remote(
            tiny_own_s.at[spot], tiny_own_s.at[spot], tiny_round_send.at[step], tiny_round_recv.at[step], ahead
        )

    def tiny_round_wait(step):
        spot = late_block(0, step + 1)
        remote(
            tiny_own_s.at[spot], tiny_own_s.at[spot], tiny_round_send.at[step], tiny_round_recv.at[step], ahead
        ).wait_recv()

    loads = []
    for piece in range(PIECES):
        for way in range(2):
            for half in range(2):
                first_row, number = PANELS[6 * way + 3 * half + piece]
                for kind, part in ((load_right, number), (load_left, first_row // D)):
                    if (kind, part) not in [entry[:2] for entry in loads]:
                        loads.append((kind, part, way, piece))
    for kind, part, _, _ in loads:
        kind(part).start()

    for part in range(RING):
        if part * 128 < D:
            tiny_s[part] = small_in[:, part * 128 : part * 128 + 128]
        else:
            tiny_s[part] = jnp.zeros((16, 128), F32)

    pl.semaphore_wait(barrier, 3)
    tiny_swap.start()

    def product(group, way, piece, pick):
        near, far = PANELS[6 * way + piece], PANELS[6 * way + 3 + piece]
        first_row = near[0] + pick * (far[0] - near[0])
        number = near[1] + pick * (far[1] - near[1])
        blocks = []
        for step in (2 * group, 2 * group + 1):
            start = pl.multiple_of(first_row + block(way, step) * PIECE, PIECE)
            blocks.append(left_s[pl.ds(start, PIECE), :])
        return dot(jnp.concatenate(blocks, axis=0), right_s[number])

    def keep_product(group, way, piece, both):
        total_s[lax.rem(2 * group, 3), way, piece] = both[:PIECE]
        total_s[lax.rem(2 * group + 1, 3), way, piece] = both[PIECE:]

    def give_product(group, way, piece, both):
        @pl.when(group >= 2)
        def _():
            give(way, 2 * group - 4, piece).wait_send()
            give(way, 2 * group - 3, piece).wait_send()

        give_s[way, lax.rem(2 * group, 4), piece] = both[:PIECE].astype(BF16)
        give_s[way, lax.rem(2 * group + 1, 4), piece] = both[PIECE:].astype(BF16)
        give(way, 2 * group, piece).start()
        give(way, 2 * group + 1, piece).start()

    def add_piece(step, way, piece, target):
        slot = lax.rem(step, 3)
        for r0 in range(0, PIECE, SUB):
            part = slice(r0, r0 + SUB)
            whole = total_s[slot, way, piece, part] + take_s[way, step, piece, part].astype(F32)
            target[part] = whole.astype(BF16)

    def reduce_step(step, carry):
        slot = lax.rem(step, 3)
        spot = block(0, step)

        @pl.when(step < RING - 1)
        def _():
            tiny_ring(step - 1).wait_recv()
            tiny_go_s[step] = tiny_sum_s[spot] + tiny_ring_s[step - 1]
            tiny_ring(step).start()

        @pl.when(step == RING - 1)
        def _():
            tiny_ring(step - 1).wait_recv()
            tiny_own_s[spot] = tiny_sum_s[spot] + tiny_ring_s[step - 1]
            tiny_round(0).start()

        for piece in range(PIECES):
            for way in range(2):
                give(way, step, piece).wait_recv()
                ring_copy(way, step - 1, piece).wait_recv()
                for r0 in range(0, PIECE, SUB):
                    part = slice(r0, r0 + SUB)
                    total_s[slot, way, piece, part] += ring_s[way, step - 1, piece, part].astype(F32)

                @pl.when(step < RING - 1)
                def _():
                    add_piece(step, way, piece, take_s.at[way, step, piece])
                    ring_copy(way, step, piece).start()

                @pl.when(step == RING - 1)
                def _():
                    add_piece(step, way, piece, region(way, late_block(way, 0), piece, core))
                    round_copy(way, 0, piece).start()
                    share_copy(way, 0, piece).start()

                @pl.when(step < RING - 2)
                def _():
                    odd = lax.rem(step, 2)
                    group = lax.div(step, 2) + 1
                    both = product(group, way, piece, odd * core + (1 - odd) * (1 - core))

                    @pl.when(odd == 1)
                    def _():
                        keep_product(group, way, piece, both)

                    @pl.when(odd == 0)
                    def _():
                        give_product(group, way, piece, both)

        return carry

    def first_piece(way, piece):
        give(way, 0, piece).wait_recv()
        add_piece(0, way, piece, take_s.at[way, 0, piece])
        ring_copy(way, 0, piece).start()

    order = [(way, piece) for piece in range(PIECES) for way in range(2)]
    for number, (way, piece) in enumerate(order):
        for kind, part, at_way, at_piece in loads:
            if (at_way, at_piece) == (way, piece):
                kind(part).wait()
        give_product(0, way, piece, product(0, way, piece, 1 - core))
        keep_product(0, way, piece, product(0, way, piece, core))
        if number > 0:
            first_piece(*order[number - 1])
    first_piece(*order[-1])
    for way, piece in order:
        give_product(1, way, piece, product(1, way, piece, 1 - core))
    tiny_swap.wait_recv()
    tiny_sum_s[...] = tiny_s[...] + tiny_take_s[...]
    tiny_go_s[0] = tiny_sum_s[block(0, 0)]
    tiny_ring(0).start()

    lax.fori_loop(1, RING, reduce_step, 0)

    def round_step(step, carry):
        tiny_round_wait(step - 1)

        @pl.when(step < RING - 1)
        def _():
            tiny_round(step).start()

        for piece in range(PIECES):
            for way in range(2):
                round_wait(way, step - 1, piece)

                @pl.when(step < RING - 1)
                def _():
                    round_copy(way, step, piece).start()

                share_copy(way, step, piece).start()
        return carry

    lax.fori_loop(1, RING, round_step, 0)

    for part in range(D // 128):
        small_out[:, part * 128 : part * 128 + 128] = tiny_own_s[part]
    tiny_swap.wait_send()

    def finish(step, carry):
        for way in range(2):
            for piece in range(PIECES):

                @pl.when(step >= RING // 2)
                def _():
                    give(way, step, piece).wait_send()

                share_wait(way, step, piece)
                share_copy(way, step, piece).wait_send()

                @pl.when(step < RING - 1)
                def _():
                    ring_copy(way, step, piece).wait_send()
                    round_copy(way, step, piece).wait_send()

        @pl.when(step < RING - 1)
        def _():
            tiny_ring(step).wait_send()
            tiny_round(step).wait_send()

        return carry

    lax.fori_loop(0, RING, finish, 0)


def run_sums(left, right, small):
    rows = right.shape[1]
    anywhere = pl.BlockSpec(memory_space=pl.ANY)
    vectors = pl.BlockSpec(memory_space=pltpu.VMEM)

    def pieces(*lead, dtype=BF16):
        return pltpu.VMEM((*lead, PIECE, D), dtype)

    dma = pltpu.SemaphoreType.DMA
    scratch = [
        pltpu.VMEM(left.shape, BF16), pltpu.VMEM(right.shape, BF16),
        pieces(3, 2, PIECES, dtype=F32), pieces(2, 4, PIECES), pieces(2, RING, PIECES),
        pieces(2, RING - 1, PIECES),
        pltpu.VMEM((RING, 16, 128), F32), pltpu.VMEM((RING, 16, 128), F32), pltpu.VMEM((RING, 16, 128), F32),
        pltpu.VMEM((RING - 1, 16, 128), F32), pltpu.VMEM((RING - 1, 16, 128), F32), pltpu.VMEM((RING, 16, 128), F32),
        dma((16,)), dma((2, RING, PIECES)), dma((2, RING, PIECES)),
        dma((2, RING - 1, PIECES)), dma((2, RING - 1, PIECES)),
        dma((2, RING - 1, PIECES)), dma((2, RING - 1, PIECES)), dma((2, RING, PIECES)), dma((2, RING, PIECES)),
        dma((2,)), dma((RING - 1,)), dma((RING - 1,)), dma((RING - 1,)), dma((RING - 1,)),
    ]
    return pl.pallas_call(
        sums_kernel,
        out_shape=(pltpu.VMEM((12, D, D), BF16), jax.ShapeDtypeStruct((16, D), F32)),
        in_specs=[anywhere, anywhere, vectors],
        out_specs=[vectors, vectors],
        scratch_shapes=scratch,
        compiler_params=pltpu.CompilerParams(
            collective_id=1, has_side_effects=True, vmem_limit_bytes=48 * 1024 * 1024
        ),
        cost_estimate=pl.CostEstimate(flops=rows * 2 * 7077888, bytes_accessed=70000000, transcendentals=0),
    )(left, right, small)


def plain_sums(left, right, small):
    panels = [dot(left[row : row + D], right[number]).astype(BF16) for row, number in PANELS]
    return lax.psum(jnp.stack(panels), "dp"), lax.psum(small, "dp")


SLOTS = 8
CUT = D // 2


def widen_kernel(
    act, dx, grads, small, act_out, dx_out, query_out, key_out, value_out, out_out, up_out, down_out,
    bias_out, up_bias_out, gain_out, shift_out, wide_s, act_s, dx_s, out_sem, move_sem,
):
    moves_in = [
        pltpu.make_async_copy(act, act_s, move_sem.at[0]), pltpu.make_async_copy(dx, dx_s, move_sem.at[1])
    ]
    moves_out = [
        pltpu.make_async_copy(act_s, act_out.at[0], move_sem.at[0]),
        pltpu.make_async_copy(dx_s, dx_out.at[0], move_sem.at[1]),
    ]
    jobs = []
    for panel in range(12):
        for half in range(2):
            rows = pl.ds(half * CUT, CUT)
            if panel < 4:
                target = (query_out, key_out, value_out, out_out)[panel].at[0, rows]
            elif panel < 8:
                target = up_out.at[0, rows, pl.ds((panel - 4) * D, D)]
            else:
                target = down_out.at[0, pl.ds((panel - 8) * D + half * CUT, CUT)]
            jobs.append((panel, half * CUT, target))

    def store(number):
        return pltpu.make_async_copy(wide_s.at[number % SLOTS], jobs[number][2], out_sem.at[number % SLOTS])

    for move in moves_in:
        move.start()
    bias_out[0] = small[0:4]
    for panel in range(FF // D):
        up_bias_out[:, panel * D : (panel + 1) * D] = small[4 + panel : 5 + panel]
    gain_out[0] = small[8:10]
    shift_out[0] = small[10:12]
    for number in range(len(jobs)):
        slot = number % SLOTS
        panel, start, _ = jobs[number]
        if number >= SLOTS:
            store(number - SLOTS).wait()

        def turn(step, carry):
            part = pl.ds(pl.multiple_of(step * SUB, SUB), SUB)
            here = pl.ds(pl.multiple_of(start + step * SUB, SUB), SUB)
            wide_s[slot, part, :] = grads[panel, here, :].astype(F32)
            return carry

        lax.fori_loop(0, CUT // SUB, turn, 0, unroll=4)
        store(number).start()
        if number == SLOTS:
            for move_in, move_out in zip(moves_in, moves_out):
                move_in.wait()
                move_out.start()
    for number in range(len(jobs) - SLOTS, len(jobs)):
        store(number).wait()
    for move in moves_out:
        move.wait()


def widen(act, dx, grads, small):
    anywhere = pl.BlockSpec(memory_space=pl.ANY)
    vectors = pl.BlockSpec(memory_space=pltpu.VMEM)
    square = jax.ShapeDtypeStruct((1, D, D), F32)
    return pl.pallas_call(
        widen_kernel,
        out_shape=(
            jax.ShapeDtypeStruct((1, *act.shape), BF16), jax.ShapeDtypeStruct((1, *dx.shape), F32),
            square, square, square, square,
            jax.ShapeDtypeStruct((1, D, FF), F32), jax.ShapeDtypeStruct((1, FF, D), F32),
            jax.ShapeDtypeStruct((1, 4, D), F32), jax.ShapeDtypeStruct((1, FF), F32),
            jax.ShapeDtypeStruct((1, 2, D), F32), jax.ShapeDtypeStruct((1, 2, D), F32),
        ),
        in_specs=[anywhere, anywhere, vectors, vectors],
        out_specs=[anywhere] * 8 + [vectors] * 4,
        scratch_shapes=[
            pltpu.VMEM((SLOTS, CUT, D), F32),
            pltpu.VMEM(act.shape, BF16), pltpu.VMEM(dx.shape, F32),
            pltpu.SemaphoreType.DMA((SLOTS,)), pltpu.SemaphoreType.DMA((2,)),
        ],
        compiler_params=pltpu.CompilerParams(vmem_limit_bytes=24 * 1024 * 1024),
        cost_estimate=pl.CostEstimate(flops=7077888, bytes_accessed=42467328, transcendentals=0),
    )(act, dx, grads, small)


def per_device(grid, tokens, cotangent, lengths, spans, *weights):
    act, dx, left, right, small = run_layers(tokens, cotangent, lengths, spans, *weights)
    grads, small = (run_sums if grid else plain_sums)(left, right, small)
    return widen(act, dx, grads, small)


def solution(mesh):
    in_specs = (
        P("dp", None), P("dp", None), P("dp"), P("dp", None),
        P("section", None, None), P("section", None, None), P("section", None, None),
        P("section", None, None), P("section", None, None), P("section", None, None),
        P("section", None, None), P("section", None), P("section", None, None), P("section", None, None),
    )
    out_specs = (
        P("section", "dp", None), P("section", "dp", None),
        P("section", None, None), P("section", None, None), P("section", None, None),
        P("section", None, None), P("section", None, None), P("section", None, None),
        P("section", None, None), P("section", None), P("section", None, None), P("section", None, None),
    )
    part = functools.partial(per_device, mesh.shape["dp"] == 2 * RING)
    return jax.shard_map(part, mesh=mesh, in_specs=in_specs, out_specs=out_specs, check_vma=False)
```

```python
import functools

import jax
import jax.numpy as jnp
from jax import lax
from jax.experimental import pallas as pl
from jax.experimental.pallas import tpu as pltpu
from jax.sharding import PartitionSpec as P

D = 768
HEADS = 12
HEAD_DIM = 64
QUADS = HEADS // 4
FF = 3072
LENGTH = 160
LEAST = 96
ROWS = LENGTH
SUB = 32
WIDE = 512
TURN = 256
PART = 256

F32 = jnp.float32
BF16 = jnp.bfloat16
MESH = pl.DeviceIdType.MESH


def dot(left, right):
    return jnp.dot(left, right, preferred_element_type=F32)


def dot_t(left, right):
    return lax.dot_general(left, right, (((1,), (1,)), ((), ())), preferred_element_type=F32)


def fold(block):
    return jnp.sum(block.reshape(-1, 8, block.shape[-1]), axis=0)


def gelu_parts(u):
    t = pl.reciprocal(1.0 + 0.23164189 * jnp.abs(u), approx=True)
    gauss = jnp.exp2(u * u * -0.7213475204444817)
    poly = t * (
        0.127414796 + t * (-0.142248368 + t * (0.7107068705 + t * (-0.7265760135 + t * 0.5307027145)))
    )
    tail = poly * gauss
    cdf = jnp.where(u >= 0, 1.0 - tail, tail)
    return u * cdf, cdf + (u * 0.3989422804014327) * gauss


def layers_kernel(
    micro_count,
    tokens, cotangent, lengths, spans,
    wq, wk, wv, wo, w1, w2, bias_in, up_bias_in, gains_in, shifts_in,
    act_out, dx_out, left_out, right_out, small_out,
    wq_s, wk_s, wv_s, wo_s, w1_s, w2_s,
    h_s, q_s, k_s, v_s, p_s, o_s, n_s, xa_s, xb_s, z_s, g_s, inva_s, invb_s,
    y_s, dy_s, df_s, da_s, dx_s, wide_s, turn_s, acc_s, accu_s,
    w_sem, in_sem, out_sem, turn_sem, fwd_send, fwd_recv, bwd_send, bwd_recv,
):
    section = lax.axis_index("section")
    other = 1 - section
    first = section == 0
    last = section == 1

    barrier = pltpu.get_barrier_semaphore()
    pl.semaphore_signal(barrier, inc=1, device_id={"section": other}, device_id_type=MESH)

    weight_pairs = ((wq, wq_s), (wk, wk_s), (wv, wv_s), (wo, wo_s), (w1, w1_s), (w2, w2_s))

    def weight_copy(index):
        source, target = weight_pairs[index]
        return pltpu.make_async_copy(source.at[0], target, w_sem.at[index])

    def rows_of(index):
        return pl.ds(pl.multiple_of(index * ROWS, ROWS), ROWS)

    def entry_copy(index):
        return pltpu.make_async_copy(tokens.at[rows_of(index)], h_s.at[rows_of(index)], in_sem.at[index])

    def cot_copy(index):
        return pltpu.make_async_copy(cotangent.at[rows_of(index)], dy_s.at[rows_of(index)], in_sem.at[index])

    def forward_send(index):
        return pltpu.make_async_remote_copy(
            src_ref=y_s.at[rows_of(index)],
            dst_ref=h_s.at[rows_of(index)],
            send_sem=fwd_send.at[index],
            recv_sem=fwd_recv.at[index],
            device_id={"section": other},
            device_id_type=MESH,
        )

    def backward_send(index):
        return pltpu.make_async_remote_copy(
            src_ref=y_s.at[rows_of(index)],
            dst_ref=dy_s.at[rows_of(index)],
            send_sem=bwd_send.at[index],
            recv_sem=bwd_recv.at[index],
            device_id={"section": other},
            device_id_type=MESH,
        )

    backward_outs = ((q_s, 0), (k_s, 1), (v_s, 2), (da_s, 3), (df_s, 8))

    def act_copy(index):
        return pltpu.make_async_copy(y_s.at[rows_of(index)], act_out.at[rows_of(index)], out_sem.at[0, index])

    def dx_copy(index):
        return pltpu.make_async_copy(dx_s.at[rows_of(index)], dx_out.at[rows_of(index)], out_sem.at[1, index])

    def right_copies(index):
        for slot, (source, place) in enumerate(backward_outs):
            yield pltpu.make_async_copy(
                source.at[rows_of(index)], right_out.at[place, rows_of(index)], out_sem.at[2 + slot, index]
            )
        for panel in range(FF // D):
            yield pltpu.make_async_copy(
                g_s.at[rows_of(index), pl.ds(panel * D, D)],
                right_out.at[4 + panel, rows_of(index)],
                out_sem.at[7 + panel, index],
            )

    def turn_copy(slot, row):
        return pltpu.make_async_copy(
            turn_s.at[slot], left_out.at[pl.ds(pl.multiple_of(row, TURN), TURN)], turn_sem.at[slot]
        )

    def transpose_all():
        done = 0
        for source, tiles in ((h_s, D // TURN), (o_s, D // TURN), (n_s, D // TURN), (z_s, FF // TURN)):

            def tile_step(tile, carry, source=source, done=done):
                number = tile + done
                slot = lax.rem(number, 2)

                @pl.when(number >= 2)
                def _():
                    turn_copy(slot, (number - 2) * TURN).wait()

                turn_s[slot] = source[:, pl.ds(pl.multiple_of(tile * TURN, TURN), TURN)].T
                turn_copy(slot, number * TURN).start()
                return carry

            lax.fori_loop(0, tiles, tile_step, 0)
            done += tiles
        for number in (done - 2, done - 1):
            turn_copy(number % 2, number * TURN).wait()

    @pl.when(first)
    def _():
        entry_copy(0).start()

    for index in range(4):
        weight_copy(index).start()

    acc_s[...] = jnp.zeros_like(acc_s)
    accu_s[...] = jnp.zeros_like(accu_s)

    bias = bias_in[0].astype(F32)
    gains = gains_in[0].astype(F32)
    shifts = shifts_in[0].astype(F32)
    low_half = lax.broadcasted_iota(jnp.int32, (1, 8, 128), 2) < HEAD_DIM
    lane = lax.broadcasted_iota(jnp.int32, (1, 16, PART), 2)
    keeps = [
        jnp.where((lane >= head * HEAD_DIM) & (lane < (head + 1) * HEAD_DIM), 1.0, 0.0).astype(BF16)
        for head in range(4)
    ]

    def stacked(quad_block):
        tiles = quad_block.reshape(-1, 16, PART)
        return jnp.concatenate([tiles * keep for keep in keeps], axis=0).reshape(4 * LENGTH, PART)

    def mixed_by(table, quad_block):
        tall = table.T
        parts = []
        for half in halves:
            start = 2 * LENGTH * (half.start // 128)
            tiles = dot(tall[start : start + 2 * LENGTH], quad_block[:, half]).reshape(2, LENGTH // 8, 8, 128)
            parts.append(jnp.where(low_half, tiles[0], tiles[1]).reshape(LENGTH, 128))
        return jnp.concatenate(parts, axis=1)

    pl.semaphore_wait(barrier, 1)

    blocks = [slice(r0, r0 + SUB) for r0 in range(0, ROWS, SUB)]
    columns = [slice(c0, c0 + PART) for c0 in range(0, D, PART)]
    panels = [slice(n0, n0 + WIDE) for n0 in range(0, FF, WIDE)]
    halves = [slice(0, 128), slice(128, 256)]
    count, chunks = len(columns), len(panels)

    def forward(index, carry):
        base = index * ROWS
        rows = rows_of(index)

        def at(block):
            return pl.ds(pl.multiple_of(base + block.start, SUB), SUB)

        @pl.when(index == 0)
        def _():
            for number in range(4):
                weight_copy(number).wait()
            for number in (4, 5):
                weight_copy(number).start()

            @pl.when(first)
            def _():
                for later in range(1, micro_count):
                    entry_copy(later).start()

            @pl.when(last)
            def _():
                for later in range(micro_count):
                    cot_copy(later).start()

        @pl.when(first)
        def _():
            entry_copy(index).wait()
            start, stop = spans[0, index], spans[1, index]
            spot = lax.broadcasted_iota(jnp.int32, (LENGTH, D), 0)
            keep = (spot < start) | (spot >= stop)
            h_s[rows, :] = jnp.where(keep, h_s[rows, :].astype(F32), 0.0).astype(BF16)

        @pl.when(last)
        def _():
            forward_send(index).wait_recv()

        hidden = h_s[rows, :]

        def project(column):
            query = ((dot(hidden, wq_s[:, column]) + bias[0:1, column]) * 0.125).astype(BF16)
            key_rows = dot(hidden, wk_s[:, column]).astype(BF16)
            value = (dot(hidden, wv_s[:, column]) + bias[1:2, column]).astype(BF16)
            q_s[rows, column] = query
            k_s[rows, column] = key_rows
            v_s[rows, column] = value
            return query, key_rows, value

        spot = lax.broadcasted_iota(jnp.int32, (LENGTH - LEAST, 4 * LENGTH), 0) + LEAST
        penalty = jnp.where(spot < lengths[index], 0.0, -1000000000.0)
        projected, attends = {}, {}
        attended = None
        for step in range(count + 2):
            if step < count:
                projected[step] = project(columns[step])
            spot = step - 1
            if 0 <= spot < count:
                query, key_rows, _ = projected[spot]
                scores = dot_t(key_rows, stacked(query))
                held = jnp.concatenate([scores[:LEAST], scores[LEAST:] + penalty], axis=0)
                raised = jnp.exp(held - jnp.max(held, axis=0, keepdims=True))
                attends[spot] = (raised * (1.0 / jnp.sum(raised, axis=0, keepdims=True))).astype(BF16)
                p_s[index, spot] = attends[spot]
            spot = step - 2
            if 0 <= spot:
                mixture = mixed_by(attends[spot], projected[spot][2]).astype(BF16)
                o_s[rows, columns[spot]] = mixture
                product = dot(mixture, wo_s[columns[spot], :])
                attended = product if attended is None else attended + product

        for block in blocks:
            r = h_s[at(block), :].astype(F32) + attended[block] + bias[2:3]
            centered = r - jnp.mean(r, axis=-1, keepdims=True)
            inv = lax.rsqrt(jnp.mean(centered * centered, axis=-1, keepdims=True) + 1e-05)
            hat = centered * inv
            normed = hat * gains[0:1] + shifts[0:1]
            xa_s[at(block), :] = hat.astype(BF16)
            inva_s[at(block), :] = jnp.broadcast_to(inv, (SUB, 128))
            n_s[at(block), :] = normed.astype(BF16)
            wide_s[block, :] = normed

        @pl.when(index == 0)
        def _():
            weight_copy(4).wait()
            weight_copy(5).wait()

        normed_low = n_s[rows, :]
        lifted = {}
        outer = None
        for step in range(chunks + 2):
            if step < chunks:
                lifted[step] = dot(normed_low, w1_s[:, panels[step]])
            spot = step - 1
            if 0 <= spot < chunks:
                up_bias = up_bias_in[0:1, panels[spot]].astype(F32)
                for block in blocks:
                    act, slope = gelu_parts(lifted[spot][block] + up_bias)
                    z_s[at(block), panels[spot]] = act.astype(BF16)
                    g_s[at(block), panels[spot]] = slope.astype(BF16)
            spot = step - 2
            if 0 <= spot:
                product = dot(z_s[rows, panels[spot]], w2_s[panels[spot], :])
                outer = product if outer is None else outer + product

        for block in blocks:
            r = wide_s[block, :] + outer[block] + bias[3:4]
            centered = r - jnp.mean(r, axis=-1, keepdims=True)
            inv = lax.rsqrt(jnp.mean(centered * centered, axis=-1, keepdims=True) + 1e-05)
            hat = centered * inv
            xb_s[at(block), :] = hat.astype(BF16)
            invb_s[at(block), :] = jnp.broadcast_to(inv, (SUB, 128))
            y_s[at(block), :] = (hat * gains[1:2] + shifts[1:2]).astype(BF16)

        @pl.when(first)
        def _():
            forward_send(index).start()

        act_copy(index).start()
        return carry

    lax.fori_loop(0, micro_count, forward, 0)

    def forward_done(index, carry):
        @pl.when(first)
        def _():
            forward_send(index).wait_send()

        act_copy(index).wait()
        return carry

    lax.fori_loop(0, micro_count, forward_done, 0)

    @pl.when(first)
    def _():
        transpose_all()

    def backward(index, carry):
        base = index * ROWS
        rows = rows_of(index)

        def at(block):
            return pl.ds(pl.multiple_of(base + block.start, SUB), SUB)

        @pl.when(first)
        def _():
            backward_send(index).wait_recv()

        @pl.when(last)
        def _():
            cot_copy(index).wait()

        for block in blocks:
            dy = dy_s[at(block), :].astype(F32)
            hat = xb_s[at(block), :].astype(F32)
            acc_s[9] += fold(dy * hat)
            acc_s[11] += fold(dy)
            scaled = dy * gains[1:2]
            mean_plain = jnp.mean(scaled, axis=-1, keepdims=True)
            mean_hat = jnp.mean(scaled * hat, axis=-1, keepdims=True)
            grad = (scaled - mean_plain - hat * mean_hat) * invb_s[at(block), 0:1]
            wide_s[block, :] = grad
            df_s[at(block), :] = grad.astype(BF16)
            acc_s[3] += fold(grad)

        outer_low = df_s[rows, :]
        dropped = {}
        total = None
        for step in range(chunks + 2):
            if step < chunks:
                dropped[step] = dot_t(outer_low, w2_s[panels[step], :])
            spot = step - 1
            if 0 <= spot < chunks:
                sums = jnp.zeros((8, WIDE), F32)
                for block in blocks:
                    part = dropped[spot][block] * g_s[at(block), panels[spot]].astype(F32)
                    g_s[at(block), panels[spot]] = part.astype(BF16)
                    sums = sums + fold(part)
                accu_s[:, panels[spot]] += sums
            spot = step - 2
            if 0 <= spot:
                product = dot_t(g_s[rows, panels[spot]], w1_s[:, panels[spot]])
                total = product if total is None else total + product

        for block in blocks:
            dn = wide_s[block, :] + total[block]
            hat = xa_s[at(block), :].astype(F32)
            acc_s[8] += fold(dn * hat)
            acc_s[10] += fold(dn)
            scaled = dn * gains[0:1]
            mean_plain = jnp.mean(scaled, axis=-1, keepdims=True)
            mean_hat = jnp.mean(scaled * hat, axis=-1, keepdims=True)
            grad = (scaled - mean_plain - hat * mean_hat) * inva_s[at(block), 0:1]
            wide_s[block, :] = grad
            da_s[at(block), :] = grad.astype(BF16)
            acc_s[2] += fold(grad)

        attended_low = da_s[rows, :]
        mixed, scored, values_back = {}, {}, {}
        total = None
        for step in range(count + 2):
            if step < count:
                mixed[step] = dot_t(attended_low, wo_s[columns[step], :]).astype(BF16)
            spot = step - 1
            if 0 <= spot < count:
                tall = stacked(mixed[spot])
                grad_attend = dot_t(v_s[rows, columns[spot]], tall)
                values_back[spot] = dot(p_s[index, spot], tall)
                attend = p_s[index, spot].astype(F32)
                weighted = attend * grad_attend
                delta = jnp.sum(weighted, axis=0, keepdims=True) / jnp.sum(attend, axis=0, keepdims=True)
                scored[spot] = (weighted - attend * delta).astype(BF16)
            spot = step - 2
            if 0 <= spot:
                column = columns[spot]
                dk = dot(scored[spot], stacked(q_s[rows, column]))
                dq = mixed_by(scored[spot], k_s[rows, column]) * 0.125
                dv = values_back[spot]
                acc_s[0, :, column] += fold(dq)
                acc_s[1, :, column] += fold(dv)
                dq, dk, dv = dq.astype(BF16), dk.astype(BF16), dv.astype(BF16)
                q_s[rows, column] = dq
                k_s[rows, column] = dk
                v_s[rows, column] = dv
                for grad, weight in ((dq, wq_s), (dk, wk_s), (dv, wv_s)):
                    product = dot_t(grad, weight[:, column])
                    total = product if total is None else total + product

        @pl.when(last)
        def _():
            low = (wide_s[...] + total).astype(BF16)
            y_s[rows, :] = low
            dx_s[rows, :] = low.astype(F32)
            backward_send(index).start()

        @pl.when(first)
        def _():
            start, stop = spans[0, index], spans[1, index]
            spot = lax.broadcasted_iota(jnp.int32, (LENGTH, D), 0)
            keep = (spot < start) | (spot >= stop)
            dx_s[rows, :] = jnp.where(keep, wide_s[...] + total, 0.0)

        dx_copy(index).start()
        for copy in right_copies(index):
            copy.start()
        return carry

    lax.fori_loop(0, micro_count, backward, 0)

    @pl.when(last)
    def _():
        transpose_all()

    for number in range(12):
        if 4 <= number < 8:
            panel = accu_s[:, (number - 4) * D : (number - 3) * D]
        else:
            panel = acc_s[number]
        small_out[number : number + 1, :] = jnp.sum(panel, axis=0, keepdims=True)
    small_out[12:16, :] = jnp.zeros((4, D), F32)

    def backward_done(index, carry):
        @pl.when(last)
        def _():
            backward_send(index).wait_send()

        dx_copy(index).wait()
        for copy in right_copies(index):
            copy.wait()
        return carry

    lax.fori_loop(0, micro_count, backward_done, 0)


def run_layers(tokens, cotangent, lengths, spans, *weights):
    rows = tokens.shape[0]
    micro_count = rows // ROWS
    anywhere = pl.BlockSpec(memory_space=pl.ANY)
    scalars = pl.BlockSpec(memory_space=pltpu.SMEM)
    vectors = pl.BlockSpec(memory_space=pltpu.VMEM)
    out_shape = (
        jax.ShapeDtypeStruct((rows, D), BF16),
        jax.ShapeDtypeStruct((rows, D), F32),
        jax.ShapeDtypeStruct((3 * D + FF, rows), BF16),
        jax.ShapeDtypeStruct((9, rows, D), BF16),
        jax.ShapeDtypeStruct((16, D), F32),
    )

    def vm(count, width=D, dtype=BF16):
        return pltpu.VMEM((count, width), dtype)

    scratch = [
        vm(D), vm(D), vm(D), vm(D), vm(D, FF), vm(FF),
        vm(rows), vm(rows), vm(rows), vm(rows),
        pltpu.VMEM((micro_count, QUADS, LENGTH, 4 * LENGTH), BF16),
        vm(rows), vm(rows), vm(rows), vm(rows), vm(rows, FF), vm(rows, FF),
        vm(rows, 128, F32), vm(rows, 128, F32),
        vm(rows), vm(rows), vm(rows), vm(rows), vm(rows, D, F32),
        vm(ROWS, D, F32), pltpu.VMEM((2, TURN, rows), BF16), pltpu.VMEM((12, 8, D), F32), vm(8, FF, F32),
        pltpu.SemaphoreType.DMA((6,)),
        pltpu.SemaphoreType.DMA((micro_count,)),
        pltpu.SemaphoreType.DMA((11, micro_count)),
        pltpu.SemaphoreType.DMA((2,)),
        pltpu.SemaphoreType.DMA((micro_count,)),
        pltpu.SemaphoreType.DMA((micro_count,)),
        pltpu.SemaphoreType.DMA((micro_count,)),
        pltpu.SemaphoreType.DMA((micro_count,)),
    ]
    return pl.pallas_call(
        functools.partial(layers_kernel, micro_count),
        out_shape=out_shape,
        in_specs=[anywhere, anywhere, scalars, scalars] + [anywhere] * 6 + [vectors] * 4,
        out_specs=[anywhere] * 4 + [vectors],
        scratch_shapes=scratch,
        compiler_params=pltpu.CompilerParams(
            collective_id=0, has_side_effects=True, vmem_limit_bytes=60 * 1024 * 1024
        ),
        cost_estimate=pl.CostEstimate(
            flops=rows * 2 * 2 * 2 * 7077888, bytes_accessed=60000000, transcendentals=rows * FF * 2
        ),
    )(tokens, cotangent, lengths, spans.T, *weights)


RING = 8
PIECES = 3
PIECE = D // RING
PANELS = (
    (0, 0), (0, 1), (0, 2), (D, 3), (2 * D, 4), (2 * D, 5),
    (2 * D, 6), (2 * D, 7), (3 * D, 8), (4 * D, 8), (5 * D, 8), (6 * D, 8),
)


def sums_kernel(
    left, right, small_in, grads_out, small_out,
    left_s, right_s, total_s, give_s, take_s, ring_s,
    tiny_s, tiny_take_s, tiny_sum_s, tiny_go_s, tiny_ring_s, tiny_own_s,
    load_sem, give_sem, take_sem, ring_send, ring_recv, round_send, round_recv, share_send, share_recv,
    tiny_sem, tiny_ring_send, tiny_ring_recv, tiny_round_send, tiny_round_recv,
):
    me = lax.axis_index("dp")
    core = lax.rem(me, 2)
    high = lax.rem(lax.div(me, 2), 2)
    depth = lax.div(me, 4)
    place = depth + high * (7 - 2 * depth)

    def device(spot, on_core):
        row = lax.div(spot, 4)
        return {"dp": 4 * (spot + row * (7 - 2 * spot)) + 2 * row + on_core}

    ahead = device(lax.rem(place + 1, RING), core)
    behind = device(lax.rem(place + RING - 1, RING), core)
    beside = device(place, 1 - core)
    targets = (ahead, behind)

    barrier = pltpu.get_barrier_semaphore()
    for peer in (ahead, behind, beside):
        pl.semaphore_signal(barrier, inc=1, device_id=peer, device_id_type=MESH)

    def block(way, step):
        return lax.rem(place - step + RING, RING) if way == 0 else lax.rem(place + step, RING)

    def late_block(way, step):
        return lax.rem(place + 1 - step + RING, RING) if way == 0 else lax.rem(place + RING - 1 + step, RING)

    def load_left(part):
        return pltpu.make_async_copy(left.at[pl.ds(part * D, D)], left_s.at[pl.ds(part * D, D)], load_sem.at[part])

    def load_right(part):
        return pltpu.make_async_copy(right.at[part], right_s.at[part], load_sem.at[7 + part])

    def remote(source, target, send, recv, peer):
        return pltpu.make_async_remote_copy(
            src_ref=source, dst_ref=target, send_sem=send, recv_sem=recv, device_id=peer, device_id_type=MESH
        )

    def give(way, step, piece):
        return remote(
            give_s.at[way, lax.rem(step, 4), piece], take_s.at[way, step, piece],
            give_sem.at[way, step, piece], take_sem.at[way, step, piece], beside,
        )

    def ring_copy(way, step, piece):
        return remote(
            take_s.at[way, step, piece], ring_s.at[way, step, piece],
            ring_send.at[way, step, piece], ring_recv.at[way, step, piece], targets[way],
        )

    def region(way, spot, piece, on_core):
        rows = pl.ds(pl.multiple_of(spot * PIECE, PIECE), PIECE)
        return grads_out.at[6 * way + 3 * on_core + piece, rows]

    def round_copy(way, step, piece):
        target = region(way, late_block(way, step), piece, core)
        return remote(
            target, target, round_send.at[way, step, piece], round_recv.at[way, step, piece], targets[way]
        )

    def round_wait(way, step, piece):
        target = region(way, late_block(way, step + 1), piece, core)
        remote(
            target, target, round_send.at[way, step, piece], round_recv.at[way, step, piece], targets[way]
        ).wait_recv()

    def share_copy(way, step, piece):
        target = region(way, late_block(way, step), piece, core)
        return remote(
            target, target, share_send.at[way, step, piece], share_recv.at[way, step, piece], beside
        )

    def share_wait(way, step, piece):
        target = region(way, late_block(way, step), piece, 1 - core)
        remote(
            target, target, share_send.at[way, step, piece], share_recv.at[way, step, piece], beside
        ).wait_recv()

    tiny_swap = remote(tiny_s, tiny_take_s, tiny_sem.at[0], tiny_sem.at[1], beside)

    def tiny_ring(step):
        return remote(
            tiny_go_s.at[step], tiny_ring_s.at[step], tiny_ring_send.at[step], tiny_ring_recv.at[step], ahead
        )

    def tiny_round(step):
        spot = late_block(0, step)
        return remote(
            tiny_own_s.at[spot], tiny_own_s.at[spot], tiny_round_send.at[step], tiny_round_recv.at[step], ahead
        )

    def tiny_round_wait(step):
        spot = late_block(0, step + 1)
        remote(
            tiny_own_s.at[spot], tiny_own_s.at[spot], tiny_round_send.at[step], tiny_round_recv.at[step], ahead
        ).wait_recv()

    loads = []
    for piece in range(PIECES):
        for way in range(2):
            for half in range(2):
                first_row, number = PANELS[6 * way + 3 * half + piece]
                for kind, part in ((load_right, number), (load_left, first_row // D)):
                    if (kind, part) not in [entry[:2] for entry in loads]:
                        loads.append((kind, part, way, piece))
    order = [(way, piece) for piece in range(PIECES) for way in range(2)]
    groups = [[kind(part) for kind, part, *spot in loads if tuple(spot) == pair] for pair in order]
    for group in groups[:2]:
        for copy in group:
            copy.start()

    for part in range(RING):
        if part * 128 < D:
            tiny_s[part] = small_in[:, part * 128 : part * 128 + 128]
        else:
            tiny_s[part] = jnp.zeros((16, 128), F32)

    pl.semaphore_wait(barrier, 3)
    tiny_swap.start()

    def product(group, way, piece, pick):
        near, far = PANELS[6 * way + piece], PANELS[6 * way + 3 + piece]
        first_row = near[0] + pick * (far[0] - near[0])
        number = near[1] + pick * (far[1] - near[1])
        blocks = []
        for step in (2 * group, 2 * group + 1):
            start = pl.multiple_of(first_row + block(way, step) * PIECE, PIECE)
            blocks.append(left_s[pl.ds(start, PIECE), :])
        return dot(jnp.concatenate(blocks, axis=0), right_s[number])

    def keep_product(group, way, piece, both):
        total_s[lax.rem(2 * group, 3), way, piece] = both[:PIECE]
        total_s[lax.rem(2 * group + 1, 3), way, piece] = both[PIECE:]

    def give_product(group, way, piece, both):
        @pl.when(group >= 2)
        def _():
            give(way, 2 * group - 4, piece).wait_send()
            give(way, 2 * group - 3, piece).wait_send()

        give_s[way, lax.rem(2 * group, 4), piece] = both[:PIECE].astype(BF16)
        give_s[way, lax.rem(2 * group + 1, 4), piece] = both[PIECE:].astype(BF16)
        give(way, 2 * group, piece).start()
        give(way, 2 * group + 1, piece).start()

    def add_piece(step, way, piece, target):
        slot = lax.rem(step, 3)
        for r0 in range(0, PIECE, SUB):
            part = slice(r0, r0 + SUB)
            whole = total_s[slot, way, piece, part] + take_s[way, step, piece, part].astype(F32)
            target[part] = whole.astype(BF16)

    def reduce_step(step, carry):
        slot = lax.rem(step, 3)
        spot = block(0, step)

        @pl.when(step < RING - 1)
        def _():
            tiny_ring(step - 1).wait_recv()
            tiny_go_s[step] = tiny_sum_s[spot] + tiny_ring_s[step - 1]
            tiny_ring(step).start()

        @pl.when(step == RING - 1)
        def _():
            tiny_ring(step - 1).wait_recv()
            tiny_own_s[spot] = tiny_sum_s[spot] + tiny_ring_s[step - 1]
            tiny_round(0).start()

        for piece in range(PIECES):
            for way in range(2):
                give(way, step, piece).wait_recv()
                ring_copy(way, step - 1, piece).wait_recv()
                for r0 in range(0, PIECE, SUB):
                    part = slice(r0, r0 + SUB)
                    total_s[slot, way, piece, part] += ring_s[way, step - 1, piece, part].astype(F32)

                @pl.when(step < RING - 1)
                def _():
                    add_piece(step, way, piece, take_s.at[way, step, piece])
                    ring_copy(way, step, piece).start()

                @pl.when(step == RING - 1)
                def _():
                    add_piece(step, way, piece, region(way, late_block(way, 0), piece, core))
                    round_copy(way, 0, piece).start()
                    share_copy(way, 0, piece).start()

                @pl.when(step < RING - 2)
                def _():
                    odd = lax.rem(step, 2)
                    group = lax.div(step, 2) + 1
                    both = product(group, way, piece, odd * core + (1 - odd) * (1 - core))

                    @pl.when(odd == 1)
                    def _():
                        keep_product(group, way, piece, both)

                    @pl.when(odd == 0)
                    def _():
                        give_product(group, way, piece, both)

        return carry

    def first_piece(way, piece):
        give(way, 0, piece).wait_recv()
        add_piece(0, way, piece, take_s.at[way, 0, piece])
        ring_copy(way, 0, piece).start()

    for number, (way, piece) in enumerate(order):
        for copy in groups[number]:
            copy.wait()
        if number + 2 < len(groups):
            for copy in groups[number + 2]:
                copy.start()
        give_product(0, way, piece, product(0, way, piece, 1 - core))
        keep_product(0, way, piece, product(0, way, piece, core))
        if number > 0:
            first_piece(*order[number - 1])
    first_piece(*order[-1])
    for way, piece in order:
        give_product(1, way, piece, product(1, way, piece, 1 - core))
    tiny_swap.wait_recv()
    tiny_sum_s[...] = tiny_s[...] + tiny_take_s[...]
    tiny_go_s[0] = tiny_sum_s[block(0, 0)]
    tiny_ring(0).start()

    lax.fori_loop(1, RING, reduce_step, 0)

    def round_step(step, carry):
        tiny_round_wait(step - 1)

        @pl.when(step < RING - 1)
        def _():
            tiny_round(step).start()

        for piece in range(PIECES):
            for way in range(2):
                round_wait(way, step - 1, piece)

                @pl.when(step < RING - 1)
                def _():
                    round_copy(way, step, piece).start()

                share_copy(way, step, piece).start()
        return carry

    lax.fori_loop(1, RING, round_step, 0)

    for part in range(D // 128):
        small_out[:, part * 128 : part * 128 + 128] = tiny_own_s[part]
    tiny_swap.wait_send()

    def finish(step, carry):
        for way in range(2):
            for piece in range(PIECES):

                @pl.when(step >= RING // 2)
                def _():
                    give(way, step, piece).wait_send()

                share_wait(way, step, piece)
                share_copy(way, step, piece).wait_send()

                @pl.when(step < RING - 1)
                def _():
                    ring_copy(way, step, piece).wait_send()
                    round_copy(way, step, piece).wait_send()

        @pl.when(step < RING - 1)
        def _():
            tiny_ring(step).wait_send()
            tiny_round(step).wait_send()

        return carry

    lax.fori_loop(0, RING, finish, 0)


def run_sums(left, right, small):
    rows = right.shape[1]
    anywhere = pl.BlockSpec(memory_space=pl.ANY)
    vectors = pl.BlockSpec(memory_space=pltpu.VMEM)

    def pieces(*lead, dtype=BF16):
        return pltpu.VMEM((*lead, PIECE, D), dtype)

    dma = pltpu.SemaphoreType.DMA
    scratch = [
        pltpu.VMEM(left.shape, BF16), pltpu.VMEM(right.shape, BF16),
        pieces(3, 2, PIECES, dtype=F32), pieces(2, 4, PIECES), pieces(2, RING, PIECES),
        pieces(2, RING - 1, PIECES),
        pltpu.VMEM((RING, 16, 128), F32), pltpu.VMEM((RING, 16, 128), F32), pltpu.VMEM((RING, 16, 128), F32),
        pltpu.VMEM((RING - 1, 16, 128), F32), pltpu.VMEM((RING - 1, 16, 128), F32), pltpu.VMEM((RING, 16, 128), F32),
        dma((16,)), dma((2, RING, PIECES)), dma((2, RING, PIECES)),
        dma((2, RING - 1, PIECES)), dma((2, RING - 1, PIECES)),
        dma((2, RING - 1, PIECES)), dma((2, RING - 1, PIECES)), dma((2, RING, PIECES)), dma((2, RING, PIECES)),
        dma((2,)), dma((RING - 1,)), dma((RING - 1,)), dma((RING - 1,)), dma((RING - 1,)),
    ]
    return pl.pallas_call(
        sums_kernel,
        out_shape=(pltpu.VMEM((12, D, D), BF16), jax.ShapeDtypeStruct((16, D), F32)),
        in_specs=[anywhere, anywhere, vectors],
        out_specs=[vectors, vectors],
        scratch_shapes=scratch,
        compiler_params=pltpu.CompilerParams(
            collective_id=1, has_side_effects=True, vmem_limit_bytes=48 * 1024 * 1024
        ),
        cost_estimate=pl.CostEstimate(flops=rows * 2 * 7077888, bytes_accessed=70000000, transcendentals=0),
    )(left, right, small)


def plain_sums(left, right, small):
    panels = [dot(left[row : row + D], right[number]).astype(BF16) for row, number in PANELS]
    return lax.psum(jnp.stack(panels), "dp"), lax.psum(small, "dp")


SLOTS = 8
CUT = D // 2


def widen_kernel(
    act, dx, grads, small, act_out, dx_out, query_out, key_out, value_out, out_out, up_out, down_out,
    bias_out, up_bias_out, gain_out, shift_out, wide_s, act_s, dx_s, out_sem, move_sem,
):
    moves_in = [
        pltpu.make_async_copy(act, act_s, move_sem.at[0]), pltpu.make_async_copy(dx, dx_s, move_sem.at[1])
    ]
    moves_out = [
        pltpu.make_async_copy(act_s, act_out.at[0], move_sem.at[0]),
        pltpu.make_async_copy(dx_s, dx_out.at[0], move_sem.at[1]),
    ]
    jobs = []
    for panel in range(12):
        for half in range(2):
            rows = pl.ds(half * CUT, CUT)
            if panel < 4:
                target = (query_out, key_out, value_out, out_out)[panel].at[0, rows]
            elif panel < 8:
                target = up_out.at[0, rows, pl.ds((panel - 4) * D, D)]
            else:
                target = down_out.at[0, pl.ds((panel - 8) * D + half * CUT, CUT)]
            jobs.append((panel, half * CUT, target))

    def store(number):
        return pltpu.make_async_copy(wide_s.at[number % SLOTS], jobs[number][2], out_sem.at[number % SLOTS])

    for move in moves_in:
        move.start()
    bias_out[0] = small[0:4]
    for panel in range(FF // D):
        up_bias_out[:, panel * D : (panel + 1) * D] = small[4 + panel : 5 + panel]
    gain_out[0] = small[8:10]
    shift_out[0] = small[10:12]
    for number in range(len(jobs)):
        slot = number % SLOTS
        panel, start, _ = jobs[number]
        if number >= SLOTS:
            store(number - SLOTS).wait()

        def turn(step, carry):
            part = pl.ds(pl.multiple_of(step * SUB, SUB), SUB)
            here = pl.ds(pl.multiple_of(start + step * SUB, SUB), SUB)
            wide_s[slot, part, :] = grads[panel, here, :].astype(F32)
            return carry

        lax.fori_loop(0, CUT // SUB, turn, 0, unroll=4)
        store(number).start()
        if number == SLOTS:
            for move_in, move_out in zip(moves_in, moves_out):
                move_in.wait()
                move_out.start()
    for number in range(len(jobs) - SLOTS, len(jobs)):
        store(number).wait()
    for move in moves_out:
        move.wait()


def widen(act, dx, grads, small):
    anywhere = pl.BlockSpec(memory_space=pl.ANY)
    vectors = pl.BlockSpec(memory_space=pltpu.VMEM)
    square = jax.ShapeDtypeStruct((1, D, D), F32)
    return pl.pallas_call(
        widen_kernel,
        out_shape=(
            jax.ShapeDtypeStruct((1, *act.shape), BF16), jax.ShapeDtypeStruct((1, *dx.shape), F32),
            square, square, square, square,
            jax.ShapeDtypeStruct((1, D, FF), F32), jax.ShapeDtypeStruct((1, FF, D), F32),
            jax.ShapeDtypeStruct((1, 4, D), F32), jax.ShapeDtypeStruct((1, FF), F32),
            jax.ShapeDtypeStruct((1, 2, D), F32), jax.ShapeDtypeStruct((1, 2, D), F32),
        ),
        in_specs=[anywhere, anywhere, vectors, vectors],
        out_specs=[anywhere] * 8 + [vectors] * 4,
        scratch_shapes=[
            pltpu.VMEM((SLOTS, CUT, D), F32),
            pltpu.VMEM(act.shape, BF16), pltpu.VMEM(dx.shape, F32),
            pltpu.SemaphoreType.DMA((SLOTS,)), pltpu.SemaphoreType.DMA((2,)),
        ],
        compiler_params=pltpu.CompilerParams(vmem_limit_bytes=24 * 1024 * 1024),
        cost_estimate=pl.CostEstimate(flops=7077888, bytes_accessed=42467328, transcendentals=0),
    )(act, dx, grads, small)


def per_device(grid, tokens, cotangent, lengths, spans, *weights):
    act, dx, left, right, small = run_layers(tokens, cotangent, lengths, spans, *weights)
    grads, small = (run_sums if grid else plain_sums)(left, right, small)
    return widen(act, dx, grads, small)


def solution(mesh):
    in_specs = (
        P("dp", None), P("dp", None), P("dp"), P("dp", None),
        P("section", None, None), P("section", None, None), P("section", None, None),
        P("section", None, None), P("section", None, None), P("section", None, None),
        P("section", None, None), P("section", None), P("section", None, None), P("section", None, None),
    )
    out_specs = (
        P("section", "dp", None), P("section", "dp", None),
        P("section", None, None), P("section", None, None), P("section", None, None),
        P("section", None, None), P("section", None, None), P("section", None, None),
        P("section", None, None), P("section", None), P("section", None, None), P("section", None, None),
    )
    part = functools.partial(per_device, mesh.shape["dp"] == 2 * RING)
    return jax.shard_map(part, mesh=mesh, in_specs=in_specs, out_specs=out_specs, check_vma=False)
```

```python
import functools

import jax
import jax.numpy as jnp
from jax import lax
from jax.experimental import pallas as pl
from jax.experimental.pallas import tpu as pltpu
from jax.sharding import PartitionSpec as P

D = 768
HEADS = 12
HEAD_DIM = 64
QUADS = HEADS // 4
FF = 3072
LENGTH = 160
LEAST = 96
ROWS = LENGTH
SUB = 32
BAND = 16
WIDE = 512
TURN = 256
PART = 256

F32 = jnp.float32
BF16 = jnp.bfloat16
MESH = pl.DeviceIdType.MESH


def dot(left, right):
    return jnp.dot(left, right, preferred_element_type=F32)


def dot_t(left, right):
    return lax.dot_general(left, right, (((1,), (1,)), ((), ())), preferred_element_type=F32)


def fold(block):
    return jnp.sum(block.reshape(-1, 8, block.shape[-1]), axis=0)


def gelu_parts(u):
    t = pl.reciprocal(1.0 + 0.23164189 * jnp.abs(u), approx=True)
    gauss = jnp.exp2(u * u * -0.7213475204444817)
    poly = t * (
        0.127414796 + t * (-0.142248368 + t * (0.7107068705 + t * (-0.7265760135 + t * 0.5307027145)))
    )
    tail = poly * gauss
    cdf = jnp.where(u >= 0, 1.0 - tail, tail)
    return u * cdf, cdf + (u * 0.3989422804014327) * gauss


def layers_kernel(
    micro_count,
    tokens, cotangent, lengths, spans,
    wq, wk, wv, wo, w1, w2, bias_in, up_bias_in, gains_in, shifts_in,
    act_out, dx_out, left_out, right_out, small_out,
    wq_s, wk_s, wv_s, wo_s, w1_s, w2_s,
    h_s, q_s, k_s, v_s, p_s, o_s, n_s, xa_s, xb_s, z_s, g_s, inva_s, invb_s,
    y_s, dy_s, df_s, da_s, dx_s, wide_s, turn_s, acc_s, accu_s,
    w_sem, in_sem, out_sem, turn_sem, fwd_send, fwd_recv, bwd_send, bwd_recv,
):
    section = lax.axis_index("section")
    other = 1 - section
    first = section == 0
    last = section == 1

    barrier = pltpu.get_barrier_semaphore()
    pl.semaphore_signal(barrier, inc=1, device_id={"section": other}, device_id_type=MESH)

    weight_pairs = ((wq, wq_s), (wk, wk_s), (wv, wv_s), (wo, wo_s), (w1, w1_s), (w2, w2_s))

    def weight_copy(index):
        source, target = weight_pairs[index]
        return pltpu.make_async_copy(source.at[0], target, w_sem.at[index])

    def rows_of(index):
        return pl.ds(pl.multiple_of(index * ROWS, ROWS), ROWS)

    def entry_copy(index):
        return pltpu.make_async_copy(tokens.at[rows_of(index)], h_s.at[rows_of(index)], in_sem.at[index])

    def cot_copy(index):
        return pltpu.make_async_copy(cotangent.at[rows_of(index)], dy_s.at[rows_of(index)], in_sem.at[index])

    def forward_send(index):
        return pltpu.make_async_remote_copy(
            src_ref=y_s.at[rows_of(index)],
            dst_ref=h_s.at[rows_of(index)],
            send_sem=fwd_send.at[index],
            recv_sem=fwd_recv.at[index],
            device_id={"section": other},
            device_id_type=MESH,
        )

    def backward_send(index):
        return pltpu.make_async_remote_copy(
            src_ref=y_s.at[rows_of(index)],
            dst_ref=dy_s.at[rows_of(index)],
            send_sem=bwd_send.at[index],
            recv_sem=bwd_recv.at[index],
            device_id={"section": other},
            device_id_type=MESH,
        )

    backward_outs = ((q_s, 0), (k_s, 1), (v_s, 2), (da_s, 3), (df_s, 8))

    def act_copy(index):
        return pltpu.make_async_copy(y_s.at[rows_of(index)], act_out.at[rows_of(index)], out_sem.at[0, index])

    def dx_copy(index):
        return pltpu.make_async_copy(dx_s.at[rows_of(index)], dx_out.at[rows_of(index)], out_sem.at[1, index])

    def right_copies(index):
        for slot, (source, place) in enumerate(backward_outs):
            yield pltpu.make_async_copy(
                source.at[rows_of(index)], right_out.at[place, rows_of(index)], out_sem.at[2 + slot, index]
            )
        for panel in range(FF // D):
            yield pltpu.make_async_copy(
                g_s.at[rows_of(index), pl.ds(panel * D, D)],
                right_out.at[4 + panel, rows_of(index)],
                out_sem.at[7 + panel, index],
            )

    def turn_copy(slot, row):
        return pltpu.make_async_copy(
            turn_s.at[slot], left_out.at[pl.ds(pl.multiple_of(row, TURN), TURN)], turn_sem.at[slot]
        )

    def transpose_all():
        done = 0
        for source, tiles in ((h_s, D // TURN), (o_s, D // TURN), (n_s, D // TURN), (z_s, FF // TURN)):

            def tile_step(tile, carry, source=source, done=done):
                number = tile + done
                slot = lax.rem(number, 2)

                @pl.when(number >= 2)
                def _():
                    turn_copy(slot, (number - 2) * TURN).wait()

                turn_s[slot] = source[:, pl.ds(pl.multiple_of(tile * TURN, TURN), TURN)].T
                turn_copy(slot, number * TURN).start()
                return carry

            lax.fori_loop(0, tiles, tile_step, 0)
            done += tiles
        for number in (done - 2, done - 1):
            turn_copy(number % 2, number * TURN).wait()

    @pl.when(first)
    def _():
        entry_copy(0).start()

    for index in range(4):
        weight_copy(index).start()

    acc_s[...] = jnp.zeros_like(acc_s)
    accu_s[...] = jnp.zeros_like(accu_s)

    bias = bias_in[0].astype(F32)
    gains = gains_in[0].astype(F32)
    shifts = shifts_in[0].astype(F32)
    low_half = lax.broadcasted_iota(jnp.int32, (1, 8, 128), 2) < HEAD_DIM
    lane = lax.broadcasted_iota(jnp.int32, (1, 16, PART), 2)
    keeps = [
        jnp.where((lane >= head * HEAD_DIM) & (lane < (head + 1) * HEAD_DIM), 1.0, 0.0).astype(BF16)
        for head in range(4)
    ]

    def stacked(quad_block):
        tiles = quad_block.reshape(-1, 16, PART)
        return jnp.concatenate([tiles * keep for keep in keeps], axis=0).reshape(4 * LENGTH, PART)

    def mixed_by(table, quad_block):
        tall = table.T
        parts = []
        for half in halves:
            start = 2 * LENGTH * (half.start // 128)
            tiles = dot(tall[start : start + 2 * LENGTH], quad_block[:, half]).reshape(2, LENGTH // 8, 8, 128)
            parts.append(jnp.where(low_half, tiles[0], tiles[1]).reshape(LENGTH, 128))
        return jnp.concatenate(parts, axis=1)

    pl.semaphore_wait(barrier, 1)

    blocks = [slice(r0, r0 + BAND) for r0 in range(0, ROWS, BAND)]
    columns = [slice(c0, c0 + PART) for c0 in range(0, D, PART)]
    panels = [slice(n0, n0 + WIDE) for n0 in range(0, FF, WIDE)]
    halves = [slice(0, 128), slice(128, 256)]
    count, chunks = len(columns), len(panels)

    def forward(index, carry):
        base = index * ROWS
        rows = rows_of(index)

        def at(block):
            return pl.ds(pl.multiple_of(base + block.start, BAND), BAND)

        @pl.when(index == 0)
        def _():
            for number in range(4):
                weight_copy(number).wait()
            for number in (4, 5):
                weight_copy(number).start()

            @pl.when(first)
            def _():
                for later in range(1, micro_count):
                    entry_copy(later).start()

            @pl.when(last)
            def _():
                for later in range(micro_count):
                    cot_copy(later).start()

        @pl.when(first)
        def _():
            entry_copy(index).wait()
            start, stop = spans[0, index], spans[1, index]
            spot = lax.broadcasted_iota(jnp.int32, (LENGTH, D), 0)
            keep = (spot < start) | (spot >= stop)
            h_s[rows, :] = jnp.where(keep, h_s[rows, :].astype(F32), 0.0).astype(BF16)

        @pl.when(last)
        def _():
            forward_send(index).wait_recv()

        hidden = h_s[rows, :]

        def project(column):
            query = ((dot(hidden, wq_s[:, column]) + bias[0:1, column]) * 0.125).astype(BF16)
            key_rows = dot(hidden, wk_s[:, column]).astype(BF16)
            value = (dot(hidden, wv_s[:, column]) + bias[1:2, column]).astype(BF16)
            q_s[rows, column] = query
            k_s[rows, column] = key_rows
            v_s[rows, column] = value
            return query, key_rows, value

        spot = lax.broadcasted_iota(jnp.int32, (LENGTH - LEAST, 4 * LENGTH), 0) + LEAST
        penalty = jnp.where(spot < lengths[index], 0.0, -1000000000.0)
        projected, attends = {}, {}
        attended = None
        for step in range(count + 2):
            if step < count:
                projected[step] = project(columns[step])
            spot = step - 1
            if 0 <= spot < count:
                query, key_rows, _ = projected[spot]
                scores = dot_t(key_rows, stacked(query))
                held = jnp.concatenate([scores[:LEAST], scores[LEAST:] + penalty], axis=0)
                raised = jnp.exp(held - jnp.max(held, axis=0, keepdims=True))
                attends[spot] = (raised * (1.0 / jnp.sum(raised, axis=0, keepdims=True))).astype(BF16)
                p_s[index, spot] = attends[spot]
            spot = step - 2
            if 0 <= spot:
                mixture = mixed_by(attends[spot], projected[spot][2]).astype(BF16)
                o_s[rows, columns[spot]] = mixture
                product = dot(mixture, wo_s[columns[spot], :])
                attended = product if attended is None else attended + product

        for block in blocks:
            r = h_s[at(block), :].astype(F32) + attended[block] + bias[2:3]
            centered = r - jnp.mean(r, axis=-1, keepdims=True)
            inv = lax.rsqrt(jnp.mean(centered * centered, axis=-1, keepdims=True) + 1e-05)
            hat = centered * inv
            normed = hat * gains[0:1] + shifts[0:1]
            xa_s[at(block), :] = hat.astype(BF16)
            inva_s[at(block), :] = jnp.broadcast_to(inv, (BAND, 128))
            n_s[at(block), :] = normed.astype(BF16)
            wide_s[block, :] = normed

        @pl.when(index == 0)
        def _():
            weight_copy(4).wait()
            weight_copy(5).wait()

        normed_low = n_s[rows, :]
        lifted = {}
        outer = None
        for step in range(chunks + 2):
            if step < chunks:
                lifted[step] = dot(normed_low, w1_s[:, panels[step]])
            spot = step - 1
            if 0 <= spot < chunks:
                up_bias = up_bias_in[0:1, panels[spot]].astype(F32)
                for block in blocks:
                    act, slope = gelu_parts(lifted[spot][block] + up_bias)
                    z_s[at(block), panels[spot]] = act.astype(BF16)
                    g_s[at(block), panels[spot]] = slope.astype(BF16)
            spot = step - 2
            if 0 <= spot:
                product = dot(z_s[rows, panels[spot]], w2_s[panels[spot], :])
                outer = product if outer is None else outer + product

        for block in blocks:
            r = wide_s[block, :] + outer[block] + bias[3:4]
            centered = r - jnp.mean(r, axis=-1, keepdims=True)
            inv = lax.rsqrt(jnp.mean(centered * centered, axis=-1, keepdims=True) + 1e-05)
            hat = centered * inv
            xb_s[at(block), :] = hat.astype(BF16)
            invb_s[at(block), :] = jnp.broadcast_to(inv, (BAND, 128))
            y_s[at(block), :] = (hat * gains[1:2] + shifts[1:2]).astype(BF16)

        @pl.when(first)
        def _():
            forward_send(index).start()

        act_copy(index).start()
        return carry

    lax.fori_loop(0, micro_count, forward, 0)

    def forward_done(index, carry):
        @pl.when(first)
        def _():
            forward_send(index).wait_send()

        act_copy(index).wait()
        return carry

    lax.fori_loop(0, micro_count, forward_done, 0)

    @pl.when(first)
    def _():
        transpose_all()

    def backward(index, carry):
        base = index * ROWS
        rows = rows_of(index)

        def at(block):
            return pl.ds(pl.multiple_of(base + block.start, BAND), BAND)

        @pl.when(first)
        def _():
            backward_send(index).wait_recv()

        @pl.when(last)
        def _():
            cot_copy(index).wait()

        for block in blocks:
            dy = dy_s[at(block), :].astype(F32)
            hat = xb_s[at(block), :].astype(F32)
            acc_s[9] += fold(dy * hat)
            acc_s[11] += fold(dy)
            scaled = dy * gains[1:2]
            mean_plain = jnp.mean(scaled, axis=-1, keepdims=True)
            mean_hat = jnp.mean(scaled * hat, axis=-1, keepdims=True)
            grad = (scaled - mean_plain - hat * mean_hat) * invb_s[at(block), 0:1]
            wide_s[block, :] = grad
            df_s[at(block), :] = grad.astype(BF16)
            acc_s[3] += fold(grad)

        outer_low = df_s[rows, :]
        dropped = {}
        total = None
        for step in range(chunks + 2):
            if step < chunks:
                dropped[step] = dot_t(outer_low, w2_s[panels[step], :])
            spot = step - 1
            if 0 <= spot < chunks:
                sums = jnp.zeros((8, WIDE), F32)
                for block in blocks:
                    part = dropped[spot][block] * g_s[at(block), panels[spot]].astype(F32)
                    g_s[at(block), panels[spot]] = part.astype(BF16)
                    sums = sums + fold(part)
                accu_s[:, panels[spot]] += sums
            spot = step - 2
            if 0 <= spot:
                product = dot_t(g_s[rows, panels[spot]], w1_s[:, panels[spot]])
                total = product if total is None else total + product

        for block in blocks:
            dn = wide_s[block, :] + total[block]
            hat = xa_s[at(block), :].astype(F32)
            acc_s[8] += fold(dn * hat)
            acc_s[10] += fold(dn)
            scaled = dn * gains[0:1]
            mean_plain = jnp.mean(scaled, axis=-1, keepdims=True)
            mean_hat = jnp.mean(scaled * hat, axis=-1, keepdims=True)
            grad = (scaled - mean_plain - hat * mean_hat) * inva_s[at(block), 0:1]
            wide_s[block, :] = grad
            da_s[at(block), :] = grad.astype(BF16)
            acc_s[2] += fold(grad)

        attended_low = da_s[rows, :]
        mixed, scored, values_back = {}, {}, {}
        total = None
        for step in range(count + 2):
            if step < count:
                mixed[step] = dot_t(attended_low, wo_s[columns[step], :]).astype(BF16)
            spot = step - 1
            if 0 <= spot < count:
                tall = stacked(mixed[spot])
                grad_attend = dot_t(v_s[rows, columns[spot]], tall)
                values_back[spot] = dot(p_s[index, spot], tall)
                attend = p_s[index, spot].astype(F32)
                weighted = attend * grad_attend
                delta = jnp.sum(weighted, axis=0, keepdims=True) / jnp.sum(attend, axis=0, keepdims=True)
                scored[spot] = (weighted - attend * delta).astype(BF16)
            spot = step - 2
            if 0 <= spot:
                column = columns[spot]
                dk = dot(scored[spot], stacked(q_s[rows, column]))
                dq = mixed_by(scored[spot], k_s[rows, column]) * 0.125
                dv = values_back[spot]
                acc_s[0, :, column] += fold(dq)
                acc_s[1, :, column] += fold(dv)
                dq, dk, dv = dq.astype(BF16), dk.astype(BF16), dv.astype(BF16)
                q_s[rows, column] = dq
                k_s[rows, column] = dk
                v_s[rows, column] = dv
                for grad, weight in ((dq, wq_s), (dk, wk_s), (dv, wv_s)):
                    product = dot_t(grad, weight[:, column])
                    total = product if total is None else total + product

        @pl.when(last)
        def _():
            low = (wide_s[...] + total).astype(BF16)
            y_s[rows, :] = low
            dx_s[rows, :] = low.astype(F32)
            backward_send(index).start()

        @pl.when(first)
        def _():
            start, stop = spans[0, index], spans[1, index]
            spot = lax.broadcasted_iota(jnp.int32, (LENGTH, D), 0)
            keep = (spot < start) | (spot >= stop)
            dx_s[rows, :] = jnp.where(keep, wide_s[...] + total, 0.0)

        dx_copy(index).start()
        for copy in right_copies(index):
            copy.start()
        return carry

    lax.fori_loop(0, micro_count, backward, 0)

    @pl.when(last)
    def _():
        transpose_all()

    for number in range(12):
        if 4 <= number < 8:
            panel = accu_s[:, (number - 4) * D : (number - 3) * D]
        else:
            panel = acc_s[number]
        small_out[number : number + 1, :] = jnp.sum(panel, axis=0, keepdims=True)
    small_out[12:16, :] = jnp.zeros((4, D), F32)

    def backward_done(index, carry):
        @pl.when(last)
        def _():
            backward_send(index).wait_send()

        dx_copy(index).wait()
        for copy in right_copies(index):
            copy.wait()
        return carry

    lax.fori_loop(0, micro_count, backward_done, 0)


def run_layers(tokens, cotangent, lengths, spans, *weights):
    rows = tokens.shape[0]
    micro_count = rows // ROWS
    anywhere = pl.BlockSpec(memory_space=pl.ANY)
    scalars = pl.BlockSpec(memory_space=pltpu.SMEM)
    vectors = pl.BlockSpec(memory_space=pltpu.VMEM)
    out_shape = (
        jax.ShapeDtypeStruct((rows, D), BF16),
        jax.ShapeDtypeStruct((rows, D), F32),
        jax.ShapeDtypeStruct((3 * D + FF, rows), BF16),
        jax.ShapeDtypeStruct((9, rows, D), BF16),
        jax.ShapeDtypeStruct((16, D), F32),
    )

    def vm(count, width=D, dtype=BF16):
        return pltpu.VMEM((count, width), dtype)

    scratch = [
        vm(D), vm(D), vm(D), vm(D), vm(D, FF), vm(FF),
        vm(rows), vm(rows), vm(rows), vm(rows),
        pltpu.VMEM((micro_count, QUADS, LENGTH, 4 * LENGTH), BF16),
        vm(rows), vm(rows), vm(rows), vm(rows), vm(rows, FF), vm(rows, FF),
        vm(rows, 128, F32), vm(rows, 128, F32),
        vm(rows), vm(rows), vm(rows), vm(rows), vm(rows, D, F32),
        vm(ROWS, D, F32), pltpu.VMEM((2, TURN, rows), BF16), pltpu.VMEM((12, 8, D), F32), vm(8, FF, F32),
        pltpu.SemaphoreType.DMA((6,)),
        pltpu.SemaphoreType.DMA((micro_count,)),
        pltpu.SemaphoreType.DMA((11, micro_count)),
        pltpu.SemaphoreType.DMA((2,)),
        pltpu.SemaphoreType.DMA((micro_count,)),
        pltpu.SemaphoreType.DMA((micro_count,)),
        pltpu.SemaphoreType.DMA((micro_count,)),
        pltpu.SemaphoreType.DMA((micro_count,)),
    ]
    return pl.pallas_call(
        functools.partial(layers_kernel, micro_count),
        out_shape=out_shape,
        in_specs=[anywhere, anywhere, scalars, scalars] + [anywhere] * 6 + [vectors] * 4,
        out_specs=[anywhere] * 4 + [vectors],
        scratch_shapes=scratch,
        compiler_params=pltpu.CompilerParams(
            collective_id=0, has_side_effects=True, vmem_limit_bytes=60 * 1024 * 1024
        ),
        cost_estimate=pl.CostEstimate(
            flops=rows * 2 * 2 * 2 * 7077888, bytes_accessed=60000000, transcendentals=rows * FF * 2
        ),
    )(tokens, cotangent, lengths, spans.T, *weights)


RING = 8
PIECES = 3
PIECE = D // RING
PANELS = (
    (0, 0), (0, 1), (0, 2), (D, 3), (2 * D, 4), (2 * D, 5),
    (2 * D, 6), (2 * D, 7), (3 * D, 8), (4 * D, 8), (5 * D, 8), (6 * D, 8),
)


def sums_kernel(
    left, right, small_in, grads_out, small_out,
    left_s, right_s, total_s, give_s, take_s, ring_s,
    tiny_s, tiny_take_s, tiny_sum_s, tiny_go_s, tiny_ring_s, tiny_own_s,
    load_sem, give_sem, take_sem, ring_send, ring_recv, round_send, round_recv, share_send, share_recv,
    tiny_sem, tiny_ring_send, tiny_ring_recv, tiny_round_send, tiny_round_recv,
):
    me = lax.axis_index("dp")
    core = lax.rem(me, 2)
    high = lax.rem(lax.div(me, 2), 2)
    depth = lax.div(me, 4)
    place = depth + high * (7 - 2 * depth)

    def device(spot, on_core):
        row = lax.div(spot, 4)
        return {"dp": 4 * (spot + row * (7 - 2 * spot)) + 2 * row + on_core}

    ahead = device(lax.rem(place + 1, RING), core)
    behind = device(lax.rem(place + RING - 1, RING), core)
    beside = device(place, 1 - core)
    targets = (ahead, behind)

    barrier = pltpu.get_barrier_semaphore()
    for peer in (ahead, behind, beside):
        pl.semaphore_signal(barrier, inc=1, device_id=peer, device_id_type=MESH)

    def block(way, step):
        return lax.rem(place - step + RING, RING) if way == 0 else lax.rem(place + step, RING)

    def late_block(way, step):
        return lax.rem(place + 1 - step + RING, RING) if way == 0 else lax.rem(place + RING - 1 + step, RING)

    def load_left(part):
        return pltpu.make_async_copy(left.at[pl.ds(part * D, D)], left_s.at[pl.ds(part * D, D)], load_sem.at[part])

    def load_right(part):
        return pltpu.make_async_copy(right.at[part], right_s.at[part], load_sem.at[7 + part])

    def remote(source, target, send, recv, peer):
        return pltpu.make_async_remote_copy(
            src_ref=source, dst_ref=target, send_sem=send, recv_sem=recv, device_id=peer, device_id_type=MESH
        )

    def give(way, step, piece):
        return remote(
            give_s.at[way, lax.rem(step, 4), piece], take_s.at[way, step, piece],
            give_sem.at[way, step, piece], take_sem.at[way, step, piece], beside,
        )

    def ring_copy(way, step, piece):
        return remote(
            take_s.at[way, step, piece], ring_s.at[way, step, piece],
            ring_send.at[way, step, piece], ring_recv.at[way, step, piece], targets[way],
        )

    def region(way, spot, piece, on_core):
        rows = pl.ds(pl.multiple_of(spot * PIECE, PIECE), PIECE)
        return grads_out.at[6 * way + 3 * on_core + piece, rows]

    def round_copy(way, step, piece):
        target = region(way, late_block(way, step), piece, core)
        return remote(
            target, target, round_send.at[way, step, piece], round_recv.at[way, step, piece], targets[way]
        )

    def round_wait(way, step, piece):
        target = region(way, late_block(way, step + 1), piece, core)
        remote(
            target, target, round_send.at[way, step, piece], round_recv.at[way, step, piece], targets[way]
        ).wait_recv()

    def share_copy(way, step, piece):
        target = region(way, late_block(way, step), piece, core)
        return remote(
            target, target, share_send.at[way, step, piece], share_recv.at[way, step, piece], beside
        )

    def share_wait(way, step, piece):
        target = region(way, late_block(way, step), piece, 1 - core)
        remote(
            target, target, share_send.at[way, step, piece], share_recv.at[way, step, piece], beside
        ).wait_recv()

    tiny_swap = remote(tiny_s, tiny_take_s, tiny_sem.at[0], tiny_sem.at[1], beside)

    def tiny_ring(step):
        return remote(
            tiny_go_s.at[step], tiny_ring_s.at[step], tiny_ring_send.at[step], tiny_ring_recv.at[step], ahead
        )

    def tiny_round(step):
        spot = late_block(0, step)
        return remote(
            tiny_own_s.at[spot], tiny_own_s.at[spot], tiny_round_send.at[step], tiny_round_recv.at[step], ahead
        )

    def tiny_round_wait(step):
        spot = late_block(0, step + 1)
        remote(
            tiny_own_s.at[spot], tiny_own_s.at[spot], tiny_round_send.at[step], tiny_round_recv.at[step], ahead
        ).wait_recv()

    loads = []
    for piece in range(PIECES):
        for way in range(2):
            for half in range(2):
                first_row, number = PANELS[6 * way + 3 * half + piece]
                for kind, part in ((load_right, number), (load_left, first_row // D)):
                    if (kind, part) not in [entry[:2] for entry in loads]:
                        loads.append((kind, part, way, piece))
    order = [(way, piece) for piece in range(PIECES) for way in range(2)]
    groups = [[kind(part) for kind, part, *spot in loads if tuple(spot) == pair] for pair in order]
    for group in groups[:2]:
        for copy in group:
            copy.start()

    for part in range(RING):
        if part * 128 < D:
            tiny_s[part] = small_in[:, part * 128 : part * 128 + 128]
        else:
            tiny_s[part] = jnp.zeros((16, 128), F32)

    pl.semaphore_wait(barrier, 3)
    tiny_swap.start()

    def product(group, way, piece, pick):
        near, far = PANELS[6 * way + piece], PANELS[6 * way + 3 + piece]
        first_row = near[0] + pick * (far[0] - near[0])
        number = near[1] + pick * (far[1] - near[1])
        blocks = []
        for step in (2 * group, 2 * group + 1):
            start = pl.multiple_of(first_row + block(way, step) * PIECE, PIECE)
            blocks.append(left_s[pl.ds(start, PIECE), :])
        return dot(jnp.concatenate(blocks, axis=0), right_s[number])

    def keep_product(group, way, piece, both):
        total_s[lax.rem(2 * group, 3), way, piece] = both[:PIECE]
        total_s[lax.rem(2 * group + 1, 3), way, piece] = both[PIECE:]

    def give_product(group, way, piece, both):
        @pl.when(group >= 2)
        def _():
            give(way, 2 * group - 4, piece).wait_send()
            give(way, 2 * group - 3, piece).wait_send()

        give_s[way, lax.rem(2 * group, 4), piece] = both[:PIECE].astype(BF16)
        give_s[way, lax.rem(2 * group + 1, 4), piece] = both[PIECE:].astype(BF16)
        give(way, 2 * group, piece).start()
        give(way, 2 * group + 1, piece).start()

    def add_piece(step, way, piece, target):
        slot = lax.rem(step, 3)
        for r0 in range(0, PIECE, SUB):
            part = slice(r0, r0 + SUB)
            whole = total_s[slot, way, piece, part] + take_s[way, step, piece, part].astype(F32)
            target[part] = whole.astype(BF16)

    def reduce_step(step, carry):
        slot = lax.rem(step, 3)
        spot = block(0, step)

        @pl.when(step < RING - 1)
        def _():
            tiny_ring(step - 1).wait_recv()
            tiny_go_s[step] = tiny_sum_s[spot] + tiny_ring_s[step - 1]
            tiny_ring(step).start()

        @pl.when(step == RING - 1)
        def _():
            tiny_ring(step - 1).wait_recv()
            tiny_own_s[spot] = tiny_sum_s[spot] + tiny_ring_s[step - 1]
            tiny_round(0).start()

        for piece in range(PIECES):
            for way in range(2):
                give(way, step, piece).wait_recv()
                ring_copy(way, step - 1, piece).wait_recv()
                for r0 in range(0, PIECE, SUB):
                    part = slice(r0, r0 + SUB)
                    total_s[slot, way, piece, part] += ring_s[way, step - 1, piece, part].astype(F32)

                @pl.when(step < RING - 1)
                def _():
                    add_piece(step, way, piece, take_s.at[way, step, piece])
                    ring_copy(way, step, piece).start()

                @pl.when(step == RING - 1)
                def _():
                    add_piece(step, way, piece, region(way, late_block(way, 0), piece, core))
                    round_copy(way, 0, piece).start()
                    share_copy(way, 0, piece).start()

                @pl.when(step < RING - 2)
                def _():
                    odd = lax.rem(step, 2)
                    group = lax.div(step, 2) + 1
                    both = product(group, way, piece, odd * core + (1 - odd) * (1 - core))

                    @pl.when(odd == 1)
                    def _():
                        keep_product(group, way, piece, both)

                    @pl.when(odd == 0)
                    def _():
                        give_product(group, way, piece, both)

        return carry

    def first_piece(way, piece):
        give(way, 0, piece).wait_recv()
        add_piece(0, way, piece, take_s.at[way, 0, piece])
        ring_copy(way, 0, piece).start()

    for number, (way, piece) in enumerate(order):
        for copy in groups[number]:
            copy.wait()
        if number + 2 < len(groups):
            for copy in groups[number + 2]:
                copy.start()
        give_product(0, way, piece, product(0, way, piece, 1 - core))
        keep_product(0, way, piece, product(0, way, piece, core))
        if number > 0:
            first_piece(*order[number - 1])
    first_piece(*order[-1])
    for way, piece in order:
        give_product(1, way, piece, product(1, way, piece, 1 - core))
    tiny_swap.wait_recv()
    tiny_sum_s[...] = tiny_s[...] + tiny_take_s[...]
    tiny_go_s[0] = tiny_sum_s[block(0, 0)]
    tiny_ring(0).start()

    lax.fori_loop(1, RING, reduce_step, 0)

    def round_step(step, carry):
        tiny_round_wait(step - 1)

        @pl.when(step < RING - 1)
        def _():
            tiny_round(step).start()

        for piece in range(PIECES):
            for way in range(2):
                round_wait(way, step - 1, piece)

                @pl.when(step < RING - 1)
                def _():
                    round_copy(way, step, piece).start()

                share_copy(way, step, piece).start()
        return carry

    lax.fori_loop(1, RING, round_step, 0)

    for part in range(D // 128):
        small_out[:, part * 128 : part * 128 + 128] = tiny_own_s[part]
    tiny_swap.wait_send()

    def finish(step, carry):
        for way in range(2):
            for piece in range(PIECES):

                @pl.when(step >= RING // 2)
                def _():
                    give(way, step, piece).wait_send()

                share_wait(way, step, piece)
                share_copy(way, step, piece).wait_send()

                @pl.when(step < RING - 1)
                def _():
                    ring_copy(way, step, piece).wait_send()
                    round_copy(way, step, piece).wait_send()

        @pl.when(step < RING - 1)
        def _():
            tiny_ring(step).wait_send()
            tiny_round(step).wait_send()

        return carry

    lax.fori_loop(0, RING, finish, 0)


def run_sums(left, right, small):
    rows = right.shape[1]
    anywhere = pl.BlockSpec(memory_space=pl.ANY)
    vectors = pl.BlockSpec(memory_space=pltpu.VMEM)

    def pieces(*lead, dtype=BF16):
        return pltpu.VMEM((*lead, PIECE, D), dtype)

    dma = pltpu.SemaphoreType.DMA
    scratch = [
        pltpu.VMEM(left.shape, BF16), pltpu.VMEM(right.shape, BF16),
        pieces(3, 2, PIECES, dtype=F32), pieces(2, 4, PIECES), pieces(2, RING, PIECES),
        pieces(2, RING - 1, PIECES),
        pltpu.VMEM((RING, 16, 128), F32), pltpu.VMEM((RING, 16, 128), F32), pltpu.VMEM((RING, 16, 128), F32),
        pltpu.VMEM((RING - 1, 16, 128), F32), pltpu.VMEM((RING - 1, 16, 128), F32), pltpu.VMEM((RING, 16, 128), F32),
        dma((16,)), dma((2, RING, PIECES)), dma((2, RING, PIECES)),
        dma((2, RING - 1, PIECES)), dma((2, RING - 1, PIECES)),
        dma((2, RING - 1, PIECES)), dma((2, RING - 1, PIECES)), dma((2, RING, PIECES)), dma((2, RING, PIECES)),
        dma((2,)), dma((RING - 1,)), dma((RING - 1,)), dma((RING - 1,)), dma((RING - 1,)),
    ]
    return pl.pallas_call(
        sums_kernel,
        out_shape=(pltpu.VMEM((12, D, D), BF16), jax.ShapeDtypeStruct((16, D), F32)),
        in_specs=[anywhere, anywhere, vectors],
        out_specs=[vectors, vectors],
        scratch_shapes=scratch,
        compiler_params=pltpu.CompilerParams(
            collective_id=1, has_side_effects=True, vmem_limit_bytes=48 * 1024 * 1024
        ),
        cost_estimate=pl.CostEstimate(flops=rows * 2 * 7077888, bytes_accessed=70000000, transcendentals=0),
    )(left, right, small)


def plain_sums(left, right, small):
    panels = [dot(left[row : row + D], right[number]).astype(BF16) for row, number in PANELS]
    return lax.psum(jnp.stack(panels), "dp"), lax.psum(small, "dp")


SLOTS = 8
CUT = D // 2


def widen_kernel(
    act, dx, grads, small, act_out, dx_out, query_out, key_out, value_out, out_out, up_out, down_out,
    bias_out, up_bias_out, gain_out, shift_out, wide_s, act_s, dx_s, out_sem, move_sem,
):
    moves_in = [
        pltpu.make_async_copy(act, act_s, move_sem.at[0]), pltpu.make_async_copy(dx, dx_s, move_sem.at[1])
    ]
    moves_out = [
        pltpu.make_async_copy(act_s, act_out.at[0], move_sem.at[0]),
        pltpu.make_async_copy(dx_s, dx_out.at[0], move_sem.at[1]),
    ]
    jobs = []
    for panel in range(12):
        for half in range(2):
            rows = pl.ds(half * CUT, CUT)
            if panel < 4:
                target = (query_out, key_out, value_out, out_out)[panel].at[0, rows]
            elif panel < 8:
                target = up_out.at[0, rows, pl.ds((panel - 4) * D, D)]
            else:
                target = down_out.at[0, pl.ds((panel - 8) * D + half * CUT, CUT)]
            jobs.append((panel, half * CUT, target))

    def store(number):
        return pltpu.make_async_copy(wide_s.at[number % SLOTS], jobs[number][2], out_sem.at[number % SLOTS])

    for move in moves_in:
        move.start()
    bias_out[0] = small[0:4]
    for panel in range(FF // D):
        up_bias_out[:, panel * D : (panel + 1) * D] = small[4 + panel : 5 + panel]
    gain_out[0] = small[8:10]
    shift_out[0] = small[10:12]
    for number in range(len(jobs)):
        slot = number % SLOTS
        panel, start, _ = jobs[number]
        if number >= SLOTS:
            store(number - SLOTS).wait()

        def turn(step, carry):
            part = pl.ds(pl.multiple_of(step * SUB, SUB), SUB)
            here = pl.ds(pl.multiple_of(start + step * SUB, SUB), SUB)
            wide_s[slot, part, :] = grads[panel, here, :].astype(F32)
            return carry

        lax.fori_loop(0, CUT // SUB, turn, 0, unroll=4)
        store(number).start()
        if number == SLOTS:
            for move_in, move_out in zip(moves_in, moves_out):
                move_in.wait()
                move_out.start()
    for number in range(len(jobs) - SLOTS, len(jobs)):
        store(number).wait()
    for move in moves_out:
        move.wait()


def widen(act, dx, grads, small):
    anywhere = pl.BlockSpec(memory_space=pl.ANY)
    vectors = pl.BlockSpec(memory_space=pltpu.VMEM)
    square = jax.ShapeDtypeStruct((1, D, D), F32)
    return pl.pallas_call(
        widen_kernel,
        out_shape=(
            jax.ShapeDtypeStruct((1, *act.shape), BF16), jax.ShapeDtypeStruct((1, *dx.shape), F32),
            square, square, square, square,
            jax.ShapeDtypeStruct((1, D, FF), F32), jax.ShapeDtypeStruct((1, FF, D), F32),
            jax.ShapeDtypeStruct((1, 4, D), F32), jax.ShapeDtypeStruct((1, FF), F32),
            jax.ShapeDtypeStruct((1, 2, D), F32), jax.ShapeDtypeStruct((1, 2, D), F32),
        ),
        in_specs=[anywhere, anywhere, vectors, vectors],
        out_specs=[anywhere] * 8 + [vectors] * 4,
        scratch_shapes=[
            pltpu.VMEM((SLOTS, CUT, D), F32),
            pltpu.VMEM(act.shape, BF16), pltpu.VMEM(dx.shape, F32),
            pltpu.SemaphoreType.DMA((SLOTS,)), pltpu.SemaphoreType.DMA((2,)),
        ],
        compiler_params=pltpu.CompilerParams(vmem_limit_bytes=46 * 1024 * 1024),
        cost_estimate=pl.CostEstimate(flops=7077888, bytes_accessed=42467328, transcendentals=0),
    )(act, dx, grads, small)


def per_device(grid, tokens, cotangent, lengths, spans, *weights):
    act, dx, left, right, small = run_layers(tokens, cotangent, lengths, spans, *weights)
    grads, small = (run_sums if grid else plain_sums)(left, right, small)
    grads = pltpu.with_memory_space_constraint(grads, pltpu.VMEM)
    return widen(act, dx, grads, small)


def solution(mesh):
    in_specs = (
        P("dp", None), P("dp", None), P("dp"), P("dp", None),
        P("section", None, None), P("section", None, None), P("section", None, None),
        P("section", None, None), P("section", None, None), P("section", None, None),
        P("section", None, None), P("section", None), P("section", None, None), P("section", None, None),
    )
    out_specs = (
        P("section", "dp", None), P("section", "dp", None),
        P("section", None, None), P("section", None, None), P("section", None, None),
        P("section", None, None), P("section", None, None), P("section", None, None),
        P("section", None, None), P("section", None), P("section", None, None), P("section", None, None),
    )
    part = functools.partial(per_device, mesh.shape["dp"] == 2 * RING)
    return jax.shard_map(part, mesh=mesh, in_specs=in_specs, out_specs=out_specs, check_vma=False)
```

```python
import functools

import jax
import jax.numpy as jnp
from jax import lax
from jax.experimental import pallas as pl
from jax.experimental.pallas import tpu as pltpu
from jax.sharding import PartitionSpec as P

D = 768
HEADS = 12
HEAD_DIM = 64
QUADS = HEADS // 4
FF = 3072
LENGTH = 160
LEAST = 96
ROWS = LENGTH
SUB = 32
BAND = 80
WIDE = 512
TURN = 256
PART = 256

F32 = jnp.float32
BF16 = jnp.bfloat16
MESH = pl.DeviceIdType.MESH


def dot(left, right):
    return jnp.dot(left, right, preferred_element_type=F32)


def dot_t(left, right):
    return lax.dot_general(left, right, (((1,), (1,)), ((), ())), preferred_element_type=F32)


def fold(block):
    return jnp.sum(block.reshape(-1, 8, block.shape[-1]), axis=0)


def gelu_parts(u):
    t = pl.reciprocal(1.0 + 0.23164189 * jnp.abs(u), approx=True)
    gauss = jnp.exp2(u * u * -0.7213475204444817)
    poly = t * (
        0.127414796 + t * (-0.142248368 + t * (0.7107068705 + t * (-0.7265760135 + t * 0.5307027145)))
    )
    tail = poly * gauss
    cdf = jnp.where(u >= 0, 1.0 - tail, tail)
    return u * cdf, cdf + (u * 0.3989422804014327) * gauss


def layers_kernel(
    micro_count,
    tokens, cotangent, lengths, spans,
    wq, wk, wv, wo, w1, w2, bias_in, up_bias_in, gains_in, shifts_in,
    act_out, dx_out, left_out, right_out, small_out,
    wq_s, wk_s, wv_s, wo_s, w1_s, w2_s,
    h_s, q_s, k_s, v_s, p_s, o_s, n_s, xa_s, xb_s, z_s, g_s, inva_s, invb_s,
    y_s, dy_s, df_s, da_s, dx_s, wide_s, turn_s, acc_s, accu_s,
    w_sem, in_sem, out_sem, turn_sem, fwd_send, fwd_recv, bwd_send, bwd_recv,
):
    section = lax.axis_index("section")
    other = 1 - section
    first = section == 0
    last = section == 1

    barrier = pltpu.get_barrier_semaphore()
    pl.semaphore_signal(barrier, inc=1, device_id={"section": other}, device_id_type=MESH)

    weight_pairs = ((wq, wq_s), (wk, wk_s), (wv, wv_s), (wo, wo_s), (w1, w1_s), (w2, w2_s))

    def weight_copy(index):
        source, target = weight_pairs[index]
        return pltpu.make_async_copy(source.at[0], target, w_sem.at[index])

    def rows_of(index):
        return pl.ds(pl.multiple_of(index * ROWS, ROWS), ROWS)

    def entry_copy(index):
        return pltpu.make_async_copy(tokens.at[rows_of(index)], h_s.at[rows_of(index)], in_sem.at[index])

    def cot_copy(index):
        return pltpu.make_async_copy(cotangent.at[rows_of(index)], dy_s.at[rows_of(index)], in_sem.at[index])

    def forward_send(index):
        return pltpu.make_async_remote_copy(
            src_ref=y_s.at[rows_of(index)],
            dst_ref=h_s.at[rows_of(index)],
            send_sem=fwd_send.at[index],
            recv_sem=fwd_recv.at[index],
            device_id={"section": other},
            device_id_type=MESH,
        )

    def backward_send(index):
        return pltpu.make_async_remote_copy(
            src_ref=y_s.at[rows_of(index)],
            dst_ref=dy_s.at[rows_of(index)],
            send_sem=bwd_send.at[index],
            recv_sem=bwd_recv.at[index],
            device_id={"section": other},
            device_id_type=MESH,
        )

    backward_outs = ((q_s, 0), (k_s, 1), (v_s, 2), (da_s, 3), (df_s, 8))

    def act_copy(index):
        return pltpu.make_async_copy(y_s.at[rows_of(index)], act_out.at[rows_of(index)], out_sem.at[0, index])

    def dx_copy(index):
        return pltpu.make_async_copy(dx_s.at[rows_of(index)], dx_out.at[rows_of(index)], out_sem.at[1, index])

    def right_copies(index):
        for slot, (source, place) in enumerate(backward_outs):
            yield pltpu.make_async_copy(
                source.at[rows_of(index)], right_out.at[place, rows_of(index)], out_sem.at[2 + slot, index]
            )
        for panel in range(FF // D):
            yield pltpu.make_async_copy(
                g_s.at[rows_of(index), pl.ds(panel * D, D)],
                right_out.at[4 + panel, rows_of(index)],
                out_sem.at[7 + panel, index],
            )

    def turn_copy(slot, row):
        return pltpu.make_async_copy(
            turn_s.at[slot], left_out.at[pl.ds(pl.multiple_of(row, TURN), TURN)], turn_sem.at[slot]
        )

    def transpose_all():
        done = 0
        for source, tiles in ((h_s, D // TURN), (o_s, D // TURN), (n_s, D // TURN), (z_s, FF // TURN)):

            def tile_step(tile, carry, source=source, done=done):
                number = tile + done
                slot = lax.rem(number, 2)

                @pl.when(number >= 2)
                def _():
                    turn_copy(slot, (number - 2) * TURN).wait()

                turn_s[slot] = source[:, pl.ds(pl.multiple_of(tile * TURN, TURN), TURN)].T
                turn_copy(slot, number * TURN).start()
                return carry

            lax.fori_loop(0, tiles, tile_step, 0)
            done += tiles
        for number in (done - 2, done - 1):
            turn_copy(number % 2, number * TURN).wait()

    @pl.when(first)
    def _():
        entry_copy(0).start()

    for index in range(4):
        weight_copy(index).start()

    acc_s[...] = jnp.zeros_like(acc_s)
    accu_s[...] = jnp.zeros_like(accu_s)

    bias = bias_in[0].astype(F32)
    gains = gains_in[0].astype(F32)
    shifts = shifts_in[0].astype(F32)
    low_half = lax.broadcasted_iota(jnp.int32, (1, 8, 128), 2) < HEAD_DIM
    lane = lax.broadcasted_iota(jnp.int32, (1, 16, PART), 2)
    keeps = [
        jnp.where((lane >= head * HEAD_DIM) & (lane < (head + 1) * HEAD_DIM), 1.0, 0.0).astype(BF16)
        for head in range(4)
    ]

    def stacked(quad_block):
        tiles = quad_block.reshape(-1, 16, PART)
        return jnp.concatenate([tiles * keep for keep in keeps], axis=0).reshape(4 * LENGTH, PART)

    def mixed_by(table, quad_block):
        tall = table.T
        parts = []
        for half in halves:
            start = 2 * LENGTH * (half.start // 128)
            tiles = dot(tall[start : start + 2 * LENGTH], quad_block[:, half]).reshape(2, LENGTH // 8, 8, 128)
            parts.append(jnp.where(low_half, tiles[0], tiles[1]).reshape(LENGTH, 128))
        return jnp.concatenate(parts, axis=1)

    pl.semaphore_wait(barrier, 1)

    blocks = [slice(r0, r0 + BAND) for r0 in range(0, ROWS, BAND)]
    columns = [slice(c0, c0 + PART) for c0 in range(0, D, PART)]
    panels = [slice(n0, n0 + WIDE) for n0 in range(0, FF, WIDE)]
    halves = [slice(0, 128), slice(128, 256)]
    count, chunks = len(columns), len(panels)

    def forward(index, carry):
        base = index * ROWS
        rows = rows_of(index)

        def at(block):
            return pl.ds(pl.multiple_of(base + block.start, BAND), BAND)

        @pl.when(index == 0)
        def _():
            for number in range(4):
                weight_copy(number).wait()
            for number in (4, 5):
                weight_copy(number).start()

            @pl.when(first)
            def _():
                for later in range(1, micro_count):
                    entry_copy(later).start()

            @pl.when(last)
            def _():
                for later in range(micro_count):
                    cot_copy(later).start()

        @pl.when(first)
        def _():
            entry_copy(index).wait()
            start, stop = spans[0, index], spans[1, index]
            spot = lax.broadcasted_iota(jnp.int32, (LENGTH, D), 0)
            keep = (spot < start) | (spot >= stop)
            h_s[rows, :] = jnp.where(keep, h_s[rows, :].astype(F32), 0.0).astype(BF16)

        @pl.when(last)
        def _():
            forward_send(index).wait_recv()

        hidden = h_s[rows, :]

        def project(column):
            query = ((dot(hidden, wq_s[:, column]) + bias[0:1, column]) * 0.125).astype(BF16)
            key_rows = dot(hidden, wk_s[:, column]).astype(BF16)
            value = (dot(hidden, wv_s[:, column]) + bias[1:2, column]).astype(BF16)
            q_s[rows, column] = query
            k_s[rows, column] = key_rows
            v_s[rows, column] = value
            return query, key_rows, value

        spot = lax.broadcasted_iota(jnp.int32, (LENGTH - LEAST, 4 * LENGTH), 0) + LEAST
        penalty = jnp.where(spot < lengths[index], 0.0, -1000000000.0)
        projected, attends = {}, {}
        attended = None
        for step in range(count + 2):
            if step < count:
                projected[step] = project(columns[step])
            spot = step - 1
            if 0 <= spot < count:
                query, key_rows, _ = projected[spot]
                scores = dot_t(key_rows, stacked(query))
                held = jnp.concatenate([scores[:LEAST], scores[LEAST:] + penalty], axis=0)
                raised = jnp.exp(held - jnp.max(held, axis=0, keepdims=True))
                attends[spot] = (raised * (1.0 / jnp.sum(raised, axis=0, keepdims=True))).astype(BF16)
                p_s[index, spot] = attends[spot]
            spot = step - 2
            if 0 <= spot:
                mixture = mixed_by(attends[spot], projected[spot][2]).astype(BF16)
                o_s[rows, columns[spot]] = mixture
                product = dot(mixture, wo_s[columns[spot], :])
                attended = product if attended is None else attended + product

        for block in blocks:
            r = h_s[at(block), :].astype(F32) + attended[block] + bias[2:3]
            centered = r - jnp.mean(r, axis=-1, keepdims=True)
            inv = lax.rsqrt(jnp.mean(centered * centered, axis=-1, keepdims=True) + 1e-05)
            hat = centered * inv
            normed = hat * gains[0:1] + shifts[0:1]
            xa_s[at(block), :] = hat.astype(BF16)
            inva_s[at(block), :] = jnp.broadcast_to(inv, (BAND, 128))
            n_s[at(block), :] = normed.astype(BF16)
            wide_s[block, :] = normed

        @pl.when(index == 0)
        def _():
            weight_copy(4).wait()
            weight_copy(5).wait()

        normed_low = n_s[rows, :]
        lifted = {}
        outer = None
        for step in range(chunks + 2):
            if step < chunks:
                lifted[step] = dot(normed_low, w1_s[:, panels[step]])
            spot = step - 1
            if 0 <= spot < chunks:
                up_bias = up_bias_in[0:1, panels[spot]].astype(F32)
                for block in blocks:
                    act, slope = gelu_parts(lifted[spot][block] + up_bias)
                    z_s[at(block), panels[spot]] = act.astype(BF16)
                    g_s[at(block), panels[spot]] = slope.astype(BF16)
            spot = step - 2
            if 0 <= spot:
                product = dot(z_s[rows, panels[spot]], w2_s[panels[spot], :])
                outer = product if outer is None else outer + product

        for block in blocks:
            r = wide_s[block, :] + outer[block] + bias[3:4]
            centered = r - jnp.mean(r, axis=-1, keepdims=True)
            inv = lax.rsqrt(jnp.mean(centered * centered, axis=-1, keepdims=True) + 1e-05)
            hat = centered * inv
            xb_s[at(block), :] = hat.astype(BF16)
            invb_s[at(block), :] = jnp.broadcast_to(inv, (BAND, 128))
            y_s[at(block), :] = (hat * gains[1:2] + shifts[1:2]).astype(BF16)

        @pl.when(first)
        def _():
            forward_send(index).start()

        act_copy(index).start()
        return carry

    lax.fori_loop(0, micro_count, forward, 0)

    def forward_done(index, carry):
        @pl.when(first)
        def _():
            forward_send(index).wait_send()

        act_copy(index).wait()
        return carry

    lax.fori_loop(0, micro_count, forward_done, 0)

    @pl.when(first)
    def _():
        transpose_all()

    def backward(index, carry):
        base = index * ROWS
        rows = rows_of(index)

        def at(block):
            return pl.ds(pl.multiple_of(base + block.start, BAND), BAND)

        @pl.when(first)
        def _():
            backward_send(index).wait_recv()

        @pl.when(last)
        def _():
            cot_copy(index).wait()

        for block in blocks:
            dy = dy_s[at(block), :].astype(F32)
            hat = xb_s[at(block), :].astype(F32)
            acc_s[9] += fold(dy * hat)
            acc_s[11] += fold(dy)
            scaled = dy * gains[1:2]
            mean_plain = jnp.mean(scaled, axis=-1, keepdims=True)
            mean_hat = jnp.mean(scaled * hat, axis=-1, keepdims=True)
            grad = (scaled - mean_plain - hat * mean_hat) * invb_s[at(block), 0:1]
            wide_s[block, :] = grad
            df_s[at(block), :] = grad.astype(BF16)
            acc_s[3] += fold(grad)

        outer_low = df_s[rows, :]
        dropped = {}
        total = None
        for step in range(chunks + 2):
            if step < chunks:
                dropped[step] = dot_t(outer_low, w2_s[panels[step], :])
            spot = step - 1
            if 0 <= spot < chunks:
                sums = jnp.zeros((8, WIDE), F32)
                for block in blocks:
                    part = dropped[spot][block] * g_s[at(block), panels[spot]].astype(F32)
                    g_s[at(block), panels[spot]] = part.astype(BF16)
                    sums = sums + fold(part)
                accu_s[:, panels[spot]] += sums
            spot = step - 2
            if 0 <= spot:
                product = dot_t(g_s[rows, panels[spot]], w1_s[:, panels[spot]])
                total = product if total is None else total + product

        for block in blocks:
            dn = wide_s[block, :] + total[block]
            hat = xa_s[at(block), :].astype(F32)
            acc_s[8] += fold(dn * hat)
            acc_s[10] += fold(dn)
            scaled = dn * gains[0:1]
            mean_plain = jnp.mean(scaled, axis=-1, keepdims=True)
            mean_hat = jnp.mean(scaled * hat, axis=-1, keepdims=True)
            grad = (scaled - mean_plain - hat * mean_hat) * inva_s[at(block), 0:1]
            wide_s[block, :] = grad
            da_s[at(block), :] = grad.astype(BF16)
            acc_s[2] += fold(grad)

        attended_low = da_s[rows, :]
        mixed, scored, values_back = {}, {}, {}
        total = None
        for step in range(count + 2):
            if step < count:
                mixed[step] = dot_t(attended_low, wo_s[columns[step], :]).astype(BF16)
            spot = step - 1
            if 0 <= spot < count:
                tall = stacked(mixed[spot])
                grad_attend = dot_t(v_s[rows, columns[spot]], tall)
                values_back[spot] = dot(p_s[index, spot], tall)
                attend = p_s[index, spot].astype(F32)
                weighted = attend * grad_attend
                delta = jnp.sum(weighted, axis=0, keepdims=True) / jnp.sum(attend, axis=0, keepdims=True)
                scored[spot] = (weighted - attend * delta).astype(BF16)
            spot = step - 2
            if 0 <= spot:
                column = columns[spot]
                dk = dot(scored[spot], stacked(q_s[rows, column]))
                dq = mixed_by(scored[spot], k_s[rows, column]) * 0.125
                dv = values_back[spot]
                acc_s[0, :, column] += fold(dq)
                acc_s[1, :, column] += fold(dv)
                dq, dk, dv = dq.astype(BF16), dk.astype(BF16), dv.astype(BF16)
                q_s[rows, column] = dq
                k_s[rows, column] = dk
                v_s[rows, column] = dv
                for grad, weight in ((dq, wq_s), (dk, wk_s), (dv, wv_s)):
                    product = dot_t(grad, weight[:, column])
                    total = product if total is None else total + product

        @pl.when(last)
        def _():
            low = (wide_s[...] + total).astype(BF16)
            y_s[rows, :] = low
            dx_s[rows, :] = low.astype(F32)
            backward_send(index).start()

        @pl.when(first)
        def _():
            start, stop = spans[0, index], spans[1, index]
            spot = lax.broadcasted_iota(jnp.int32, (LENGTH, D), 0)
            keep = (spot < start) | (spot >= stop)
            dx_s[rows, :] = jnp.where(keep, wide_s[...] + total, 0.0)

        dx_copy(index).start()
        for copy in right_copies(index):
            copy.start()
        return carry

    lax.fori_loop(0, micro_count, backward, 0)

    @pl.when(last)
    def _():
        transpose_all()

    for number in range(12):
        if 4 <= number < 8:
            panel = accu_s[:, (number - 4) * D : (number - 3) * D]
        else:
            panel = acc_s[number]
        small_out[number : number + 1, :] = jnp.sum(panel, axis=0, keepdims=True)
    small_out[12:16, :] = jnp.zeros((4, D), F32)

    def backward_done(index, carry):
        @pl.when(last)
        def _():
            backward_send(index).wait_send()

        dx_copy(index).wait()
        for copy in right_copies(index):
            copy.wait()
        return carry

    lax.fori_loop(0, micro_count, backward_done, 0)


def run_layers(tokens, cotangent, lengths, spans, *weights):
    rows = tokens.shape[0]
    micro_count = rows // ROWS
    anywhere = pl.BlockSpec(memory_space=pl.ANY)
    scalars = pl.BlockSpec(memory_space=pltpu.SMEM)
    vectors = pl.BlockSpec(memory_space=pltpu.VMEM)
    out_shape = (
        jax.ShapeDtypeStruct((rows, D), BF16),
        jax.ShapeDtypeStruct((rows, D), F32),
        jax.ShapeDtypeStruct((3 * D + FF, rows), BF16),
        jax.ShapeDtypeStruct((9, rows, D), BF16),
        jax.ShapeDtypeStruct((16, D), F32),
    )

    def vm(count, width=D, dtype=BF16):
        return pltpu.VMEM((count, width), dtype)

    scratch = [
        vm(D), vm(D), vm(D), vm(D), vm(D, FF), vm(FF),
        vm(rows), vm(rows), vm(rows), vm(rows),
        pltpu.VMEM((micro_count, QUADS, LENGTH, 4 * LENGTH), BF16),
        vm(rows), vm(rows), vm(rows), vm(rows), vm(rows, FF), vm(rows, FF),
        vm(rows, 128, F32), vm(rows, 128, F32),
        vm(rows), vm(rows), vm(rows), vm(rows), vm(rows, D, F32),
        vm(ROWS, D, F32), pltpu.VMEM((2, TURN, rows), BF16), pltpu.VMEM((12, 8, D), F32), vm(8, FF, F32),
        pltpu.SemaphoreType.DMA((6,)),
        pltpu.SemaphoreType.DMA((micro_count,)),
        pltpu.SemaphoreType.DMA((11, micro_count)),
        pltpu.SemaphoreType.DMA((2,)),
        pltpu.SemaphoreType.DMA((micro_count,)),
        pltpu.SemaphoreType.DMA((micro_count,)),
        pltpu.SemaphoreType.DMA((micro_count,)),
        pltpu.SemaphoreType.DMA((micro_count,)),
    ]
    return pl.pallas_call(
        functools.partial(layers_kernel, micro_count),
        out_shape=out_shape,
        in_specs=[anywhere, anywhere, scalars, scalars] + [anywhere] * 6 + [vectors] * 4,
        out_specs=[anywhere] * 4 + [vectors],
        scratch_shapes=scratch,
        compiler_params=pltpu.CompilerParams(
            collective_id=0, has_side_effects=True, vmem_limit_bytes=60 * 1024 * 1024
        ),
        cost_estimate=pl.CostEstimate(
            flops=rows * 2 * 2 * 2 * 7077888, bytes_accessed=60000000, transcendentals=rows * FF * 2
        ),
    )(tokens, cotangent, lengths, spans.T, *weights)


RING = 8
PIECES = 3
PIECE = D // RING
PANELS = (
    (0, 0), (0, 1), (0, 2), (D, 3), (2 * D, 4), (2 * D, 5),
    (2 * D, 6), (2 * D, 7), (3 * D, 8), (4 * D, 8), (5 * D, 8), (6 * D, 8),
)


def sums_kernel(
    left, right, small_in, grads_out, small_out,
    left_s, right_s, total_s, give_s, take_s, ring_s,
    tiny_s, tiny_take_s, tiny_sum_s, tiny_go_s, tiny_ring_s, tiny_own_s,
    load_sem, give_sem, take_sem, ring_send, ring_recv, round_send, round_recv, share_send, share_recv,
    tiny_sem, tiny_ring_send, tiny_ring_recv, tiny_round_send, tiny_round_recv,
):
    me = lax.axis_index("dp")
    core = lax.rem(me, 2)
    high = lax.rem(lax.div(me, 2), 2)
    depth = lax.div(me, 4)
    place = depth + high * (7 - 2 * depth)

    def device(spot, on_core):
        row = lax.div(spot, 4)
        return {"dp": 4 * (spot + row * (7 - 2 * spot)) + 2 * row + on_core}

    ahead = device(lax.rem(place + 1, RING), core)
    behind = device(lax.rem(place + RING - 1, RING), core)
    beside = device(place, 1 - core)
    targets = (ahead, behind)

    barrier = pltpu.get_barrier_semaphore()
    for peer in (ahead, behind, beside):
        pl.semaphore_signal(barrier, inc=1, device_id=peer, device_id_type=MESH)

    def block(way, step):
        return lax.rem(place - step + RING, RING) if way == 0 else lax.rem(place + step, RING)

    def late_block(way, step):
        return lax.rem(place + 1 - step + RING, RING) if way == 0 else lax.rem(place + RING - 1 + step, RING)

    def load_left(part):
        return pltpu.make_async_copy(left.at[pl.ds(part * D, D)], left_s.at[pl.ds(part * D, D)], load_sem.at[part])

    def load_right(part):
        return pltpu.make_async_copy(right.at[part], right_s.at[part], load_sem.at[7 + part])

    def remote(source, target, send, recv, peer):
        return pltpu.make_async_remote_copy(
            src_ref=source, dst_ref=target, send_sem=send, recv_sem=recv, device_id=peer, device_id_type=MESH
        )

    def give(way, step, piece):
        return remote(
            give_s.at[way, lax.rem(step, 4), piece], take_s.at[way, step, piece],
            give_sem.at[way, step, piece], take_sem.at[way, step, piece], beside,
        )

    def ring_copy(way, step, piece):
        return remote(
            take_s.at[way, step, piece], ring_s.at[way, step, piece],
            ring_send.at[way, step, piece], ring_recv.at[way, step, piece], targets[way],
        )

    def region(way, spot, piece, on_core):
        rows = pl.ds(pl.multiple_of(spot * PIECE, PIECE), PIECE)
        return grads_out.at[6 * way + 3 * on_core + piece, rows]

    def round_copy(way, step, piece):
        target = region(way, late_block(way, step), piece, core)
        return remote(
            target, target, round_send.at[way, step, piece], round_recv.at[way, step, piece], targets[way]
        )

    def round_wait(way, step, piece):
        target = region(way, late_block(way, step + 1), piece, core)
        remote(
            target, target, round_send.at[way, step, piece], round_recv.at[way, step, piece], targets[way]
        ).wait_recv()

    def share_copy(way, step, piece):
        target = region(way, late_block(way, step), piece, core)
        return remote(
            target, target, share_send.at[way, step, piece], share_recv.at[way, step, piece], beside
        )

    def share_wait(way, step, piece):
        target = region(way, late_block(way, step), piece, 1 - core)
        remote(
            target, target, share_send.at[way, step, piece], share_recv.at[way, step, piece], beside
        ).wait_recv()

    tiny_swap = remote(tiny_s, tiny_take_s, tiny_sem.at[0], tiny_sem.at[1], beside)

    def tiny_ring(step):
        return remote(
            tiny_go_s.at[step], tiny_ring_s.at[step], tiny_ring_send.at[step], tiny_ring_recv.at[step], ahead
        )

    def tiny_round(step):
        spot = late_block(0, step)
        return remote(
            tiny_own_s.at[spot], tiny_own_s.at[spot], tiny_round_send.at[step], tiny_round_recv.at[step], ahead
        )

    def tiny_round_wait(step):
        spot = late_block(0, step + 1)
        remote(
            tiny_own_s.at[spot], tiny_own_s.at[spot], tiny_round_send.at[step], tiny_round_recv.at[step], ahead
        ).wait_recv()

    loads = []
    for piece in range(PIECES):
        for way in range(2):
            for half in range(2):
                first_row, number = PANELS[6 * way + 3 * half + piece]
                for kind, part in ((load_right, number), (load_left, first_row // D)):
                    if (kind, part) not in [entry[:2] for entry in loads]:
                        loads.append((kind, part, way, piece))
    order = [(way, piece) for piece in range(PIECES) for way in range(2)]
    groups = [[kind(part) for kind, part, *spot in loads if tuple(spot) == pair] for pair in order]
    for group in groups[:2]:
        for copy in group:
            copy.start()

    for part in range(RING):
        if part * 128 < D:
            tiny_s[part] = small_in[:, part * 128 : part * 128 + 128]
        else:
            tiny_s[part] = jnp.zeros((16, 128), F32)

    pl.semaphore_wait(barrier, 3)
    tiny_swap.start()

    def product(group, way, piece, pick):
        near, far = PANELS[6 * way + piece], PANELS[6 * way + 3 + piece]
        first_row = near[0] + pick * (far[0] - near[0])
        number = near[1] + pick * (far[1] - near[1])
        blocks = []
        for step in (2 * group, 2 * group + 1):
            start = pl.multiple_of(first_row + block(way, step) * PIECE, PIECE)
            blocks.append(left_s[pl.ds(start, PIECE), :])
        return dot(jnp.concatenate(blocks, axis=0), right_s[number])

    def keep_product(group, way, piece, both):
        total_s[lax.rem(2 * group, 3), way, piece] = both[:PIECE]
        total_s[lax.rem(2 * group + 1, 3), way, piece] = both[PIECE:]

    def give_product(group, way, piece, both):
        @pl.when(group >= 2)
        def _():
            give(way, 2 * group - 4, piece).wait_send()
            give(way, 2 * group - 3, piece).wait_send()

        give_s[way, lax.rem(2 * group, 4), piece] = both[:PIECE].astype(BF16)
        give_s[way, lax.rem(2 * group + 1, 4), piece] = both[PIECE:].astype(BF16)
        give(way, 2 * group, piece).start()
        give(way, 2 * group + 1, piece).start()

    def add_piece(step, way, piece, target):
        slot = lax.rem(step, 3)
        for r0 in range(0, PIECE, SUB):
            part = slice(r0, r0 + SUB)
            whole = total_s[slot, way, piece, part] + take_s[way, step, piece, part].astype(F32)
            target[part] = whole.astype(BF16)

    def reduce_step(step, carry):
        slot = lax.rem(step, 3)
        spot = block(0, step)

        @pl.when(step < RING - 1)
        def _():
            tiny_ring(step - 1).wait_recv()
            tiny_go_s[step] = tiny_sum_s[spot] + tiny_ring_s[step - 1]
            tiny_ring(step).start()

        @pl.when(step == RING - 1)
        def _():
            tiny_ring(step - 1).wait_recv()
            tiny_own_s[spot] = tiny_sum_s[spot] + tiny_ring_s[step - 1]
            tiny_round(0).start()

        for piece in range(PIECES):
            for way in range(2):
                give(way, step, piece).wait_recv()
                ring_copy(way, step - 1, piece).wait_recv()
                for r0 in range(0, PIECE, SUB):
                    part = slice(r0, r0 + SUB)
                    total_s[slot, way, piece, part] += ring_s[way, step - 1, piece, part].astype(F32)

                @pl.when(step < RING - 1)
                def _():
                    add_piece(step, way, piece, take_s.at[way, step, piece])
                    ring_copy(way, step, piece).start()

                @pl.when(step == RING - 1)
                def _():
                    add_piece(step, way, piece, region(way, late_block(way, 0), piece, core))
                    round_copy(way, 0, piece).start()
                    share_copy(way, 0, piece).start()

                @pl.when(step < RING - 2)
                def _():
                    odd = lax.rem(step, 2)
                    group = lax.div(step, 2) + 1
                    both = product(group, way, piece, odd * core + (1 - odd) * (1 - core))

                    @pl.when(odd == 1)
                    def _():
                        keep_product(group, way, piece, both)

                    @pl.when(odd == 0)
                    def _():
                        give_product(group, way, piece, both)

        return carry

    def first_piece(way, piece):
        give(way, 0, piece).wait_recv()
        add_piece(0, way, piece, take_s.at[way, 0, piece])
        ring_copy(way, 0, piece).start()

    for number, (way, piece) in enumerate(order):
        for copy in groups[number]:
            copy.wait()
        if number + 2 < len(groups):
            for copy in groups[number + 2]:
                copy.start()
        give_product(0, way, piece, product(0, way, piece, 1 - core))
        keep_product(0, way, piece, product(0, way, piece, core))
        if number > 0:
            first_piece(*order[number - 1])
    first_piece(*order[-1])
    for way, piece in order:
        give_product(1, way, piece, product(1, way, piece, 1 - core))
    tiny_swap.wait_recv()
    tiny_sum_s[...] = tiny_s[...] + tiny_take_s[...]
    tiny_go_s[0] = tiny_sum_s[block(0, 0)]
    tiny_ring(0).start()

    lax.fori_loop(1, RING, reduce_step, 0)

    def round_step(step, carry):
        tiny_round_wait(step - 1)

        @pl.when(step < RING - 1)
        def _():
            tiny_round(step).start()

        for piece in range(PIECES):
            for way in range(2):
                round_wait(way, step - 1, piece)

                @pl.when(step < RING - 1)
                def _():
                    round_copy(way, step, piece).start()

                share_copy(way, step, piece).start()
        return carry

    lax.fori_loop(1, RING, round_step, 0)

    for part in range(D // 128):
        small_out[:, part * 128 : part * 128 + 128] = tiny_own_s[part]
    tiny_swap.wait_send()

    def finish(step, carry):
        for way in range(2):
            for piece in range(PIECES):

                @pl.when(step >= RING // 2)
                def _():
                    give(way, step, piece).wait_send()

                share_wait(way, step, piece)
                share_copy(way, step, piece).wait_send()

                @pl.when(step < RING - 1)
                def _():
                    ring_copy(way, step, piece).wait_send()
                    round_copy(way, step, piece).wait_send()

        @pl.when(step < RING - 1)
        def _():
            tiny_ring(step).wait_send()
            tiny_round(step).wait_send()

        return carry

    lax.fori_loop(0, RING, finish, 0)


def run_sums(left, right, small):
    rows = right.shape[1]
    anywhere = pl.BlockSpec(memory_space=pl.ANY)
    vectors = pl.BlockSpec(memory_space=pltpu.VMEM)

    def pieces(*lead, dtype=BF16):
        return pltpu.VMEM((*lead, PIECE, D), dtype)

    dma = pltpu.SemaphoreType.DMA
    scratch = [
        pltpu.VMEM(left.shape, BF16), pltpu.VMEM(right.shape, BF16),
        pieces(3, 2, PIECES, dtype=F32), pieces(2, 4, PIECES), pieces(2, RING, PIECES),
        pieces(2, RING - 1, PIECES),
        pltpu.VMEM((RING, 16, 128), F32), pltpu.VMEM((RING, 16, 128), F32), pltpu.VMEM((RING, 16, 128), F32),
        pltpu.VMEM((RING - 1, 16, 128), F32), pltpu.VMEM((RING - 1, 16, 128), F32), pltpu.VMEM((RING, 16, 128), F32),
        dma((16,)), dma((2, RING, PIECES)), dma((2, RING, PIECES)),
        dma((2, RING - 1, PIECES)), dma((2, RING - 1, PIECES)),
        dma((2, RING - 1, PIECES)), dma((2, RING - 1, PIECES)), dma((2, RING, PIECES)), dma((2, RING, PIECES)),
        dma((2,)), dma((RING - 1,)), dma((RING - 1,)), dma((RING - 1,)), dma((RING - 1,)),
    ]
    return pl.pallas_call(
        sums_kernel,
        out_shape=(pltpu.VMEM((12, D, D), BF16), jax.ShapeDtypeStruct((16, D), F32)),
        in_specs=[anywhere, anywhere, vectors],
        out_specs=[vectors, vectors],
        scratch_shapes=scratch,
        compiler_params=pltpu.CompilerParams(
            collective_id=1, has_side_effects=True, vmem_limit_bytes=48 * 1024 * 1024
        ),
        cost_estimate=pl.CostEstimate(flops=rows * 2 * 7077888, bytes_accessed=70000000, transcendentals=0),
    )(left, right, small)


def plain_sums(left, right, small):
    panels = [dot(left[row : row + D], right[number]).astype(BF16) for row, number in PANELS]
    return lax.psum(jnp.stack(panels), "dp"), lax.psum(small, "dp")


SLOTS = 8
CUT = D // 2


def widen_kernel(
    act, dx, grads, small, act_out, dx_out, query_out, key_out, value_out, out_out, up_out, down_out,
    bias_out, up_bias_out, gain_out, shift_out, wide_s, act_s, dx_s, out_sem, move_sem,
):
    moves_in = [
        pltpu.make_async_copy(act, act_s, move_sem.at[0]), pltpu.make_async_copy(dx, dx_s, move_sem.at[1])
    ]
    moves_out = [
        pltpu.make_async_copy(act_s, act_out.at[0], move_sem.at[0]),
        pltpu.make_async_copy(dx_s, dx_out.at[0], move_sem.at[1]),
    ]
    jobs = []
    for panel in range(12):
        for half in range(2):
            rows = pl.ds(half * CUT, CUT)
            if panel < 4:
                target = (query_out, key_out, value_out, out_out)[panel].at[0, rows]
            elif panel < 8:
                target = up_out.at[0, rows, pl.ds((panel - 4) * D, D)]
            else:
                target = down_out.at[0, pl.ds((panel - 8) * D + half * CUT, CUT)]
            jobs.append((panel, half * CUT, target))

    def store(number):
        return pltpu.make_async_copy(wide_s.at[number % SLOTS], jobs[number][2], out_sem.at[number % SLOTS])

    for move in moves_in:
        move.start()
    bias_out[0] = small[0:4]
    for panel in range(FF // D):
        up_bias_out[:, panel * D : (panel + 1) * D] = small[4 + panel : 5 + panel]
    gain_out[0] = small[8:10]
    shift_out[0] = small[10:12]
    for number in range(len(jobs)):
        slot = number % SLOTS
        panel, start, _ = jobs[number]
        if number >= SLOTS:
            store(number - SLOTS).wait()

        def turn(step, carry):
            part = pl.ds(pl.multiple_of(step * SUB, SUB), SUB)
            here = pl.ds(pl.multiple_of(start + step * SUB, SUB), SUB)
            wide_s[slot, part, :] = grads[panel, here, :].astype(F32)
            return carry

        lax.fori_loop(0, CUT // SUB, turn, 0, unroll=4)
        store(number).start()
        if number == SLOTS:
            for move_in, move_out in zip(moves_in, moves_out):
                move_in.wait()
                move_out.start()
    for number in range(len(jobs) - SLOTS, len(jobs)):
        store(number).wait()
    for move in moves_out:
        move.wait()


def widen(act, dx, grads, small):
    anywhere = pl.BlockSpec(memory_space=pl.ANY)
    vectors = pl.BlockSpec(memory_space=pltpu.VMEM)
    square = jax.ShapeDtypeStruct((1, D, D), F32)
    return pl.pallas_call(
        widen_kernel,
        out_shape=(
            jax.ShapeDtypeStruct((1, *act.shape), BF16), jax.ShapeDtypeStruct((1, *dx.shape), F32),
            square, square, square, square,
            jax.ShapeDtypeStruct((1, D, FF), F32), jax.ShapeDtypeStruct((1, FF, D), F32),
            jax.ShapeDtypeStruct((1, 4, D), F32), jax.ShapeDtypeStruct((1, FF), F32),
            jax.ShapeDtypeStruct((1, 2, D), F32), jax.ShapeDtypeStruct((1, 2, D), F32),
        ),
        in_specs=[anywhere, anywhere, vectors, vectors],
        out_specs=[anywhere] * 8 + [vectors] * 4,
        scratch_shapes=[
            pltpu.VMEM((SLOTS, CUT, D), F32),
            pltpu.VMEM(act.shape, BF16), pltpu.VMEM(dx.shape, F32),
            pltpu.SemaphoreType.DMA((SLOTS,)), pltpu.SemaphoreType.DMA((2,)),
        ],
        compiler_params=pltpu.CompilerParams(vmem_limit_bytes=46 * 1024 * 1024),
        cost_estimate=pl.CostEstimate(flops=7077888, bytes_accessed=42467328, transcendentals=0),
    )(act, dx, grads, small)


def per_device(grid, tokens, cotangent, lengths, spans, *weights):
    act, dx, left, right, small = run_layers(tokens, cotangent, lengths, spans, *weights)
    grads, small = (run_sums if grid else plain_sums)(left, right, small)
    grads = pltpu.with_memory_space_constraint(grads, pltpu.VMEM)
    return widen(act, dx, grads, small)


def solution(mesh):
    in_specs = (
        P("dp", None), P("dp", None), P("dp"), P("dp", None),
        P("section", None, None), P("section", None, None), P("section", None, None),
        P("section", None, None), P("section", None, None), P("section", None, None),
        P("section", None, None), P("section", None), P("section", None, None), P("section", None, None),
    )
    out_specs = (
        P("section", "dp", None), P("section", "dp", None),
        P("section", None, None), P("section", None, None), P("section", None, None),
        P("section", None, None), P("section", None, None), P("section", None, None),
        P("section", None, None), P("section", None), P("section", None, None), P("section", None, None),
    )
    part = functools.partial(per_device, mesh.shape["dp"] == 2 * RING)
    return jax.shard_map(part, mesh=mesh, in_specs=in_specs, out_specs=out_specs, check_vma=False)
```

```python
import functools

import jax
import jax.numpy as jnp
from jax import lax
from jax.experimental import pallas as pl
from jax.experimental.pallas import tpu as pltpu
from jax.sharding import PartitionSpec as P

D = 768
HEADS = 12
HEAD_DIM = 64
QUADS = HEADS // 4
FF = 3072
LENGTH = 160
LEAST = 96
ROWS = LENGTH
SUB = 32
BAND = 80
WIDE = 512
TURN = 256
PART = 256

F32 = jnp.float32
BF16 = jnp.bfloat16
MESH = pl.DeviceIdType.MESH


def dot(left, right):
    return jnp.dot(left, right, preferred_element_type=F32)


def dot_t(left, right):
    return lax.dot_general(left, right, (((1,), (1,)), ((), ())), preferred_element_type=F32)


def fold(block):
    return jnp.sum(block.reshape(-1, 8, block.shape[-1]), axis=0)


def gelu_parts(u):
    t = pl.reciprocal(1.0 + 0.23164189 * jnp.abs(u), approx=True)
    gauss = jnp.exp2(u * u * -0.7213475204444817)
    poly = t * (
        0.127414796 + t * (-0.142248368 + t * (0.7107068705 + t * (-0.7265760135 + t * 0.5307027145)))
    )
    tail = poly * gauss
    cdf = jnp.where(u >= 0, 1.0 - tail, tail)
    return u * cdf, cdf + (u * 0.3989422804014327) * gauss


def layers_kernel(
    micro_count,
    tokens, cotangent, lengths, spans,
    wq, wk, wv, wo, w1, w2, bias_in, up_bias_in, gains_in, shifts_in,
    act_out, dx_out, left_out, right_out, small_out,
    wq_s, wk_s, wv_s, wo_s, w1_s, w2_s,
    h_s, q_s, k_s, v_s, p_s, o_s, n_s, xa_s, xb_s, z_s, g_s, inva_s, invb_s,
    y_s, dy_s, df_s, da_s, dx_s, wide_s, turn_s, acc_s, accu_s,
    w_sem, in_sem, out_sem, turn_sem, fwd_send, fwd_recv, bwd_send, bwd_recv,
):
    section = lax.axis_index("section")
    other = 1 - section
    first = section == 0
    last = section == 1
    core = lax.rem(lax.axis_index("dp"), 2)

    barrier = pltpu.get_barrier_semaphore()
    pl.semaphore_signal(barrier, inc=1, device_id={"section": other}, device_id_type=MESH)

    weight_pairs = ((wq, wq_s), (wk, wk_s), (wv, wv_s), (wo, wo_s), (w1, w1_s), (w2, w2_s))

    def weight_copy(index):
        source, target = weight_pairs[index]
        return pltpu.make_async_copy(source.at[0], target, w_sem.at[index])

    def rows_of(index):
        return pl.ds(pl.multiple_of(index * ROWS, ROWS), ROWS)

    def entry_copy(index):
        return pltpu.make_async_copy(tokens.at[rows_of(index)], h_s.at[rows_of(index)], in_sem.at[index])

    def cot_copy(index):
        return pltpu.make_async_copy(cotangent.at[rows_of(index)], dy_s.at[rows_of(index)], in_sem.at[index])

    def forward_send(index):
        return pltpu.make_async_remote_copy(
            src_ref=y_s.at[rows_of(index)],
            dst_ref=h_s.at[rows_of(index)],
            send_sem=fwd_send.at[index],
            recv_sem=fwd_recv.at[index],
            device_id={"section": other},
            device_id_type=MESH,
        )

    def backward_send(index):
        return pltpu.make_async_remote_copy(
            src_ref=y_s.at[rows_of(index)],
            dst_ref=dy_s.at[rows_of(index)],
            send_sem=bwd_send.at[index],
            recv_sem=bwd_recv.at[index],
            device_id={"section": other},
            device_id_type=MESH,
        )

    backward_outs = ((q_s, 0), (k_s, 1), (v_s, 2), (da_s, 3), (df_s, 8))

    def act_copy(index):
        return pltpu.make_async_copy(y_s.at[rows_of(index)], act_out.at[rows_of(index)], out_sem.at[0, index])

    def dx_copy(index):
        return pltpu.make_async_copy(dx_s.at[rows_of(index)], dx_out.at[rows_of(index)], out_sem.at[1, index])

    def right_copies(index):
        for slot, (source, place) in enumerate(backward_outs):
            yield pltpu.make_async_copy(
                source.at[rows_of(index)], right_out.at[place, rows_of(index)], out_sem.at[2 + slot, index]
            )
        for panel in range(FF // D):
            yield pltpu.make_async_copy(
                g_s.at[rows_of(index), pl.ds(panel * D, D)],
                right_out.at[4 + panel, rows_of(index)],
                out_sem.at[7 + panel, index],
            )

    def turn_copy(slot, row):
        return pltpu.make_async_copy(
            turn_s.at[slot], left_out.at[pl.ds(pl.multiple_of(row, TURN), TURN)], turn_sem.at[slot]
        )

    def transpose_all():
        done = 0
        for source, tiles in ((h_s, D // TURN), (o_s, D // TURN), (n_s, D // TURN), (z_s, FF // TURN)):

            def tile_step(tile, carry, source=source, done=done):
                number = tile + done
                slot = lax.rem(number, 2)

                @pl.when(number >= 2)
                def _():
                    turn_copy(slot, (number - 2) * TURN).wait()

                turn_s[slot] = source[:, pl.ds(pl.multiple_of(tile * TURN, TURN), TURN)].T
                turn_copy(slot, number * TURN).start()
                return carry

            lax.fori_loop(0, tiles, tile_step, 0)
            done += tiles
        for number in (done - 2, done - 1):
            turn_copy(number % 2, number * TURN).wait()

    @pl.when(first)
    def _():
        entry_copy(0).start()

    for index in range(4):
        weight_copy(index).start()

    acc_s[...] = jnp.zeros_like(acc_s)
    accu_s[...] = jnp.zeros_like(accu_s)

    bias = bias_in[0].astype(F32)
    gains = gains_in[0].astype(F32)
    shifts = shifts_in[0].astype(F32)
    low_half = lax.broadcasted_iota(jnp.int32, (1, 8, 128), 2) < HEAD_DIM
    lane = lax.broadcasted_iota(jnp.int32, (1, 16, PART), 2)
    keeps = [
        jnp.where((lane >= head * HEAD_DIM) & (lane < (head + 1) * HEAD_DIM), 1.0, 0.0).astype(BF16)
        for head in range(4)
    ]

    def stacked(quad_block):
        tiles = quad_block.reshape(-1, 16, PART)
        return jnp.concatenate([tiles * keep for keep in keeps], axis=0).reshape(4 * LENGTH, PART)

    def mixed_by(table, quad_block):
        tall = table.T
        parts = []
        for half in halves:
            start = 2 * LENGTH * (half.start // 128)
            tiles = dot(tall[start : start + 2 * LENGTH], quad_block[:, half]).reshape(2, LENGTH // 8, 8, 128)
            parts.append(jnp.where(low_half, tiles[0], tiles[1]).reshape(LENGTH, 128))
        return jnp.concatenate(parts, axis=1)

    pl.semaphore_wait(barrier, 1)

    blocks = [slice(r0, r0 + BAND) for r0 in range(0, ROWS, BAND)]
    columns = [slice(c0, c0 + PART) for c0 in range(0, D, PART)]
    panels = [slice(n0, n0 + WIDE) for n0 in range(0, FF, WIDE)]
    halves = [slice(0, 128), slice(128, 256)]
    count, chunks = len(columns), len(panels)

    def forward(index, carry):
        base = index * ROWS
        rows = rows_of(index)

        def at(block):
            return pl.ds(pl.multiple_of(base + block.start, BAND), BAND)

        @pl.when(index == 0)
        def _():
            for number in range(4):
                weight_copy(number).wait()
            for number in (4, 5):
                weight_copy(number).start()

            @pl.when(first)
            def _():
                for later in range(1, micro_count):
                    entry_copy(later).start()

            @pl.when(last)
            def _():
                for later in range(micro_count):
                    cot_copy(later).start()

            @pl.when(core == 1)
            def _():
                weight_copy(4).wait()
                weight_copy(5).wait()

        @pl.when(first)
        def _():
            entry_copy(index).wait()
            start, stop = spans[0, index], spans[1, index]
            spot = lax.broadcasted_iota(jnp.int32, (LENGTH, D), 0)
            keep = (spot < start) | (spot >= stop)
            h_s[rows, :] = jnp.where(keep, h_s[rows, :].astype(F32), 0.0).astype(BF16)

        @pl.when(last)
        def _():
            forward_send(index).wait_recv()

        hidden = h_s[rows, :]

        def project(column):
            query = ((dot(hidden, wq_s[:, column]) + bias[0:1, column]) * 0.125).astype(BF16)
            key_rows = dot(hidden, wk_s[:, column]).astype(BF16)
            value = (dot(hidden, wv_s[:, column]) + bias[1:2, column]).astype(BF16)
            q_s[rows, column] = query
            k_s[rows, column] = key_rows
            v_s[rows, column] = value
            return query, key_rows, value

        spot = lax.broadcasted_iota(jnp.int32, (LENGTH - LEAST, 4 * LENGTH), 0) + LEAST
        penalty = jnp.where(spot < lengths[index], 0.0, -1000000000.0)
        projected, attends = {}, {}
        attended = None
        for step in range(count + 2):
            if step < count:
                projected[step] = project(columns[step])
            spot = step - 1
            if 0 <= spot < count:
                query, key_rows, _ = projected[spot]
                scores = dot_t(key_rows, stacked(query))
                held = jnp.concatenate([scores[:LEAST], scores[LEAST:] + penalty], axis=0)
                raised = jnp.exp(held - jnp.max(held, axis=0, keepdims=True))
                attends[spot] = (raised * (1.0 / jnp.sum(raised, axis=0, keepdims=True))).astype(BF16)
                p_s[index, spot] = attends[spot]
            spot = step - 2
            if 0 <= spot:
                mixture = mixed_by(attends[spot], projected[spot][2]).astype(BF16)
                o_s[rows, columns[spot]] = mixture
                product = dot(mixture, wo_s[columns[spot], :])
                attended = product if attended is None else attended + product

        for block in blocks:
            r = h_s[at(block), :].astype(F32) + attended[block] + bias[2:3]
            centered = r - jnp.mean(r, axis=-1, keepdims=True)
            inv = lax.rsqrt(jnp.mean(centered * centered, axis=-1, keepdims=True) + 1e-05)
            hat = centered * inv
            normed = hat * gains[0:1] + shifts[0:1]
            xa_s[at(block), :] = hat.astype(BF16)
            inva_s[at(block), :] = jnp.broadcast_to(inv, (BAND, 128))
            n_s[at(block), :] = normed.astype(BF16)
            wide_s[block, :] = normed

        @pl.when((index == 0) & (core == 0))
        def _():
            weight_copy(4).wait()
            weight_copy(5).wait()

        normed_low = n_s[rows, :]
        lifted = {}
        outer = None
        for step in range(chunks + 2):
            if step < chunks:
                lifted[step] = dot(normed_low, w1_s[:, panels[step]])
            spot = step - 1
            if 0 <= spot < chunks:
                up_bias = up_bias_in[0:1, panels[spot]].astype(F32)
                for block in blocks:
                    act, slope = gelu_parts(lifted[spot][block] + up_bias)
                    z_s[at(block), panels[spot]] = act.astype(BF16)
                    g_s[at(block), panels[spot]] = slope.astype(BF16)
            spot = step - 2
            if 0 <= spot:
                product = dot(z_s[rows, panels[spot]], w2_s[panels[spot], :])
                outer = product if outer is None else outer + product

        for block in blocks:
            r = wide_s[block, :] + outer[block] + bias[3:4]
            centered = r - jnp.mean(r, axis=-1, keepdims=True)
            inv = lax.rsqrt(jnp.mean(centered * centered, axis=-1, keepdims=True) + 1e-05)
            hat = centered * inv
            xb_s[at(block), :] = hat.astype(BF16)
            invb_s[at(block), :] = jnp.broadcast_to(inv, (BAND, 128))
            y_s[at(block), :] = (hat * gains[1:2] + shifts[1:2]).astype(BF16)

        @pl.when(first)
        def _():
            forward_send(index).start()

        act_copy(index).start()
        return carry

    lax.fori_loop(0, micro_count, forward, 0)

    def forward_done(index, carry):
        @pl.when(first)
        def _():
            forward_send(index).wait_send()

        act_copy(index).wait()
        return carry

    lax.fori_loop(0, micro_count, forward_done, 0)

    @pl.when(first)
    def _():
        transpose_all()

    def backward(index, carry):
        base = index * ROWS
        rows = rows_of(index)

        def at(block):
            return pl.ds(pl.multiple_of(base + block.start, BAND), BAND)

        @pl.when(first)
        def _():
            backward_send(index).wait_recv()

        @pl.when(last)
        def _():
            cot_copy(index).wait()

        for block in blocks:
            dy = dy_s[at(block), :].astype(F32)
            hat = xb_s[at(block), :].astype(F32)
            acc_s[9] += fold(dy * hat)
            acc_s[11] += fold(dy)
            scaled = dy * gains[1:2]
            mean_plain = jnp.mean(scaled, axis=-1, keepdims=True)
            mean_hat = jnp.mean(scaled * hat, axis=-1, keepdims=True)
            grad = (scaled - mean_plain - hat * mean_hat) * invb_s[at(block), 0:1]
            wide_s[block, :] = grad
            df_s[at(block), :] = grad.astype(BF16)
            acc_s[3] += fold(grad)

        outer_low = df_s[rows, :]
        dropped = {}
        total = None
        for step in range(chunks + 2):
            if step < chunks:
                dropped[step] = dot_t(outer_low, w2_s[panels[step], :])
            spot = step - 1
            if 0 <= spot < chunks:
                sums = jnp.zeros((8, WIDE), F32)
                for block in blocks:
                    part = dropped[spot][block] * g_s[at(block), panels[spot]].astype(F32)
                    g_s[at(block), panels[spot]] = part.astype(BF16)
                    sums = sums + fold(part)
                accu_s[:, panels[spot]] += sums
            spot = step - 2
            if 0 <= spot:
                product = dot_t(g_s[rows, panels[spot]], w1_s[:, panels[spot]])
                total = product if total is None else total + product

        for block in blocks:
            dn = wide_s[block, :] + total[block]
            hat = xa_s[at(block), :].astype(F32)
            acc_s[8] += fold(dn * hat)
            acc_s[10] += fold(dn)
            scaled = dn * gains[0:1]
            mean_plain = jnp.mean(scaled, axis=-1, keepdims=True)
            mean_hat = jnp.mean(scaled * hat, axis=-1, keepdims=True)
            grad = (scaled - mean_plain - hat * mean_hat) * inva_s[at(block), 0:1]
            wide_s[block, :] = grad
            da_s[at(block), :] = grad.astype(BF16)
            acc_s[2] += fold(grad)

        attended_low = da_s[rows, :]
        mixed, scored, values_back = {}, {}, {}
        total = None
        for step in range(count + 2):
            if step < count:
                mixed[step] = dot_t(attended_low, wo_s[columns[step], :]).astype(BF16)
            spot = step - 1
            if 0 <= spot < count:
                tall = stacked(mixed[spot])
                grad_attend = dot_t(v_s[rows, columns[spot]], tall)
                values_back[spot] = dot(p_s[index, spot], tall)
                attend = p_s[index, spot].astype(F32)
                weighted = attend * grad_attend
                delta = jnp.sum(weighted, axis=0, keepdims=True) / jnp.sum(attend, axis=0, keepdims=True)
                scored[spot] = (weighted - attend * delta).astype(BF16)
            spot = step - 2
            if 0 <= spot:
                column = columns[spot]
                dk = dot(scored[spot], stacked(q_s[rows, column]))
                dq = mixed_by(scored[spot], k_s[rows, column]) * 0.125
                dv = values_back[spot]
                acc_s[0, :, column] += fold(dq)
                acc_s[1, :, column] += fold(dv)
                dq, dk, dv = dq.astype(BF16), dk.astype(BF16), dv.astype(BF16)
                q_s[rows, column] = dq
                k_s[rows, column] = dk
                v_s[rows, column] = dv
                for grad, weight in ((dq, wq_s), (dk, wk_s), (dv, wv_s)):
                    product = dot_t(grad, weight[:, column])
                    total = product if total is None else total + product

        @pl.when(last)
        def _():
            low = (wide_s[...] + total).astype(BF16)
            y_s[rows, :] = low
            dx_s[rows, :] = low.astype(F32)
            backward_send(index).start()

        @pl.when(first)
        def _():
            start, stop = spans[0, index], spans[1, index]
            spot = lax.broadcasted_iota(jnp.int32, (LENGTH, D), 0)
            keep = (spot < start) | (spot >= stop)
            dx_s[rows, :] = jnp.where(keep, wide_s[...] + total, 0.0)

        dx_copy(index).start()
        for copy in right_copies(index):
            copy.start()
        return carry

    lax.fori_loop(0, micro_count, backward, 0)

    @pl.when(last)
    def _():
        transpose_all()

    for number in range(12):
        if 4 <= number < 8:
            panel = accu_s[:, (number - 4) * D : (number - 3) * D]
        else:
            panel = acc_s[number]
        small_out[number : number + 1, :] = jnp.sum(panel, axis=0, keepdims=True)
    small_out[12:16, :] = jnp.zeros((4, D), F32)

    def backward_done(index, carry):
        @pl.when(last)
        def _():
            backward_send(index).wait_send()

        dx_copy(index).wait()
        for copy in right_copies(index):
            copy.wait()
        return carry

    lax.fori_loop(0, micro_count, backward_done, 0)


def run_layers(tokens, cotangent, lengths, spans, *weights):
    rows = tokens.shape[0]
    micro_count = rows // ROWS
    anywhere = pl.BlockSpec(memory_space=pl.ANY)
    scalars = pl.BlockSpec(memory_space=pltpu.SMEM)
    vectors = pl.BlockSpec(memory_space=pltpu.VMEM)
    out_shape = (
        jax.ShapeDtypeStruct((rows, D), BF16),
        jax.ShapeDtypeStruct((rows, D), F32),
        jax.ShapeDtypeStruct((3 * D + FF, rows), BF16),
        jax.ShapeDtypeStruct((9, rows, D), BF16),
        jax.ShapeDtypeStruct((16, D), F32),
    )

    def vm(count, width=D, dtype=BF16):
        return pltpu.VMEM((count, width), dtype)

    scratch = [
        vm(D), vm(D), vm(D), vm(D), vm(D, FF), vm(FF),
        vm(rows), vm(rows), vm(rows), vm(rows),
        pltpu.VMEM((micro_count, QUADS, LENGTH, 4 * LENGTH), BF16),
        vm(rows), vm(rows), vm(rows), vm(rows), vm(rows, FF), vm(rows, FF),
        vm(rows, 128, F32), vm(rows, 128, F32),
        vm(rows), vm(rows), vm(rows), vm(rows), vm(rows, D, F32),
        vm(ROWS, D, F32), pltpu.VMEM((2, TURN, rows), BF16), pltpu.VMEM((12, 8, D), F32), vm(8, FF, F32),
        pltpu.SemaphoreType.DMA((6,)),
        pltpu.SemaphoreType.DMA((micro_count,)),
        pltpu.SemaphoreType.DMA((11, micro_count)),
        pltpu.SemaphoreType.DMA((2,)),
        pltpu.SemaphoreType.DMA((micro_count,)),
        pltpu.SemaphoreType.DMA((micro_count,)),
        pltpu.SemaphoreType.DMA((micro_count,)),
        pltpu.SemaphoreType.DMA((micro_count,)),
    ]
    return pl.pallas_call(
        functools.partial(layers_kernel, micro_count),
        out_shape=out_shape,
        in_specs=[anywhere, anywhere, scalars, scalars] + [anywhere] * 6 + [vectors] * 4,
        out_specs=[anywhere] * 4 + [vectors],
        scratch_shapes=scratch,
        compiler_params=pltpu.CompilerParams(
            collective_id=0, has_side_effects=True, vmem_limit_bytes=60 * 1024 * 1024
        ),
        cost_estimate=pl.CostEstimate(
            flops=rows * 2 * 2 * 2 * 7077888, bytes_accessed=60000000, transcendentals=rows * FF * 2
        ),
    )(tokens, cotangent, lengths, spans.T, *weights)


RING = 8
PIECES = 3
PIECE = D // RING
PANELS = (
    (0, 0), (0, 1), (0, 2), (D, 3), (2 * D, 4), (2 * D, 5),
    (2 * D, 6), (2 * D, 7), (3 * D, 8), (4 * D, 8), (5 * D, 8), (6 * D, 8),
)


def sums_kernel(
    left, right, small_in, grads_out, small_out,
    left_s, right_s, total_s, give_s, take_s, ring_s,
    tiny_s, tiny_take_s, tiny_sum_s, tiny_go_s, tiny_ring_s, tiny_own_s,
    load_sem, give_sem, take_sem, ring_send, ring_recv, round_send, round_recv, share_send, share_recv,
    tiny_sem, tiny_ring_send, tiny_ring_recv, tiny_round_send, tiny_round_recv,
):
    me = lax.axis_index("dp")
    core = lax.rem(me, 2)
    high = lax.rem(lax.div(me, 2), 2)
    depth = lax.div(me, 4)
    place = depth + high * (7 - 2 * depth)

    def device(spot, on_core):
        row = lax.div(spot, 4)
        return {"dp": 4 * (spot + row * (7 - 2 * spot)) + 2 * row + on_core}

    ahead = device(lax.rem(place + 1, RING), core)
    behind = device(lax.rem(place + RING - 1, RING), core)
    beside = device(place, 1 - core)
    targets = (ahead, behind)

    barrier = pltpu.get_barrier_semaphore()
    for peer in (ahead, behind, beside):
        pl.semaphore_signal(barrier, inc=1, device_id=peer, device_id_type=MESH)

    def block(way, step):
        return lax.rem(place - step + RING, RING) if way == 0 else lax.rem(place + step, RING)

    def late_block(way, step):
        return lax.rem(place + 1 - step + RING, RING) if way == 0 else lax.rem(place + RING - 1 + step, RING)

    def load_left(part):
        return pltpu.make_async_copy(left.at[pl.ds(part * D, D)], left_s.at[pl.ds(part * D, D)], load_sem.at[part])

    def load_right(part):
        return pltpu.make_async_copy(right.at[part], right_s.at[part], load_sem.at[7 + part])

    def remote(source, target, send, recv, peer):
        return pltpu.make_async_remote_copy(
            src_ref=source, dst_ref=target, send_sem=send, recv_sem=recv, device_id=peer, device_id_type=MESH
        )

    def give(way, step, piece):
        return remote(
            give_s.at[way, lax.rem(step, 4), piece], take_s.at[way, step, piece],
            give_sem.at[way, step, piece], take_sem.at[way, step, piece], beside,
        )

    def ring_copy(way, step, piece):
        return remote(
            take_s.at[way, step, piece], ring_s.at[way, step, piece],
            ring_send.at[way, step, piece], ring_recv.at[way, step, piece], targets[way],
        )

    def region(way, spot, piece, on_core):
        rows = pl.ds(pl.multiple_of(spot * PIECE, PIECE), PIECE)
        return grads_out.at[6 * way + 3 * on_core + piece, rows]

    def round_copy(way, step, piece):
        target = region(way, late_block(way, step), piece, core)
        return remote(
            target, target, round_send.at[way, step, piece], round_recv.at[way, step, piece], targets[way]
        )

    def round_wait(way, step, piece):
        target = region(way, late_block(way, step + 1), piece, core)
        remote(
            target, target, round_send.at[way, step, piece], round_recv.at[way, step, piece], targets[way]
        ).wait_recv()

    def share_copy(way, step, piece):
        target = region(way, late_block(way, step), piece, core)
        return remote(
            target, target, share_send.at[way, step, piece], share_recv.at[way, step, piece], beside
        )

    def share_wait(way, step, piece):
        target = region(way, late_block(way, step), piece, 1 - core)
        remote(
            target, target, share_send.at[way, step, piece], share_recv.at[way, step, piece], beside
        ).wait_recv()

    tiny_swap = remote(tiny_s, tiny_take_s, tiny_sem.at[0], tiny_sem.at[1], beside)

    def tiny_ring(step):
        return remote(
            tiny_go_s.at[step], tiny_ring_s.at[step], tiny_ring_send.at[step], tiny_ring_recv.at[step], ahead
        )

    def tiny_round(step):
        spot = late_block(0, step)
        return remote(
            tiny_own_s.at[spot], tiny_own_s.at[spot], tiny_round_send.at[step], tiny_round_recv.at[step], ahead
        )

    def tiny_round_wait(step):
        spot = late_block(0, step + 1)
        remote(
            tiny_own_s.at[spot], tiny_own_s.at[spot], tiny_round_send.at[step], tiny_round_recv.at[step], ahead
        ).wait_recv()

    loads = []
    for piece in range(PIECES):
        for way in range(2):
            for half in range(2):
                first_row, number = PANELS[6 * way + 3 * half + piece]
                for kind, part in ((load_right, number), (load_left, first_row // D)):
                    if (kind, part) not in [entry[:2] for entry in loads]:
                        loads.append((kind, part, way, piece))
    order = [(way, piece) for piece in range(PIECES) for way in range(2)]
    groups = [[kind(part) for kind, part, *spot in loads if tuple(spot) == pair] for pair in order]
    for group in groups[:2]:
        for copy in group:
            copy.start()

    for part in range(RING):
        if part * 128 < D:
            tiny_s[part] = small_in[:, part * 128 : part * 128 + 128]
        else:
            tiny_s[part] = jnp.zeros((16, 128), F32)

    pl.semaphore_wait(barrier, 3)
    tiny_swap.start()

    def product(group, way, piece, pick):
        near, far = PANELS[6 * way + piece], PANELS[6 * way + 3 + piece]
        first_row = near[0] + pick * (far[0] - near[0])
        number = near[1] + pick * (far[1] - near[1])
        blocks = []
        for step in (2 * group, 2 * group + 1):
            start = pl.multiple_of(first_row + block(way, step) * PIECE, PIECE)
            blocks.append(left_s[pl.ds(start, PIECE), :])
        return dot(jnp.concatenate(blocks, axis=0), right_s[number])

    def keep_product(group, way, piece, both):
        total_s[lax.rem(2 * group, 3), way, piece] = both[:PIECE]
        total_s[lax.rem(2 * group + 1, 3), way, piece] = both[PIECE:]

    def give_product(group, way, piece, both):
        @pl.when(group >= 2)
        def _():
            give(way, 2 * group - 4, piece).wait_send()
            give(way, 2 * group - 3, piece).wait_send()

        give_s[way, lax.rem(2 * group, 4), piece] = both[:PIECE].astype(BF16)
        give_s[way, lax.rem(2 * group + 1, 4), piece] = both[PIECE:].astype(BF16)
        give(way, 2 * group, piece).start()
        give(way, 2 * group + 1, piece).start()

    def add_piece(step, way, piece, target):
        slot = lax.rem(step, 3)
        for r0 in range(0, PIECE, SUB):
            part = slice(r0, r0 + SUB)
            whole = total_s[slot, way, piece, part] + take_s[way, step, piece, part].astype(F32)
            target[part] = whole.astype(BF16)

    def reduce_step(step, carry):
        slot = lax.rem(step, 3)
        spot = block(0, step)

        @pl.when(step < RING - 1)
        def _():
            tiny_ring(step - 1).wait_recv()
            tiny_go_s[step] = tiny_sum_s[spot] + tiny_ring_s[step - 1]
            tiny_ring(step).start()

        @pl.when(step == RING - 1)
        def _():
            tiny_ring(step - 1).wait_recv()
            tiny_own_s[spot] = tiny_sum_s[spot] + tiny_ring_s[step - 1]
            tiny_round(0).start()

        for piece in range(PIECES):
            for way in range(2):
                give(way, step, piece).wait_recv()
                ring_copy(way, step - 1, piece).wait_recv()
                for r0 in range(0, PIECE, SUB):
                    part = slice(r0, r0 + SUB)
                    total_s[slot, way, piece, part] += ring_s[way, step - 1, piece, part].astype(F32)

                @pl.when(step < RING - 1)
                def _():
                    add_piece(step, way, piece, take_s.at[way, step, piece])
                    ring_copy(way, step, piece).start()

                @pl.when(step == RING - 1)
                def _():
                    add_piece(step, way, piece, region(way, late_block(way, 0), piece, core))
                    round_copy(way, 0, piece).start()
                    share_copy(way, 0, piece).start()

                @pl.when(step < RING - 2)
                def _():
                    odd = lax.rem(step, 2)
                    group = lax.div(step, 2) + 1
                    both = product(group, way, piece, odd * core + (1 - odd) * (1 - core))

                    @pl.when(odd == 1)
                    def _():
                        keep_product(group, way, piece, both)

                    @pl.when(odd == 0)
                    def _():
                        give_product(group, way, piece, both)

        return carry

    def first_piece(way, piece):
        give(way, 0, piece).wait_recv()
        add_piece(0, way, piece, take_s.at[way, 0, piece])
        ring_copy(way, 0, piece).start()

    for number, (way, piece) in enumerate(order):
        for copy in groups[number]:
            copy.wait()
        if number + 2 < len(groups):
            for copy in groups[number + 2]:
                copy.start()
        give_product(0, way, piece, product(0, way, piece, 1 - core))
        keep_product(0, way, piece, product(0, way, piece, core))
        if number > 0:
            first_piece(*order[number - 1])
    first_piece(*order[-1])
    for way, piece in order:
        give_product(1, way, piece, product(1, way, piece, 1 - core))
    tiny_swap.wait_recv()
    tiny_sum_s[...] = tiny_s[...] + tiny_take_s[...]
    tiny_go_s[0] = tiny_sum_s[block(0, 0)]
    tiny_ring(0).start()

    lax.fori_loop(1, RING, reduce_step, 0)

    def round_step(step, carry):
        tiny_round_wait(step - 1)

        @pl.when(step < RING - 1)
        def _():
            tiny_round(step).start()

        for piece in range(PIECES):
            for way in range(2):
                round_wait(way, step - 1, piece)

                @pl.when(step < RING - 1)
                def _():
                    round_copy(way, step, piece).start()

                share_copy(way, step, piece).start()
        return carry

    lax.fori_loop(1, RING, round_step, 0)

    for part in range(D // 128):
        small_out[:, part * 128 : part * 128 + 128] = tiny_own_s[part]
    tiny_swap.wait_send()

    def finish(step, carry):
        for way in range(2):
            for piece in range(PIECES):

                @pl.when(step >= RING // 2)
                def _():
                    give(way, step, piece).wait_send()

                share_wait(way, step, piece)
                share_copy(way, step, piece).wait_send()

                @pl.when(step < RING - 1)
                def _():
                    ring_copy(way, step, piece).wait_send()
                    round_copy(way, step, piece).wait_send()

        @pl.when(step < RING - 1)
        def _():
            tiny_ring(step).wait_send()
            tiny_round(step).wait_send()

        return carry

    lax.fori_loop(0, RING, finish, 0)


def run_sums(left, right, small):
    rows = right.shape[1]
    anywhere = pl.BlockSpec(memory_space=pl.ANY)
    vectors = pl.BlockSpec(memory_space=pltpu.VMEM)

    def pieces(*lead, dtype=BF16):
        return pltpu.VMEM((*lead, PIECE, D), dtype)

    dma = pltpu.SemaphoreType.DMA
    scratch = [
        pltpu.VMEM(left.shape, BF16), pltpu.VMEM(right.shape, BF16),
        pieces(3, 2, PIECES, dtype=F32), pieces(2, 4, PIECES), pieces(2, RING, PIECES),
        pieces(2, RING - 1, PIECES),
        pltpu.VMEM((RING, 16, 128), F32), pltpu.VMEM((RING, 16, 128), F32), pltpu.VMEM((RING, 16, 128), F32),
        pltpu.VMEM((RING - 1, 16, 128), F32), pltpu.VMEM((RING - 1, 16, 128), F32), pltpu.VMEM((RING, 16, 128), F32),
        dma((16,)), dma((2, RING, PIECES)), dma((2, RING, PIECES)),
        dma((2, RING - 1, PIECES)), dma((2, RING - 1, PIECES)),
        dma((2, RING - 1, PIECES)), dma((2, RING - 1, PIECES)), dma((2, RING, PIECES)), dma((2, RING, PIECES)),
        dma((2,)), dma((RING - 1,)), dma((RING - 1,)), dma((RING - 1,)), dma((RING - 1,)),
    ]
    return pl.pallas_call(
        sums_kernel,
        out_shape=(pltpu.VMEM((12, D, D), BF16), jax.ShapeDtypeStruct((16, D), F32)),
        in_specs=[anywhere, anywhere, vectors],
        out_specs=[vectors, vectors],
        scratch_shapes=scratch,
        compiler_params=pltpu.CompilerParams(
            collective_id=1, has_side_effects=True, vmem_limit_bytes=48 * 1024 * 1024
        ),
        cost_estimate=pl.CostEstimate(flops=rows * 2 * 7077888, bytes_accessed=70000000, transcendentals=0),
    )(left, right, small)


def plain_sums(left, right, small):
    panels = [dot(left[row : row + D], right[number]).astype(BF16) for row, number in PANELS]
    return lax.psum(jnp.stack(panels), "dp"), lax.psum(small, "dp")


SLOTS = 8
CUT = D // 2


def widen_kernel(
    act, dx, grads, small, act_out, dx_out, query_out, key_out, value_out, out_out, up_out, down_out,
    bias_out, up_bias_out, gain_out, shift_out, wide_s, act_s, dx_s, out_sem, move_sem,
):
    moves_in = [
        pltpu.make_async_copy(act, act_s, move_sem.at[0]), pltpu.make_async_copy(dx, dx_s, move_sem.at[1])
    ]
    moves_out = [
        pltpu.make_async_copy(act_s, act_out.at[0], move_sem.at[0]),
        pltpu.make_async_copy(dx_s, dx_out.at[0], move_sem.at[1]),
    ]
    jobs = []
    for panel in range(12):
        for half in range(2):
            rows = pl.ds(half * CUT, CUT)
            if panel < 4:
                target = (query_out, key_out, value_out, out_out)[panel].at[0, rows]
            elif panel < 8:
                target = up_out.at[0, rows, pl.ds((panel - 4) * D, D)]
            else:
                target = down_out.at[0, pl.ds((panel - 8) * D + half * CUT, CUT)]
            jobs.append((panel, half * CUT, target))

    def store(number):
        return pltpu.make_async_copy(wide_s.at[number % SLOTS], jobs[number][2], out_sem.at[number % SLOTS])

    for move in moves_in:
        move.start()
    bias_out[0] = small[0:4]
    for panel in range(FF // D):
        up_bias_out[:, panel * D : (panel + 1) * D] = small[4 + panel : 5 + panel]
    gain_out[0] = small[8:10]
    shift_out[0] = small[10:12]
    for number in range(len(jobs)):
        slot = number % SLOTS
        panel, start, _ = jobs[number]
        if number >= SLOTS:
            store(number - SLOTS).wait()

        def turn(step, carry):
            part = pl.ds(pl.multiple_of(step * SUB, SUB), SUB)
            here = pl.ds(pl.multiple_of(start + step * SUB, SUB), SUB)
            wide_s[slot, part, :] = grads[panel, here, :].astype(F32)
            return carry

        lax.fori_loop(0, CUT // SUB, turn, 0, unroll=4)
        store(number).start()
        if number == SLOTS:
            for move_in, move_out in zip(moves_in, moves_out):
                move_in.wait()
                move_out.start()
    for number in range(len(jobs) - SLOTS, len(jobs)):
        store(number).wait()
    for move in moves_out:
        move.wait()


def widen(act, dx, grads, small):
    anywhere = pl.BlockSpec(memory_space=pl.ANY)
    vectors = pl.BlockSpec(memory_space=pltpu.VMEM)
    square = jax.ShapeDtypeStruct((1, D, D), F32)
    return pl.pallas_call(
        widen_kernel,
        out_shape=(
            jax.ShapeDtypeStruct((1, *act.shape), BF16), jax.ShapeDtypeStruct((1, *dx.shape), F32),
            square, square, square, square,
            jax.ShapeDtypeStruct((1, D, FF), F32), jax.ShapeDtypeStruct((1, FF, D), F32),
            jax.ShapeDtypeStruct((1, 4, D), F32), jax.ShapeDtypeStruct((1, FF), F32),
            jax.ShapeDtypeStruct((1, 2, D), F32), jax.ShapeDtypeStruct((1, 2, D), F32),
        ),
        in_specs=[anywhere, anywhere, vectors, vectors],
        out_specs=[anywhere] * 8 + [vectors] * 4,
        scratch_shapes=[
            pltpu.VMEM((SLOTS, CUT, D), F32),
            pltpu.VMEM(act.shape, BF16), pltpu.VMEM(dx.shape, F32),
            pltpu.SemaphoreType.DMA((SLOTS,)), pltpu.SemaphoreType.DMA((2,)),
        ],
        compiler_params=pltpu.CompilerParams(vmem_limit_bytes=46 * 1024 * 1024),
        cost_estimate=pl.CostEstimate(flops=7077888, bytes_accessed=42467328, transcendentals=0),
    )(act, dx, grads, small)


def per_device(grid, tokens, cotangent, lengths, spans, *weights):
    act, dx, left, right, small = run_layers(tokens, cotangent, lengths, spans, *weights)
    grads, small = (run_sums if grid else plain_sums)(left, right, small)
    grads = pltpu.with_memory_space_constraint(grads, pltpu.VMEM)
    return widen(act, dx, grads, small)


def solution(mesh):
    in_specs = (
        P("dp", None), P("dp", None), P("dp"), P("dp", None),
        P("section", None, None), P("section", None, None), P("section", None, None),
        P("section", None, None), P("section", None, None), P("section", None, None),
        P("section", None, None), P("section", None), P("section", None, None), P("section", None, None),
    )
    out_specs = (
        P("section", "dp", None), P("section", "dp", None),
        P("section", None, None), P("section", None, None), P("section", None, None),
        P("section", None, None), P("section", None, None), P("section", None, None),
        P("section", None, None), P("section", None), P("section", None, None), P("section", None, None),
    )
    part = functools.partial(per_device, mesh.shape["dp"] == 2 * RING)
    return jax.shard_map(part, mesh=mesh, in_specs=in_specs, out_specs=out_specs, check_vma=False)
```

```python
import functools

import jax
import jax.numpy as jnp
from jax import lax
from jax.experimental import pallas as pl
from jax.experimental.pallas import tpu as pltpu
from jax.sharding import PartitionSpec as P

D = 768
HEADS = 12
HEAD_DIM = 64
QUADS = HEADS // 4
FF = 3072
LENGTH = 160
LEAST = 96
ROWS = LENGTH
SUB = 32
BAND = 80
WIDE = 1024
TURN = 256
PART = 256

F32 = jnp.float32
BF16 = jnp.bfloat16
MESH = pl.DeviceIdType.MESH


def dot(left, right):
    return jnp.dot(left, right, preferred_element_type=F32)


def dot_t(left, right):
    return lax.dot_general(left, right, (((1,), (1,)), ((), ())), preferred_element_type=F32)


def fold(block):
    return jnp.sum(block.reshape(-1, 8, block.shape[-1]), axis=0)


def gelu_parts(u):
    t = pl.reciprocal(1.0 + 0.23164189 * jnp.abs(u), approx=True)
    gauss = jnp.exp2(u * u * -0.7213475204444817)
    poly = t * (
        0.127414796 + t * (-0.142248368 + t * (0.7107068705 + t * (-0.7265760135 + t * 0.5307027145)))
    )
    tail = poly * gauss
    cdf = jnp.where(u >= 0, 1.0 - tail, tail)
    return u * cdf, cdf + (u * 0.3989422804014327) * gauss


def layers_kernel(
    micro_count,
    tokens, cotangent, lengths, spans,
    wq, wk, wv, wo, w1, w2, bias_in, up_bias_in, gains_in, shifts_in,
    act_out, dx_out, left_out, right_out, small_out,
    wq_s, wk_s, wv_s, wo_s, w1_s, w2_s,
    h_s, q_s, k_s, v_s, p_s, o_s, n_s, xa_s, xb_s, z_s, g_s, inva_s, invb_s,
    y_s, dy_s, df_s, da_s, dx_s, wide_s, turn_s, acc_s, accu_s,
    w_sem, in_sem, out_sem, turn_sem, fwd_send, fwd_recv, bwd_send, bwd_recv,
):
    section = lax.axis_index("section")
    other = 1 - section
    first = section == 0
    last = section == 1

    barrier = pltpu.get_barrier_semaphore()
    pl.semaphore_signal(barrier, inc=1, device_id={"section": other}, device_id_type=MESH)

    weight_pairs = ((wq, wq_s), (wk, wk_s), (wv, wv_s), (wo, wo_s), (w1, w1_s), (w2, w2_s))

    def weight_copy(index):
        source, target = weight_pairs[index]
        return pltpu.make_async_copy(source.at[0], target, w_sem.at[index])

    def rows_of(index):
        return pl.ds(pl.multiple_of(index * ROWS, ROWS), ROWS)

    def entry_copy(index):
        return pltpu.make_async_copy(tokens.at[rows_of(index)], h_s.at[rows_of(index)], in_sem.at[index])

    def cot_copy(index):
        return pltpu.make_async_copy(cotangent.at[rows_of(index)], dy_s.at[rows_of(index)], in_sem.at[index])

    def forward_send(index):
        return pltpu.make_async_remote_copy(
            src_ref=y_s.at[rows_of(index)],
            dst_ref=h_s.at[rows_of(index)],
            send_sem=fwd_send.at[index],
            recv_sem=fwd_recv.at[index],
            device_id={"section": other},
            device_id_type=MESH,
        )

    def backward_send(index):
        return pltpu.make_async_remote_copy(
            src_ref=y_s.at[rows_of(index)],
            dst_ref=dy_s.at[rows_of(index)],
            send_sem=bwd_send.at[index],
            recv_sem=bwd_recv.at[index],
            device_id={"section": other},
            device_id_type=MESH,
        )

    backward_outs = ((q_s, 0), (k_s, 1), (v_s, 2), (da_s, 3), (df_s, 8))

    def act_copy(index):
        return pltpu.make_async_copy(y_s.at[rows_of(index)], act_out.at[rows_of(index)], out_sem.at[0, index])

    def dx_copy(index):
        return pltpu.make_async_copy(dx_s.at[rows_of(index)], dx_out.at[rows_of(index)], out_sem.at[1, index])

    def right_copies(index):
        for slot, (source, place) in enumerate(backward_outs):
            yield pltpu.make_async_copy(
                source.at[rows_of(index)], right_out.at[place, rows_of(index)], out_sem.at[2 + slot, index]
            )
        for panel in range(FF // D):
            yield pltpu.make_async_copy(
                g_s.at[rows_of(index), pl.ds(panel * D, D)],
                right_out.at[4 + panel, rows_of(index)],
                out_sem.at[7 + panel, index],
            )

    def turn_copy(slot, row):
        return pltpu.make_async_copy(
            turn_s.at[slot], left_out.at[pl.ds(pl.multiple_of(row, TURN), TURN)], turn_sem.at[slot]
        )

    def transpose_all():
        done = 0
        for source, tiles in ((h_s, D // TURN), (o_s, D // TURN), (n_s, D // TURN), (z_s, FF // TURN)):

            def tile_step(tile, carry, source=source, done=done):
                number = tile + done
                slot = lax.rem(number, 2)

                @pl.when(number >= 2)
                def _():
                    turn_copy(slot, (number - 2) * TURN).wait()

                turn_s[slot] = source[:, pl.ds(pl.multiple_of(tile * TURN, TURN), TURN)].T
                turn_copy(slot, number * TURN).start()
                return carry

            lax.fori_loop(0, tiles, tile_step, 0)
            done += tiles
        for number in (done - 2, done - 1):
            turn_copy(number % 2, number * TURN).wait()

    @pl.when(first)
    def _():
        entry_copy(0).start()

    for index in range(4):
        weight_copy(index).start()

    acc_s[...] = jnp.zeros_like(acc_s)
    accu_s[...] = jnp.zeros_like(accu_s)

    bias = bias_in[0].astype(F32)
    gains = gains_in[0].astype(F32)
    shifts = shifts_in[0].astype(F32)
    low_half = lax.broadcasted_iota(jnp.int32, (1, 8, 128), 2) < HEAD_DIM
    lane = lax.broadcasted_iota(jnp.int32, (1, 16, PART), 2)
    keeps = [
        jnp.where((lane >= head * HEAD_DIM) & (lane < (head + 1) * HEAD_DIM), 1.0, 0.0).astype(BF16)
        for head in range(4)
    ]

    def stacked(quad_block):
        tiles = quad_block.reshape(-1, 16, PART)
        return jnp.concatenate([tiles * keep for keep in keeps], axis=0).reshape(4 * LENGTH, PART)

    def mixed_by(table, quad_block):
        tall = table.T
        parts = []
        for half in halves:
            start = 2 * LENGTH * (half.start // 128)
            tiles = dot(tall[start : start + 2 * LENGTH], quad_block[:, half]).reshape(2, LENGTH // 8, 8, 128)
            parts.append(jnp.where(low_half, tiles[0], tiles[1]).reshape(LENGTH, 128))
        return jnp.concatenate(parts, axis=1)

    pl.semaphore_wait(barrier, 1)

    blocks = [slice(r0, r0 + BAND) for r0 in range(0, ROWS, BAND)]
    columns = [slice(c0, c0 + PART) for c0 in range(0, D, PART)]
    panels = [slice(n0, n0 + WIDE) for n0 in range(0, FF, WIDE)]
    halves = [slice(0, 128), slice(128, 256)]
    count, chunks = len(columns), len(panels)

    def forward(index, carry):
        base = index * ROWS
        rows = rows_of(index)

        def at(block):
            return pl.ds(pl.multiple_of(base + block.start, BAND), BAND)

        @pl.when(index == 0)
        def _():
            for number in range(4):
                weight_copy(number).wait()
            for number in (4, 5):
                weight_copy(number).start()

            @pl.when(first)
            def _():
                for later in range(1, micro_count):
                    entry_copy(later).start()

            @pl.when(last)
            def _():
                for later in range(micro_count):
                    cot_copy(later).start()

        @pl.when(first)
        def _():
            entry_copy(index).wait()
            start, stop = spans[0, index], spans[1, index]
            spot = lax.broadcasted_iota(jnp.int32, (LENGTH, D), 0)
            keep = (spot < start) | (spot >= stop)
            h_s[rows, :] = jnp.where(keep, h_s[rows, :].astype(F32), 0.0).astype(BF16)

        @pl.when(last)
        def _():
            forward_send(index).wait_recv()

        hidden = h_s[rows, :]

        def project(column):
            query = ((dot(hidden, wq_s[:, column]) + bias[0:1, column]) * 0.125).astype(BF16)
            key_rows = dot(hidden, wk_s[:, column]).astype(BF16)
            value = (dot(hidden, wv_s[:, column]) + bias[1:2, column]).astype(BF16)
            q_s[rows, column] = query
            k_s[rows, column] = key_rows
            v_s[rows, column] = value
            return query, key_rows, value

        spot = lax.broadcasted_iota(jnp.int32, (LENGTH - LEAST, 4 * LENGTH), 0) + LEAST
        penalty = jnp.where(spot < lengths[index], 0.0, -1000000000.0)
        projected, attends = {}, {}
        attended = None
        for step in range(count + 2):
            if step < count:
                projected[step] = project(columns[step])
            spot = step - 1
            if 0 <= spot < count:
                query, key_rows, _ = projected[spot]
                scores = dot_t(key_rows, stacked(query))
                held = jnp.concatenate([scores[:LEAST], scores[LEAST:] + penalty], axis=0)
                raised = jnp.exp(held - jnp.max(held, axis=0, keepdims=True))
                attends[spot] = (raised * (1.0 / jnp.sum(raised, axis=0, keepdims=True))).astype(BF16)
                p_s[index, spot] = attends[spot]
            spot = step - 2
            if 0 <= spot:
                mixture = mixed_by(attends[spot], projected[spot][2]).astype(BF16)
                o_s[rows, columns[spot]] = mixture
                product = dot(mixture, wo_s[columns[spot], :])
                attended = product if attended is None else attended + product

        for block in blocks:
            r = h_s[at(block), :].astype(F32) + attended[block] + bias[2:3]
            centered = r - jnp.mean(r, axis=-1, keepdims=True)
            inv = lax.rsqrt(jnp.mean(centered * centered, axis=-1, keepdims=True) + 1e-05)
            hat = centered * inv
            normed = hat * gains[0:1] + shifts[0:1]
            xa_s[at(block), :] = hat.astype(BF16)
            inva_s[at(block), :] = jnp.broadcast_to(inv, (BAND, 128))
            n_s[at(block), :] = normed.astype(BF16)
            wide_s[block, :] = normed

        @pl.when(index == 0)
        def _():
            weight_copy(4).wait()
            weight_copy(5).wait()

        normed_low = n_s[rows, :]
        lifted = {}
        outer = None
        for step in range(chunks + 2):
            if step < chunks:
                lifted[step] = dot(normed_low, w1_s[:, panels[step]])
            spot = step - 1
            if 0 <= spot < chunks:
                up_bias = up_bias_in[0:1, panels[spot]].astype(F32)
                for block in blocks:
                    act, slope = gelu_parts(lifted[spot][block] + up_bias)
                    z_s[at(block), panels[spot]] = act.astype(BF16)
                    g_s[at(block), panels[spot]] = slope.astype(BF16)
            spot = step - 2
            if 0 <= spot:
                product = dot(z_s[rows, panels[spot]], w2_s[panels[spot], :])
                outer = product if outer is None else outer + product

        for block in blocks:
            r = wide_s[block, :] + outer[block] + bias[3:4]
            centered = r - jnp.mean(r, axis=-1, keepdims=True)
            inv = lax.rsqrt(jnp.mean(centered * centered, axis=-1, keepdims=True) + 1e-05)
            hat = centered * inv
            xb_s[at(block), :] = hat.astype(BF16)
            invb_s[at(block), :] = jnp.broadcast_to(inv, (BAND, 128))
            y_s[at(block), :] = (hat * gains[1:2] + shifts[1:2]).astype(BF16)

        @pl.when(first)
        def _():
            forward_send(index).start()

        act_copy(index).start()
        return carry

    lax.fori_loop(0, micro_count, forward, 0)

    def forward_done(index, carry):
        @pl.when(first)
        def _():
            forward_send(index).wait_send()

        act_copy(index).wait()
        return carry

    lax.fori_loop(0, micro_count, forward_done, 0)

    @pl.when(first)
    def _():
        transpose_all()

    def backward(index, carry):
        base = index * ROWS
        rows = rows_of(index)

        def at(block):
            return pl.ds(pl.multiple_of(base + block.start, BAND), BAND)

        @pl.when(first)
        def _():
            backward_send(index).wait_recv()

        @pl.when(last)
        def _():
            cot_copy(index).wait()

        for block in blocks:
            dy = dy_s[at(block), :].astype(F32)
            hat = xb_s[at(block), :].astype(F32)
            acc_s[9] += fold(dy * hat)
            acc_s[11] += fold(dy)
            scaled = dy * gains[1:2]
            mean_plain = jnp.mean(scaled, axis=-1, keepdims=True)
            mean_hat = jnp.mean(scaled * hat, axis=-1, keepdims=True)
            grad = (scaled - mean_plain - hat * mean_hat) * invb_s[at(block), 0:1]
            wide_s[block, :] = grad
            df_s[at(block), :] = grad.astype(BF16)
            acc_s[3] += fold(grad)

        outer_low = df_s[rows, :]
        dropped = {}
        total = None
        for step in range(chunks + 2):
            if step < chunks:
                dropped[step] = dot_t(outer_low, w2_s[panels[step], :])
            spot = step - 1
            if 0 <= spot < chunks:
                sums = jnp.zeros((8, WIDE), F32)
                for block in blocks:
                    part = dropped[spot][block] * g_s[at(block), panels[spot]].astype(F32)
                    g_s[at(block), panels[spot]] = part.astype(BF16)
                    sums = sums + fold(part)
                accu_s[:, panels[spot]] += sums
            spot = step - 2
            if 0 <= spot:
                product = dot_t(g_s[rows, panels[spot]], w1_s[:, panels[spot]])
                total = product if total is None else total + product

        for block in blocks:
            dn = wide_s[block, :] + total[block]
            hat = xa_s[at(block), :].astype(F32)
            acc_s[8] += fold(dn * hat)
            acc_s[10] += fold(dn)
            scaled = dn * gains[0:1]
            mean_plain = jnp.mean(scaled, axis=-1, keepdims=True)
            mean_hat = jnp.mean(scaled * hat, axis=-1, keepdims=True)
            grad = (scaled - mean_plain - hat * mean_hat) * inva_s[at(block), 0:1]
            wide_s[block, :] = grad
            da_s[at(block), :] = grad.astype(BF16)
            acc_s[2] += fold(grad)

        attended_low = da_s[rows, :]
        mixed, scored, values_back = {}, {}, {}
        total = None
        for step in range(count + 2):
            if step < count:
                mixed[step] = dot_t(attended_low, wo_s[columns[step], :]).astype(BF16)
            spot = step - 1
            if 0 <= spot < count:
                tall = stacked(mixed[spot])
                grad_attend = dot_t(v_s[rows, columns[spot]], tall)
                values_back[spot] = dot(p_s[index, spot], tall)
                attend = p_s[index, spot].astype(F32)
                weighted = attend * grad_attend
                delta = jnp.sum(weighted, axis=0, keepdims=True) / jnp.sum(attend, axis=0, keepdims=True)
                scored[spot] = (weighted - attend * delta).astype(BF16)
            spot = step - 2
            if 0 <= spot:
                column = columns[spot]
                dk = dot(scored[spot], stacked(q_s[rows, column]))
                dq = mixed_by(scored[spot], k_s[rows, column]) * 0.125
                dv = values_back[spot]
                acc_s[0, :, column] += fold(dq)
                acc_s[1, :, column] += fold(dv)
                dq, dk, dv = dq.astype(BF16), dk.astype(BF16), dv.astype(BF16)
                q_s[rows, column] = dq
                k_s[rows, column] = dk
                v_s[rows, column] = dv
                for grad, weight in ((dq, wq_s), (dk, wk_s), (dv, wv_s)):
                    product = dot_t(grad, weight[:, column])
                    total = product if total is None else total + product

        @pl.when(last)
        def _():
            low = (wide_s[...] + total).astype(BF16)
            y_s[rows, :] = low
            dx_s[rows, :] = low.astype(F32)
            backward_send(index).start()

        @pl.when(first)
        def _():
            start, stop = spans[0, index], spans[1, index]
            spot = lax.broadcasted_iota(jnp.int32, (LENGTH, D), 0)
            keep = (spot < start) | (spot >= stop)
            dx_s[rows, :] = jnp.where(keep, wide_s[...] + total, 0.0)

        dx_copy(index).start()
        for copy in right_copies(index):
            copy.start()
        return carry

    lax.fori_loop(0, micro_count, backward, 0)

    @pl.when(last)
    def _():
        transpose_all()

    for number in range(12):
        if 4 <= number < 8:
            panel = accu_s[:, (number - 4) * D : (number - 3) * D]
        else:
            panel = acc_s[number]
        small_out[number : number + 1, :] = jnp.sum(panel, axis=0, keepdims=True)
    small_out[12:16, :] = jnp.zeros((4, D), F32)

    def backward_done(index, carry):
        @pl.when(last)
        def _():
            backward_send(index).wait_send()

        dx_copy(index).wait()
        for copy in right_copies(index):
            copy.wait()
        return carry

    lax.fori_loop(0, micro_count, backward_done, 0)


def run_layers(tokens, cotangent, lengths, spans, *weights):
    rows = tokens.shape[0]
    micro_count = rows // ROWS
    anywhere = pl.BlockSpec(memory_space=pl.ANY)
    scalars = pl.BlockSpec(memory_space=pltpu.SMEM)
    vectors = pl.BlockSpec(memory_space=pltpu.VMEM)
    out_shape = (
        jax.ShapeDtypeStruct((rows, D), BF16),
        jax.ShapeDtypeStruct((rows, D), F32),
        jax.ShapeDtypeStruct((3 * D + FF, rows), BF16),
        jax.ShapeDtypeStruct((9, rows, D), BF16),
        jax.ShapeDtypeStruct((16, D), F32),
    )

    def vm(count, width=D, dtype=BF16):
        return pltpu.VMEM((count, width), dtype)

    scratch = [
        vm(D), vm(D), vm(D), vm(D), vm(D, FF), vm(FF),
        vm(rows), vm(rows), vm(rows), vm(rows),
        pltpu.VMEM((micro_count, QUADS, LENGTH, 4 * LENGTH), BF16),
        vm(rows), vm(rows), vm(rows), vm(rows), vm(rows, FF), vm(rows, FF),
        vm(rows, 128, F32), vm(rows, 128, F32),
        vm(rows), vm(rows), vm(rows), vm(rows), vm(rows, D, F32),
        vm(ROWS, D, F32), pltpu.VMEM((2, TURN, rows), BF16), pltpu.VMEM((12, 8, D), F32), vm(8, FF, F32),
        pltpu.SemaphoreType.DMA((6,)),
        pltpu.SemaphoreType.DMA((micro_count,)),
        pltpu.SemaphoreType.DMA((11, micro_count)),
        pltpu.SemaphoreType.DMA((2,)),
        pltpu.SemaphoreType.DMA((micro_count,)),
        pltpu.SemaphoreType.DMA((micro_count,)),
        pltpu.SemaphoreType.DMA((micro_count,)),
        pltpu.SemaphoreType.DMA((micro_count,)),
    ]
    return pl.pallas_call(
        functools.partial(layers_kernel, micro_count),
        out_shape=out_shape,
        in_specs=[anywhere, anywhere, scalars, scalars] + [anywhere] * 6 + [vectors] * 4,
        out_specs=[anywhere] * 4 + [vectors],
        scratch_shapes=scratch,
        compiler_params=pltpu.CompilerParams(
            collective_id=0, has_side_effects=True, vmem_limit_bytes=60 * 1024 * 1024
        ),
        cost_estimate=pl.CostEstimate(
            flops=rows * 2 * 2 * 2 * 7077888, bytes_accessed=60000000, transcendentals=rows * FF * 2
        ),
    )(tokens, cotangent, lengths, spans.T, *weights)


RING = 8
PIECES = 3
PIECE = D // RING
PANELS = (
    (0, 0), (0, 1), (0, 2), (D, 3), (2 * D, 4), (2 * D, 5),
    (2 * D, 6), (2 * D, 7), (3 * D, 8), (4 * D, 8), (5 * D, 8), (6 * D, 8),
)


def sums_kernel(
    left, right, small_in, grads_out, small_out,
    left_s, right_s, total_s, give_s, take_s, ring_s,
    tiny_s, tiny_take_s, tiny_sum_s, tiny_go_s, tiny_ring_s, tiny_own_s,
    load_sem, give_sem, take_sem, ring_send, ring_recv, round_send, round_recv, share_send, share_recv,
    tiny_sem, tiny_ring_send, tiny_ring_recv, tiny_round_send, tiny_round_recv,
):
    me = lax.axis_index("dp")
    core = lax.rem(me, 2)
    high = lax.rem(lax.div(me, 2), 2)
    depth = lax.div(me, 4)
    place = depth + high * (7 - 2 * depth)

    def device(spot, on_core):
        row = lax.div(spot, 4)
        return {"dp": 4 * (spot + row * (7 - 2 * spot)) + 2 * row + on_core}

    ahead = device(lax.rem(place + 1, RING), core)
    behind = device(lax.rem(place + RING - 1, RING), core)
    beside = device(place, 1 - core)
    targets = (ahead, behind)

    barrier = pltpu.get_barrier_semaphore()
    for peer in (ahead, behind, beside):
        pl.semaphore_signal(barrier, inc=1, device_id=peer, device_id_type=MESH)

    def block(way, step):
        return lax.rem(place - step + RING, RING) if way == 0 else lax.rem(place + step, RING)

    def late_block(way, step):
        return lax.rem(place + 1 - step + RING, RING) if way == 0 else lax.rem(place + RING - 1 + step, RING)

    def load_left(part):
        return pltpu.make_async_copy(left.at[pl.ds(part * D, D)], left_s.at[pl.ds(part * D, D)], load_sem.at[part])

    def load_right(part):
        return pltpu.make_async_copy(right.at[part], right_s.at[part], load_sem.at[7 + part])

    def remote(source, target, send, recv, peer):
        return pltpu.make_async_remote_copy(
            src_ref=source, dst_ref=target, send_sem=send, recv_sem=recv, device_id=peer, device_id_type=MESH
        )

    def give(way, step, piece):
        return remote(
            give_s.at[way, lax.rem(step, 4), piece], take_s.at[way, step, piece],
            give_sem.at[way, step, piece], take_sem.at[way, step, piece], beside,
        )

    def ring_copy(way, step, piece):
        return remote(
            take_s.at[way, step, piece], ring_s.at[way, step, piece],
            ring_send.at[way, step, piece], ring_recv.at[way, step, piece], targets[way],
        )

    def region(way, spot, piece, on_core):
        rows = pl.ds(pl.multiple_of(spot * PIECE, PIECE), PIECE)
        return grads_out.at[6 * way + 3 * on_core + piece, rows]

    def round_copy(way, step, piece):
        target = region(way, late_block(way, step), piece, core)
        return remote(
            target, target, round_send.at[way, step, piece], round_recv.at[way, step, piece], targets[way]
        )

    def round_wait(way, step, piece):
        target = region(way, late_block(way, step + 1), piece, core)
        remote(
            target, target, round_send.at[way, step, piece], round_recv.at[way, step, piece], targets[way]
        ).wait_recv()

    def share_copy(way, step, piece):
        target = region(way, late_block(way, step), piece, core)
        return remote(
            target, target, share_send.at[way, step, piece], share_recv.at[way, step, piece], beside
        )

    def share_wait(way, step, piece):
        target = region(way, late_block(way, step), piece, 1 - core)
        remote(
            target, target, share_send.at[way, step, piece], share_recv.at[way, step, piece], beside
        ).wait_recv()

    tiny_swap = remote(tiny_s, tiny_take_s, tiny_sem.at[0], tiny_sem.at[1], beside)

    def tiny_ring(step):
        return remote(
            tiny_go_s.at[step], tiny_ring_s.at[step], tiny_ring_send.at[step], tiny_ring_recv.at[step], ahead
        )

    def tiny_round(step):
        spot = late_block(0, step)
        return remote(
            tiny_own_s.at[spot], tiny_own_s.at[spot], tiny_round_send.at[step], tiny_round_recv.at[step], ahead
        )

    def tiny_round_wait(step):
        spot = late_block(0, step + 1)
        remote(
            tiny_own_s.at[spot], tiny_own_s.at[spot], tiny_round_send.at[step], tiny_round_recv.at[step], ahead
        ).wait_recv()

    loads = []
    for piece in range(PIECES):
        for way in range(2):
            for half in range(2):
                first_row, number = PANELS[6 * way + 3 * half + piece]
                for kind, part in ((load_right, number), (load_left, first_row // D)):
                    if (kind, part) not in [entry[:2] for entry in loads]:
                        loads.append((kind, part, way, piece))
    order = [(way, piece) for piece in range(PIECES) for way in range(2)]
    groups = [[kind(part) for kind, part, *spot in loads if tuple(spot) == pair] for pair in order]
    for group in groups[:2]:
        for copy in group:
            copy.start()

    for part in range(RING):
        if part * 128 < D:
            tiny_s[part] = small_in[:, part * 128 : part * 128 + 128]
        else:
            tiny_s[part] = jnp.zeros((16, 128), F32)

    pl.semaphore_wait(barrier, 3)
    tiny_swap.start()

    def product(group, way, piece, pick):
        near, far = PANELS[6 * way + piece], PANELS[6 * way + 3 + piece]
        first_row = near[0] + pick * (far[0] - near[0])
        number = near[1] + pick * (far[1] - near[1])
        blocks = []
        for step in (2 * group, 2 * group + 1):
            start = pl.multiple_of(first_row + block(way, step) * PIECE, PIECE)
            blocks.append(left_s[pl.ds(start, PIECE), :])
        return dot(jnp.concatenate(blocks, axis=0), right_s[number])

    def keep_product(group, way, piece, both):
        total_s[lax.rem(2 * group, 3), way, piece] = both[:PIECE]
        total_s[lax.rem(2 * group + 1, 3), way, piece] = both[PIECE:]

    def give_product(group, way, piece, both):
        @pl.when(group >= 2)
        def _():
            give(way, 2 * group - 4, piece).wait_send()
            give(way, 2 * group - 3, piece).wait_send()

        give_s[way, lax.rem(2 * group, 4), piece] = both[:PIECE].astype(BF16)
        give_s[way, lax.rem(2 * group + 1, 4), piece] = both[PIECE:].astype(BF16)
        give(way, 2 * group, piece).start()
        give(way, 2 * group + 1, piece).start()

    def add_piece(step, way, piece, target):
        slot = lax.rem(step, 3)
        for r0 in range(0, PIECE, SUB):
            part = slice(r0, r0 + SUB)
            whole = total_s[slot, way, piece, part] + take_s[way, step, piece, part].astype(F32)
            target[part] = whole.astype(BF16)

    def reduce_step(step, carry):
        slot = lax.rem(step, 3)
        spot = block(0, step)

        @pl.when(step < RING - 1)
        def _():
            tiny_ring(step - 1).wait_recv()
            tiny_go_s[step] = tiny_sum_s[spot] + tiny_ring_s[step - 1]
            tiny_ring(step).start()

        @pl.when(step == RING - 1)
        def _():
            tiny_ring(step - 1).wait_recv()
            tiny_own_s[spot] = tiny_sum_s[spot] + tiny_ring_s[step - 1]
            tiny_round(0).start()

        for piece in range(PIECES):
            for way in range(2):
                give(way, step, piece).wait_recv()
                ring_copy(way, step - 1, piece).wait_recv()
                for r0 in range(0, PIECE, SUB):
                    part = slice(r0, r0 + SUB)
                    total_s[slot, way, piece, part] += ring_s[way, step - 1, piece, part].astype(F32)

                @pl.when(step < RING - 1)
                def _():
                    add_piece(step, way, piece, take_s.at[way, step, piece])
                    ring_copy(way, step, piece).start()

                @pl.when(step == RING - 1)
                def _():
                    add_piece(step, way, piece, region(way, late_block(way, 0), piece, core))
                    round_copy(way, 0, piece).start()
                    share_copy(way, 0, piece).start()

                @pl.when(step < RING - 2)
                def _():
                    odd = lax.rem(step, 2)
                    group = lax.div(step, 2) + 1
                    both = product(group, way, piece, odd * core + (1 - odd) * (1 - core))

                    @pl.when(odd == 1)
                    def _():
                        keep_product(group, way, piece, both)

                    @pl.when(odd == 0)
                    def _():
                        give_product(group, way, piece, both)

        return carry

    def first_piece(way, piece):
        give(way, 0, piece).wait_recv()
        add_piece(0, way, piece, take_s.at[way, 0, piece])
        ring_copy(way, 0, piece).start()

    for number, (way, piece) in enumerate(order):
        for copy in groups[number]:
            copy.wait()
        if number + 2 < len(groups):
            for copy in groups[number + 2]:
                copy.start()
        give_product(0, way, piece, product(0, way, piece, 1 - core))
        keep_product(0, way, piece, product(0, way, piece, core))
        if number > 0:
            first_piece(*order[number - 1])
    first_piece(*order[-1])
    for way, piece in order:
        give_product(1, way, piece, product(1, way, piece, 1 - core))
    tiny_swap.wait_recv()
    tiny_sum_s[...] = tiny_s[...] + tiny_take_s[...]
    tiny_go_s[0] = tiny_sum_s[block(0, 0)]
    tiny_ring(0).start()

    lax.fori_loop(1, RING, reduce_step, 0)

    def round_step(step, carry):
        tiny_round_wait(step - 1)

        @pl.when(step < RING - 1)
        def _():
            tiny_round(step).start()

        for piece in range(PIECES):
            for way in range(2):
                round_wait(way, step - 1, piece)

                @pl.when(step < RING - 1)
                def _():
                    round_copy(way, step, piece).start()

                share_copy(way, step, piece).start()
        return carry

    lax.fori_loop(1, RING, round_step, 0)

    for part in range(D // 128):
        small_out[:, part * 128 : part * 128 + 128] = tiny_own_s[part]
    tiny_swap.wait_send()

    def finish(step, carry):
        for way in range(2):
            for piece in range(PIECES):

                @pl.when(step >= RING // 2)
                def _():
                    give(way, step, piece).wait_send()

                share_wait(way, step, piece)
                share_copy(way, step, piece).wait_send()

                @pl.when(step < RING - 1)
                def _():
                    ring_copy(way, step, piece).wait_send()
                    round_copy(way, step, piece).wait_send()

        @pl.when(step < RING - 1)
        def _():
            tiny_ring(step).wait_send()
            tiny_round(step).wait_send()

        return carry

    lax.fori_loop(0, RING, finish, 0)


def run_sums(left, right, small):
    rows = right.shape[1]
    anywhere = pl.BlockSpec(memory_space=pl.ANY)
    vectors = pl.BlockSpec(memory_space=pltpu.VMEM)

    def pieces(*lead, dtype=BF16):
        return pltpu.VMEM((*lead, PIECE, D), dtype)

    dma = pltpu.SemaphoreType.DMA
    scratch = [
        pltpu.VMEM(left.shape, BF16), pltpu.VMEM(right.shape, BF16),
        pieces(3, 2, PIECES, dtype=F32), pieces(2, 4, PIECES), pieces(2, RING, PIECES),
        pieces(2, RING - 1, PIECES),
        pltpu.VMEM((RING, 16, 128), F32), pltpu.VMEM((RING, 16, 128), F32), pltpu.VMEM((RING, 16, 128), F32),
        pltpu.VMEM((RING - 1, 16, 128), F32), pltpu.VMEM((RING - 1, 16, 128), F32), pltpu.VMEM((RING, 16, 128), F32),
        dma((16,)), dma((2, RING, PIECES)), dma((2, RING, PIECES)),
        dma((2, RING - 1, PIECES)), dma((2, RING - 1, PIECES)),
        dma((2, RING - 1, PIECES)), dma((2, RING - 1, PIECES)), dma((2, RING, PIECES)), dma((2, RING, PIECES)),
        dma((2,)), dma((RING - 1,)), dma((RING - 1,)), dma((RING - 1,)), dma((RING - 1,)),
    ]
    return pl.pallas_call(
        sums_kernel,
        out_shape=(pltpu.VMEM((12, D, D), BF16), jax.ShapeDtypeStruct((16, D), F32)),
        in_specs=[anywhere, anywhere, vectors],
        out_specs=[vectors, vectors],
        scratch_shapes=scratch,
        compiler_params=pltpu.CompilerParams(
            collective_id=1, has_side_effects=True, vmem_limit_bytes=48 * 1024 * 1024
        ),
        cost_estimate=pl.CostEstimate(flops=rows * 2 * 7077888, bytes_accessed=70000000, transcendentals=0),
    )(left, right, small)


def plain_sums(left, right, small):
    panels = [dot(left[row : row + D], right[number]).astype(BF16) for row, number in PANELS]
    return lax.psum(jnp.stack(panels), "dp"), lax.psum(small, "dp")


SLOTS = 8
CUT = D // 2


def widen_kernel(
    act, dx, grads, small, act_out, dx_out, query_out, key_out, value_out, out_out, up_out, down_out,
    bias_out, up_bias_out, gain_out, shift_out, wide_s, act_s, dx_s, out_sem, move_sem,
):
    moves_in = [
        pltpu.make_async_copy(act, act_s, move_sem.at[0]), pltpu.make_async_copy(dx, dx_s, move_sem.at[1])
    ]
    moves_out = [
        pltpu.make_async_copy(act_s, act_out.at[0], move_sem.at[0]),
        pltpu.make_async_copy(dx_s, dx_out.at[0], move_sem.at[1]),
    ]
    jobs = []
    for panel in range(12):
        for half in range(2):
            rows = pl.ds(half * CUT, CUT)
            if panel < 4:
                target = (query_out, key_out, value_out, out_out)[panel].at[0, rows]
            elif panel < 8:
                target = up_out.at[0, rows, pl.ds((panel - 4) * D, D)]
            else:
                target = down_out.at[0, pl.ds((panel - 8) * D + half * CUT, CUT)]
            jobs.append((panel, half * CUT, target))

    def store(number):
        return pltpu.make_async_copy(wide_s.at[number % SLOTS], jobs[number][2], out_sem.at[number % SLOTS])

    for move in moves_in:
        move.start()
    bias_out[0] = small[0:4]
    for panel in range(FF // D):
        up_bias_out[:, panel * D : (panel + 1) * D] = small[4 + panel : 5 + panel]
    gain_out[0] = small[8:10]
    shift_out[0] = small[10:12]
    for number in range(len(jobs)):
        slot = number % SLOTS
        panel, start, _ = jobs[number]
        if number >= SLOTS:
            store(number - SLOTS).wait()

        def turn(step, carry):
            part = pl.ds(pl.multiple_of(step * SUB, SUB), SUB)
            here = pl.ds(pl.multiple_of(start + step * SUB, SUB), SUB)
            wide_s[slot, part, :] = grads[panel, here, :].astype(F32)
            return carry

        lax.fori_loop(0, CUT // SUB, turn, 0, unroll=4)
        store(number).start()
        if number == SLOTS:
            for move_in, move_out in zip(moves_in, moves_out):
                move_in.wait()
                move_out.start()
    for number in range(len(jobs) - SLOTS, len(jobs)):
        store(number).wait()
    for move in moves_out:
        move.wait()


def widen(act, dx, grads, small):
    anywhere = pl.BlockSpec(memory_space=pl.ANY)
    vectors = pl.BlockSpec(memory_space=pltpu.VMEM)
    square = jax.ShapeDtypeStruct((1, D, D), F32)
    return pl.pallas_call(
        widen_kernel,
        out_shape=(
            jax.ShapeDtypeStruct((1, *act.shape), BF16), jax.ShapeDtypeStruct((1, *dx.shape), F32),
            square, square, square, square,
            jax.ShapeDtypeStruct((1, D, FF), F32), jax.ShapeDtypeStruct((1, FF, D), F32),
            jax.ShapeDtypeStruct((1, 4, D), F32), jax.ShapeDtypeStruct((1, FF), F32),
            jax.ShapeDtypeStruct((1, 2, D), F32), jax.ShapeDtypeStruct((1, 2, D), F32),
        ),
        in_specs=[anywhere, anywhere, vectors, vectors],
        out_specs=[anywhere] * 8 + [vectors] * 4,
        scratch_shapes=[
            pltpu.VMEM((SLOTS, CUT, D), F32),
            pltpu.VMEM(act.shape, BF16), pltpu.VMEM(dx.shape, F32),
            pltpu.SemaphoreType.DMA((SLOTS,)), pltpu.SemaphoreType.DMA((2,)),
        ],
        compiler_params=pltpu.CompilerParams(vmem_limit_bytes=46 * 1024 * 1024),
        cost_estimate=pl.CostEstimate(flops=7077888, bytes_accessed=42467328, transcendentals=0),
    )(act, dx, grads, small)


def per_device(grid, tokens, cotangent, lengths, spans, *weights):
    act, dx, left, right, small = run_layers(tokens, cotangent, lengths, spans, *weights)
    grads, small = (run_sums if grid else plain_sums)(left, right, small)
    grads = pltpu.with_memory_space_constraint(grads, pltpu.VMEM)
    return widen(act, dx, grads, small)


def solution(mesh):
    in_specs = (
        P("dp", None), P("dp", None), P("dp"), P("dp", None),
        P("section", None, None), P("section", None, None), P("section", None, None),
        P("section", None, None), P("section", None, None), P("section", None, None),
        P("section", None, None), P("section", None), P("section", None, None), P("section", None, None),
    )
    out_specs = (
        P("section", "dp", None), P("section", "dp", None),
        P("section", None, None), P("section", None, None), P("section", None, None),
        P("section", None, None), P("section", None, None), P("section", None, None),
        P("section", None, None), P("section", None), P("section", None, None), P("section", None, None),
    )
    part = functools.partial(per_device, mesh.shape["dp"] == 2 * RING)
    return jax.shard_map(part, mesh=mesh, in_specs=in_specs, out_specs=out_specs, check_vma=False)
```

```python
import functools

import jax
import jax.numpy as jnp
from jax import lax
from jax.experimental import pallas as pl
from jax.experimental.pallas import tpu as pltpu
from jax.sharding import PartitionSpec as P

D = 768
HEADS = 12
HEAD_DIM = 64
QUADS = HEADS // 4
FF = 3072
LENGTH = 160
LEAST = 96
ROWS = LENGTH
SUB = 32
BAND = 80
WIDE = 256
TURN = 256
PART = 256

F32 = jnp.float32
BF16 = jnp.bfloat16
MESH = pl.DeviceIdType.MESH


def dot(left, right):
    return jnp.dot(left, right, preferred_element_type=F32)


def dot_t(left, right):
    return lax.dot_general(left, right, (((1,), (1,)), ((), ())), preferred_element_type=F32)


def fold(block):
    return jnp.sum(block.reshape(-1, 8, block.shape[-1]), axis=0)


def gelu_parts(u):
    t = pl.reciprocal(1.0 + 0.23164189 * jnp.abs(u), approx=True)
    gauss = jnp.exp2(u * u * -0.7213475204444817)
    poly = t * (
        0.127414796 + t * (-0.142248368 + t * (0.7107068705 + t * (-0.7265760135 + t * 0.5307027145)))
    )
    tail = poly * gauss
    cdf = jnp.where(u >= 0, 1.0 - tail, tail)
    return u * cdf, cdf + (u * 0.3989422804014327) * gauss


def layers_kernel(
    micro_count,
    tokens, cotangent, lengths, spans,
    wq, wk, wv, wo, w1, w2, bias_in, up_bias_in, gains_in, shifts_in,
    act_out, dx_out, left_out, right_out, small_out,
    wq_s, wk_s, wv_s, wo_s, w1_s, w2_s,
    h_s, q_s, k_s, v_s, p_s, o_s, n_s, xa_s, xb_s, z_s, g_s, inva_s, invb_s,
    y_s, dy_s, df_s, da_s, dx_s, wide_s, turn_s, acc_s, accu_s,
    w_sem, in_sem, out_sem, turn_sem, fwd_send, fwd_recv, bwd_send, bwd_recv,
):
    section = lax.axis_index("section")
    other = 1 - section
    first = section == 0
    last = section == 1

    barrier = pltpu.get_barrier_semaphore()
    pl.semaphore_signal(barrier, inc=1, device_id={"section": other}, device_id_type=MESH)

    weight_pairs = ((wq, wq_s), (wk, wk_s), (wv, wv_s), (wo, wo_s), (w1, w1_s), (w2, w2_s))

    def weight_copy(index):
        source, target = weight_pairs[index]
        return pltpu.make_async_copy(source.at[0], target, w_sem.at[index])

    def rows_of(index):
        return pl.ds(pl.multiple_of(index * ROWS, ROWS), ROWS)

    def entry_copy(index):
        return pltpu.make_async_copy(tokens.at[rows_of(index)], h_s.at[rows_of(index)], in_sem.at[index])

    def cot_copy(index):
        return pltpu.make_async_copy(cotangent.at[rows_of(index)], dy_s.at[rows_of(index)], in_sem.at[index])

    def forward_send(index):
        return pltpu.make_async_remote_copy(
            src_ref=y_s.at[rows_of(index)],
            dst_ref=h_s.at[rows_of(index)],
            send_sem=fwd_send.at[index],
            recv_sem=fwd_recv.at[index],
            device_id={"section": other},
            device_id_type=MESH,
        )

    def backward_send(index):
        return pltpu.make_async_remote_copy(
            src_ref=y_s.at[rows_of(index)],
            dst_ref=dy_s.at[rows_of(index)],
            send_sem=bwd_send.at[index],
            recv_sem=bwd_recv.at[index],
            device_id={"section": other},
            device_id_type=MESH,
        )

    backward_outs = ((q_s, 0), (k_s, 1), (v_s, 2), (da_s, 3), (df_s, 8))

    def act_copy(index):
        return pltpu.make_async_copy(y_s.at[rows_of(index)], act_out.at[rows_of(index)], out_sem.at[0, index])

    def dx_copy(index):
        return pltpu.make_async_copy(dx_s.at[rows_of(index)], dx_out.at[rows_of(index)], out_sem.at[1, index])

    def right_copies(index):
        for slot, (source, place) in enumerate(backward_outs):
            yield pltpu.make_async_copy(
                source.at[rows_of(index)], right_out.at[place, rows_of(index)], out_sem.at[2 + slot, index]
            )
        for panel in range(FF // D):
            yield pltpu.make_async_copy(
                g_s.at[rows_of(index), pl.ds(panel * D, D)],
                right_out.at[4 + panel, rows_of(index)],
                out_sem.at[7 + panel, index],
            )

    def turn_copy(slot, row):
        return pltpu.make_async_copy(
            turn_s.at[slot], left_out.at[pl.ds(pl.multiple_of(row, TURN), TURN)], turn_sem.at[slot]
        )

    def transpose_all():
        done = 0
        for source, tiles in ((h_s, D // TURN), (o_s, D // TURN), (n_s, D // TURN), (z_s, FF // TURN)):

            def tile_step(tile, carry, source=source, done=done):
                number = tile + done
                slot = lax.rem(number, 2)

                @pl.when(number >= 2)
                def _():
                    turn_copy(slot, (number - 2) * TURN).wait()

                turn_s[slot] = source[:, pl.ds(pl.multiple_of(tile * TURN, TURN), TURN)].T
                turn_copy(slot, number * TURN).start()
                return carry

            lax.fori_loop(0, tiles, tile_step, 0)
            done += tiles
        for number in (done - 2, done - 1):
            turn_copy(number % 2, number * TURN).wait()

    @pl.when(first)
    def _():
        entry_copy(0).start()

    for index in range(4):
        weight_copy(index).start()

    acc_s[...] = jnp.zeros_like(acc_s)
    accu_s[...] = jnp.zeros_like(accu_s)

    bias = bias_in[0].astype(F32)
    gains = gains_in[0].astype(F32)
    shifts = shifts_in[0].astype(F32)
    low_half = lax.broadcasted_iota(jnp.int32, (1, 8, 128), 2) < HEAD_DIM
    lane = lax.broadcasted_iota(jnp.int32, (1, 16, PART), 2)
    keeps = [
        jnp.where((lane >= head * HEAD_DIM) & (lane < (head + 1) * HEAD_DIM), 1.0, 0.0).astype(BF16)
        for head in range(4)
    ]

    def stacked(quad_block):
        tiles = quad_block.reshape(-1, 16, PART)
        return jnp.concatenate([tiles * keep for keep in keeps], axis=0).reshape(4 * LENGTH, PART)

    def mixed_by(table, quad_block):
        tall = table.T
        parts = []
        for half in halves:
            start = 2 * LENGTH * (half.start // 128)
            tiles = dot(tall[start : start + 2 * LENGTH], quad_block[:, half]).reshape(2, LENGTH // 8, 8, 128)
            parts.append(jnp.where(low_half, tiles[0], tiles[1]).reshape(LENGTH, 128))
        return jnp.concatenate(parts, axis=1)

    pl.semaphore_wait(barrier, 1)

    blocks = [slice(r0, r0 + BAND) for r0 in range(0, ROWS, BAND)]
    columns = [slice(c0, c0 + PART) for c0 in range(0, D, PART)]
    panels = [slice(n0, n0 + WIDE) for n0 in range(0, FF, WIDE)]
    halves = [slice(0, 128), slice(128, 256)]
    count, chunks = len(columns), len(panels)

    def forward(index, carry):
        base = index * ROWS
        rows = rows_of(index)

        def at(block):
            return pl.ds(pl.multiple_of(base + block.start, BAND), BAND)

        @pl.when(index == 0)
        def _():
            for number in range(4):
                weight_copy(number).wait()
            for number in (4, 5):
                weight_copy(number).start()

            @pl.when(first)
            def _():
                for later in range(1, micro_count):
                    entry_copy(later).start()

            @pl.when(last)
            def _():
                for later in range(micro_count):
                    cot_copy(later).start()

        @pl.when(first)
        def _():
            entry_copy(index).wait()
            start, stop = spans[0, index], spans[1, index]
            spot = lax.broadcasted_iota(jnp.int32, (LENGTH, D), 0)
            keep = (spot < start) | (spot >= stop)
            h_s[rows, :] = jnp.where(keep, h_s[rows, :].astype(F32), 0.0).astype(BF16)

        @pl.when(last)
        def _():
            forward_send(index).wait_recv()

        hidden = h_s[rows, :]

        def project(column):
            query = ((dot(hidden, wq_s[:, column]) + bias[0:1, column]) * 0.125).astype(BF16)
            key_rows = dot(hidden, wk_s[:, column]).astype(BF16)
            value = (dot(hidden, wv_s[:, column]) + bias[1:2, column]).astype(BF16)
            q_s[rows, column] = query
            k_s[rows, column] = key_rows
            v_s[rows, column] = value
            return query, key_rows, value

        spot = lax.broadcasted_iota(jnp.int32, (LENGTH - LEAST, 4 * LENGTH), 0) + LEAST
        penalty = jnp.where(spot < lengths[index], 0.0, -1000000000.0)
        projected, attends = {}, {}
        attended = None
        for step in range(count + 2):
            if step < count:
                projected[step] = project(columns[step])
            spot = step - 1
            if 0 <= spot < count:
                query, key_rows, _ = projected[spot]
                scores = dot_t(key_rows, stacked(query))
                held = jnp.concatenate([scores[:LEAST], scores[LEAST:] + penalty], axis=0)
                raised = jnp.exp(held - jnp.max(held, axis=0, keepdims=True))
                attends[spot] = (raised * (1.0 / jnp.sum(raised, axis=0, keepdims=True))).astype(BF16)
                p_s[index, spot] = attends[spot]
            spot = step - 2
            if 0 <= spot:
                mixture = mixed_by(attends[spot], projected[spot][2]).astype(BF16)
                o_s[rows, columns[spot]] = mixture
                product = dot(mixture, wo_s[columns[spot], :])
                attended = product if attended is None else attended + product

        for block in blocks:
            r = h_s[at(block), :].astype(F32) + attended[block] + bias[2:3]
            centered = r - jnp.mean(r, axis=-1, keepdims=True)
            inv = lax.rsqrt(jnp.mean(centered * centered, axis=-1, keepdims=True) + 1e-05)
            hat = centered * inv
            normed = hat * gains[0:1] + shifts[0:1]
            xa_s[at(block), :] = hat.astype(BF16)
            inva_s[at(block), :] = jnp.broadcast_to(inv, (BAND, 128))
            n_s[at(block), :] = normed.astype(BF16)
            wide_s[block, :] = normed

        @pl.when(index == 0)
        def _():
            weight_copy(4).wait()
            weight_copy(5).wait()

        normed_low = n_s[rows, :]
        lifted = {}
        outer = None
        for step in range(chunks + 2):
            if step < chunks:
                lifted[step] = dot(normed_low, w1_s[:, panels[step]])
            spot = step - 1
            if 0 <= spot < chunks:
                up_bias = up_bias_in[0:1, panels[spot]].astype(F32)
                for block in blocks:
                    act, slope = gelu_parts(lifted[spot][block] + up_bias)
                    z_s[at(block), panels[spot]] = act.astype(BF16)
                    g_s[at(block), panels[spot]] = slope.astype(BF16)
            spot = step - 2
            if 0 <= spot:
                product = dot(z_s[rows, panels[spot]], w2_s[panels[spot], :])
                outer = product if outer is None else outer + product

        for block in blocks:
            r = wide_s[block, :] + outer[block] + bias[3:4]
            centered = r - jnp.mean(r, axis=-1, keepdims=True)
            inv = lax.rsqrt(jnp.mean(centered * centered, axis=-1, keepdims=True) + 1e-05)
            hat = centered * inv
            xb_s[at(block), :] = hat.astype(BF16)
            invb_s[at(block), :] = jnp.broadcast_to(inv, (BAND, 128))
            y_s[at(block), :] = (hat * gains[1:2] + shifts[1:2]).astype(BF16)

        @pl.when(first)
        def _():
            forward_send(index).start()

        act_copy(index).start()
        return carry

    lax.fori_loop(0, micro_count, forward, 0)

    def forward_done(index, carry):
        @pl.when(first)
        def _():
            forward_send(index).wait_send()

        act_copy(index).wait()
        return carry

    lax.fori_loop(0, micro_count, forward_done, 0)

    @pl.when(first)
    def _():
        transpose_all()

    def backward(index, carry):
        base = index * ROWS
        rows = rows_of(index)

        def at(block):
            return pl.ds(pl.multiple_of(base + block.start, BAND), BAND)

        @pl.when(first)
        def _():
            backward_send(index).wait_recv()

        @pl.when(last)
        def _():
            cot_copy(index).wait()

        for block in blocks:
            dy = dy_s[at(block), :].astype(F32)
            hat = xb_s[at(block), :].astype(F32)
            acc_s[9] += fold(dy * hat)
            acc_s[11] += fold(dy)
            scaled = dy * gains[1:2]
            mean_plain = jnp.mean(scaled, axis=-1, keepdims=True)
            mean_hat = jnp.mean(scaled * hat, axis=-1, keepdims=True)
            grad = (scaled - mean_plain - hat * mean_hat) * invb_s[at(block), 0:1]
            wide_s[block, :] = grad
            df_s[at(block), :] = grad.astype(BF16)
            acc_s[3] += fold(grad)

        outer_low = df_s[rows, :]
        dropped = {}
        total = None
        for step in range(chunks + 2):
            if step < chunks:
                dropped[step] = dot_t(outer_low, w2_s[panels[step], :])
            spot = step - 1
            if 0 <= spot < chunks:
                sums = jnp.zeros((8, WIDE), F32)
                for block in blocks:
                    part = dropped[spot][block] * g_s[at(block), panels[spot]].astype(F32)
                    g_s[at(block), panels[spot]] = part.astype(BF16)
                    sums = sums + fold(part)
                accu_s[:, panels[spot]] += sums
            spot = step - 2
            if 0 <= spot:
                product = dot_t(g_s[rows, panels[spot]], w1_s[:, panels[spot]])
                total = product if total is None else total + product

        for block in blocks:
            dn = wide_s[block, :] + total[block]
            hat = xa_s[at(block), :].astype(F32)
            acc_s[8] += fold(dn * hat)
            acc_s[10] += fold(dn)
            scaled = dn * gains[0:1]
            mean_plain = jnp.mean(scaled, axis=-1, keepdims=True)
            mean_hat = jnp.mean(scaled * hat, axis=-1, keepdims=True)
            grad = (scaled - mean_plain - hat * mean_hat) * inva_s[at(block), 0:1]
            wide_s[block, :] = grad
            da_s[at(block), :] = grad.astype(BF16)
            acc_s[2] += fold(grad)

        attended_low = da_s[rows, :]
        mixed, scored, values_back = {}, {}, {}
        total = None
        for step in range(count + 2):
            if step < count:
                mixed[step] = dot_t(attended_low, wo_s[columns[step], :]).astype(BF16)
            spot = step - 1
            if 0 <= spot < count:
                tall = stacked(mixed[spot])
                grad_attend = dot_t(v_s[rows, columns[spot]], tall)
                values_back[spot] = dot(p_s[index, spot], tall)
                attend = p_s[index, spot].astype(F32)
                weighted = attend * grad_attend
                delta = jnp.sum(weighted, axis=0, keepdims=True) / jnp.sum(attend, axis=0, keepdims=True)
                scored[spot] = (weighted - attend * delta).astype(BF16)
            spot = step - 2
            if 0 <= spot:
                column = columns[spot]
                dk = dot(scored[spot], stacked(q_s[rows, column]))
                dq = mixed_by(scored[spot], k_s[rows, column]) * 0.125
                dv = values_back[spot]
                acc_s[0, :, column] += fold(dq)
                acc_s[1, :, column] += fold(dv)
                dq, dk, dv = dq.astype(BF16), dk.astype(BF16), dv.astype(BF16)
                q_s[rows, column] = dq
                k_s[rows, column] = dk
                v_s[rows, column] = dv
                for grad, weight in ((dq, wq_s), (dk, wk_s), (dv, wv_s)):
                    product = dot_t(grad, weight[:, column])
                    total = product if total is None else total + product

        @pl.when(last)
        def _():
            low = (wide_s[...] + total).astype(BF16)
            y_s[rows, :] = low
            dx_s[rows, :] = low.astype(F32)
            backward_send(index).start()

        @pl.when(first)
        def _():
            start, stop = spans[0, index], spans[1, index]
            spot = lax.broadcasted_iota(jnp.int32, (LENGTH, D), 0)
            keep = (spot < start) | (spot >= stop)
            dx_s[rows, :] = jnp.where(keep, wide_s[...] + total, 0.0)

        dx_copy(index).start()
        for copy in right_copies(index):
            copy.start()
        return carry

    lax.fori_loop(0, micro_count, backward, 0)

    @pl.when(last)
    def _():
        transpose_all()

    for number in range(12):
        if 4 <= number < 8:
            panel = accu_s[:, (number - 4) * D : (number - 3) * D]
        else:
            panel = acc_s[number]
        small_out[number : number + 1, :] = jnp.sum(panel, axis=0, keepdims=True)
    small_out[12:16, :] = jnp.zeros((4, D), F32)

    def backward_done(index, carry):
        @pl.when(last)
        def _():
            backward_send(index).wait_send()

        dx_copy(index).wait()
        for copy in right_copies(index):
            copy.wait()
        return carry

    lax.fori_loop(0, micro_count, backward_done, 0)


def run_layers(tokens, cotangent, lengths, spans, *weights):
    rows = tokens.shape[0]
    micro_count = rows // ROWS
    anywhere = pl.BlockSpec(memory_space=pl.ANY)
    scalars = pl.BlockSpec(memory_space=pltpu.SMEM)
    vectors = pl.BlockSpec(memory_space=pltpu.VMEM)
    out_shape = (
        jax.ShapeDtypeStruct((rows, D), BF16),
        jax.ShapeDtypeStruct((rows, D), F32),
        jax.ShapeDtypeStruct((3 * D + FF, rows), BF16),
        jax.ShapeDtypeStruct((9, rows, D), BF16),
        jax.ShapeDtypeStruct((16, D), F32),
    )

    def vm(count, width=D, dtype=BF16):
        return pltpu.VMEM((count, width), dtype)

    scratch = [
        vm(D), vm(D), vm(D), vm(D), vm(D, FF), vm(FF),
        vm(rows), vm(rows), vm(rows), vm(rows),
        pltpu.VMEM((micro_count, QUADS, LENGTH, 4 * LENGTH), BF16),
        vm(rows), vm(rows), vm(rows), vm(rows), vm(rows, FF), vm(rows, FF),
        vm(rows, 128, F32), vm(rows, 128, F32),
        vm(rows), vm(rows), vm(rows), vm(rows), vm(rows, D, F32),
        vm(ROWS, D, F32), pltpu.VMEM((2, TURN, rows), BF16), pltpu.VMEM((12, 8, D), F32), vm(8, FF, F32),
        pltpu.SemaphoreType.DMA((6,)),
        pltpu.SemaphoreType.DMA((micro_count,)),
        pltpu.SemaphoreType.DMA((11, micro_count)),
        pltpu.SemaphoreType.DMA((2,)),
        pltpu.SemaphoreType.DMA((micro_count,)),
        pltpu.SemaphoreType.DMA((micro_count,)),
        pltpu.SemaphoreType.DMA((micro_count,)),
        pltpu.SemaphoreType.DMA((micro_count,)),
    ]
    return pl.pallas_call(
        functools.partial(layers_kernel, micro_count),
        out_shape=out_shape,
        in_specs=[anywhere, anywhere, scalars, scalars] + [anywhere] * 6 + [vectors] * 4,
        out_specs=[anywhere] * 4 + [vectors],
        scratch_shapes=scratch,
        compiler_params=pltpu.CompilerParams(
            collective_id=0, has_side_effects=True, vmem_limit_bytes=60 * 1024 * 1024
        ),
        cost_estimate=pl.CostEstimate(
            flops=rows * 2 * 2 * 2 * 7077888, bytes_accessed=60000000, transcendentals=rows * FF * 2
        ),
    )(tokens, cotangent, lengths, spans.T, *weights)


RING = 8
PIECES = 3
PIECE = D // RING
PANELS = (
    (0, 0), (0, 1), (0, 2), (D, 3), (2 * D, 4), (2 * D, 5),
    (2 * D, 6), (2 * D, 7), (3 * D, 8), (4 * D, 8), (5 * D, 8), (6 * D, 8),
)


def sums_kernel(
    left, right, small_in, grads_out, small_out,
    left_s, right_s, total_s, give_s, take_s, ring_s,
    tiny_s, tiny_take_s, tiny_sum_s, tiny_go_s, tiny_ring_s, tiny_own_s,
    load_sem, give_sem, take_sem, ring_send, ring_recv, round_send, round_recv, share_send, share_recv,
    tiny_sem, tiny_ring_send, tiny_ring_recv, tiny_round_send, tiny_round_recv,
):
    me = lax.axis_index("dp")
    core = lax.rem(me, 2)
    high = lax.rem(lax.div(me, 2), 2)
    depth = lax.div(me, 4)
    place = depth + high * (7 - 2 * depth)

    def device(spot, on_core):
        row = lax.div(spot, 4)
        return {"dp": 4 * (spot + row * (7 - 2 * spot)) + 2 * row + on_core}

    ahead = device(lax.rem(place + 1, RING), core)
    behind = device(lax.rem(place + RING - 1, RING), core)
    beside = device(place, 1 - core)
    targets = (ahead, behind)

    barrier = pltpu.get_barrier_semaphore()
    for peer in (ahead, behind, beside):
        pl.semaphore_signal(barrier, inc=1, device_id=peer, device_id_type=MESH)

    def block(way, step):
        return lax.rem(place - step + RING, RING) if way == 0 else lax.rem(place + step, RING)

    def late_block(way, step):
        return lax.rem(place + 1 - step + RING, RING) if way == 0 else lax.rem(place + RING - 1 + step, RING)

    def load_left(part):
        return pltpu.make_async_copy(left.at[pl.ds(part * D, D)], left_s.at[pl.ds(part * D, D)], load_sem.at[part])

    def load_right(part):
        return pltpu.make_async_copy(right.at[part], right_s.at[part], load_sem.at[7 + part])

    def remote(source, target, send, recv, peer):
        return pltpu.make_async_remote_copy(
            src_ref=source, dst_ref=target, send_sem=send, recv_sem=recv, device_id=peer, device_id_type=MESH
        )

    def give(way, step, piece):
        return remote(
            give_s.at[way, lax.rem(step, 4), piece], take_s.at[way, step, piece],
            give_sem.at[way, step, piece], take_sem.at[way, step, piece], beside,
        )

    def ring_copy(way, step, piece):
        return remote(
            take_s.at[way, step, piece], ring_s.at[way, step, piece],
            ring_send.at[way, step, piece], ring_recv.at[way, step, piece], targets[way],
        )

    def region(way, spot, piece, on_core):
        rows = pl.ds(pl.multiple_of(spot * PIECE, PIECE), PIECE)
        return grads_out.at[6 * way + 3 * on_core + piece, rows]

    def round_copy(way, step, piece):
        target = region(way, late_block(way, step), piece, core)
        return remote(
            target, target, round_send.at[way, step, piece], round_recv.at[way, step, piece], targets[way]
        )

    def round_wait(way, step, piece):
        target = region(way, late_block(way, step + 1), piece, core)
        remote(
            target, target, round_send.at[way, step, piece], round_recv.at[way, step, piece], targets[way]
        ).wait_recv()

    def share_copy(way, step, piece):
        target = region(way, late_block(way, step), piece, core)
        return remote(
            target, target, share_send.at[way, step, piece], share_recv.at[way, step, piece], beside
        )

    def share_wait(way, step, piece):
        target = region(way, late_block(way, step), piece, 1 - core)
        remote(
            target, target, share_send.at[way, step, piece], share_recv.at[way, step, piece], beside
        ).wait_recv()

    tiny_swap = remote(tiny_s, tiny_take_s, tiny_sem.at[0], tiny_sem.at[1], beside)

    def tiny_ring(step):
        return remote(
            tiny_go_s.at[step], tiny_ring_s.at[step], tiny_ring_send.at[step], tiny_ring_recv.at[step], ahead
        )

    def tiny_round(step):
        spot = late_block(0, step)
        return remote(
            tiny_own_s.at[spot], tiny_own_s.at[spot], tiny_round_send.at[step], tiny_round_recv.at[step], ahead
        )

    def tiny_round_wait(step):
        spot = late_block(0, step + 1)
        remote(
            tiny_own_s.at[spot], tiny_own_s.at[spot], tiny_round_send.at[step], tiny_round_recv.at[step], ahead
        ).wait_recv()

    loads = []
    for piece in range(PIECES):
        for way in range(2):
            for half in range(2):
                first_row, number = PANELS[6 * way + 3 * half + piece]
                for kind, part in ((load_right, number), (load_left, first_row // D)):
                    if (kind, part) not in [entry[:2] for entry in loads]:
                        loads.append((kind, part, way, piece))
    order = [(way, piece) for piece in range(PIECES) for way in range(2)]
    groups = [[kind(part) for kind, part, *spot in loads if tuple(spot) == pair] for pair in order]
    for group in groups[:2]:
        for copy in group:
            copy.start()

    for part in range(RING):
        if part * 128 < D:
            tiny_s[part] = small_in[:, part * 128 : part * 128 + 128]
        else:
            tiny_s[part] = jnp.zeros((16, 128), F32)

    pl.semaphore_wait(barrier, 3)
    tiny_swap.start()

    def product(group, way, piece, pick):
        near, far = PANELS[6 * way + piece], PANELS[6 * way + 3 + piece]
        first_row = near[0] + pick * (far[0] - near[0])
        number = near[1] + pick * (far[1] - near[1])
        blocks = []
        for step in (2 * group, 2 * group + 1):
            start = pl.multiple_of(first_row + block(way, step) * PIECE, PIECE)
            blocks.append(left_s[pl.ds(start, PIECE), :])
        return dot(jnp.concatenate(blocks, axis=0), right_s[number])

    def keep_product(group, way, piece, both):
        total_s[lax.rem(2 * group, 3), way, piece] = both[:PIECE]
        total_s[lax.rem(2 * group + 1, 3), way, piece] = both[PIECE:]

    def give_product(group, way, piece, both):
        @pl.when(group >= 2)
        def _():
            give(way, 2 * group - 4, piece).wait_send()
            give(way, 2 * group - 3, piece).wait_send()

        give_s[way, lax.rem(2 * group, 4), piece] = both[:PIECE].astype(BF16)
        give_s[way, lax.rem(2 * group + 1, 4), piece] = both[PIECE:].astype(BF16)
        give(way, 2 * group, piece).start()
        give(way, 2 * group + 1, piece).start()

    def add_piece(step, way, piece, target):
        slot = lax.rem(step, 3)
        for r0 in range(0, PIECE, SUB):
            part = slice(r0, r0 + SUB)
            whole = total_s[slot, way, piece, part] + take_s[way, step, piece, part].astype(F32)
            target[part] = whole.astype(BF16)

    def reduce_step(step, carry):
        slot = lax.rem(step, 3)
        spot = block(0, step)

        @pl.when(step < RING - 1)
        def _():
            tiny_ring(step - 1).wait_recv()
            tiny_go_s[step] = tiny_sum_s[spot] + tiny_ring_s[step - 1]
            tiny_ring(step).start()

        @pl.when(step == RING - 1)
        def _():
            tiny_ring(step - 1).wait_recv()
            tiny_own_s[spot] = tiny_sum_s[spot] + tiny_ring_s[step - 1]
            tiny_round(0).start()

        for piece in range(PIECES):
            for way in range(2):
                give(way, step, piece).wait_recv()
                ring_copy(way, step - 1, piece).wait_recv()
                for r0 in range(0, PIECE, SUB):
                    part = slice(r0, r0 + SUB)
                    total_s[slot, way, piece, part] += ring_s[way, step - 1, piece, part].astype(F32)

                @pl.when(step < RING - 1)
                def _():
                    add_piece(step, way, piece, take_s.at[way, step, piece])
                    ring_copy(way, step, piece).start()

                @pl.when(step == RING - 1)
                def _():
                    add_piece(step, way, piece, region(way, late_block(way, 0), piece, core))
                    round_copy(way, 0, piece).start()
                    share_copy(way, 0, piece).start()

                @pl.when(step < RING - 2)
                def _():
                    odd = lax.rem(step, 2)
                    group = lax.div(step, 2) + 1
                    both = product(group, way, piece, odd * core + (1 - odd) * (1 - core))

                    @pl.when(odd == 1)
                    def _():
                        keep_product(group, way, piece, both)

                    @pl.when(odd == 0)
                    def _():
                        give_product(group, way, piece, both)

        return carry

    def first_piece(way, piece):
        give(way, 0, piece).wait_recv()
        add_piece(0, way, piece, take_s.at[way, 0, piece])
        ring_copy(way, 0, piece).start()

    for number, (way, piece) in enumerate(order):
        for copy in groups[number]:
            copy.wait()
        if number + 2 < len(groups):
            for copy in groups[number + 2]:
                copy.start()
        give_product(0, way, piece, product(0, way, piece, 1 - core))
        keep_product(0, way, piece, product(0, way, piece, core))
        if number > 0:
            first_piece(*order[number - 1])
    first_piece(*order[-1])
    for way, piece in order:
        give_product(1, way, piece, product(1, way, piece, 1 - core))
    tiny_swap.wait_recv()
    tiny_sum_s[...] = tiny_s[...] + tiny_take_s[...]
    tiny_go_s[0] = tiny_sum_s[block(0, 0)]
    tiny_ring(0).start()

    lax.fori_loop(1, RING, reduce_step, 0)

    def round_step(step, carry):
        tiny_round_wait(step - 1)

        @pl.when(step < RING - 1)
        def _():
            tiny_round(step).start()

        for piece in range(PIECES):
            for way in range(2):
                round_wait(way, step - 1, piece)

                @pl.when(step < RING - 1)
                def _():
                    round_copy(way, step, piece).start()

                share_copy(way, step, piece).start()
        return carry

    lax.fori_loop(1, RING, round_step, 0)

    for part in range(D // 128):
        small_out[:, part * 128 : part * 128 + 128] = tiny_own_s[part]
    tiny_swap.wait_send()

    def finish(step, carry):
        for way in range(2):
            for piece in range(PIECES):

                @pl.when(step >= RING // 2)
                def _():
                    give(way, step, piece).wait_send()

                share_wait(way, step, piece)
                share_copy(way, step, piece).wait_send()

                @pl.when(step < RING - 1)
                def _():
                    ring_copy(way, step, piece).wait_send()
                    round_copy(way, step, piece).wait_send()

        @pl.when(step < RING - 1)
        def _():
            tiny_ring(step).wait_send()
            tiny_round(step).wait_send()

        return carry

    lax.fori_loop(0, RING, finish, 0)


def run_sums(left, right, small):
    rows = right.shape[1]
    anywhere = pl.BlockSpec(memory_space=pl.ANY)
    vectors = pl.BlockSpec(memory_space=pltpu.VMEM)

    def pieces(*lead, dtype=BF16):
        return pltpu.VMEM((*lead, PIECE, D), dtype)

    dma = pltpu.SemaphoreType.DMA
    scratch = [
        pltpu.VMEM(left.shape, BF16), pltpu.VMEM(right.shape, BF16),
        pieces(3, 2, PIECES, dtype=F32), pieces(2, 4, PIECES), pieces(2, RING, PIECES),
        pieces(2, RING - 1, PIECES),
        pltpu.VMEM((RING, 16, 128), F32), pltpu.VMEM((RING, 16, 128), F32), pltpu.VMEM((RING, 16, 128), F32),
        pltpu.VMEM((RING - 1, 16, 128), F32), pltpu.VMEM((RING - 1, 16, 128), F32), pltpu.VMEM((RING, 16, 128), F32),
        dma((16,)), dma((2, RING, PIECES)), dma((2, RING, PIECES)),
        dma((2, RING - 1, PIECES)), dma((2, RING - 1, PIECES)),
        dma((2, RING - 1, PIECES)), dma((2, RING - 1, PIECES)), dma((2, RING, PIECES)), dma((2, RING, PIECES)),
        dma((2,)), dma((RING - 1,)), dma((RING - 1,)), dma((RING - 1,)), dma((RING - 1,)),
    ]
    return pl.pallas_call(
        sums_kernel,
        out_shape=(pltpu.VMEM((12, D, D), BF16), jax.ShapeDtypeStruct((16, D), F32)),
        in_specs=[anywhere, anywhere, vectors],
        out_specs=[vectors, vectors],
        scratch_shapes=scratch,
        compiler_params=pltpu.CompilerParams(
            collective_id=1, has_side_effects=True, vmem_limit_bytes=48 * 1024 * 1024
        ),
        cost_estimate=pl.CostEstimate(flops=rows * 2 * 7077888, bytes_accessed=70000000, transcendentals=0),
    )(left, right, small)


def plain_sums(left, right, small):
    panels = [dot(left[row : row + D], right[number]).astype(BF16) for row, number in PANELS]
    return lax.psum(jnp.stack(panels), "dp"), lax.psum(small, "dp")


SLOTS = 8
CUT = D // 2


def widen_kernel(
    act, dx, grads, small, act_out, dx_out, query_out, key_out, value_out, out_out, up_out, down_out,
    bias_out, up_bias_out, gain_out, shift_out, wide_s, act_s, dx_s, out_sem, move_sem,
):
    moves_in = [
        pltpu.make_async_copy(act, act_s, move_sem.at[0]), pltpu.make_async_copy(dx, dx_s, move_sem.at[1])
    ]
    moves_out = [
        pltpu.make_async_copy(act_s, act_out.at[0], move_sem.at[0]),
        pltpu.make_async_copy(dx_s, dx_out.at[0], move_sem.at[1]),
    ]
    jobs = []
    for panel in range(12):
        for half in range(2):
            rows = pl.ds(half * CUT, CUT)
            if panel < 4:
                target = (query_out, key_out, value_out, out_out)[panel].at[0, rows]
            elif panel < 8:
                target = up_out.at[0, rows, pl.ds((panel - 4) * D, D)]
            else:
                target = down_out.at[0, pl.ds((panel - 8) * D + half * CUT, CUT)]
            jobs.append((panel, half * CUT, target))

    def store(number):
        return pltpu.make_async_copy(wide_s.at[number % SLOTS], jobs[number][2], out_sem.at[number % SLOTS])

    for move in moves_in:
        move.start()
    bias_out[0] = small[0:4]
    for panel in range(FF // D):
        up_bias_out[:, panel * D : (panel + 1) * D] = small[4 + panel : 5 + panel]
    gain_out[0] = small[8:10]
    shift_out[0] = small[10:12]
    for number in range(len(jobs)):
        slot = number % SLOTS
        panel, start, _ = jobs[number]
        if number >= SLOTS:
            store(number - SLOTS).wait()

        def turn(step, carry):
            part = pl.ds(pl.multiple_of(step * SUB, SUB), SUB)
            here = pl.ds(pl.multiple_of(start + step * SUB, SUB), SUB)
            wide_s[slot, part, :] = grads[panel, here, :].astype(F32)
            return carry

        lax.fori_loop(0, CUT // SUB, turn, 0, unroll=4)
        store(number).start()
        if number == SLOTS:
            for move_in, move_out in zip(moves_in, moves_out):
                move_in.wait()
                move_out.start()
    for number in range(len(jobs) - SLOTS, len(jobs)):
        store(number).wait()
    for move in moves_out:
        move.wait()


def widen(act, dx, grads, small):
    anywhere = pl.BlockSpec(memory_space=pl.ANY)
    vectors = pl.BlockSpec(memory_space=pltpu.VMEM)
    square = jax.ShapeDtypeStruct((1, D, D), F32)
    return pl.pallas_call(
        widen_kernel,
        out_shape=(
            jax.ShapeDtypeStruct((1, *act.shape), BF16), jax.ShapeDtypeStruct((1, *dx.shape), F32),
            square, square, square, square,
            jax.ShapeDtypeStruct((1, D, FF), F32), jax.ShapeDtypeStruct((1, FF, D), F32),
            jax.ShapeDtypeStruct((1, 4, D), F32), jax.ShapeDtypeStruct((1, FF), F32),
            jax.ShapeDtypeStruct((1, 2, D), F32), jax.ShapeDtypeStruct((1, 2, D), F32),
        ),
        in_specs=[anywhere, anywhere, vectors, vectors],
        out_specs=[anywhere] * 8 + [vectors] * 4,
        scratch_shapes=[
            pltpu.VMEM((SLOTS, CUT, D), F32),
            pltpu.VMEM(act.shape, BF16), pltpu.VMEM(dx.shape, F32),
            pltpu.SemaphoreType.DMA((SLOTS,)), pltpu.SemaphoreType.DMA((2,)),
        ],
        compiler_params=pltpu.CompilerParams(vmem_limit_bytes=46 * 1024 * 1024),
        cost_estimate=pl.CostEstimate(flops=7077888, bytes_accessed=42467328, transcendentals=0),
    )(act, dx, grads, small)


def per_device(grid, tokens, cotangent, lengths, spans, *weights):
    act, dx, left, right, small = run_layers(tokens, cotangent, lengths, spans, *weights)
    grads, small = (run_sums if grid else plain_sums)(left, right, small)
    grads = pltpu.with_memory_space_constraint(grads, pltpu.VMEM)
    return widen(act, dx, grads, small)


def solution(mesh):
    in_specs = (
        P("dp", None), P("dp", None), P("dp"), P("dp", None),
        P("section", None, None), P("section", None, None), P("section", None, None),
        P("section", None, None), P("section", None, None), P("section", None, None),
        P("section", None, None), P("section", None), P("section", None, None), P("section", None, None),
    )
    out_specs = (
        P("section", "dp", None), P("section", "dp", None),
        P("section", None, None), P("section", None, None), P("section", None, None),
        P("section", None, None), P("section", None, None), P("section", None, None),
        P("section", None, None), P("section", None), P("section", None, None), P("section", None, None),
    )
    part = functools.partial(per_device, mesh.shape["dp"] == 2 * RING)
    return jax.shard_map(part, mesh=mesh, in_specs=in_specs, out_specs=out_specs, check_vma=False)
```
